32 devices in a mesh: dp: 4 (over y, x), ctx: 8 (over z, core).
Axes of the slice: x: 2, y: 2, z: 4, core: 2. Of those that a mesh axis runs over, the one named last changes fastest.
Arguments:
- gate_in: bfloat16 [4, 1024, 2048], P('dp', 'ctx'), may hold values from -6 to 6
- key_in: bfloat16 [4, 1024, 2048], P('dp', 'ctx'), may hold values from -6 to 6
- value_in: bfloat16 [4, 1024, 2048], P('dp', 'ctx'), may hold values from -6 to 6
- cotangent: bfloat16 [4, 1024, 2048], P('dp', 'ctx'), may hold values from -6 to 6
- doc_starts: int32 [4, 3], P('dp'), may hold values from 0 to 768, as said below
- filters: bfloat16 [128, 128], replicated, may hold values from -0.5 to 0.5
Outputs:
- output: bfloat16 [4, 1024, 2048], P('dp', 'ctx')
- grad_query: bfloat16 [4, 1024, 2048], P('dp', 'ctx')
- grad_key: bfloat16 [4, 1024, 2048], P('dp', 'ctx')
- grad_value: bfloat16 [4, 1024, 2048], P('dp', 'ctx')
- filter_grad: float32 [128, 128], replicated
The draws below stay inside these ranges and needn't reach their ends.
Inputs may be any that keep to these rules, and one draw needn't show every extreme that they name: `doc_starts`: each row holds 3 strictly rising multiples of 128; the first is 0 and the last is 768.
All inputs are finite; a program needn't handle non-finite values.
Results may differ from the reference program's by a relative error of at most 0.0049.
Values may be sent and summed in bfloat16 or wider, within the bound.
No kernel may reach another device: no remote copies, remote signals or barrier semaphores. Data moves between devices by JAX's collectives and lax.ppermute only.
A program may use at most 192 MiB of HBM per device.

```python
import jax
import jax.numpy as jnp
from jax import lax

D = 2048
TAPS = 128
ROWS_DEV = 128
FILTERS = 128
SEQ = 1024
DOCS = 3
N_DP = 4
N_CTX = 8


def draw_doc_starts(key, part):
    tile_total = SEQ // TAPS
    per_device = ROWS_DEV // TAPS
    tile_ids = jnp.arange(tile_total, dtype=jnp.int32)
    allowed = (tile_ids >= 2) & (tile_ids <= tile_total - 3)
    allowed = allowed & (tile_ids != per_device * (N_CTX // 2))
    allowed = allowed & (tile_ids != per_device * (N_CTX // 2 + 1))

    def one_row(index):
        subkey = jax.random.fold_in(key, index)
        ranks = jax.random.permutation(subkey, tile_total).astype(jnp.int32) + 1
        scores = jnp.where(allowed, ranks, 0).astype(jnp.int32)
        picked = lax.top_k(scores, DOCS - 2)[1].astype(jnp.int32)
        inner = jnp.sort(picked)
        head = jnp.zeros((1,), jnp.int32)
        tail = jnp.full((1,), tile_total - 2, jnp.int32)
        return jnp.concatenate([head, inner, tail]) * TAPS
    return jax.vmap(one_row)(jnp.arange(N_DP, dtype=jnp.int32)).astype(jnp.int32)


def block_levels(key, dims, cuts, low, top_value):
    def one(position, blocks):
        draws = jax.random.uniform(jax.random.fold_in(jax.random.fold_in(key, 6), position), (blocks,), jnp.float32, low / len(cuts), top_value / len(cuts))
        return jnp.repeat(jnp.exp(draws), dims[position] // blocks).reshape((-1,) + (1,) * (len(dims) - position - 1))

    factor_of = one(*cuts[0])
    for cut in cuts[1:]:
        factor_of = factor_of * one(*cut)
    return factor_of


def centred(rng, extent, scale, most, split=(), held_as=jnp.bfloat16):
    values = jax.random.normal(rng, extent, jnp.float32) * scale
    if len(split) > 0:
        values = block_levels(rng, extent, split, -0.22, 0.18) * values
    return jnp.clip(values, min=-most, max=most).astype(held_as)


def setup_inputs(seed: int = 0) -> dict:
    arg_keys = jax.random.split(jax.random.key(seed), 7)
    gate_in = centred(arg_keys[0], (N_DP, SEQ, D), 1.0, 6.0, ((0, 4), (1, 8)))
    key_in = centred(arg_keys[1], (N_DP, SEQ, D), 1.0, 6.0, ((0, 4), (1, 8)))
    value_in = centred(arg_keys[2], (N_DP, SEQ, D), 1.0, 6.0, ((0, 4), (1, 8)))
    cotangent = centred(arg_keys[3], (N_DP, SEQ, D), 1.0, 6.0, ((0, 4), (1, 8)))
    doc_starts = draw_doc_starts(jax.random.fold_in(arg_keys[6], 71), 0)
    filters = centred(arg_keys[5], (FILTERS, TAPS), TAPS ** -0.5, 0.5)
    return dict(gate_in=gate_in, key_in=key_in, value_in=value_in, cotangent=cotangent, doc_starts=doc_starts, filters=filters)


def build_tiles(filters):
    group_count = filters.shape[0]
    tap_count = filters.shape[1]
    zero_block = jnp.zeros((group_count, tap_count), filters.dtype)
    diag_line = jnp.concatenate([zero_block, filters[:, ::-1], zero_block], axis=1)
    flattened = jnp.tile(diag_line, (1, tap_count))
    stride = 3 * tap_count - 1
    flattened = flattened[:, tap_count - 1: tap_count - 1 + tap_count * stride]
    return flattened.reshape(group_count, tap_count, stride)[:, :, :2 * tap_count]


def diagonal_sums(tile_grads):
    group_count = tile_grads.shape[0]
    tap_count = tile_grads.shape[1]
    stride = 3 * tap_count - 1
    padded = jnp.pad(tile_grads, ((0, 0), (0, 0), (0, stride - 2 * tap_count)))
    flattened = padded.reshape(group_count, tap_count * stride)
    flattened = jnp.pad(flattened, ((0, 0), (tap_count - 1, 1)))
    diag_line = jnp.sum(flattened.reshape(group_count, tap_count, 3 * tap_count), axis=1)
    return diag_line[:, tap_count:2 * tap_count][:, ::-1]


def keep_mask(starts_row, first_block, block_total, tap_count):
    block_ids = first_block + jnp.arange(block_total, dtype=jnp.int32)
    is_start = jnp.any(starts_row[None, :] == block_ids[:, None] * tap_count, axis=1)
    return jnp.where(is_start, 0.0, 1.0).astype(jnp.float32)


def reference(gate_in, key_in, value_in, cotangent, doc_starts, filters):
    toeplitz = build_tiles(filters).astype(jnp.float32)
    tap_count = filters.shape[1]
    group_count = filters.shape[0]
    channels = gate_in.shape[2]
    group_width = channels // group_count
    seq_len = gate_in.shape[1]
    block_count = seq_len // tap_count
    highest = lax.Precision.HIGHEST

    def one_sequence(packed):
        gate_local, key_local, value_local, upstream, starts_row = packed
        keep_vals = keep_mask(starts_row, 0, block_count, tap_count)
        product = (key_local.astype(jnp.float32) * value_local.astype(jnp.float32)).astype(jnp.bfloat16)
        shaped = product.reshape(block_count, tap_count, group_count, group_width)
        earlier = jnp.concatenate([jnp.zeros((1, tap_count, group_count, group_width), jnp.bfloat16), shaped[:-1]], axis=0)
        earlier = earlier * keep_vals[:, None, None, None].astype(jnp.bfloat16)
        window = jnp.concatenate([earlier, shaped], axis=1).astype(jnp.float32)
        conv_out = jnp.einsum("ftj,bjfc->btfc", toeplitz, window, precision=highest).reshape(seq_len, channels)
        gated = (gate_local.astype(jnp.float32) * conv_out).astype(jnp.bfloat16)
        grad_query = (upstream.astype(jnp.float32) * conv_out).astype(jnp.bfloat16)
        grad_conv = (upstream.astype(jnp.float32) * gate_local.astype(jnp.float32)).astype(jnp.bfloat16)
        grad_blocks = grad_conv.reshape(block_count, tap_count, group_count, group_width).astype(jnp.float32)
        spread = jnp.einsum("ftj,btfc->bjfc", toeplitz, grad_blocks, precision=highest)
        current = spread[:, tap_count:]
        carried = spread[:, :tap_count] * keep_vals[:, None, None, None]
        following = jnp.concatenate([carried[1:], jnp.zeros((1, tap_count, group_count, group_width), jnp.float32)], axis=0)
        grad_mixed = (current + following).reshape(seq_len, channels)
        grad_key = (grad_mixed * value_local.astype(jnp.float32)).astype(jnp.bfloat16)
        grad_value = (grad_mixed * key_local.astype(jnp.float32)).astype(jnp.bfloat16)
        tile_grads = jnp.einsum("btfc,bjfc->ftj", grad_blocks, window, precision=highest)
        return gated, grad_query, grad_key, grad_value, tile_grads

    results = lax.map(one_sequence, (gate_in, key_in, value_in, cotangent, doc_starts))
    filter_grad = diagonal_sums(jnp.sum(results[4], axis=0))
    return (results[0], results[1], results[2], results[3], filter_grad)
```

```python
import functools

import jax
import jax.numpy as jnp
from jax import lax
from jax.experimental import pallas as pl
from jax.experimental.pallas import tpu as pltpu
from jax.sharding import PartitionSpec as P

LANES = 128
ROW_BLOCK = 32
MIB = 1024 * 1024


def iota(shape, dim):
    return lax.broadcasted_iota(jnp.int32, shape, dim)


def exchange(array, axis, first):
    size = lax.axis_size(axis)
    pairs = []
    for low in range(first, size - 1, 2):
        pairs += [(low, low + 1), (low + 1, low)]
    return lax.ppermute(array, axis, pairs)


def sum_over(array, axis):
    size = lax.axis_size(axis)
    step = 1
    while step < size:
        array = array + lax.ppermute(array, axis, [(i, i ^ step) for i in range(size)])
        step *= 2
    return array


def reversal(taps):
    flip = iota((taps, taps), 0) + iota((taps, taps), 1) == taps - 1
    return jnp.where(flip, 1.0, 0.0).astype(jnp.bfloat16)


def gates_kernel(
    flags_ref, q_ref, k_ref, v_ref, ct_ref, u_ref, dy_ref, near_ref, far_ref
):
    taps = u_ref.shape[0]
    odd = flags_ref[0] == 1
    u = (k_ref[...].astype(jnp.float32) * v_ref[...].astype(jnp.float32)).astype(jnp.bfloat16)
    dy = (ct_ref[...].astype(jnp.float32) * q_ref[...].astype(jnp.float32)).astype(jnp.bfloat16)
    dy = jnp.dot(reversal(taps), dy, preferred_element_type=jnp.float32).astype(jnp.bfloat16)
    u_ref[...] = u
    dy_ref[...] = dy
    onward = jnp.where(flags_ref[2] == 1, jnp.zeros_like(u), u)
    backward = jnp.where(flags_ref[1] == 1, jnp.zeros_like(dy), dy)
    near_ref[...] = jnp.where(odd, backward, onward)
    far_ref[...] = jnp.where(odd, onward, backward)


def gates(flags, q, k, v, ct):
    taps, channels = q.shape
    steps = 4
    spec = pl.BlockSpec((taps, channels // steps), lambda i, flags_ref: (0, i))
    shape = jax.ShapeDtypeStruct((taps, channels), jnp.bfloat16)
    return pl.pallas_call(
        gates_kernel,
        grid_spec=pltpu.PrefetchScalarGridSpec(
            num_scalar_prefetch=1, grid=(steps,), in_specs=[spec] * 4, out_specs=[spec] * 4
        ),
        out_shape=[shape] * 4,
        name="gates",
        cost_estimate=pl.CostEstimate(
            flops=2 * taps * taps * channels, bytes_accessed=16 * taps * channels, transcendentals=0
        ),
        compiler_params=pltpu.CompilerParams(vmem_limit_bytes=32 * MIB),
    )(flags, q, k, v, ct)


def circulant_kernel(filters_ref, out_ref):
    count, taps = filters_ref.shape
    flip = jnp.where((iota((taps, taps), 0) + iota((taps, taps), 1)) % taps == 0, 1.0, 0.0)
    lines = jnp.dot(filters_ref[...], flip.astype(jnp.bfloat16), preferred_element_type=jnp.float32)
    for f in range(count):
        tile = jnp.broadcast_to(lines[f : f + 1], (taps, taps))
        out_ref[f] = pltpu.roll(tile, 0, 1, stride=1, stride_axis=0).astype(jnp.bfloat16)


def circulants(filters):
    count, taps = filters.shape
    block = 16
    return pl.pallas_call(
        circulant_kernel,
        grid=(count // block,),
        in_specs=[pl.BlockSpec((block, taps), lambda i: (i, 0))],
        out_specs=pl.BlockSpec((block, taps, taps), lambda i: (i, 0, 0)),
        out_shape=jax.ShapeDtypeStruct((count, taps, taps), jnp.bfloat16),
        name="circulants",
        cost_estimate=pl.CostEstimate(
            flops=count * taps * taps * 8, bytes_accessed=2 * count * taps * taps, transcendentals=0
        ),
        compiler_params=pltpu.CompilerParams(vmem_limit_bytes=32 * MIB),
    )(filters)


def filter_grad_kernel(width, flags_ref, u_ref, dy_ref, near_ref, far_ref, out_ref):
    taps, channels = u_ref.shape
    per_group = LANES // width
    odd = flags_ref[0] == 1
    lane_filter = iota((ROW_BLOCK, LANES), 1) // width
    fold = iota((ROW_BLOCK, taps), 1) + iota((ROW_BLOCK, taps), 0) < ROW_BLOCK
    rows = []
    for group in range(channels // LANES):
        cols = pl.ds(group * LANES, LANES)
        before = jnp.where(odd, near_ref[:, cols], far_ref[:, cols])
        window = jnp.concatenate([before, u_ref[:, cols]], axis=0)
        dy = dy_ref[:, cols]
        left, right = [], []
        for at in range(0, taps, ROW_BLOCK):
            piece = dy[at : at + ROW_BLOCK]
            left.append(
                jnp.concatenate(
                    [jnp.where(lane_filter == i, piece, 0) for i in range(per_group)], axis=0
                )
            )
            right.append(window[taps - ROW_BLOCK - at : 2 * taps - at])
        left = jnp.concatenate(left, axis=1)
        right = jnp.concatenate(right, axis=1)
        product = lax.dot_general(
            left, right, (((1,), (1,)), ((), ())), preferred_element_type=jnp.float32
        )
        for i in range(per_group):
            tile = product[i * ROW_BLOCK : (i + 1) * ROW_BLOCK]
            high = jnp.concatenate(
                [tile[:, taps:], jnp.zeros((ROW_BLOCK, taps - ROW_BLOCK), jnp.float32)], axis=1
            )
            tile = jnp.where(fold, high, tile[:, :taps])
            tile = pltpu.roll(tile, taps - ROW_BLOCK + 1, 1, stride=1, stride_axis=0)
            rows.append(jnp.sum(tile, axis=0, keepdims=True))
    lines = jnp.concatenate(rows, axis=0)
    flip = jnp.where((iota((taps, taps), 0) + iota((taps, taps), 1)) % taps == 0, 1.0, 0.0)
    out_ref[...] = jnp.dot(
        lines, flip, preferred_element_type=jnp.float32, precision=lax.Precision.HIGHEST
    )


def filter_gradient(flags, u, dy, near, far, width):
    taps, channels = u.shape
    steps = 4
    block = channels // steps
    filters = block // width
    spec = pl.BlockSpec((taps, block), lambda i, flags_ref: (0, i))
    return pl.pallas_call(
        functools.partial(filter_grad_kernel, width),
        grid_spec=pltpu.PrefetchScalarGridSpec(
            num_scalar_prefetch=1,
            grid=(steps,),
            in_specs=[spec] * 4,
            out_specs=pl.BlockSpec((filters, taps), lambda i, flags_ref: (i, 0)),
        ),
        out_shape=jax.ShapeDtypeStruct((channels // width, taps), jnp.float32),
        name="filter_gradient",
        cost_estimate=pl.CostEstimate(
            flops=2 * (channels // width) * taps * taps * 256,
            bytes_accessed=8 * taps * channels,
            transcendentals=0,
        ),
        compiler_params=pltpu.CompilerParams(vmem_limit_bytes=32 * MIB),
    )(flags, u, dy, near, far)


def outputs_kernel(
    width, flags_ref, q_ref, k_ref, v_ref, ct_ref, u_ref, dy_ref, near_ref, far_ref, tiles_ref,
    out_ref, grad_q_ref, grad_k_ref, grad_v_ref,
):
    taps, channels = u_ref.shape
    per_group = LANES // width
    odd = flags_ref[0] == 1
    reverse = reversal(taps)
    current = iota((taps, taps), 1) <= iota((taps, taps), 0)
    lane_filter = (iota((taps, 2 * LANES), 1) % LANES) // width

    def flipped(array):
        return jnp.dot(reverse, array, preferred_element_type=jnp.float32)

    for group in range(channels // LANES):
        cols = pl.ds(group * LANES, LANES)
        near = near_ref[:, cols]
        far = far_ref[:, cols]
        before = jnp.where(odd, near, far)
        after = jnp.where(odd, far, near)
        k = k_ref[:, cols]
        v = v_ref[:, cols]
        window = jnp.concatenate(
            [
                jnp.concatenate([before, after], axis=1),
                jnp.concatenate([u_ref[:, cols], dy_ref[:, cols]], axis=1),
            ],
            axis=0,
        )
        total = jnp.zeros((taps, 2 * LANES), jnp.float32)
        for i in range(per_group):
            tile = tiles_ref[group * per_group + i]
            line = jnp.concatenate(
                [jnp.where(current, 0, tile), jnp.where(current, tile, 0)], axis=1
            )
            part = jnp.dot(line, window, preferred_element_type=jnp.float32)
            total = jnp.where(lane_filter == i, part, total)
        y = total[:, :LANES]
        out_ref[:, cols] = (q_ref[:, cols].astype(jnp.float32) * y).astype(jnp.bfloat16)
        grad_q_ref[:, cols] = (ct_ref[:, cols].astype(jnp.float32) * y).astype(jnp.bfloat16)
        mixed = total[:, LANES:]
        turned = flipped(jnp.concatenate([v, k], axis=1))
        grads = (turned * jnp.concatenate([mixed, mixed], axis=1)).astype(jnp.bfloat16)
        grads = flipped(grads).astype(jnp.bfloat16)
        grad_k_ref[:, cols] = grads[:, :LANES]
        grad_v_ref[:, cols] = grads[:, LANES:]


def outputs(flags, q, k, v, ct, u, dy, near, far, tiles, width):
    taps, channels = u.shape
    steps = 4
    block = channels // steps
    spec = pl.BlockSpec((taps, block), lambda i, flags_ref: (0, i))
    tile_spec = pl.BlockSpec((block // width, taps, taps), lambda i, flags_ref: (i, 0, 0))
    shape = jax.ShapeDtypeStruct((taps, channels), jnp.bfloat16)
    return pl.pallas_call(
        functools.partial(outputs_kernel, width),
        grid_spec=pltpu.PrefetchScalarGridSpec(
            num_scalar_prefetch=1,
            grid=(steps,),
            in_specs=[spec] * 8 + [tile_spec],
            out_specs=[spec] * 4,
        ),
        out_shape=[shape] * 4,
        name="outputs",
        cost_estimate=pl.CostEstimate(
            flops=4 * (channels // width) * taps * taps * 256,
            bytes_accessed=24 * taps * channels + 2 * taps * taps * (channels // width),
            transcendentals=0,
        ),
        compiler_params=pltpu.CompilerParams(vmem_limit_bytes=48 * MIB),
    )(flags, q, k, v, ct, u, dy, near, far, tiles)


def per_device(gate_in, key_in, value_in, cotangent, doc_starts, filters):
    taps = filters.shape[1]
    width = gate_in.shape[2] // filters.shape[0]
    assert gate_in.shape[1] == taps
    q, k, v, ct = gate_in[0], key_in[0], value_in[0], cotangent[0]
    block = lax.axis_index("ctx")
    begins = [jnp.any(doc_starts[0] == at * taps) for at in (block, block + 1)]
    flags = jnp.stack([block % 2] + [flag.astype(jnp.int32) for flag in begins])
    u, dy, near, far = gates(flags, q, k, v, ct)
    far = exchange(far, "ctx", 1)
    near = exchange(near, "ctx", 0)
    tiles = circulants(filters)
    filter_grad = filter_gradient(flags, u, dy, near, far, width)
    filter_grad = sum_over(sum_over(filter_grad, "ctx"), "dp")
    results = outputs(flags, q, k, v, ct, u, dy, near, far, tiles, width)
    return tuple(array[None] for array in results) + (filter_grad,)


def solution(mesh):
    split = P("dp", "ctx", None)
    return jax.shard_map(
        per_device,
        mesh=mesh,
        in_specs=(split, split, split, split, P("dp", None), P()),
        out_specs=(split, split, split, split, P()),
        check_vma=False,
    )
```

```python
import functools

import jax
import jax.numpy as jnp
from jax import lax
from jax.experimental import pallas as pl
from jax.experimental.pallas import tpu as pltpu
from jax.sharding import PartitionSpec as P

LANES = 128
ROW_BLOCK = 32
MIB = 1024 * 1024
CHUNKS = 4
PIECES = 4
VMEM = pl.BlockSpec(memory_space=pltpu.VMEM)


def iota(shape, dim):
    return lax.broadcasted_iota(jnp.int32, shape, dim)


def exchange(array, axis, first):
    size = lax.axis_size(axis)
    pairs = []
    for low in range(first, size - 1, 2):
        pairs += [(low, low + 1), (low + 1, low)]
    return lax.ppermute(array, axis, pairs)


def sum_over(array, axis):
    size = lax.axis_size(axis)
    step = 1
    while step < size:
        array = array + lax.ppermute(array, axis, [(i, i ^ step) for i in range(size)])
        step *= 2
    return array


def reversal(taps):
    flip = iota((taps, taps), 0) + iota((taps, taps), 1) == taps - 1
    return jnp.where(flip, 1.0, 0.0).astype(jnp.bfloat16)


def gates_kernel(
    starts_ref, q_hbm, k_hbm, v_hbm, ct_hbm,
    u_ref, dy_ref, near_1_ref, far_1_ref, near_2_ref, far_2_ref, held, sems,
):
    taps, channels = u_ref.shape
    half = channels // 2
    block = channels // CHUNKS
    copies = []
    for c in range(CHUNKS):
        cols = pl.ds(c * block, block)
        for a, source in enumerate((k_hbm, v_hbm, q_hbm, ct_hbm)):
            copy = pltpu.make_async_copy(source.at[:, cols], held.at[a, :, cols], sems.at[c, a])
            copy.start()
            copies.append(copy)
    here = lax.axis_index("ctx")
    odd = here % 2 == 1
    begins, ends = here < 0, here < 0
    for d in range(starts_ref.shape[0]):
        begins = jnp.logical_or(begins, starts_ref[d] == here * taps)
        ends = jnp.logical_or(ends, starts_ref[d] == (here + 1) * taps)
    reverse = reversal(taps)
    for c in range(CHUNKS):
        cols = pl.ds(c * block, block)
        for copy in copies[4 * c : 4 * c + 4]:
            copy.wait()
        k, v, q, ct = [held[a, :, cols].astype(jnp.float32) for a in range(4)]
        u = (k * v).astype(jnp.bfloat16)
        dy = (ct * q).astype(jnp.bfloat16)
        dy = jnp.dot(reverse, dy, preferred_element_type=jnp.float32).astype(jnp.bfloat16)
        u_ref[:, cols] = u
        dy_ref[:, cols] = dy
        onward = jnp.where(ends, jnp.zeros_like(u), u)
        backward = jnp.where(begins, jnp.zeros_like(dy), dy)
        first = c * block < half
        sent = pl.ds(c * block % half, block)
        near_u, far_u = (near_1_ref, far_1_ref) if first else (near_2_ref, far_2_ref)
        near_dy, far_dy = (near_2_ref, far_2_ref) if first else (near_1_ref, far_1_ref)

        @pl.when(odd)
        def _():
            far_u[:, sent] = onward
            near_dy[:, sent] = backward

        @pl.when(jnp.logical_not(odd))
        def _():
            near_u[:, sent] = onward
            far_dy[:, sent] = backward


def gates(starts, q, k, v, ct):
    taps, channels = q.shape
    whole = jax.ShapeDtypeStruct((taps, channels), jnp.bfloat16)
    part = jax.ShapeDtypeStruct((taps, channels // 2), jnp.bfloat16)
    return pl.pallas_call(
        gates_kernel,
        in_specs=[pl.BlockSpec(memory_space=pltpu.SMEM)] + [pl.BlockSpec(memory_space=pltpu.HBM)] * 4,
        out_specs=[VMEM] * 6,
        out_shape=[whole] * 2 + [part] * 4,
        scratch_shapes=[
            pltpu.VMEM((4, taps, channels), jnp.bfloat16),
            pltpu.SemaphoreType.DMA((CHUNKS, 4)),
        ],
        name="gates",
        cost_estimate=pl.CostEstimate(
            flops=2 * taps * taps * channels, bytes_accessed=16 * taps * channels, transcendentals=0
        ),
        compiler_params=pltpu.CompilerParams(vmem_limit_bytes=51 * MIB),
    )(starts, q, k, v, ct)


def circulant_kernel(filters_ref, out_ref):
    count, taps = filters_ref.shape
    flip = jnp.where((iota((taps, taps), 0) + iota((taps, taps), 1)) % taps == 0, 1.0, 0.0)
    lines = jnp.dot(filters_ref[...], flip.astype(jnp.bfloat16), preferred_element_type=jnp.float32)
    current = iota((taps, taps), 1) <= iota((taps, taps), 0)
    for f in range(count):
        tile = jnp.broadcast_to(lines[f : f + 1], (taps, taps))
        tile = pltpu.roll(tile, 0, 1, stride=1, stride_axis=0)
        out_ref[f, :, :taps] = jnp.where(current, 0.0, tile).astype(jnp.bfloat16)
        out_ref[f, :, taps:] = jnp.where(current, tile, 0.0).astype(jnp.bfloat16)


def circulants(filters):
    count, taps = filters.shape
    return pl.pallas_call(
        circulant_kernel,
        in_specs=[VMEM],
        out_specs=VMEM,
        out_shape=jax.ShapeDtypeStruct((count, taps, 2 * taps), jnp.bfloat16),
        name="circulants",
        cost_estimate=pl.CostEstimate(
            flops=count * taps * taps * 64, bytes_accessed=4 * count * taps * taps, transcendentals=0
        ),
        compiler_params=pltpu.CompilerParams(vmem_limit_bytes=16 * MIB),
    )(filters)


def filter_grad_kernel(width, u_ref, dy_ref, near_ref, far_ref, tiles_ref, out_ref):
    del tiles_ref
    taps, channels = u_ref.shape
    half = channels // 2
    per_group = LANES // width
    odd = lax.axis_index("ctx") % 2 == 1
    lane_filter = iota((ROW_BLOCK, LANES), 1) // width
    fold = iota((ROW_BLOCK, taps), 1) + iota((ROW_BLOCK, taps), 0) < ROW_BLOCK
    rows = []
    for group in range(channels // LANES):
        cols = pl.ds(group * LANES, LANES)
        sent = pl.ds(group * LANES % half, LANES)
        near, far = near_ref[:, sent], far_ref[:, sent]
        if group * LANES < half:
            moving, fixed, other = dy_ref[:, cols], u_ref[:, cols], jnp.where(odd, near, far)
        else:
            moving, fixed, other = u_ref[:, cols], dy_ref[:, cols], jnp.where(odd, far, near)
        window = jnp.concatenate([other, fixed], axis=0)
        left, right = [], []
        for at in range(0, taps, ROW_BLOCK):
            piece = moving[at : at + ROW_BLOCK]
            left.append(
                jnp.concatenate(
                    [jnp.where(lane_filter == i, piece, 0) for i in range(per_group)], axis=0
                )
            )
            right.append(window[taps - ROW_BLOCK - at : 2 * taps - at])
        left = jnp.concatenate(left, axis=1)
        right = jnp.concatenate(right, axis=1)
        product = lax.dot_general(
            left, right, (((1,), (1,)), ((), ())), preferred_element_type=jnp.float32
        )
        for i in range(per_group):
            tile = product[i * ROW_BLOCK : (i + 1) * ROW_BLOCK]
            high = jnp.concatenate(
                [tile[:, taps:], jnp.zeros((ROW_BLOCK, taps - ROW_BLOCK), jnp.float32)], axis=1
            )
            tile = jnp.where(fold, high, tile[:, :taps])
            tile = pltpu.roll(tile, taps - ROW_BLOCK + 1, 1, stride=1, stride_axis=0)
            rows.append(jnp.sum(tile, axis=0, keepdims=True))
    lines = jnp.concatenate(rows, axis=0)
    flip = jnp.where((iota((taps, taps), 0) + iota((taps, taps), 1)) % taps == 0, 1.0, 0.0)
    out_ref[...] = jnp.dot(
        lines, flip, preferred_element_type=jnp.float32, precision=lax.Precision.HIGHEST
    )


def filter_gradient(u, dy, near, far, tiles, width):
    taps, channels = u.shape
    return pl.pallas_call(
        functools.partial(filter_grad_kernel, width),
        in_specs=[VMEM] * 4 + [pl.BlockSpec(memory_space=pl.ANY)],
        out_specs=VMEM,
        out_shape=jax.ShapeDtypeStruct((channels // width, taps), jnp.float32),
        name="filter_gradient",
        cost_estimate=pl.CostEstimate(
            flops=2 * (channels // width) * taps * taps * 256,
            bytes_accessed=8 * taps * channels,
            transcendentals=0,
        ),
        compiler_params=pltpu.CompilerParams(vmem_limit_bytes=16 * MIB),
    )(u, dy, near, far, tiles)


def outputs_kernel(
    width, base, first, q_ref, k_ref, v_ref, ct_ref, u_ref, dy_ref,
    near_1_ref, far_1_ref, near_2_ref, far_2_ref, tiles_ref, *rest,
):
    out_ref, grad_q_ref, grad_k_ref, grad_v_ref = rest[-4:]
    taps, channels = out_ref.shape
    half = u_ref.shape[1] // 2
    per_group = LANES // width
    odd = lax.axis_index("ctx") % 2 == 1
    reverse = reversal(taps)
    lane_filter = (iota((taps, 2 * LANES), 1) % LANES) // width
    base = base + pl.program_id(0) * channels

    def flipped(array):
        return jnp.dot(reverse, array, preferred_element_type=jnp.float32)

    for group in range(channels // LANES):
        own = pl.ds(group * LANES, LANES)
        at = pl.multiple_of(base + group * LANES, LANES)
        cols = pl.ds(at, LANES)
        sent = pl.ds(at if first else pl.multiple_of(at - half, LANES), LANES)
        near_1, far_1 = near_1_ref[:, sent], far_1_ref[:, sent]
        near_2, far_2 = near_2_ref[:, sent], far_2_ref[:, sent]
        if first:
            before, after = jnp.where(odd, near_1, far_1), jnp.where(odd, far_2, near_2)
        else:
            before, after = jnp.where(odd, near_2, far_2), jnp.where(odd, far_1, near_1)
        window = jnp.concatenate(
            [
                jnp.concatenate([before, after], axis=1),
                jnp.concatenate([u_ref[:, cols], dy_ref[:, cols]], axis=1),
            ],
            axis=0,
        )
        tiles = tiles_ref[pl.ds(at // width, per_group)]
        parts = jnp.dot(
            tiles.reshape(per_group * taps, 2 * taps), window, preferred_element_type=jnp.float32
        )
        total = parts[:taps]
        for i in range(1, per_group):
            total = jnp.where(lane_filter == i, parts[i * taps : (i + 1) * taps], total)
        y = total[:, :LANES]
        out_ref[:, own] = (q_ref[:, cols].astype(jnp.float32) * y).astype(jnp.bfloat16)
        grad_q_ref[:, own] = (ct_ref[:, cols].astype(jnp.float32) * y).astype(jnp.bfloat16)
        mixed = total[:, LANES:]
        turned = flipped(jnp.concatenate([v_ref[:, cols], k_ref[:, cols]], axis=1))
        grads = (turned * jnp.concatenate([mixed, mixed], axis=1)).astype(jnp.bfloat16)
        grads = flipped(grads).astype(jnp.bfloat16)
        grad_k_ref[:, own] = grads[:, :LANES]
        grad_v_ref[:, own] = grads[:, LANES:]


def outputs(q, k, v, ct, u, dy, halos, tiles, width):
    taps, channels = u.shape
    part = channels // PIECES
    steps = 2
    shape = jax.ShapeDtypeStruct((taps, channels), jnp.bfloat16)
    results = ()
    for piece in range(PIECES):
        spec = pl.BlockSpec((taps, part // steps), lambda i, piece=piece: (0, piece * steps + i))
        operands = (q, k, v, ct, u, dy, *halos, tiles)
        results = pl.pallas_call(
            functools.partial(
                outputs_kernel, width, piece * part, piece * part < channels // 2
            ),
            grid=(steps,),
            in_specs=[VMEM] * len(operands) + [pl.BlockSpec(memory_space=pl.ANY)] * len(results),
            out_specs=[spec] * 4,
            out_shape=[shape] * 4,
            input_output_aliases={len(operands) + i: i for i in range(len(results))},
            name=f"outputs_{piece}",
            cost_estimate=pl.CostEstimate(
                flops=16 * (part // width) * taps * taps * 256,
                bytes_accessed=24 * taps * part,
                transcendentals=0,
            ),
            compiler_params=pltpu.CompilerParams(vmem_limit_bytes=16 * MIB),
        )(*operands, *results)
    return results


def per_device(gate_in, key_in, value_in, cotangent, doc_starts, filters):
    taps = filters.shape[1]
    width = gate_in.shape[2] // filters.shape[0]
    assert gate_in.shape[1] == taps
    q, k, v, ct = gate_in[0], key_in[0], value_in[0], cotangent[0]
    u, dy, near_1, far_1, near_2, far_2 = gates(doc_starts[0], q, k, v, ct)
    far_1 = exchange(far_1, "ctx", 1)
    near_1 = exchange(near_1, "ctx", 0)
    far_2 = exchange(far_2, "ctx", 1)
    near_2 = exchange(near_2, "ctx", 0)
    tiles = circulants(filters)
    filter_grad = filter_gradient(u, dy, near_1, far_1, tiles, width)
    filter_grad = sum_over(sum_over(filter_grad, "ctx"), "dp")
    results = outputs(q, k, v, ct, u, dy, (near_1, far_1, near_2, far_2), tiles, width)
    return tuple(array[None] for array in results) + (filter_grad,)


def solution(mesh):
    split = P("dp", "ctx", None)
    return jax.shard_map(
        per_device,
        mesh=mesh,
        in_specs=(split, split, split, split, P("dp", None), P()),
        out_specs=(split, split, split, split, P()),
        check_vma=False,
    )
```

```python
import functools
import math

import jax
import jax.numpy as jnp
from jax import lax
from jax.experimental import pallas as pl
from jax.experimental.pallas import tpu as pltpu
from jax.sharding import PartitionSpec as P

LANES = 128
ROW_BLOCK = 32
MIB = 1024 * 1024
CHUNKS = 4
PIECES = 4
VMEM = pl.BlockSpec(memory_space=pltpu.VMEM)


def iota(shape, dim):
    return lax.broadcasted_iota(jnp.int32, shape, dim)


def exchange(array, axis, first):
    size = lax.axis_size(axis)
    pairs = {i: i for i in range(size)}
    for low in range(first, size - 1, 2):
        pairs[low], pairs[low + 1] = low + 1, low
    return lax.ppermute(array, axis, list(pairs.items()))


def sum_over(array, axes):
    size = math.prod(lax.axis_size(axis) for axis in axes)
    lanes = min(LANES, array.size // size)
    parts = array.reshape(size, array.size // size // lanes, lanes)
    parts = lax.all_to_all(parts, axes, 0, 0)
    parts = jnp.broadcast_to(jnp.sum(parts, axis=0, keepdims=True), parts.shape)
    return lax.all_to_all(parts, axes, 0, 0).reshape(array.shape)


def reversal(taps):
    flip = iota((taps, taps), 0) + iota((taps, taps), 1) == taps - 1
    return jnp.where(flip, 1.0, 0.0).astype(jnp.bfloat16)


def gates_kernel(
    starts_ref, q_hbm, k_hbm, v_hbm, ct_hbm,
    u_ref, dy_ref, near_1_ref, far_1_ref, near_2_ref, far_2_ref, held, sems,
):
    taps, channels = u_ref.shape
    half = channels // 2
    block = channels // CHUNKS
    copies = []
    for c in range(CHUNKS):
        cols = pl.ds(c * block, block)
        for a, source in enumerate((k_hbm, v_hbm, q_hbm, ct_hbm)):
            copy = pltpu.make_async_copy(source.at[:, cols], held.at[a, :, cols], sems.at[c, a])
            copy.start()
            copies.append(copy)
    here = lax.axis_index("ctx")
    odd = here % 2 == 1
    begins, ends = here == 0, here == lax.axis_size("ctx") - 1
    for d in range(starts_ref.shape[0]):
        begins = jnp.logical_or(begins, starts_ref[d] == here * taps)
        ends = jnp.logical_or(ends, starts_ref[d] == (here + 1) * taps)
    reverse = reversal(taps)
    for c in range(CHUNKS):
        cols = pl.ds(c * block, block)
        for copy in copies[4 * c : 4 * c + 4]:
            copy.wait()
        k, v, q, ct = [held[a, :, cols].astype(jnp.float32) for a in range(4)]
        u = (k * v).astype(jnp.bfloat16)
        dy = (ct * q).astype(jnp.bfloat16)
        dy = jnp.dot(reverse, dy, preferred_element_type=jnp.float32).astype(jnp.bfloat16)
        u_ref[:, cols] = u
        dy_ref[:, cols] = dy
        onward = jnp.where(ends, jnp.zeros_like(u), u)
        backward = jnp.where(begins, jnp.zeros_like(dy), dy)
        first = c * block < half
        sent = pl.ds(c * block % half, block)
        near_u, far_u = (near_1_ref, far_1_ref) if first else (near_2_ref, far_2_ref)
        near_dy, far_dy = (near_2_ref, far_2_ref) if first else (near_1_ref, far_1_ref)

        @pl.when(odd)
        def _():
            far_u[:, sent] = onward
            near_dy[:, sent] = backward

        @pl.when(jnp.logical_not(odd))
        def _():
            near_u[:, sent] = onward
            far_dy[:, sent] = backward


def gates(starts, q, k, v, ct):
    taps, channels = q.shape
    whole = jax.ShapeDtypeStruct((taps, channels), jnp.bfloat16)
    part = jax.ShapeDtypeStruct((taps, channels // 2), jnp.bfloat16)
    return pl.pallas_call(
        gates_kernel,
        in_specs=[pl.BlockSpec(memory_space=pltpu.SMEM)] + [pl.BlockSpec(memory_space=pltpu.HBM)] * 4,
        out_specs=[VMEM] * 6,
        out_shape=[whole] * 2 + [part] * 4,
        scratch_shapes=[
            pltpu.VMEM((4, taps, channels), jnp.bfloat16),
            pltpu.SemaphoreType.DMA((CHUNKS, 4)),
        ],
        name="gates",
        cost_estimate=pl.CostEstimate(
            flops=2 * taps * taps * channels, bytes_accessed=16 * taps * channels, transcendentals=0
        ),
        compiler_params=pltpu.CompilerParams(vmem_limit_bytes=52 * MIB),
    )(starts, q, k, v, ct)


def circulant_kernel(filters_ref, out_ref):
    count, taps = filters_ref.shape
    flip = jnp.where((iota((taps, taps), 0) + iota((taps, taps), 1)) % taps == 0, 1.0, 0.0)
    lines = jnp.dot(filters_ref[...], flip.astype(jnp.bfloat16), preferred_element_type=jnp.float32)
    current = iota((taps, taps), 1) <= iota((taps, taps), 0)
    for f in range(count):
        tile = jnp.broadcast_to(lines[f : f + 1], (taps, taps))
        tile = pltpu.roll(tile, 0, 1, stride=1, stride_axis=0)
        out_ref[f, :, :taps] = jnp.where(current, 0.0, tile).astype(jnp.bfloat16)
        out_ref[f, :, taps:] = jnp.where(current, tile, 0.0).astype(jnp.bfloat16)


def circulants(filters):
    count, taps = filters.shape
    return pl.pallas_call(
        circulant_kernel,
        in_specs=[VMEM],
        out_specs=VMEM,
        out_shape=jax.ShapeDtypeStruct((count, taps, 2 * taps), jnp.bfloat16),
        name="circulants",
        cost_estimate=pl.CostEstimate(
            flops=count * taps * taps * 64, bytes_accessed=4 * count * taps * taps, transcendentals=0
        ),
        compiler_params=pltpu.CompilerParams(vmem_limit_bytes=16 * MIB),
    )(filters)


def filter_grad_kernel(width, u_ref, dy_ref, near_ref, far_ref, tiles_ref, out_ref):
    del tiles_ref
    taps, channels = u_ref.shape
    half = channels // 2
    per_group = LANES // width
    odd = lax.axis_index("ctx") % 2 == 1
    lane_filter = iota((ROW_BLOCK, LANES), 1) // width
    fold = iota((ROW_BLOCK, taps), 1) + iota((ROW_BLOCK, taps), 0) < ROW_BLOCK
    rows = []
    for group in range(channels // LANES):
        cols = pl.ds(group * LANES, LANES)
        sent = pl.ds(group * LANES % half, LANES)
        near, far = near_ref[:, sent], far_ref[:, sent]
        if group * LANES < half:
            moving, fixed, other = dy_ref[:, cols], u_ref[:, cols], jnp.where(odd, near, far)
        else:
            moving, fixed, other = u_ref[:, cols], dy_ref[:, cols], jnp.where(odd, far, near)
        window = jnp.concatenate([other, fixed], axis=0)
        left, right = [], []
        for at in range(0, taps, ROW_BLOCK):
            piece = moving[at : at + ROW_BLOCK]
            left.append(
                jnp.concatenate(
                    [jnp.where(lane_filter == i, piece, 0) for i in range(per_group)], axis=0
                )
            )
            right.append(window[taps - ROW_BLOCK - at : 2 * taps - at])
        left = jnp.concatenate(left, axis=1)
        right = jnp.concatenate(right, axis=1)
        product = lax.dot_general(
            left, right, (((1,), (1,)), ((), ())), preferred_element_type=jnp.float32
        )
        for i in range(per_group):
            tile = product[i * ROW_BLOCK : (i + 1) * ROW_BLOCK]
            high = jnp.concatenate(
                [tile[:, taps:], jnp.zeros((ROW_BLOCK, taps - ROW_BLOCK), jnp.float32)], axis=1
            )
            tile = jnp.where(fold, high, tile[:, :taps])
            tile = pltpu.roll(tile, taps - ROW_BLOCK + 1, 1, stride=1, stride_axis=0)
            rows.append(jnp.sum(tile, axis=0, keepdims=True))
    lines = jnp.concatenate(rows, axis=0)
    flip = jnp.where((iota((taps, taps), 0) + iota((taps, taps), 1)) % taps == 0, 1.0, 0.0)
    out_ref[...] = jnp.dot(
        lines, flip, preferred_element_type=jnp.float32, precision=lax.Precision.HIGHEST
    )


def filter_gradient(u, dy, near, far, tiles, width):
    taps, channels = u.shape
    return pl.pallas_call(
        functools.partial(filter_grad_kernel, width),
        in_specs=[VMEM] * 4 + [pl.BlockSpec(memory_space=pl.ANY)],
        out_specs=VMEM,
        out_shape=jax.ShapeDtypeStruct((channels // width, taps), jnp.float32),
        name="filter_gradient",
        cost_estimate=pl.CostEstimate(
            flops=2 * (channels // width) * taps * taps * 256,
            bytes_accessed=8 * taps * channels,
            transcendentals=0,
        ),
        compiler_params=pltpu.CompilerParams(vmem_limit_bytes=16 * MIB),
    )(u, dy, near, far, tiles)


def outputs_kernel(
    width, base, first, q_ref, k_ref, v_ref, ct_ref, u_ref, dy_ref,
    near_1_ref, far_1_ref, near_2_ref, far_2_ref, tiles_ref, *rest,
):
    out_ref, grad_q_ref, grad_k_ref, grad_v_ref = rest[-4:]
    taps, channels = out_ref.shape
    half = u_ref.shape[1] // 2
    per_group = LANES // width
    odd = lax.axis_index("ctx") % 2 == 1
    reverse = reversal(taps)
    lane_filter = (iota((taps, 2 * LANES), 1) % LANES) // width
    base = base + pl.program_id(0) * channels

    def flipped(array):
        return jnp.dot(reverse, array, preferred_element_type=jnp.float32)

    for group in range(channels // LANES):
        own = pl.ds(group * LANES, LANES)
        at = pl.multiple_of(base + group * LANES, LANES)
        cols = pl.ds(at, LANES)
        sent = pl.ds(at if first else pl.multiple_of(at - half, LANES), LANES)
        near_1, far_1 = near_1_ref[:, sent], far_1_ref[:, sent]
        near_2, far_2 = near_2_ref[:, sent], far_2_ref[:, sent]
        if first:
            before, after = jnp.where(odd, near_1, far_1), jnp.where(odd, far_2, near_2)
        else:
            before, after = jnp.where(odd, near_2, far_2), jnp.where(odd, far_1, near_1)
        window = jnp.concatenate(
            [
                jnp.concatenate([before, after], axis=1),
                jnp.concatenate([u_ref[:, cols], dy_ref[:, cols]], axis=1),
            ],
            axis=0,
        )
        tiles = tiles_ref[pl.ds(at // width, per_group)]
        parts = jnp.dot(
            tiles.reshape(per_group * taps, 2 * taps), window, preferred_element_type=jnp.float32
        )
        total = parts[:taps]
        for i in range(1, per_group):
            total = jnp.where(lane_filter == i, parts[i * taps : (i + 1) * taps], total)
        y = total[:, :LANES]
        out_ref[:, own] = (q_ref[:, cols].astype(jnp.float32) * y).astype(jnp.bfloat16)
        grad_q_ref[:, own] = (ct_ref[:, cols].astype(jnp.float32) * y).astype(jnp.bfloat16)
        mixed = total[:, LANES:]
        turned = flipped(jnp.concatenate([v_ref[:, cols], k_ref[:, cols]], axis=1))
        grads = (turned * jnp.concatenate([mixed, mixed], axis=1)).astype(jnp.bfloat16)
        grads = flipped(grads).astype(jnp.bfloat16)
        grad_k_ref[:, own] = grads[:, :LANES]
        grad_v_ref[:, own] = grads[:, LANES:]


def outputs(q, k, v, ct, u, dy, halos, tiles, width):
    taps, channels = u.shape
    part = channels // PIECES
    steps = 2
    shape = jax.ShapeDtypeStruct((taps, channels), jnp.bfloat16)
    results = ()
    for piece in range(PIECES):
        spec = pl.BlockSpec((taps, part // steps), lambda i, piece=piece: (0, piece * steps + i))
        operands = (q, k, v, ct, u, dy, *halos, tiles)
        results = pl.pallas_call(
            functools.partial(
                outputs_kernel, width, piece * part, piece * part < channels // 2
            ),
            grid=(steps,),
            in_specs=[VMEM] * len(operands) + [pl.BlockSpec(memory_space=pl.ANY)] * len(results),
            out_specs=[spec] * 4,
            out_shape=[shape] * 4,
            input_output_aliases={len(operands) + i: i for i in range(len(results))},
            name=f"outputs_{piece}",
            cost_estimate=pl.CostEstimate(
                flops=16 * (part // width) * taps * taps * 256,
                bytes_accessed=24 * taps * part,
                transcendentals=0,
            ),
            compiler_params=pltpu.CompilerParams(vmem_limit_bytes=16 * MIB),
        )(*operands, *results)
    return results


def per_device(gate_in, key_in, value_in, cotangent, doc_starts, filters):
    taps = filters.shape[1]
    width = gate_in.shape[2] // filters.shape[0]
    assert gate_in.shape[1] == taps
    q, k, v, ct = gate_in[0], key_in[0], value_in[0], cotangent[0]
    u, dy, near_1, far_1, near_2, far_2 = gates(doc_starts[0], q, k, v, ct)
    far_1 = exchange(far_1, "ctx", 1)
    near_1 = exchange(near_1, "ctx", 0)
    far_2 = exchange(far_2, "ctx", 1)
    near_2 = exchange(near_2, "ctx", 0)
    tiles = circulants(filters)
    filter_grad = filter_gradient(u, dy, near_1, far_1, tiles, width)
    filter_grad = sum_over(filter_grad, ("dp", "ctx"))
    results = outputs(q, k, v, ct, u, dy, (near_1, far_1, near_2, far_2), tiles, width)
    return tuple(array[None] for array in results) + (filter_grad,)


def solution(mesh):
    split = P("dp", "ctx", None)
    return jax.shard_map(
        per_device,
        mesh=mesh,
        in_specs=(split, split, split, split, P("dp", None), P()),
        out_specs=(split, split, split, split, P()),
        check_vma=False,
    )
```

```python
import functools

import jax
import jax.numpy as jnp
from jax import lax
from jax.experimental import pallas as pl
from jax.experimental.pallas import tpu as pltpu
from jax.sharding import PartitionSpec as P

LANES = 128
ROW_BLOCK = 32
MIB = 1024 * 1024
CHUNKS = 4
PIECES = 4
STEPS = 2
VMEM = pl.BlockSpec(memory_space=pltpu.VMEM)
SMEM = pl.BlockSpec(memory_space=pltpu.SMEM)


def iota(shape, dim):
    return lax.broadcasted_iota(jnp.int32, shape, dim)


def exchange(array, axis, first):
    size = lax.axis_size(axis)
    pairs = []
    for low in range(first, size - 1, 2):
        pairs += [(low, low + 1), (low + 1, low)]
    return lax.ppermute(array, axis, pairs)


def sum_halves(mine, other):
    total = mine + exchange(other, "ctx", 0)
    for axis, step in (("ctx", 2), ("dp", 1)):
        size = lax.axis_size(axis)
        while step < size:
            total = total + lax.ppermute(total, axis, [(i, i ^ step) for i in range(size)])
            step *= 2
    other = exchange(total, "ctx", 0)
    odd = lax.axis_index("ctx") % 2 == 1
    return jnp.concatenate([jnp.where(odd, other, total), jnp.where(odd, total, other)], axis=0)


def reversal(taps):
    flip = iota((taps, taps), 0) + iota((taps, taps), 1) == taps - 1
    return jnp.where(flip, 1.0, 0.0).astype(jnp.bfloat16)


def gates_kernel(
    q_hbm, k_hbm, v_hbm, ct_hbm, q_ref, k_ref, v_ref, ct_ref, near_ref, far_1_ref, far_2_ref, sems
):
    taps, channels = near_ref.shape
    half = channels // 2
    block = channels // CHUNKS
    pairs = ((k_hbm, k_ref), (v_hbm, v_ref), (q_hbm, q_ref), (ct_hbm, ct_ref))
    copies = []
    for c in range(CHUNKS):
        cols = pl.ds(c * block, block)
        for a, (source, target) in enumerate(pairs):
            copy = pltpu.make_async_copy(source.at[:, cols], target.at[:, cols], sems.at[c, a])
            copy.start()
            copies.append(copy)
    odd = lax.axis_index("ctx") % 2 == 1
    reverse = reversal(taps)
    for c in range(CHUNKS):
        cols = pl.ds(c * block, block)
        for copy in copies[4 * c : 4 * c + 4]:
            copy.wait()
        k, v, q, ct = [target[:, cols].astype(jnp.float32) for _, target in pairs]
        u = (k * v).astype(jnp.bfloat16)
        dy = (ct * q).astype(jnp.bfloat16)
        dy = jnp.dot(reverse, dy, preferred_element_type=jnp.float32).astype(jnp.bfloat16)
        sent = pl.ds(c * block % half, block)
        far_u, far_dy = (far_1_ref, far_2_ref) if c * block < half else (far_2_ref, far_1_ref)
        near_ref[:, cols] = jnp.where(odd, dy, u)

        @pl.when(odd)
        def _():
            far_u[:, sent] = u

        @pl.when(jnp.logical_not(odd))
        def _():
            far_dy[:, sent] = dy


def gates(q, k, v, ct):
    taps, channels = q.shape
    whole = jax.ShapeDtypeStruct((taps, channels), jnp.bfloat16)
    part = jax.ShapeDtypeStruct((taps, channels // 2), jnp.bfloat16)
    return pl.pallas_call(
        gates_kernel,
        in_specs=[pl.BlockSpec(memory_space=pltpu.HBM)] * 4,
        out_specs=[VMEM] * 7,
        out_shape=[whole] * 5 + [part] * 2,
        scratch_shapes=[
            pltpu.SemaphoreType.DMA((CHUNKS, 4)),
        ],
        name="gates",
        cost_estimate=pl.CostEstimate(
            flops=2 * taps * taps * channels, bytes_accessed=12 * taps * channels, transcendentals=0
        ),
        compiler_params=pltpu.CompilerParams(vmem_limit_bytes=101 * MIB // 2),
    )(q, k, v, ct)


def masks_kernel(starts_ref, near_in_ref, keep_ref):
    del near_in_ref
    here = lax.axis_index("ctx")
    for side in range(2):
        found = here + side < 0
        for d in range(starts_ref.shape[0]):
            found = jnp.logical_or(found, starts_ref[d] == (here + side) * keep_ref.shape[1])
        keep = jnp.where(found, 0.0, 1.0)
        keep_ref[side] = jnp.full(keep_ref.shape[1:], keep).astype(jnp.bfloat16)


def masks(starts, near_in):
    return pl.pallas_call(
        masks_kernel,
        in_specs=[SMEM, pl.BlockSpec(memory_space=pl.ANY)],
        out_specs=VMEM,
        out_shape=jax.ShapeDtypeStruct((2, near_in.shape[0], LANES), jnp.bfloat16),
        name="masks",
    )(starts, near_in)


def toeplitz_kernel(filters_ref, out_ref):
    count, taps = filters_ref.shape
    lines = filters_ref[...].astype(jnp.float32)
    current = iota((taps, taps), 0) <= iota((taps, taps), 1)
    for f in range(count):
        tile = jnp.broadcast_to(lines[f : f + 1], (taps, taps))
        tile = pltpu.roll(tile, 0, 1, stride=1, stride_axis=0)
        out_ref[f, :taps] = jnp.where(current, 0.0, tile).astype(jnp.bfloat16)
        out_ref[f, taps:] = jnp.where(current, tile, 0.0).astype(jnp.bfloat16)


def toeplitz(filters):
    count, taps = filters.shape
    return pl.pallas_call(
        toeplitz_kernel,
        in_specs=[VMEM],
        out_specs=VMEM,
        out_shape=jax.ShapeDtypeStruct((count, 2 * taps, taps), jnp.bfloat16),
        name="toeplitz",
        cost_estimate=pl.CostEstimate(
            flops=count * taps * taps * 64, bytes_accessed=4 * count * taps * taps, transcendentals=0
        ),
        compiler_params=pltpu.CompilerParams(vmem_limit_bytes=16 * MIB),
    )(filters)


def filter_grad_kernel(
    width, near_ref, far_1_ref, far_2_ref, keep_ref, near_in_ref, far_in_ref, mine_ref, other_ref
):
    taps, channels = near_ref.shape
    half = channels // 2
    per_group = LANES // width
    odd = lax.axis_index("ctx") % 2 == 1
    lane_filter = iota((ROW_BLOCK, LANES), 1) // width
    fold = iota((ROW_BLOCK, taps), 1) + iota((ROW_BLOCK, taps), 0) < ROW_BLOCK
    rows = []
    for group in range(channels // LANES):
        cols = pl.ds(group * LANES, LANES)
        sent = pl.ds(group * LANES % half, LANES)
        near, far_1, far_2 = near_ref[:, cols], far_1_ref[:, sent], far_2_ref[:, sent]
        near_in, far_in = near_in_ref[:, cols], far_in_ref[:, sent]
        if group * LANES < half:
            moving, fixed = jnp.where(odd, near, far_2), jnp.where(odd, far_1, near)
            beyond = jnp.where(odd, near_in, far_in) * keep_ref[0]
        else:
            moving, fixed = jnp.where(odd, far_2, near), jnp.where(odd, near, far_1)
            beyond = jnp.where(odd, far_in, near_in) * keep_ref[1]
        window = jnp.concatenate([beyond, fixed], axis=0)
        left, right = [], []
        for at in range(0, taps, ROW_BLOCK):
            piece = moving[at : at + ROW_BLOCK]
            left.append(
                jnp.concatenate(
                    [jnp.where(lane_filter == i, piece, 0) for i in range(per_group)], axis=0
                )
            )
            right.append(window[taps - ROW_BLOCK - at : 2 * taps - at])
        left = jnp.concatenate(left, axis=1)
        right = jnp.concatenate(right, axis=1)
        product = lax.dot_general(
            left, right, (((1,), (1,)), ((), ())), preferred_element_type=jnp.float32
        )
        for i in range(per_group):
            tile = product[i * ROW_BLOCK : (i + 1) * ROW_BLOCK]
            high = jnp.concatenate(
                [tile[:, taps:], jnp.zeros((ROW_BLOCK, taps - ROW_BLOCK), jnp.float32)], axis=1
            )
            tile = jnp.where(fold, high, tile[:, :taps])
            tile = pltpu.roll(tile, taps - ROW_BLOCK + 1, 1, stride=1, stride_axis=0)
            rows.append(jnp.sum(tile, axis=0, keepdims=True))
    lines = jnp.concatenate(rows, axis=0)
    flip = jnp.where((iota((taps, taps), 0) + iota((taps, taps), 1)) % taps == 0, 1.0, 0.0)
    grads = jnp.dot(
        lines, flip, preferred_element_type=jnp.float32, precision=lax.Precision.HIGHEST
    )
    low, high = jnp.split(grads, 2, axis=0)
    mine_ref[...] = jnp.where(odd, high, low)
    other_ref[...] = jnp.where(odd, low, high)


def filter_gradient(sent, near_in, far_in, width):
    taps, channels = near_in.shape
    count = channels // width
    shape = jax.ShapeDtypeStruct((count // 2, taps), jnp.float32)
    return pl.pallas_call(
        functools.partial(filter_grad_kernel, width),
        in_specs=[VMEM] * 6,
        out_specs=[VMEM] * 2,
        out_shape=[shape] * 2,
        name="filter_gradient",
        cost_estimate=pl.CostEstimate(
            flops=2 * count * taps * taps * 256, bytes_accessed=8 * taps * channels, transcendentals=0
        ),
        compiler_params=pltpu.CompilerParams(vmem_limit_bytes=16 * MIB),
    )(*sent, near_in, far_in)


def outputs_kernel(
    width, base, first, q_ref, k_ref, v_ref, ct_ref, near_ref, far_1_ref, far_2_ref, keep_ref,
    near_in_ref, far_in_1_ref, far_in_2_ref, tiles_ref, *rest,
):
    out_ref, grad_q_ref, grad_k_ref, grad_v_ref = rest[-4:]
    taps, channels = out_ref.shape
    half = near_ref.shape[1] // 2
    per_group = LANES // width
    odd = lax.axis_index("ctx") % 2 == 1
    reverse = reversal(taps)
    base = base + pl.program_id(0) * channels

    def flipped(array):
        return jnp.dot(reverse, array, preferred_element_type=jnp.float32)

    whole = pl.ds(pl.multiple_of(base, LANES), channels)
    k_turned = flipped(k_ref[:, whole])
    v_turned = flipped(v_ref[:, whole])
    grad_k, grad_v = [], []
    for group in range(channels // LANES):
        own = pl.ds(group * LANES, LANES)
        at = pl.multiple_of(base + group * LANES, LANES)
        cols = pl.ds(at, LANES)
        sent = pl.ds(at if first else pl.multiple_of(at - half, LANES), LANES)
        near, far_1, far_2 = near_ref[:, cols], far_1_ref[:, sent], far_2_ref[:, sent]
        near_in, far_in_1, far_in_2 = near_in_ref[:, cols], far_in_1_ref[:, sent], far_in_2_ref[:, sent]
        if first:
            u, dy = jnp.where(odd, far_1, near), jnp.where(odd, near, far_2)
            before, after = jnp.where(odd, near_in, far_in_1), jnp.where(odd, far_in_2, near_in)
        else:
            u, dy = jnp.where(odd, far_2, near), jnp.where(odd, near, far_1)
            before, after = jnp.where(odd, near_in, far_in_2), jnp.where(odd, far_in_1, near_in)
        before = before * keep_ref[0]
        after = after * keep_ref[1]
        u_lines = jnp.concatenate([before.T, u.T], axis=1)
        dy_lines = jnp.concatenate([after.T, dy.T], axis=1)
        y, mixed = [], []
        for i in range(per_group):
            rows = slice(i * width, (i + 1) * width)
            both = jnp.concatenate([u_lines[rows], dy_lines[rows]], axis=0)
            part = jnp.dot(both, tiles_ref[at // width + i], preferred_element_type=jnp.float32)
            y.append(part[:width])
            mixed.append(part[width:])
        y = jnp.concatenate(y, axis=0).T
        mixed = jnp.concatenate(mixed, axis=0).T
        out_ref[:, own] = (q_ref[:, cols].astype(jnp.float32) * y).astype(jnp.bfloat16)
        grad_q_ref[:, own] = (ct_ref[:, cols].astype(jnp.float32) * y).astype(jnp.bfloat16)
        lanes = slice(group * LANES, (group + 1) * LANES)
        grad_k.append((mixed * v_turned[:, lanes]).astype(jnp.bfloat16))
        grad_v.append((mixed * k_turned[:, lanes]).astype(jnp.bfloat16))
    grad_k_ref[...] = flipped(jnp.concatenate(grad_k, axis=1)).astype(jnp.bfloat16)
    grad_v_ref[...] = flipped(jnp.concatenate(grad_v, axis=1)).astype(jnp.bfloat16)


def outputs(q, k, v, ct, sent, halos, tiles, width):
    taps, channels = q.shape
    part = channels // PIECES
    steps = STEPS
    shape = jax.ShapeDtypeStruct((taps, channels), jnp.bfloat16)
    results = ()
    for piece in range(PIECES):
        spec = pl.BlockSpec((taps, part // steps), lambda i, piece=piece: (0, piece * steps + i))
        operands = (q, k, v, ct, *sent, *halos, tiles)
        results = pl.pallas_call(
            functools.partial(
                outputs_kernel, width, piece * part, piece * part < channels // 2
            ),
            grid=(steps,),
            in_specs=[VMEM] * len(operands) + [pl.BlockSpec(memory_space=pl.ANY)] * len(results),
            out_specs=[spec] * 4,
            out_shape=[shape] * 4,
            input_output_aliases={len(operands) + i: i for i in range(len(results))},
            name=f"outputs_{piece}",
            cost_estimate=pl.CostEstimate(
                flops=16 * (part // width) * taps * taps * 256,
                bytes_accessed=24 * taps * part,
                transcendentals=0,
            ),
            compiler_params=pltpu.CompilerParams(vmem_limit_bytes=16 * MIB),
        )(*operands, *results)
    return results


def per_device(gate_in, key_in, value_in, cotangent, doc_starts, filters):
    taps = filters.shape[1]
    width = gate_in.shape[2] // filters.shape[0]
    assert gate_in.shape[1] == taps
    q, k, v, ct = gate_in[0], key_in[0], value_in[0], cotangent[0]
    q, k, v, ct, near, far_1, far_2 = gates(q, k, v, ct)
    far_in_1 = exchange(far_1, "ctx", 1)
    near_in = exchange(near, "ctx", 0)
    far_in_2 = exchange(far_2, "ctx", 1)
    sent = (near, far_1, far_2, masks(doc_starts[0], near_in))
    filter_grad = sum_halves(*filter_gradient(sent, near_in, far_in_1, width))
    tiles = toeplitz(filters)
    halos = (near_in, far_in_1, far_in_2)
    results = outputs(q, k, v, ct, sent, halos, tiles, width)
    return tuple(array[None] for array in results) + (filter_grad,)


def solution(mesh):
    split = P("dp", "ctx", None)
    return jax.shard_map(
        per_device,
        mesh=mesh,
        in_specs=(split, split, split, split, P("dp", None), P()),
        out_specs=(split, split, split, split, P()),
        check_vma=False,
    )
```

```python
import functools

import jax
import jax.numpy as jnp
from jax import lax
from jax.experimental import pallas as pl
from jax.experimental.pallas import tpu as pltpu
from jax.sharding import PartitionSpec as P

LANES = 128
ROW_BLOCK = 32
MIB = 1024 * 1024
CHUNKS = 4
PIECES = 4
VMEM = pl.BlockSpec(memory_space=pltpu.VMEM)
SMEM = pl.BlockSpec(memory_space=pltpu.SMEM)


def iota(shape, dim):
    return lax.broadcasted_iota(jnp.int32, shape, dim)


def exchange(array, axis, first):
    size = lax.axis_size(axis)
    pairs = []
    for low in range(first, size - 1, 2):
        pairs += [(low, low + 1), (low + 1, low)]
    return lax.ppermute(array, axis, pairs)


def sum_halves(mine, other):
    total = mine + exchange(other, "ctx", 0)
    for axis, step in (("ctx", 2), ("dp", 1)):
        size = lax.axis_size(axis)
        while step < size:
            total = total + lax.ppermute(total, axis, [(i, i ^ step) for i in range(size)])
            step *= 2
    other = exchange(total, "ctx", 0)
    odd = lax.axis_index("ctx") % 2 == 1
    return jnp.concatenate([jnp.where(odd, other, total), jnp.where(odd, total, other)], axis=0)


def reversal(taps):
    flip = iota((taps, taps), 0) + iota((taps, taps), 1) == taps - 1
    return jnp.where(flip, 1.0, 0.0).astype(jnp.bfloat16)


def gates_kernel(
    q_hbm, k_hbm, v_hbm, ct_hbm, q_ref, k_ref, v_ref, ct_ref, near_ref, far_1_ref, far_2_ref, sems
):
    taps, channels = near_ref.shape
    half = channels // 2
    block = channels // CHUNKS
    pairs = ((k_hbm, k_ref), (v_hbm, v_ref), (q_hbm, q_ref), (ct_hbm, ct_ref))
    copies = []
    for c in range(CHUNKS):
        cols = pl.ds(c * block, block)
        for a, (source, target) in enumerate(pairs):
            copy = pltpu.make_async_copy(source.at[:, cols], target.at[:, cols], sems.at[c, a])
            copy.start()
            copies.append(copy)
    odd = lax.axis_index("ctx") % 2 == 1
    reverse = reversal(taps)
    for c in range(CHUNKS):
        cols = pl.ds(c * block, block)
        for copy in copies[4 * c : 4 * c + 4]:
            copy.wait()
        k, v, q, ct = [target[:, cols].astype(jnp.float32) for _, target in pairs]
        u = (k * v).astype(jnp.bfloat16)
        dy = (ct * q).astype(jnp.bfloat16)
        dy = jnp.dot(reverse, dy, preferred_element_type=jnp.float32).astype(jnp.bfloat16)
        sent = pl.ds(c * block % half, block)
        far_u, far_dy = (far_1_ref, far_2_ref) if c * block < half else (far_2_ref, far_1_ref)

        @pl.when(odd)
        def _():
            near_ref[:, cols] = dy
            far_u[:, sent] = u

        @pl.when(jnp.logical_not(odd))
        def _():
            near_ref[:, cols] = u
            far_dy[:, sent] = dy


def gates(q, k, v, ct):
    taps, channels = q.shape
    whole = jax.ShapeDtypeStruct((taps, channels), jnp.bfloat16)
    part = jax.ShapeDtypeStruct((taps, channels // 2), jnp.bfloat16)
    return pl.pallas_call(
        gates_kernel,
        in_specs=[pl.BlockSpec(memory_space=pltpu.HBM)] * 4,
        out_specs=[VMEM] * 7,
        out_shape=[whole] * 5 + [part] * 2,
        scratch_shapes=[
            pltpu.SemaphoreType.DMA((CHUNKS, 4)),
        ],
        name="gates",
        cost_estimate=pl.CostEstimate(
            flops=2 * taps * taps * channels, bytes_accessed=12 * taps * channels, transcendentals=0
        ),
        compiler_params=pltpu.CompilerParams(vmem_limit_bytes=101 * MIB // 2),
    )(q, k, v, ct)


def masks_kernel(starts_ref, near_in_ref, keep_ref):
    del near_in_ref
    here = lax.axis_index("ctx")
    for side in range(2):
        found = here + side < 0
        for d in range(starts_ref.shape[0]):
            found = jnp.logical_or(found, starts_ref[d] == (here + side) * keep_ref.shape[1])
        keep = jnp.where(found, 0.0, 1.0)
        keep_ref[side] = jnp.full(keep_ref.shape[1:], keep).astype(jnp.bfloat16)


def masks(starts, near_in):
    return pl.pallas_call(
        masks_kernel,
        in_specs=[SMEM, pl.BlockSpec(memory_space=pl.ANY)],
        out_specs=VMEM,
        out_shape=jax.ShapeDtypeStruct((2, near_in.shape[0], LANES), jnp.bfloat16),
        name="masks",
        compiler_params=pltpu.CompilerParams(vmem_limit_bytes=MIB),
    )(starts, near_in)


def toeplitz_kernel(filters_ref, out_ref):
    count, taps = filters_ref.shape
    lines = filters_ref[...].astype(jnp.float32)
    current = iota((taps, taps), 0) <= iota((taps, taps), 1)
    for f in range(count):
        tile = jnp.broadcast_to(lines[f : f + 1], (taps, taps))
        tile = pltpu.roll(tile, 0, 1, stride=1, stride_axis=0)
        out_ref[f, :taps] = jnp.where(current, 0.0, tile).astype(jnp.bfloat16)
        out_ref[f, taps:] = jnp.where(current, tile, 0.0).astype(jnp.bfloat16)


def toeplitz(filters):
    count, taps = filters.shape
    return pl.pallas_call(
        toeplitz_kernel,
        in_specs=[VMEM],
        out_specs=VMEM,
        out_shape=jax.ShapeDtypeStruct((count, 2 * taps, taps), jnp.bfloat16),
        name="toeplitz",
        cost_estimate=pl.CostEstimate(
            flops=count * taps * taps * 64, bytes_accessed=4 * count * taps * taps, transcendentals=0
        ),
        compiler_params=pltpu.CompilerParams(vmem_limit_bytes=16 * MIB),
    )(filters)


def filter_lines(width, block, out_ref):
    count, taps = out_ref.shape
    per_group = LANES // width
    lane_filter = iota((ROW_BLOCK, LANES), 1) // width
    fold = iota((ROW_BLOCK, taps), 1) + iota((ROW_BLOCK, taps), 0) < ROW_BLOCK
    for group in range(count // per_group):
        moving, fixed, beyond = block(group * LANES)
        window = jnp.concatenate([beyond, fixed], axis=0)
        left, right = [], []
        for at in range(0, taps, ROW_BLOCK):
            piece = moving[at : at + ROW_BLOCK]
            left.append(
                jnp.concatenate(
                    [jnp.where(lane_filter == i, piece, 0) for i in range(per_group)], axis=0
                )
            )
            right.append(window[taps - ROW_BLOCK - at : 2 * taps - at])
        left = jnp.concatenate(left, axis=1)
        right = jnp.concatenate(right, axis=1)
        product = lax.dot_general(
            left, right, (((1,), (1,)), ((), ())), preferred_element_type=jnp.float32
        )
        rows = []
        for i in range(per_group):
            tile = product[i * ROW_BLOCK : (i + 1) * ROW_BLOCK]
            high = jnp.concatenate(
                [tile[:, taps:], jnp.zeros((ROW_BLOCK, taps - ROW_BLOCK), jnp.float32)], axis=1
            )
            tile = jnp.where(fold, high, tile[:, :taps])
            tile = pltpu.roll(tile, taps - ROW_BLOCK + 1, 1, stride=1, stride_axis=0)
            rows.append(jnp.sum(tile, axis=0, keepdims=True))
        out_ref[group * per_group : (group + 1) * per_group] = jnp.concatenate(rows, axis=0)


def filter_grad_kernel(
    width, near_ref, far_1_ref, far_2_ref, keep_ref, near_in_ref, far_in_ref, mine_ref, other_ref, lines
):
    taps, channels = near_ref.shape
    half = channels // 2
    odd = lax.axis_index("ctx") % 2 == 1

    def block(odd, at):
        cols, sent = pl.ds(at, LANES), pl.ds(at % half, LANES)
        near, near_in, far_in = near_ref[:, cols], near_in_ref[:, cols], far_in_ref[:, sent]
        far = (far_1_ref if odd == (at < half) else far_2_ref)[:, sent]
        beyond = (near_in if odd == (at < half) else far_in) * keep_ref[0 if at < half else 1]
        return (near, far, beyond) if odd == (at < half) else (far, near, beyond)

    @pl.when(odd)
    def _():
        filter_lines(width, functools.partial(block, True), lines)

    @pl.when(jnp.logical_not(odd))
    def _():
        filter_lines(width, functools.partial(block, False), lines)

    flip = jnp.where((iota((taps, taps), 0) + iota((taps, taps), 1)) % taps == 0, 1.0, 0.0)
    grads = jnp.dot(
        lines[...], flip, preferred_element_type=jnp.float32, precision=lax.Precision.HIGHEST
    )
    low, high = jnp.split(grads, 2, axis=0)
    mine_ref[...] = jnp.where(odd, high, low)
    other_ref[...] = jnp.where(odd, low, high)


def filter_gradient(sent, near_in, far_in, width):
    taps, channels = near_in.shape
    count = channels // width
    shape = jax.ShapeDtypeStruct((count // 2, taps), jnp.float32)
    return pl.pallas_call(
        functools.partial(filter_grad_kernel, width),
        in_specs=[VMEM] * 6,
        out_specs=[VMEM] * 2,
        out_shape=[shape] * 2,
        scratch_shapes=[pltpu.VMEM((count, taps), jnp.float32)],
        name="filter_gradient",
        cost_estimate=pl.CostEstimate(
            flops=2 * count * taps * taps * 256, bytes_accessed=8 * taps * channels, transcendentals=0
        ),
        compiler_params=pltpu.CompilerParams(vmem_limit_bytes=16 * MIB),
    )(*sent, near_in, far_in)


def convolve(width, base, operands, block, results, sems, targets):
    q_ref, k_ref, v_ref, ct_ref, tiles_ref = operands
    out, grad_q, grad_k, grad_v = results
    taps, channels = out.shape
    per_group = LANES // width
    reverse = reversal(taps)
    copies = []

    def flipped(array):
        return jnp.dot(reverse, array, preferred_element_type=jnp.float32)

    def send(which, own, cols):
        copy = pltpu.make_async_copy(
            results[which].at[:, own], targets[which].at[:, cols], sems.at[len(copies)]
        )
        copy.start()
        copies.append(copy)

    whole = pl.ds(base, channels)
    k_turned = flipped(k_ref[:, whole])
    v_turned = flipped(v_ref[:, whole])
    k_parts, v_parts = [], []
    for group in range(channels // LANES):
        own = pl.ds(group * LANES, LANES)
        at = base + group * LANES
        cols = pl.ds(at, LANES)
        u, dy, before, after = block(at)
        u_lines = jnp.concatenate([before.T, u.T], axis=1)
        dy_lines = jnp.concatenate([after.T, dy.T], axis=1)
        y, mixed = [], []
        for i in range(per_group):
            rows = slice(i * width, (i + 1) * width)
            both = jnp.concatenate([u_lines[rows], dy_lines[rows]], axis=0)
            part = jnp.dot(both, tiles_ref[at // width + i], preferred_element_type=jnp.float32)
            y.append(part[:width])
            mixed.append(part[width:])
        y = jnp.concatenate(y, axis=0).T
        mixed = jnp.concatenate(mixed, axis=0).T
        out[:, own] = (q_ref[:, cols].astype(jnp.float32) * y).astype(jnp.bfloat16)
        grad_q[:, own] = (ct_ref[:, cols].astype(jnp.float32) * y).astype(jnp.bfloat16)
        lanes = slice(group * LANES, (group + 1) * LANES)
        k_parts.append((mixed * v_turned[:, lanes]).astype(jnp.bfloat16))
        v_parts.append((mixed * k_turned[:, lanes]).astype(jnp.bfloat16))
    every = pl.ds(0, channels)
    send(0, every, whole)
    send(1, every, whole)
    grad_k[...] = flipped(jnp.concatenate(k_parts, axis=1)).astype(jnp.bfloat16)
    send(2, every, whole)
    grad_v[...] = flipped(jnp.concatenate(v_parts, axis=1)).astype(jnp.bfloat16)
    send(3, every, whole)
    for copy in copies:
        copy.wait()


def outputs_kernel(
    width, base, q_ref, k_ref, v_ref, ct_ref, tiles_ref, near_ref, far_1_ref, far_2_ref, keep_ref,
    near_in_ref, far_in_1_ref, far_in_2_ref, *rest,
):
    *results, sems = rest[-5:]
    targets = rest[-9:-5]
    half = near_ref.shape[1] // 2
    odd = lax.axis_index("ctx") % 2 == 1

    def block(odd, at):
        cols, sent = pl.ds(at, LANES), pl.ds(at % half, LANES)
        near, near_in = near_ref[:, cols], near_in_ref[:, cols]
        far = (far_1_ref if odd == (at < half) else far_2_ref)[:, sent]
        far_in = (far_in_2_ref if odd == (at < half) else far_in_1_ref)[:, sent]
        if odd:
            return far, near, near_in * keep_ref[0], far_in * keep_ref[1]
        return near, far, far_in * keep_ref[0], near_in * keep_ref[1]

    operands = (q_ref, k_ref, v_ref, ct_ref, tiles_ref)

    @pl.when(odd)
    def _():
        convolve(width, base, operands, functools.partial(block, True), results, sems, targets)

    @pl.when(jnp.logical_not(odd))
    def _():
        convolve(width, base, operands, functools.partial(block, False), results, sems, targets)


def outputs(q, k, v, ct, tiles, sent, halos, width):
    taps, channels = q.shape
    part = channels // PIECES
    anywhere = pl.BlockSpec(memory_space=pl.ANY)
    results = ()
    for piece in range(PIECES):
        operands = (q, k, v, ct, tiles, *sent, *halos)
        results = pl.pallas_call(
            functools.partial(outputs_kernel, width, piece * part),
            in_specs=[VMEM] * len(operands) + [anywhere] * len(results),
            out_specs=[anywhere] * 4,
            out_shape=[jax.ShapeDtypeStruct((taps, channels), jnp.bfloat16)] * 4,
            input_output_aliases={len(operands) + i: i for i in range(len(results))},
            scratch_shapes=[pltpu.VMEM((taps, part), jnp.bfloat16)] * 4
            + [pltpu.SemaphoreType.DMA((4,))],
            name=f"outputs_{piece}",
            cost_estimate=pl.CostEstimate(
                flops=16 * (part // width) * taps * taps * 256,
                bytes_accessed=24 * taps * part,
                transcendentals=0,
            ),
            compiler_params=pltpu.CompilerParams(vmem_limit_bytes=8 * MIB),
        )(*operands, *results)
    return results


def per_device(gate_in, key_in, value_in, cotangent, doc_starts, filters):
    taps = filters.shape[1]
    width = gate_in.shape[2] // filters.shape[0]
    assert gate_in.shape[1] == taps
    q, k, v, ct = gate_in[0], key_in[0], value_in[0], cotangent[0]
    q, k, v, ct, near, far_1, far_2 = gates(q, k, v, ct)
    far_in_1 = exchange(far_1, "ctx", 1)
    near_in = exchange(near, "ctx", 0)
    far_in_2 = exchange(far_2, "ctx", 1)
    sent = (near, far_1, far_2, masks(doc_starts[0], near_in))
    filter_grad = sum_halves(*filter_gradient(sent, near_in, far_in_1, width))
    tiles = toeplitz(filters)
    halos = (near_in, far_in_1, far_in_2)
    results = outputs(q, k, v, ct, tiles, sent, halos, width)
    return tuple(array[None] for array in results) + (filter_grad,)


def solution(mesh):
    split = P("dp", "ctx", None)
    return jax.shard_map(
        per_device,
        mesh=mesh,
        in_specs=(split, split, split, split, P("dp", None), P()),
        out_specs=(split, split, split, split, P()),
        check_vma=False,
    )
```

```python
import functools

import jax
import jax.numpy as jnp
from jax import lax
from jax.experimental import pallas as pl
from jax.experimental.pallas import tpu as pltpu
from jax.sharding import PartitionSpec as P

LANES = 128
ROW_BLOCK = 32
MIB = 1024 * 1024
CHUNKS = 4
PIECES = 4
GATES_VMEM = 101 * MIB // 2
VMEM = pl.BlockSpec(memory_space=pltpu.VMEM)
SMEM = pl.BlockSpec(memory_space=pltpu.SMEM)


def iota(shape, dim):
    return lax.broadcasted_iota(jnp.int32, shape, dim)


def exchange(array, axis, first):
    size = lax.axis_size(axis)
    pairs = []
    for low in range(first, size - 1, 2):
        pairs += [(low, low + 1), (low + 1, low)]
    return lax.ppermute(array, axis, pairs)


def swapped(array, axis, step):
    size = lax.axis_size(axis)
    return lax.ppermute(array, axis, [(i, i ^ step) for i in range(size)])


def sum_over(array, axis, step):
    size = lax.axis_size(axis)
    while step < size:
        if axis == "dp" and 4 * step <= size:
            pair = array + swapped(array, axis, step)
            array = pair + (swapped(array, axis, 2 * step) + swapped(array, axis, 3 * step))
            step *= 4
        else:
            array = array + swapped(array, axis, step)
            step *= 2
    return array


def join_kernel(mine_ref, other_ref, out_ref):
    count = mine_ref.shape[0]
    odd = lax.axis_index("ctx") % 2
    out_ref[pl.ds(pl.multiple_of(odd * count, count), count)] = mine_ref[...]
    out_ref[pl.ds(pl.multiple_of((1 - odd) * count, count), count)] = other_ref[...]


def join(mine, other):
    count, taps = mine.shape
    return pl.pallas_call(
        join_kernel,
        in_specs=[VMEM] * 2,
        out_specs=VMEM,
        out_shape=jax.ShapeDtypeStruct((2 * count, taps), mine.dtype),
        name="join",
        compiler_params=pltpu.CompilerParams(vmem_limit_bytes=MIB),
    )(mine, other)


def reversal(taps):
    flip = iota((taps, taps), 0) + iota((taps, taps), 1) == taps - 1
    return jnp.where(flip, 1.0, 0.0).astype(jnp.bfloat16)


def gates_kernel(
    q_hbm, k_hbm, v_hbm, ct_hbm, q_ref, k_ref, v_ref, ct_ref, near_ref, far_1_ref, far_2_ref, sems
):
    taps, channels = q_ref.shape
    half = channels // 2
    block = channels // CHUNKS
    pairs = ((k_hbm, k_ref), (v_hbm, v_ref), (q_hbm, q_ref), (ct_hbm, ct_ref))
    copies = []
    for c in range(CHUNKS):
        cols = pl.ds(c * block, block)
        for a, (source, target) in enumerate(pairs):
            copy = pltpu.make_async_copy(source.at[:, cols], target.at[:, cols], sems.at[c, a])
            copy.start()
            copies.append(copy)
    odd = lax.axis_index("ctx") % 2 == 1
    reverse = reversal(taps)
    for c in range(CHUNKS):
        cols = pl.ds(c * block, block)
        for copy in copies[4 * c : 4 * c + 4]:
            copy.wait()
        k, v, q, ct = [target[:, cols].astype(jnp.float32) for _, target in pairs]
        u = (k * v).astype(jnp.bfloat16)
        dy = (ct * q).astype(jnp.bfloat16)
        dy = jnp.dot(reverse, dy, preferred_element_type=jnp.float32).astype(jnp.bfloat16)
        first = c * block < half
        sent = pl.ds(c * block % half, block)

        @pl.when(odd)
        def _():
            near_ref[:, cols] = dy
            (far_1_ref if first else far_2_ref)[:, sent] = u

        @pl.when(jnp.logical_not(odd))
        def _():
            near_ref[:, cols] = u
            (far_2_ref if first else far_1_ref)[:, sent] = dy


def gates(q, k, v, ct):
    taps, channels = q.shape

    def shape(columns):
        return jax.ShapeDtypeStruct((taps, columns), jnp.bfloat16)

    half = channels // 2
    return pl.pallas_call(
        gates_kernel,
        in_specs=[pl.BlockSpec(memory_space=pltpu.HBM)] * 4,
        out_specs=[VMEM] * 7,
        out_shape=[shape(channels)] * 5 + [shape(half)] * 2,
        scratch_shapes=[pltpu.SemaphoreType.DMA((CHUNKS, 4))],
        name="gates",
        cost_estimate=pl.CostEstimate(
            flops=2 * taps * taps * channels, bytes_accessed=12 * taps * channels, transcendentals=0
        ),
        compiler_params=pltpu.CompilerParams(vmem_limit_bytes=GATES_VMEM),
    )(q, k, v, ct)


def masks_kernel(starts_ref, after_ref, keep_ref):
    del after_ref
    here = lax.axis_index("ctx")
    for side in range(2):
        found = here + side < 0
        for d in range(starts_ref.shape[0]):
            found = jnp.logical_or(found, starts_ref[d] == (here + side) * keep_ref.shape[1])
        keep = jnp.where(found, 0.0, 1.0)
        keep_ref[side] = jnp.full(keep_ref.shape[1:], keep).astype(jnp.bfloat16)


def masks(starts, after):
    return pl.pallas_call(
        masks_kernel,
        in_specs=[SMEM, pl.BlockSpec(memory_space=pl.ANY)],
        out_specs=VMEM,
        out_shape=jax.ShapeDtypeStruct((2, after.shape[0], LANES), jnp.bfloat16),
        name="masks",
        compiler_params=pltpu.CompilerParams(vmem_limit_bytes=MIB),
    )(starts, after)


def toeplitz_kernel(filters_ref, out_ref):
    count, taps = filters_ref.shape
    lines = filters_ref[...].astype(jnp.float32)
    current = iota((taps, taps), 0) <= iota((taps, taps), 1)
    for f in range(count):
        tile = jnp.broadcast_to(lines[f : f + 1], (taps, taps))
        tile = pltpu.roll(tile, 0, 1, stride=1, stride_axis=0)
        out_ref[f, :taps] = jnp.where(current, 0.0, tile).astype(jnp.bfloat16)
        out_ref[f, taps:] = jnp.where(current, tile, 0.0).astype(jnp.bfloat16)


def toeplitz(filters):
    count, taps = filters.shape
    return pl.pallas_call(
        toeplitz_kernel,
        in_specs=[VMEM],
        out_specs=VMEM,
        out_shape=jax.ShapeDtypeStruct((count, 2 * taps, taps), jnp.bfloat16),
        name="toeplitz",
        cost_estimate=pl.CostEstimate(
            flops=count * taps * taps * 64, bytes_accessed=4 * count * taps * taps, transcendentals=0
        ),
        compiler_params=pltpu.CompilerParams(vmem_limit_bytes=16 * MIB),
    )(filters)


def filter_grad_kernel(
    width, near_ref, far_2_ref, keep_ref, near_in_ref, extra_ref, far_in_ref, out_ref, lines
):
    taps, half = far_in_ref.shape
    per_group = LANES // width
    odd = lax.axis_index("ctx") % 2
    first = pl.multiple_of(odd * half, half)
    keep_far = keep_ref[odd]
    keep_near = keep_ref[1 - odd]
    lane_filter = iota((ROW_BLOCK, LANES), 1) // width
    fold = iota((ROW_BLOCK, taps), 1) + iota((ROW_BLOCK, taps), 0) < ROW_BLOCK
    for group in range(half // LANES):
        at = group * LANES
        cols = pl.ds(at, LANES)
        own = pl.ds(pl.multiple_of(first + at, LANES), LANES)
        near = near_ref[:, own]
        pairs = (
            (far_2_ref[:, cols], far_in_ref[:, cols] * keep_far, near),
            (near_in_ref[:, own], near * keep_near, extra_ref[:, cols]),
        )
        left, right = [], []
        for moving, beyond, fixed in pairs:
            window = jnp.concatenate([beyond, fixed], axis=0)
            for start in range(0, taps, ROW_BLOCK):
                piece = moving[start : start + ROW_BLOCK]
                left.append(
                    jnp.concatenate(
                        [jnp.where(lane_filter == i, piece, 0) for i in range(per_group)], axis=0
                    )
                )
                right.append(window[taps - ROW_BLOCK - start : 2 * taps - start])
        product = lax.dot_general(
            jnp.concatenate(left, axis=1),
            jnp.concatenate(right, axis=1),
            (((1,), (1,)), ((), ())),
            preferred_element_type=jnp.float32,
        )
        rows = []
        for i in range(per_group):
            tile = product[i * ROW_BLOCK : (i + 1) * ROW_BLOCK]
            high = jnp.concatenate(
                [tile[:, taps:], jnp.zeros((ROW_BLOCK, taps - ROW_BLOCK), jnp.float32)], axis=1
            )
            tile = jnp.where(fold, high, tile[:, :taps])
            tile = pltpu.roll(tile, taps - ROW_BLOCK + 1, 1, stride=1, stride_axis=0)
            rows.append(jnp.sum(tile, axis=0, keepdims=True))
        lines[group * per_group : (group + 1) * per_group] = jnp.concatenate(rows, axis=0)
    flip = jnp.where((iota((taps, taps), 0) + iota((taps, taps), 1)) % taps == 0, 1.0, 0.0)
    out_ref[...] = jnp.dot(
        lines[...], flip, preferred_element_type=jnp.float32, precision=lax.Precision.HIGHEST
    )


def filter_gradient(near, far_2, keep, near_in, extra, far_in, width):
    taps, half = far_2.shape
    count = half // width
    return pl.pallas_call(
        functools.partial(filter_grad_kernel, width),
        in_specs=[VMEM] * 6,
        out_specs=VMEM,
        out_shape=jax.ShapeDtypeStruct((count, taps), jnp.float32),
        scratch_shapes=[pltpu.VMEM((count, taps), jnp.float32)],
        name="filter_gradient",
        cost_estimate=pl.CostEstimate(
            flops=4 * count * taps * taps * 256, bytes_accessed=16 * taps * half, transcendentals=0
        ),
        compiler_params=pltpu.CompilerParams(vmem_limit_bytes=8 * MIB),
    )(near, far_2, keep, near_in, extra, far_in)


def outputs_kernel(
    width, base, q_ref, k_ref, v_ref, ct_ref, tiles_ref, near_ref, far_ref, keep_ref,
    near_in_ref, far_in_ref, *rest,
):
    *results, sems = rest[-5:]
    targets = rest[-9:-5]
    out, grad_q, grad_k, grad_v = results
    taps, half = far_ref.shape
    channels = out.shape[1]
    per_group = LANES // width
    odd = lax.axis_index("ctx") % 2
    keep_far = keep_ref[odd]
    keep_near = keep_ref[1 - odd]
    second = odd if base < half else 1 - odd
    base = base % half
    first = pl.multiple_of(second * half, half)
    whole = pl.ds(pl.multiple_of(first + base, channels), channels)
    reverse = reversal(taps)
    copies = []

    def flipped(array):
        return jnp.dot(reverse, array, preferred_element_type=jnp.float32)

    def send(which):
        copy = pltpu.make_async_copy(results[which], targets[which].at[:, whole], sems.at[which])
        copy.start()
        copies.append(copy)

    k_turned = flipped(k_ref[:, whole])
    v_turned = flipped(v_ref[:, whole])
    k_parts, v_parts = [], []
    for group in range(channels // LANES):
        own = pl.ds(group * LANES, LANES)
        sent = pl.ds(base + group * LANES, LANES)
        at = pl.multiple_of(first + base + group * LANES, LANES)
        cols = pl.ds(at, LANES)
        near_lines = jnp.concatenate(
            [(far_in_ref[:, sent] * keep_far).T, near_ref[:, cols].T], axis=1
        )
        far_lines = jnp.concatenate(
            [(near_in_ref[:, cols] * keep_near).T, far_ref[:, sent].T], axis=1
        )
        near_parts, far_parts = [], []
        for i in range(per_group):
            rows = slice(i * width, (i + 1) * width)
            both = jnp.concatenate([near_lines[rows], far_lines[rows]], axis=0)
            part = jnp.dot(both, tiles_ref[at // width + i], preferred_element_type=jnp.float32)
            near_parts.append(part[:width])
            far_parts.append(part[width:])
        near_sum = jnp.concatenate(near_parts, axis=0)
        far_sum = jnp.concatenate(far_parts, axis=0)
        y = jnp.where(odd == 1, far_sum, near_sum).T
        mixed = jnp.where(odd == 1, near_sum, far_sum).T
        out[:, own] = (q_ref[:, cols].astype(jnp.float32) * y).astype(jnp.bfloat16)
        grad_q[:, own] = (ct_ref[:, cols].astype(jnp.float32) * y).astype(jnp.bfloat16)
        lanes = slice(group * LANES, (group + 1) * LANES)
        k_parts.append((mixed * v_turned[:, lanes]).astype(jnp.bfloat16))
        v_parts.append((mixed * k_turned[:, lanes]).astype(jnp.bfloat16))
    send(0)
    send(1)
    grad_k[...] = flipped(jnp.concatenate(k_parts, axis=1)).astype(jnp.bfloat16)
    send(2)
    grad_v[...] = flipped(jnp.concatenate(v_parts, axis=1)).astype(jnp.bfloat16)
    send(3)
    for copy in copies:
        copy.wait()


def outputs(q, k, v, ct, tiles, near, fars, keep, near_in, far_ins, width):
    taps, channels = q.shape
    part = channels // PIECES
    anywhere = pl.BlockSpec(memory_space=pl.ANY)
    results = ()
    for piece in range(PIECES):
        base = piece * part
        side = 0 if base < channels // 2 else 1
        operands = (q, k, v, ct, tiles, near, fars[1 - side], keep, near_in, far_ins[side])
        results = pl.pallas_call(
            functools.partial(outputs_kernel, width, base),
            in_specs=[VMEM] * len(operands) + [anywhere] * len(results),
            out_specs=[anywhere] * 4,
            out_shape=[jax.ShapeDtypeStruct((taps, channels), jnp.bfloat16)] * 4,
            input_output_aliases={len(operands) + i: i for i in range(len(results))},
            scratch_shapes=[pltpu.VMEM((taps, part), jnp.bfloat16)] * 4
            + [pltpu.SemaphoreType.DMA((4,))],
            name=f"outputs_{piece}",
            cost_estimate=pl.CostEstimate(
                flops=16 * (part // width) * taps * taps * 256,
                bytes_accessed=24 * taps * part,
                transcendentals=0,
            ),
            compiler_params=pltpu.CompilerParams(vmem_limit_bytes=8 * MIB),
        )(*operands, *results)
    return results


def per_device(gate_in, key_in, value_in, cotangent, doc_starts, filters):
    taps = filters.shape[1]
    width = gate_in.shape[2] // filters.shape[0]
    assert gate_in.shape[1] == taps
    q, k, v, ct = gate_in[0], key_in[0], value_in[0], cotangent[0]
    q, k, v, ct, near, *fars = gates(q, k, v, ct)
    far_ins = [exchange(fars[0], "ctx", 1)]
    near_in = exchange(near, "ctx", 0)
    extra = exchange(fars[0], "ctx", 0)
    far_ins.append(exchange(fars[1], "ctx", 1))
    keep = masks(doc_starts[0], near)
    mine = filter_gradient(near, fars[1], keep, near_in, extra, far_ins[0], width)
    mine = sum_over(sum_over(mine, "ctx", 2), "dp", 1)
    filter_grad = join(mine, exchange(mine, "ctx", 0))
    tiles = toeplitz(filters)
    results = outputs(q, k, v, ct, tiles, near, fars, keep, near_in, far_ins, width)
    return tuple(array[None] for array in results) + (filter_grad,)


def solution(mesh):
    split = P("dp", "ctx", None)
    return jax.shard_map(
        per_device,
        mesh=mesh,
        in_specs=(split, split, split, split, P("dp", None), P()),
        out_specs=(split, split, split, split, P()),
        check_vma=False,
    )
```

```python
import functools

import jax
import jax.numpy as jnp
from jax import lax
from jax.experimental import pallas as pl
from jax.experimental.pallas import tpu as pltpu
from jax.sharding import PartitionSpec as P

LANES = 128
ROW_BLOCK = 32
MIB = 1024 * 1024
CHUNKS = 4
PIECES = 4
GATES_VMEM = 101 * MIB // 2
VMEM = pl.BlockSpec(memory_space=pltpu.VMEM)
SMEM = pl.BlockSpec(memory_space=pltpu.SMEM)


def iota(shape, dim):
    return lax.broadcasted_iota(jnp.int32, shape, dim)


def exchange(array, axis, first):
    size = lax.axis_size(axis)
    pairs = []
    for low in range(first, size - 1, 2):
        pairs += [(low, low + 1), (low + 1, low)]
    return lax.ppermute(array, axis, pairs)


def sum_halves(low, high):
    low = lax.psum(low, ("dp", "ctx"))
    low, high = lax.optimization_barrier((low, high))
    return jnp.concatenate([low, lax.psum(high, ("dp", "ctx"))], axis=0)


def reversal(taps):
    flip = iota((taps, taps), 0) + iota((taps, taps), 1) == taps - 1
    return jnp.where(flip, 1.0, 0.0).astype(jnp.bfloat16)


def gates_kernel(
    q_hbm, k_hbm, v_hbm, ct_hbm, q_ref, k_ref, v_ref, ct_ref, near_ref, far_1_ref, far_2_ref, sems
):
    taps, channels = q_ref.shape
    half = channels // 2
    block = channels // CHUNKS
    pairs = ((k_hbm, k_ref), (v_hbm, v_ref), (q_hbm, q_ref), (ct_hbm, ct_ref))
    copies = []
    for c in range(CHUNKS):
        cols = pl.ds(c * block, block)
        for a, (source, target) in enumerate(pairs):
            copy = pltpu.make_async_copy(source.at[:, cols], target.at[:, cols], sems.at[c, a])
            copy.start()
            copies.append(copy)
    odd = lax.axis_index("ctx") % 2 == 1
    reverse = reversal(taps)
    for c in range(CHUNKS):
        cols = pl.ds(c * block, block)
        for copy in copies[4 * c : 4 * c + 4]:
            copy.wait()
        k, v, q, ct = [target[:, cols].astype(jnp.float32) for _, target in pairs]
        u = (k * v).astype(jnp.bfloat16)
        dy = (ct * q).astype(jnp.bfloat16)
        dy = jnp.dot(reverse, dy, preferred_element_type=jnp.float32).astype(jnp.bfloat16)
        first = c * block < half
        sent = pl.ds(c * block % half, block)

        @pl.when(odd)
        def _():
            near_ref[:, cols] = dy
            (far_1_ref if first else far_2_ref)[:, sent] = u

        @pl.when(jnp.logical_not(odd))
        def _():
            near_ref[:, cols] = u
            (far_2_ref if first else far_1_ref)[:, sent] = dy


def gates(q, k, v, ct):
    taps, channels = q.shape

    def shape(columns):
        return jax.ShapeDtypeStruct((taps, columns), jnp.bfloat16)

    half = channels // 2
    return pl.pallas_call(
        gates_kernel,
        in_specs=[pl.BlockSpec(memory_space=pltpu.HBM)] * 4,
        out_specs=[VMEM] * 7,
        out_shape=[shape(channels)] * 5 + [shape(half)] * 2,
        scratch_shapes=[pltpu.SemaphoreType.DMA((CHUNKS, 4))],
        name="gates",
        cost_estimate=pl.CostEstimate(
            flops=2 * taps * taps * channels, bytes_accessed=12 * taps * channels, transcendentals=0
        ),
        compiler_params=pltpu.CompilerParams(vmem_limit_bytes=GATES_VMEM),
    )(q, k, v, ct)


def masks_kernel(starts_ref, after_ref, keep_ref):
    del after_ref
    here = lax.axis_index("ctx")
    for side in range(2):
        found = here + side < 0
        for d in range(starts_ref.shape[0]):
            found = jnp.logical_or(found, starts_ref[d] == (here + side) * keep_ref.shape[1])
        keep = jnp.where(found, 0.0, 1.0)
        keep_ref[side] = jnp.full(keep_ref.shape[1:], keep).astype(jnp.bfloat16)


def masks(starts, after):
    return pl.pallas_call(
        masks_kernel,
        in_specs=[SMEM, pl.BlockSpec(memory_space=pl.ANY)],
        out_specs=VMEM,
        out_shape=jax.ShapeDtypeStruct((2, after.shape[0], LANES), jnp.bfloat16),
        name="masks",
        compiler_params=pltpu.CompilerParams(vmem_limit_bytes=MIB),
    )(starts, after)


def toeplitz_kernel(filters_ref, out_ref):
    count, taps = filters_ref.shape
    lines = filters_ref[...].astype(jnp.float32)
    current = iota((taps, taps), 0) <= iota((taps, taps), 1)
    for f in range(count):
        tile = jnp.broadcast_to(lines[f : f + 1], (taps, taps))
        tile = pltpu.roll(tile, 0, 1, stride=1, stride_axis=0)
        out_ref[f, :taps] = jnp.where(current, 0.0, tile).astype(jnp.bfloat16)
        out_ref[f, taps:] = jnp.where(current, tile, 0.0).astype(jnp.bfloat16)


def toeplitz(filters):
    count, taps = filters.shape
    return pl.pallas_call(
        toeplitz_kernel,
        in_specs=[VMEM],
        out_specs=VMEM,
        out_shape=jax.ShapeDtypeStruct((count, 2 * taps, taps), jnp.bfloat16),
        name="toeplitz",
        cost_estimate=pl.CostEstimate(
            flops=count * taps * taps * 64, bytes_accessed=4 * count * taps * taps, transcendentals=0
        ),
        compiler_params=pltpu.CompilerParams(vmem_limit_bytes=16 * MIB),
    )(filters)


def filter_grad_kernel(
    width, near_ref, far_2_ref, keep_ref, near_in_ref, extra_ref, far_in_ref, low_ref, high_ref, lines
):
    taps, half = far_in_ref.shape
    per_group = LANES // width
    odd = lax.axis_index("ctx") % 2
    first = pl.multiple_of(odd * half, half)
    keep_far = keep_ref[odd]
    keep_near = keep_ref[1 - odd]
    lane_filter = iota((ROW_BLOCK, LANES), 1) // width
    fold = iota((ROW_BLOCK, taps), 1) + iota((ROW_BLOCK, taps), 0) < ROW_BLOCK
    for group in range(half // LANES):
        at = group * LANES
        cols = pl.ds(at, LANES)
        own = pl.ds(pl.multiple_of(first + at, LANES), LANES)
        near = near_ref[:, own]
        pairs = (
            (far_2_ref[:, cols], far_in_ref[:, cols] * keep_far, near),
            (near_in_ref[:, own], near * keep_near, extra_ref[:, cols]),
        )
        left, right = [], []
        for moving, beyond, fixed in pairs:
            window = jnp.concatenate([beyond, fixed], axis=0)
            for start in range(0, taps, ROW_BLOCK):
                piece = moving[start : start + ROW_BLOCK]
                left.append(
                    jnp.concatenate(
                        [jnp.where(lane_filter == i, piece, 0) for i in range(per_group)], axis=0
                    )
                )
                right.append(window[taps - ROW_BLOCK - start : 2 * taps - start])
        product = lax.dot_general(
            jnp.concatenate(left, axis=1),
            jnp.concatenate(right, axis=1),
            (((1,), (1,)), ((), ())),
            preferred_element_type=jnp.float32,
        )
        rows = []
        for i in range(per_group):
            tile = product[i * ROW_BLOCK : (i + 1) * ROW_BLOCK]
            high = jnp.concatenate(
                [tile[:, taps:], jnp.zeros((ROW_BLOCK, taps - ROW_BLOCK), jnp.float32)], axis=1
            )
            tile = jnp.where(fold, high, tile[:, :taps])
            tile = pltpu.roll(tile, taps - ROW_BLOCK + 1, 1, stride=1, stride_axis=0)
            rows.append(jnp.sum(tile, axis=0, keepdims=True))
        lines[group * per_group : (group + 1) * per_group] = jnp.concatenate(rows, axis=0)
    flip = jnp.where((iota((taps, taps), 0) + iota((taps, taps), 1)) % taps == 0, 1.0, 0.0)
    grads = jnp.dot(
        lines[...], flip, preferred_element_type=jnp.float32, precision=lax.Precision.HIGHEST
    )
    low_ref[...] = jnp.where(odd == 1, 0.0, grads)
    high_ref[...] = jnp.where(odd == 1, grads, 0.0)


def filter_gradient(near, far_2, keep, near_in, extra, far_in, width):
    taps, half = far_2.shape
    count = half // width
    return pl.pallas_call(
        functools.partial(filter_grad_kernel, width),
        in_specs=[VMEM] * 6,
        out_specs=[VMEM] * 2,
        out_shape=[jax.ShapeDtypeStruct((count, taps), jnp.float32)] * 2,
        scratch_shapes=[pltpu.VMEM((count, taps), jnp.float32)],
        name="filter_gradient",
        cost_estimate=pl.CostEstimate(
            flops=4 * count * taps * taps * 256, bytes_accessed=16 * taps * half, transcendentals=0
        ),
        compiler_params=pltpu.CompilerParams(vmem_limit_bytes=8 * MIB),
    )(near, far_2, keep, near_in, extra, far_in)


def outputs_kernel(
    width, base, q_ref, k_ref, v_ref, ct_ref, tiles_ref, near_ref, far_ref, keep_ref,
    near_in_ref, far_in_ref, *rest,
):
    *results, sems = rest[-5:]
    targets = rest[-9:-5]
    out, grad_q, grad_k, grad_v = results
    taps, half = far_ref.shape
    channels = out.shape[1]
    per_group = LANES // width
    odd = lax.axis_index("ctx") % 2
    keep_far = keep_ref[odd]
    keep_near = keep_ref[1 - odd]
    second = odd if base < half else 1 - odd
    base = base % half
    first = pl.multiple_of(second * half, half)
    whole = pl.ds(pl.multiple_of(first + base, channels), channels)
    reverse = reversal(taps)
    copies = []

    def flipped(array):
        return jnp.dot(reverse, array, preferred_element_type=jnp.float32)

    def send(which):
        copy = pltpu.make_async_copy(results[which], targets[which].at[:, whole], sems.at[which])
        copy.start()
        copies.append(copy)

    k_turned = flipped(k_ref[:, whole])
    v_turned = flipped(v_ref[:, whole])
    k_parts, v_parts = [], []
    for group in range(channels // LANES):
        own = pl.ds(group * LANES, LANES)
        sent = pl.ds(base + group * LANES, LANES)
        at = pl.multiple_of(first + base + group * LANES, LANES)
        cols = pl.ds(at, LANES)
        near_lines = jnp.concatenate(
            [(far_in_ref[:, sent] * keep_far).T, near_ref[:, cols].T], axis=1
        )
        far_lines = jnp.concatenate(
            [(near_in_ref[:, cols] * keep_near).T, far_ref[:, sent].T], axis=1
        )
        near_parts, far_parts = [], []
        for i in range(per_group):
            rows = slice(i * width, (i + 1) * width)
            both = jnp.concatenate([near_lines[rows], far_lines[rows]], axis=0)
            part = jnp.dot(both, tiles_ref[at // width + i], preferred_element_type=jnp.float32)
            near_parts.append(part[:width])
            far_parts.append(part[width:])
        near_sum = jnp.concatenate(near_parts, axis=0)
        far_sum = jnp.concatenate(far_parts, axis=0)
        y = jnp.where(odd == 1, far_sum, near_sum).T
        mixed = jnp.where(odd == 1, near_sum, far_sum).T
        out[:, own] = (q_ref[:, cols].astype(jnp.float32) * y).astype(jnp.bfloat16)
        grad_q[:, own] = (ct_ref[:, cols].astype(jnp.float32) * y).astype(jnp.bfloat16)
        lanes = slice(group * LANES, (group + 1) * LANES)
        k_parts.append((mixed * v_turned[:, lanes]).astype(jnp.bfloat16))
        v_parts.append((mixed * k_turned[:, lanes]).astype(jnp.bfloat16))
    send(0)
    send(1)
    grad_k[...] = flipped(jnp.concatenate(k_parts, axis=1)).astype(jnp.bfloat16)
    send(2)
    grad_v[...] = flipped(jnp.concatenate(v_parts, axis=1)).astype(jnp.bfloat16)
    send(3)
    for copy in copies:
        copy.wait()


def outputs(low, q, k, v, ct, tiles, near, fars, keep, near_in, far_ins, width):
    taps, channels = q.shape
    part = channels // PIECES
    anywhere = pl.BlockSpec(memory_space=pl.ANY)
    results = (low,)
    for piece in range(PIECES):
        base = piece * part
        side = 0 if base < channels // 2 else 1
        operands = (q, k, v, ct, tiles, near, fars[1 - side], keep, near_in, far_ins[side])
        results = pl.pallas_call(
            functools.partial(outputs_kernel, width, base),
            in_specs=[VMEM] * len(operands) + [anywhere] * len(results),
            out_specs=[anywhere] * 5,
            out_shape=[jax.ShapeDtypeStruct(low.shape, low.dtype)]
            + [jax.ShapeDtypeStruct((taps, channels), jnp.bfloat16)] * 4,
            input_output_aliases={len(operands) + i: i for i in range(len(results))},
            scratch_shapes=[pltpu.VMEM((taps, part), jnp.bfloat16)] * 4
            + [pltpu.SemaphoreType.DMA((4,))],
            name=f"outputs_{piece}",
            cost_estimate=pl.CostEstimate(
                flops=16 * (part // width) * taps * taps * 256,
                bytes_accessed=24 * taps * part,
                transcendentals=0,
            ),
            compiler_params=pltpu.CompilerParams(vmem_limit_bytes=8 * MIB),
        )(*operands, *results)
    return results


def per_device(gate_in, key_in, value_in, cotangent, doc_starts, filters):
    taps = filters.shape[1]
    width = gate_in.shape[2] // filters.shape[0]
    assert gate_in.shape[1] == taps
    q, k, v, ct = gate_in[0], key_in[0], value_in[0], cotangent[0]
    q, k, v, ct, near, *fars = gates(q, k, v, ct)
    far_ins = [exchange(fars[0], "ctx", 1)]
    near_in = exchange(near, "ctx", 0)
    extra = exchange(fars[0], "ctx", 0)
    far_ins.append(exchange(fars[1], "ctx", 1))
    keep = masks(doc_starts[0], near)
    low, high = filter_gradient(near, fars[1], keep, near_in, extra, far_ins[0], width)
    tiles = toeplitz(filters)
    low, *results = outputs(low, q, k, v, ct, tiles, near, fars, keep, near_in, far_ins, width)
    filter_grad = sum_halves(low, high)
    return tuple(array[None] for array in results) + (filter_grad,)


def solution(mesh):
    split = P("dp", "ctx", None)
    return jax.shard_map(
        per_device,
        mesh=mesh,
        in_specs=(split, split, split, split, P("dp", None), P()),
        out_specs=(split, split, split, split, P()),
        check_vma=False,
    )
```

```python
import functools

import jax
import jax.numpy as jnp
from jax import lax
from jax.experimental import pallas as pl
from jax.experimental.pallas import tpu as pltpu
from jax.sharding import PartitionSpec as P

LANES = 128
ROW_BLOCK = 32
MIB = 1024 * 1024
CHUNKS = 4
PIECES = 2
CHUNK = 512
GATES_VMEM = 101 * MIB // 2
VMEM = pl.BlockSpec(memory_space=pltpu.VMEM)
SMEM = pl.BlockSpec(memory_space=pltpu.SMEM)


def iota(shape, dim):
    return lax.broadcasted_iota(jnp.int32, shape, dim)


def exchange(array, axis, first):
    size = lax.axis_size(axis)
    pairs = []
    for low in range(first, size - 1, 2):
        pairs += [(low, low + 1), (low + 1, low)]
    return lax.ppermute(array, axis, pairs)


def swapped(array, axis, step):
    size = lax.axis_size(axis)
    return lax.ppermute(array, axis, [(i, i ^ step) for i in range(size)])


def spread_kernel(mine_ref, other_ref, after_ref, out_ref):
    del after_ref
    total = mine_ref[...] + other_ref[...]
    for i in range(out_ref.shape[0]):
        out_ref[i] = total


def spread(mine, other, after, copies):
    return pl.pallas_call(
        spread_kernel,
        in_specs=[VMEM] * 2 + [pl.BlockSpec(memory_space=pl.ANY)],
        out_specs=VMEM,
        out_shape=jax.ShapeDtypeStruct((copies, *mine.shape), mine.dtype),
        name="spread",
        compiler_params=pltpu.CompilerParams(vmem_limit_bytes=2 * MIB),
    )(mine, other, after)


def sum_planes(copies):
    seqs, blocks = lax.axis_size("dp"), lax.axis_size("ctx")
    groups = [
        [seq * blocks + chip + core for seq in range(seqs) for core in range(2)]
        for chip in range(0, blocks, 2)
    ]
    parts = lax.all_to_all(copies, ("dp", "ctx"), 0, 0, axis_index_groups=groups)
    parts = parts.reshape(seqs, 2, *parts.shape[1:])
    return jnp.sum(parts, axis=0).reshape(-1, parts.shape[-1])


def reversal(taps):
    flip = iota((taps, taps), 0) + iota((taps, taps), 1) == taps - 1
    return jnp.where(flip, 1.0, 0.0).astype(jnp.bfloat16)


def gates_kernel(
    q_hbm, k_hbm, v_hbm, ct_hbm, q_ref, k_ref, v_ref, ct_ref, near_ref, far_1_ref, far_2_ref, sems
):
    taps, channels = q_ref.shape
    half = channels // 2
    block = channels // CHUNKS
    pairs = ((k_hbm, k_ref), (v_hbm, v_ref), (q_hbm, q_ref), (ct_hbm, ct_ref))
    copies = []
    for c in range(CHUNKS):
        cols = pl.ds(c * block, block)
        for a, (source, target) in enumerate(pairs):
            copy = pltpu.make_async_copy(source.at[:, cols], target.at[:, cols], sems.at[c, a])
            copy.start()
            copies.append(copy)
    odd = lax.axis_index("ctx") % 2 == 1
    reverse = reversal(taps)
    for c in range(CHUNKS):
        cols = pl.ds(c * block, block)
        for copy in copies[4 * c : 4 * c + 4]:
            copy.wait()
        k, v, q, ct = [target[:, cols].astype(jnp.float32) for _, target in pairs]
        u = (k * v).astype(jnp.bfloat16)
        dy = (ct * q).astype(jnp.bfloat16)
        dy = jnp.dot(reverse, dy, preferred_element_type=jnp.float32).astype(jnp.bfloat16)
        first = c * block < half
        sent = pl.ds(c * block % half, block)

        @pl.when(odd)
        def _():
            near_ref[:, cols] = dy
            (far_1_ref if first else far_2_ref)[:, sent] = u

        @pl.when(jnp.logical_not(odd))
        def _():
            near_ref[:, cols] = u
            (far_2_ref if first else far_1_ref)[:, sent] = dy


def gates(q, k, v, ct):
    taps, channels = q.shape

    def shape(columns):
        return jax.ShapeDtypeStruct((taps, columns), jnp.bfloat16)

    half = channels // 2
    return pl.pallas_call(
        gates_kernel,
        in_specs=[pl.BlockSpec(memory_space=pltpu.HBM)] * 4,
        out_specs=[VMEM] * 7,
        out_shape=[shape(channels)] * 5 + [shape(half)] * 2,
        scratch_shapes=[pltpu.SemaphoreType.DMA((CHUNKS, 4))],
        name="gates",
        cost_estimate=pl.CostEstimate(
            flops=2 * taps * taps * channels, bytes_accessed=12 * taps * channels, transcendentals=0
        ),
        compiler_params=pltpu.CompilerParams(vmem_limit_bytes=GATES_VMEM),
    )(q, k, v, ct)


def prepare_kernel(filters_ref, starts_ref, through_in_ref, tiles_ref, keep_ref, through_ref):
    del through_in_ref, through_ref
    count, taps = filters_ref.shape
    lines = filters_ref[...].astype(jnp.float32)
    current = iota((taps, taps), 0) <= iota((taps, taps), 1)
    for f in range(count):
        tile = jnp.broadcast_to(lines[f : f + 1], (taps, taps))
        tile = pltpu.roll(tile, 0, 1, stride=1, stride_axis=0)
        tiles_ref[f, :taps] = jnp.where(current, 0.0, tile).astype(jnp.bfloat16)
        tiles_ref[f, taps:] = jnp.where(current, tile, 0.0).astype(jnp.bfloat16)
    here = lax.axis_index("ctx")
    for side in range(2):
        found = here + side < 0
        for d in range(starts_ref.shape[0]):
            found = jnp.logical_or(found, starts_ref[d] == (here + side) * taps)
        keep = jnp.where(found, 0.0, 1.0)
        keep_ref[side] = jnp.full(keep_ref.shape[1:], keep).astype(jnp.bfloat16)


def prepare(filters, starts, through):
    count, taps = filters.shape
    anywhere = pl.BlockSpec(memory_space=pl.ANY)
    return pl.pallas_call(
        prepare_kernel,
        in_specs=[VMEM, SMEM, anywhere],
        out_specs=[VMEM, VMEM, anywhere],
        out_shape=[
            jax.ShapeDtypeStruct((count, 2 * taps, taps), jnp.bfloat16),
            jax.ShapeDtypeStruct((2, taps, LANES), jnp.bfloat16),
            jax.ShapeDtypeStruct(through.shape, through.dtype),
        ],
        input_output_aliases={2: 2},
        name="prepare",
        cost_estimate=pl.CostEstimate(
            flops=count * taps * taps * 64, bytes_accessed=4 * count * taps * taps, transcendentals=0
        ),
        compiler_params=pltpu.CompilerParams(vmem_limit_bytes=8 * MIB),
    )(filters, starts, through)


def filter_grad_kernel(
    width, near_ref, far_2_ref, keep_ref, near_in_ref, extra_ref, far_in_ref, out_ref, lines
):
    taps, half = far_in_ref.shape
    per_group = LANES // width
    odd = lax.axis_index("ctx") % 2
    first = pl.multiple_of(odd * half, half)
    keep_far = keep_ref[odd]
    keep_near = keep_ref[1 - odd]
    lane_filter = iota((ROW_BLOCK, LANES), 1) // width
    fold = iota((ROW_BLOCK, taps), 1) + iota((ROW_BLOCK, taps), 0) < ROW_BLOCK
    for group in range(half // LANES):
        at = group * LANES
        cols = pl.ds(at, LANES)
        own = pl.ds(pl.multiple_of(first + at, LANES), LANES)
        near = near_ref[:, own]
        pairs = (
            (far_2_ref[:, cols], far_in_ref[:, cols] * keep_far, near),
            (near_in_ref[:, own], near * keep_near, extra_ref[:, cols]),
        )
        left, right = [], []
        for moving, beyond, fixed in pairs:
            window = jnp.concatenate([beyond, fixed], axis=0)
            for start in range(0, taps, ROW_BLOCK):
                piece = moving[start : start + ROW_BLOCK]
                left.append(
                    jnp.concatenate(
                        [jnp.where(lane_filter == i, piece, 0) for i in range(per_group)], axis=0
                    )
                )
                right.append(window[taps - ROW_BLOCK - start : 2 * taps - start])
        product = lax.dot_general(
            jnp.concatenate(left, axis=1),
            jnp.concatenate(right, axis=1),
            (((1,), (1,)), ((), ())),
            preferred_element_type=jnp.float32,
        )
        rows = []
        for i in range(per_group):
            tile = product[i * ROW_BLOCK : (i + 1) * ROW_BLOCK]
            high = jnp.concatenate(
                [tile[:, taps:], jnp.zeros((ROW_BLOCK, taps - ROW_BLOCK), jnp.float32)], axis=1
            )
            tile = jnp.where(fold, high, tile[:, :taps])
            tile = pltpu.roll(tile, taps - ROW_BLOCK + 1, 1, stride=1, stride_axis=0)
            rows.append(jnp.sum(tile, axis=0, keepdims=True))
        lines[group * per_group : (group + 1) * per_group] = jnp.concatenate(rows, axis=0)
    flip = jnp.where((iota((taps, taps), 0) + iota((taps, taps), 1)) % taps == 0, 1.0, 0.0)
    out_ref[...] = jnp.dot(
        lines[...], flip, preferred_element_type=jnp.float32, precision=lax.Precision.HIGHEST
    )


def filter_gradient(near, far_2, keep, near_in, extra, far_in, width):
    taps, half = far_2.shape
    count = half // width
    return pl.pallas_call(
        functools.partial(filter_grad_kernel, width),
        in_specs=[VMEM] * 6,
        out_specs=VMEM,
        out_shape=jax.ShapeDtypeStruct((count, taps), jnp.float32),
        scratch_shapes=[pltpu.VMEM((count, taps), jnp.float32)],
        name="filter_gradient",
        cost_estimate=pl.CostEstimate(
            flops=4 * count * taps * taps * 256, bytes_accessed=16 * taps * half, transcendentals=0
        ),
        compiler_params=pltpu.CompilerParams(vmem_limit_bytes=8 * MIB),
    )(near, far_2, keep, near_in, extra, far_in)


def outputs_kernel(
    width, base, q_ref, k_ref, v_ref, ct_ref, tiles_ref, near_ref, far_ref, keep_ref,
    near_in_ref, far_in_ref, *rest,
):
    *results, sems = rest[-5:]
    *targets, done_ref = rest[-10:-5]
    out, grad_q, grad_k, grad_v = results
    taps, half = far_ref.shape
    channels = out.shape[1]
    per_group = LANES // width
    odd = lax.axis_index("ctx") % 2
    keep_far = keep_ref[odd]
    keep_near = keep_ref[1 - odd]
    second = odd if base < half else 1 - odd
    base = base % half
    first = pl.multiple_of(second * half, half)
    reverse = reversal(taps)
    copies = []

    def flipped(array):
        return jnp.dot(reverse, array, preferred_element_type=jnp.float32)

    def send(which, at, sem):
        own = pl.ds(at, CHUNK)
        cols = pl.ds(pl.multiple_of(first + base + at, CHUNK), CHUNK)
        copy = pltpu.make_async_copy(results[which].at[:, own], targets[which].at[:, cols], sem)
        copy.start()
        copies.append(copy)

    for chunk in range(0, channels, CHUNK):
        whole = pl.ds(pl.multiple_of(first + base + chunk, CHUNK), CHUNK)
        k_turned = flipped(k_ref[:, whole])
        v_turned = flipped(v_ref[:, whole])
        k_parts, v_parts = [], []
        for lane in range(0, CHUNK, LANES):
            own = pl.ds(chunk + lane, LANES)
            sent = pl.ds(base + chunk + lane, LANES)
            at = pl.multiple_of(first + base + chunk + lane, LANES)
            cols = pl.ds(at, LANES)
            near_lines = jnp.concatenate(
                [(far_in_ref[:, sent] * keep_far).T, near_ref[:, cols].T], axis=1
            )
            far_lines = jnp.concatenate(
                [(near_in_ref[:, cols] * keep_near).T, far_ref[:, sent].T], axis=1
            )
            near_parts, far_parts = [], []
            for i in range(per_group):
                rows = slice(i * width, (i + 1) * width)
                both = jnp.concatenate([near_lines[rows], far_lines[rows]], axis=0)
                part = jnp.dot(both, tiles_ref[at // width + i], preferred_element_type=jnp.float32)
                near_parts.append(part[:width])
                far_parts.append(part[width:])
            near_sum = jnp.concatenate(near_parts, axis=0)
            far_sum = jnp.concatenate(far_parts, axis=0)
            y = jnp.where(odd == 1, far_sum, near_sum).T
            mixed = jnp.where(odd == 1, near_sum, far_sum).T
            out[:, own] = (q_ref[:, cols].astype(jnp.float32) * y).astype(jnp.bfloat16)
            grad_q[:, own] = (ct_ref[:, cols].astype(jnp.float32) * y).astype(jnp.bfloat16)
            lanes = slice(lane, lane + LANES)
            k_parts.append((mixed * v_turned[:, lanes]).astype(jnp.bfloat16))
            v_parts.append((mixed * k_turned[:, lanes]).astype(jnp.bfloat16))
        own = pl.ds(chunk, CHUNK)
        turn = chunk // CHUNK
        send(0, chunk, sems.at[turn, 0])
        send(1, chunk, sems.at[turn, 1])
        grad_k[:, own] = flipped(jnp.concatenate(k_parts, axis=1)).astype(jnp.bfloat16)
        send(2, chunk, sems.at[turn, 2])
        grad_v[:, own] = flipped(jnp.concatenate(v_parts, axis=1)).astype(jnp.bfloat16)
        send(3, chunk, sems.at[turn, 3])
    for copy in copies:
        copy.wait()
    done_ref[...] = jnp.zeros_like(done_ref)


def outputs(q, k, v, ct, tiles, near, fars, keep, near_in, far_ins, width):
    taps, channels = q.shape
    part = channels // PIECES
    anywhere = pl.BlockSpec(memory_space=pl.ANY)
    results = ()
    for piece in range(PIECES):
        base = piece * part
        side = 0 if base < channels // 2 else 1
        operands = (q, k, v, ct, tiles, near, fars[1 - side], keep, near_in, far_ins[side])
        *results, done = pl.pallas_call(
            functools.partial(outputs_kernel, width, base),
            in_specs=[VMEM] * len(operands) + [anywhere] * len(results),
            out_specs=[anywhere] * 4 + [VMEM],
            out_shape=[jax.ShapeDtypeStruct((taps, channels), jnp.bfloat16)] * 4
            + [jax.ShapeDtypeStruct((8, LANES), jnp.float32)],
            input_output_aliases={len(operands) + i: i for i in range(len(results))},
            scratch_shapes=[pltpu.VMEM((taps, part), jnp.bfloat16)] * 4
            + [pltpu.SemaphoreType.DMA((part // CHUNK, 4))],
            name=f"outputs_{piece}",
            cost_estimate=pl.CostEstimate(
                flops=16 * (part // width) * taps * taps * 256,
                bytes_accessed=24 * taps * part,
                transcendentals=0,
            ),
            compiler_params=pltpu.CompilerParams(vmem_limit_bytes=8 * MIB),
        )(*operands, *results)
    return results, done


def per_device(gate_in, key_in, value_in, cotangent, doc_starts, filters):
    taps = filters.shape[1]
    width = gate_in.shape[2] // filters.shape[0]
    assert gate_in.shape[1] == taps
    q, k, v, ct = gate_in[0], key_in[0], value_in[0], cotangent[0]
    q, k, v, ct, near, far_1, far_2 = gates(q, k, v, ct)
    far_in_1 = exchange(far_1, "ctx", 1)
    near_in = exchange(near, "ctx", 0)
    extra = exchange(far_1, "ctx", 0)
    tiles, keep, far_2 = prepare(filters, doc_starts[0], far_2)
    far_in_2 = exchange(far_2, "ctx", 1)
    mine = filter_gradient(near, far_2, keep, near_in, extra, far_in_1, width)
    fars, far_ins = (far_1, far_2), (far_in_1, far_in_2)
    results, done = outputs(q, k, v, ct, tiles, near, fars, keep, near_in, far_ins, width)
    blocks = lax.axis_size("ctx")
    step = 2
    while 2 * step < blocks:
        mine = mine + swapped(mine, "ctx", step)
        step *= 2
    copies = spread(mine, swapped(mine, "ctx", step), done, 2 * lax.axis_size("dp"))
    return tuple(array[None] for array in results) + (sum_planes(copies),)


def solution(mesh):
    split = P("dp", "ctx", None)
    return jax.shard_map(
        per_device,
        mesh=mesh,
        in_specs=(split, split, split, split, P("dp", None), P()),
        out_specs=(split, split, split, split, P()),
        check_vma=False,
    )
```

```python
import functools

import jax
import jax.numpy as jnp
from jax import lax
from jax.experimental import pallas as pl
from jax.experimental.pallas import tpu as pltpu
from jax.sharding import PartitionSpec as P

LANES = 128
ROW_BLOCK = 32
MIB = 1024 * 1024
CHUNKS = 4
PIECES = 2
CHUNK = 512
GATES_VMEM = 101 * MIB // 2
VMEM = pl.BlockSpec(memory_space=pltpu.VMEM)
SMEM = pl.BlockSpec(memory_space=pltpu.SMEM)


def iota(shape, dim):
    return lax.broadcasted_iota(jnp.int32, shape, dim)


def exchange(array, axis, first):
    size = lax.axis_size(axis)
    pairs = []
    for low in range(first, size - 1, 2):
        pairs += [(low, low + 1), (low + 1, low)]
    return lax.ppermute(array, axis, pairs)


def swapped(array, axis, step):
    size = lax.axis_size(axis)
    return lax.ppermute(array, axis, [(i, i ^ step) for i in range(size)])


def along(array, axis):
    size = lax.axis_size(axis)
    pairs = [(i, i + 2 if i % 2 else i - 2) for i in range(size)]
    return lax.ppermute(array, axis, [(i, j) for i, j in pairs if 0 <= j < size])


def add_kernel(mine_ref, other_ref, after_ref, out_ref):
    del after_ref
    out_ref[...] = mine_ref[...] + other_ref[...]


def add(mine, other, after):
    return pl.pallas_call(
        add_kernel,
        in_specs=[VMEM] * 2 + [pl.BlockSpec(memory_space=pl.ANY)],
        out_specs=VMEM,
        out_shape=jax.ShapeDtypeStruct(mine.shape, mine.dtype),
        name="add",
        compiler_params=pltpu.CompilerParams(vmem_limit_bytes=MIB),
    )(mine, other, after)


def sum_chips(mine, beside):
    size = lax.axis_size("ctx")
    step, turn = 2, 0
    while step < size:
        mine = add(mine, swapped(mine, "ctx", step), beside(mine, turn))
        step, turn = 2 * step, turn + 1
    return mine


def sum_sequences(mine):
    size = lax.axis_size("dp")
    step = 1
    while 4 * step <= size:
        pair = mine + swapped(mine, "dp", step)
        mine = pair + (swapped(mine, "dp", 2 * step) + swapped(mine, "dp", 3 * step))
        step *= 4
    while step < size:
        mine = mine + swapped(mine, "dp", step)
        step *= 2
    return mine


def join_kernel(mine_ref, other_ref, out_ref):
    count = mine_ref.shape[0]
    odd = lax.axis_index("ctx") % 2
    out_ref[pl.ds(pl.multiple_of(odd * count, count), count)] = mine_ref[...]
    out_ref[pl.ds(pl.multiple_of((1 - odd) * count, count), count)] = other_ref[...]


def join(mine, other):
    count, taps = mine.shape
    return pl.pallas_call(
        join_kernel,
        in_specs=[VMEM] * 2,
        out_specs=VMEM,
        out_shape=jax.ShapeDtypeStruct((2 * count, taps), mine.dtype),
        name="join",
        compiler_params=pltpu.CompilerParams(vmem_limit_bytes=MIB),
    )(mine, other)


def reversal(taps):
    flip = iota((taps, taps), 0) + iota((taps, taps), 1) == taps - 1
    return jnp.where(flip, 1.0, 0.0).astype(jnp.bfloat16)


def gates_kernel(
    q_hbm, k_hbm, v_hbm, ct_hbm, q_ref, k_ref, v_ref, ct_ref, near_ref, other_ref, own_ref, sems
):
    taps, channels = q_ref.shape
    half = channels // 2
    block = channels // CHUNKS
    pairs = ((k_hbm, k_ref), (v_hbm, v_ref), (q_hbm, q_ref), (ct_hbm, ct_ref))
    copies = []
    for c in range(CHUNKS):
        cols = pl.ds(c * block, block)
        for a, (source, target) in enumerate(pairs):
            copy = pltpu.make_async_copy(source.at[:, cols], target.at[:, cols], sems.at[c, a])
            copy.start()
            copies.append(copy)
    odd = lax.axis_index("ctx") % 2 == 1
    reverse = reversal(taps)
    for c in range(CHUNKS):
        cols = pl.ds(c * block, block)
        for copy in copies[4 * c : 4 * c + 4]:
            copy.wait()
        k, v, q, ct = [target[:, cols].astype(jnp.float32) for _, target in pairs]
        u = (k * v).astype(jnp.bfloat16)
        dy = (ct * q).astype(jnp.bfloat16)
        dy = jnp.dot(reverse, dy, preferred_element_type=jnp.float32).astype(jnp.bfloat16)
        first = c * block < half
        sent = pl.ds(c * block % half, block)

        @pl.when(odd)
        def _():
            near_ref[:, cols] = dy
            (other_ref if first else own_ref)[:, sent] = u

        @pl.when(jnp.logical_not(odd))
        def _():
            near_ref[:, cols] = u
            (own_ref if first else other_ref)[:, sent] = dy


def gates(q, k, v, ct):
    taps, channels = q.shape

    def shape(columns):
        return jax.ShapeDtypeStruct((taps, columns), jnp.bfloat16)

    half = channels // 2
    return pl.pallas_call(
        gates_kernel,
        in_specs=[pl.BlockSpec(memory_space=pltpu.HBM)] * 4,
        out_specs=[VMEM] * 7,
        out_shape=[shape(channels)] * 5 + [shape(half)] * 2,
        scratch_shapes=[pltpu.SemaphoreType.DMA((CHUNKS, 4))],
        name="gates",
        cost_estimate=pl.CostEstimate(
            flops=2 * taps * taps * channels, bytes_accessed=12 * taps * channels, transcendentals=0
        ),
        compiler_params=pltpu.CompilerParams(vmem_limit_bytes=GATES_VMEM),
    )(q, k, v, ct)


def prepare_kernel(filters_ref, starts_ref, through_in_ref, tiles_ref, keep_ref, through_ref):
    del through_in_ref, through_ref
    count, taps = filters_ref.shape
    lines = filters_ref[...].astype(jnp.float32)
    current = iota((taps, taps), 0) <= iota((taps, taps), 1)
    for f in range(count):
        tile = jnp.broadcast_to(lines[f : f + 1], (taps, taps))
        tile = pltpu.roll(tile, 0, 1, stride=1, stride_axis=0)
        tiles_ref[f, :taps] = jnp.where(current, 0.0, tile).astype(jnp.bfloat16)
        tiles_ref[f, taps:] = jnp.where(current, tile, 0.0).astype(jnp.bfloat16)
    here = lax.axis_index("ctx")
    for i in range(keep_ref.shape[0]):
        found = here < 0
        for d in range(starts_ref.shape[0]):
            found = jnp.logical_or(found, starts_ref[d] == (here + i - 1) * taps)
        keep = jnp.where(found, 0.0, 1.0)
        keep_ref[i] = jnp.full(keep_ref.shape[1:], keep).astype(jnp.bfloat16)


def prepare(filters, starts, through):
    count, taps = filters.shape
    anywhere = pl.BlockSpec(memory_space=pl.ANY)
    return pl.pallas_call(
        prepare_kernel,
        in_specs=[VMEM, SMEM, anywhere],
        out_specs=[VMEM, VMEM, anywhere],
        out_shape=[
            jax.ShapeDtypeStruct((count, 2 * taps, taps), jnp.bfloat16),
            jax.ShapeDtypeStruct((4, taps, LANES), jnp.bfloat16),
            jax.ShapeDtypeStruct(through.shape, through.dtype),
        ],
        input_output_aliases={2: 2},
        name="prepare",
        cost_estimate=pl.CostEstimate(
            flops=count * taps * taps * 64, bytes_accessed=4 * count * taps * taps, transcendentals=0
        ),
        compiler_params=pltpu.CompilerParams(vmem_limit_bytes=8 * MIB),
    )(filters, starts, through)


def filter_grad_kernel(
    width, near_ref, own_ref, keep_ref, near_in_ref, extra_ref, far_in_ref, out_ref, far_ref, lines
):
    del far_ref
    taps, half = own_ref.shape
    per_group = LANES // width
    odd = lax.axis_index("ctx") % 2
    first = pl.multiple_of(odd * half, half)
    keep_far = keep_ref[3 - 3 * odd]
    keep_near = keep_ref[2 - odd]
    lane_filter = iota((ROW_BLOCK, LANES), 1) // width
    fold = iota((ROW_BLOCK, taps), 1) + iota((ROW_BLOCK, taps), 0) < ROW_BLOCK
    for group in range(half // LANES):
        at = group * LANES
        cols = pl.ds(at, LANES)
        own = pl.ds(pl.multiple_of(first + at, LANES), LANES)
        near_in = near_in_ref[:, own]
        pairs = (
            (extra_ref[:, cols], far_in_ref[:, cols] * keep_far, near_in),
            (near_ref[:, own], near_in * keep_near, own_ref[:, cols]),
        )
        left, right = [], []
        for moving, beyond, fixed in pairs:
            window = jnp.concatenate([beyond, fixed], axis=0)
            for start in range(0, taps, ROW_BLOCK):
                piece = moving[start : start + ROW_BLOCK]
                left.append(
                    jnp.concatenate(
                        [jnp.where(lane_filter == i, piece, 0) for i in range(per_group)], axis=0
                    )
                )
                right.append(window[taps - ROW_BLOCK - start : 2 * taps - start])
        product = lax.dot_general(
            jnp.concatenate(left, axis=1),
            jnp.concatenate(right, axis=1),
            (((1,), (1,)), ((), ())),
            preferred_element_type=jnp.float32,
        )
        rows = []
        for i in range(per_group):
            tile = product[i * ROW_BLOCK : (i + 1) * ROW_BLOCK]
            high = jnp.concatenate(
                [tile[:, taps:], jnp.zeros((ROW_BLOCK, taps - ROW_BLOCK), jnp.float32)], axis=1
            )
            tile = jnp.where(fold, high, tile[:, :taps])
            tile = pltpu.roll(tile, taps - ROW_BLOCK + 1, 1, stride=1, stride_axis=0)
            rows.append(jnp.sum(tile, axis=0, keepdims=True))
        lines[group * per_group : (group + 1) * per_group] = jnp.concatenate(rows, axis=0)
    flip = jnp.where((iota((taps, taps), 0) + iota((taps, taps), 1)) % taps == 0, 1.0, 0.0)
    out_ref[...] = jnp.dot(
        lines[...], flip, preferred_element_type=jnp.float32, precision=lax.Precision.HIGHEST
    )


def filter_gradient(near, own, keep, near_in, extra, far_in, width):
    taps, half = own.shape
    count = half // width
    return pl.pallas_call(
        functools.partial(filter_grad_kernel, width),
        in_specs=[VMEM] * 6,
        out_specs=[VMEM, VMEM],
        out_shape=[
            jax.ShapeDtypeStruct((count, taps), jnp.float32),
            jax.ShapeDtypeStruct(far_in.shape, far_in.dtype),
        ],
        input_output_aliases={5: 1},
        scratch_shapes=[pltpu.VMEM((count, taps), jnp.float32)],
        name="filter_gradient",
        cost_estimate=pl.CostEstimate(
            flops=4 * count * taps * taps * 256, bytes_accessed=16 * taps * half, transcendentals=0
        ),
        compiler_params=pltpu.CompilerParams(vmem_limit_bytes=8 * MIB),
    )(near, own, keep, near_in, extra, far_in)


def outputs_kernel(
    width, base, q_ref, k_ref, v_ref, ct_ref, tiles_ref, near_ref, far_ref, keep_ref,
    near_in_ref, far_in_ref, *rest,
):
    *results, sems = rest[-5:]
    *targets, done_ref = rest[-10:-5]
    out, grad_q, grad_k, grad_v = results
    taps, half = far_ref.shape
    channels = out.shape[1]
    per_group = LANES // width
    odd = lax.axis_index("ctx") % 2
    keep_far = keep_ref[1 + odd]
    keep_near = keep_ref[2 - odd]
    second = 1 - odd if base < half else odd
    base = base % half
    first = pl.multiple_of(second * half, half)
    reverse = reversal(taps)
    copies = []

    def flipped(array):
        return jnp.dot(reverse, array, preferred_element_type=jnp.float32)

    def send(which, at, sem):
        own = pl.ds(at, CHUNK)
        cols = pl.ds(pl.multiple_of(first + base + at, CHUNK), CHUNK)
        copy = pltpu.make_async_copy(results[which].at[:, own], targets[which].at[:, cols], sem)
        copy.start()
        copies.append(copy)

    for chunk in range(0, channels, CHUNK):
        whole = pl.ds(pl.multiple_of(first + base + chunk, CHUNK), CHUNK)
        k_turned = flipped(k_ref[:, whole])
        v_turned = flipped(v_ref[:, whole])
        k_parts, v_parts = [], []
        for lane in range(0, CHUNK, LANES):
            own = pl.ds(chunk + lane, LANES)
            sent = pl.ds(base + chunk + lane, LANES)
            at = pl.multiple_of(first + base + chunk + lane, LANES)
            cols = pl.ds(at, LANES)
            near_lines = jnp.concatenate(
                [(far_in_ref[:, sent] * keep_far).T, near_ref[:, cols].T], axis=1
            )
            far_lines = jnp.concatenate(
                [(near_in_ref[:, cols] * keep_near).T, far_ref[:, sent].T], axis=1
            )
            near_parts, far_parts = [], []
            for i in range(per_group):
                rows = slice(i * width, (i + 1) * width)
                both = jnp.concatenate([near_lines[rows], far_lines[rows]], axis=0)
                part = jnp.dot(both, tiles_ref[at // width + i], preferred_element_type=jnp.float32)
                near_parts.append(part[:width])
                far_parts.append(part[width:])
            near_sum = jnp.concatenate(near_parts, axis=0)
            far_sum = jnp.concatenate(far_parts, axis=0)
            y = jnp.where(odd == 1, far_sum, near_sum).T
            mixed = jnp.where(odd == 1, near_sum, far_sum).T
            out[:, own] = (q_ref[:, cols].astype(jnp.float32) * y).astype(jnp.bfloat16)
            grad_q[:, own] = (ct_ref[:, cols].astype(jnp.float32) * y).astype(jnp.bfloat16)
            lanes = slice(lane, lane + LANES)
            k_parts.append((mixed * v_turned[:, lanes]).astype(jnp.bfloat16))
            v_parts.append((mixed * k_turned[:, lanes]).astype(jnp.bfloat16))
        own = pl.ds(chunk, CHUNK)
        turn = chunk // CHUNK
        send(0, chunk, sems.at[turn, 0])
        send(1, chunk, sems.at[turn, 1])
        grad_k[:, own] = flipped(jnp.concatenate(k_parts, axis=1)).astype(jnp.bfloat16)
        send(2, chunk, sems.at[turn, 2])
        grad_v[:, own] = flipped(jnp.concatenate(v_parts, axis=1)).astype(jnp.bfloat16)
        send(3, chunk, sems.at[turn, 3])
    for copy in copies:
        copy.wait()
    done_ref[...] = jnp.zeros_like(done_ref)


def outputs(piece, operands, results, after, width):
    taps, channels = operands[0].shape
    part = channels // PIECES
    anywhere = pl.BlockSpec(memory_space=pl.ANY)
    shape = jax.ShapeDtypeStruct((taps, channels), jnp.bfloat16)
    *results, done = pl.pallas_call(
        functools.partial(outputs_kernel, width, piece * part),
        in_specs=[VMEM] * len(operands) + [anywhere] * (1 + len(results)),
        out_specs=[anywhere] * 4 + [VMEM],
        out_shape=[shape] * 4 + [jax.ShapeDtypeStruct((8, LANES), jnp.float32)],
        input_output_aliases={len(operands) + 1 + i: i for i in range(len(results))},
        scratch_shapes=[pltpu.VMEM((taps, part), jnp.bfloat16)] * 4
        + [pltpu.SemaphoreType.DMA((part // CHUNK, 4))],
        name=f"outputs_{piece}",
        cost_estimate=pl.CostEstimate(
            flops=16 * (part // width) * taps * taps * 256,
            bytes_accessed=24 * taps * part,
            transcendentals=0,
        ),
        compiler_params=pltpu.CompilerParams(vmem_limit_bytes=8 * MIB),
    )(*operands, after, *results)
    return results, done


def per_device(gate_in, key_in, value_in, cotangent, doc_starts, filters):
    taps = filters.shape[1]
    width = gate_in.shape[2] // filters.shape[0]
    assert gate_in.shape[1] == taps
    q, k, v, ct = gate_in[0], key_in[0], value_in[0], cotangent[0]
    q, k, v, ct, near, other, own = gates(q, k, v, ct)
    near_in = exchange(near, "ctx", 0)
    extra = exchange(other, "ctx", 0)
    own_in = along(own, "ctx")
    tiles, keep, other = prepare(filters, doc_starts[0], other)
    other_in = along(other, "ctx")
    mine, own_in = filter_gradient(near, own, keep, near_in, extra, own_in, width)
    fars = (other, own)
    far_ins = (exchange(own_in, "ctx", 0), exchange(other_in, "ctx", 0))
    results = []

    def next_piece(after, piece):
        nonlocal results
        if piece >= PIECES:
            return after
        operands = (q, k, v, ct, tiles, near, fars[piece], keep, near_in, far_ins[piece])
        results, done = outputs(piece, operands, results, after, width)
        return done

    mine = sum_sequences(sum_chips(mine, next_piece))
    filter_grad = join(mine, exchange(mine, "ctx", 0))
    return tuple(array[None] for array in results) + (filter_grad,)


def solution(mesh):
    split = P("dp", "ctx", None)
    return jax.shard_map(
        per_device,
        mesh=mesh,
        in_specs=(split, split, split, split, P("dp", None), P()),
        out_specs=(split, split, split, split, P()),
        check_vma=False,
    )
```

```python
import functools

import jax
import jax.numpy as jnp
from jax import lax
from jax.experimental import pallas as pl
from jax.experimental.pallas import tpu as pltpu
from jax.sharding import PartitionSpec as P

LANES = 128
ROW_BLOCK = 32
MIB = 1024 * 1024
CHUNKS = 4
PIECES = 2
CHUNK = 512
FIRST_VMEM = 213 * MIB // 4
GATES_VMEM = 101 * MIB // 2
VMEM = pl.BlockSpec(memory_space=pltpu.VMEM)
SMEM = pl.BlockSpec(memory_space=pltpu.SMEM)


def iota(shape, dim):
    return lax.broadcasted_iota(jnp.int32, shape, dim)


def exchange(array, axis, first):
    size = lax.axis_size(axis)
    pairs = []
    for low in range(first, size - 1, 2):
        pairs += [(low, low + 1), (low + 1, low)]
    return lax.ppermute(array, axis, pairs)


def swapped(array, axis, step):
    size = lax.axis_size(axis)
    return lax.ppermute(array, axis, [(i, i ^ step) for i in range(size)])


def swapped(array, axis, step):
    size = lax.axis_size(axis)
    return lax.ppermute(array, axis, [(i, i ^ step) for i in range(size)])


def along(array, axis):
    size = lax.axis_size(axis)
    pairs = [(i, i + 2 if i % 2 else i - 2) for i in range(size)]
    return lax.ppermute(array, axis, [(i, j) for i, j in pairs if 0 <= j < size])


def add_kernel(mine_ref, other_ref, after_ref, out_ref):
    del after_ref
    out_ref[...] = mine_ref[...] + other_ref[...]


def add(mine, other, after):
    return pl.pallas_call(
        add_kernel,
        in_specs=[VMEM] * 2 + [pl.BlockSpec(memory_space=pl.ANY)],
        out_specs=VMEM,
        out_shape=jax.ShapeDtypeStruct(mine.shape, mine.dtype),
        name="add",
        compiler_params=pltpu.CompilerParams(vmem_limit_bytes=MIB),
    )(mine, other, after)


def sum_devices(mine, beside):
    turn = 0
    for axis, step in (("dp", 1), ("ctx", 2)):
        while step < lax.axis_size(axis):
            mine = add(mine, swapped(mine, axis, step), beside(mine, turn))
            step, turn = 2 * step, turn + 1
    return mine


def join_kernel(mine_ref, other_ref, out_ref):
    count = mine_ref.shape[0]
    odd = lax.axis_index("ctx") % 2
    out_ref[pl.ds(pl.multiple_of(odd * count, count), count)] = mine_ref[...]
    out_ref[pl.ds(pl.multiple_of((1 - odd) * count, count), count)] = other_ref[...]


def join(mine, other):
    count, taps = mine.shape
    return pl.pallas_call(
        join_kernel,
        in_specs=[VMEM] * 2,
        out_specs=VMEM,
        out_shape=jax.ShapeDtypeStruct((2 * count, taps), mine.dtype),
        name="join",
        compiler_params=pltpu.CompilerParams(vmem_limit_bytes=MIB),
    )(mine, other)


def reversal(taps):
    flip = iota((taps, taps), 0) + iota((taps, taps), 1) == taps - 1
    return jnp.where(flip, 1.0, 0.0).astype(jnp.bfloat16)


def flipped(reverse, array):
    return jnp.dot(reverse, array, preferred_element_type=jnp.float32)


def masked(array, keep):
    return array * jnp.concatenate([keep] * (array.shape[0] // keep.shape[0]), axis=0)


def bf16_product(one, two):
    return (one.astype(jnp.float32) * two.astype(jnp.float32)).astype(jnp.bfloat16)


def first_kernel(q_hbm, k_hbm, v_hbm, ct_hbm, other_ref, held, sems):
    taps, half = other_ref.shape
    block = half // CHUNKS
    odd = lax.axis_index("ctx") % 2 == 1
    reverse = reversal(taps)

    def make(sources, start, finish):
        copies = []
        for c in range(CHUNKS):
            for a, source in enumerate(sources):
                copy = pltpu.make_async_copy(
                    source.at[:, pl.ds(start + c * block, block)],
                    held.at[a, :, pl.ds(c * block, block)],
                    sems.at[c, a],
                )
                copy.start()
                copies.append(copy)
        for c in range(CHUNKS):
            cols = pl.ds(c * block, block)
            for copy in copies[2 * c : 2 * c + 2]:
                copy.wait()
            other_ref[:, cols] = finish(bf16_product(held[0, :, cols], held[1, :, cols]))

    @pl.when(odd)
    def _():
        make((k_hbm, v_hbm), 0, lambda u: u)

    @pl.when(jnp.logical_not(odd))
    def _():
        make((ct_hbm, q_hbm), half, lambda dy: flipped(reverse, dy).astype(jnp.bfloat16))


def first_gate(q, k, v, ct):
    taps, channels = q.shape
    half = channels // 2
    return pl.pallas_call(
        first_kernel,
        in_specs=[pl.BlockSpec(memory_space=pltpu.HBM)] * 4,
        out_specs=VMEM,
        out_shape=jax.ShapeDtypeStruct((taps, half), jnp.bfloat16),
        scratch_shapes=[
            pltpu.VMEM((2, taps, half), jnp.bfloat16),
            pltpu.SemaphoreType.DMA((CHUNKS, 2)),
        ],
        name="first_gate",
        cost_estimate=pl.CostEstimate(
            flops=taps * taps * channels, bytes_accessed=3 * taps * channels, transcendentals=0
        ),
        compiler_params=pltpu.CompilerParams(vmem_limit_bytes=FIRST_VMEM),
    )(q, k, v, ct)


def gates_kernel(
    starts_ref, after_ref, q_hbm, k_hbm, v_hbm, ct_hbm,
    q_ref, k_ref, v_ref, ct_ref, near_own_ref, near_other_ref, own_ref, keep_ref, sems,
):
    del after_ref
    taps, channels = q_ref.shape
    half = channels // 2
    block = channels // CHUNKS
    pairs = ((k_hbm, k_ref), (v_hbm, v_ref), (q_hbm, q_ref), (ct_hbm, ct_ref))
    copies = []
    for c in range(CHUNKS):
        cols = pl.ds(c * block, block)
        for a, (source, target) in enumerate(pairs):
            copy = pltpu.make_async_copy(source.at[:, cols], target.at[:, cols], sems.at[c, a])
            copy.start()
            copies.append(copy)
    here = lax.axis_index("ctx")
    odd = here % 2 == 1
    reverse = reversal(taps)
    for side in range(2):
        found = here < 0
        for d in range(starts_ref.shape[0]):
            found = jnp.logical_or(found, starts_ref[d] == (here + side) * taps)
        keep = jnp.where(found, 0.0, 1.0)
        keep_ref[side] = jnp.full(keep_ref.shape[1:], keep).astype(jnp.bfloat16)
    for c in range(CHUNKS):
        cols = pl.ds(c * block, block)
        sent = pl.ds(c * block % half, block)
        for copy in copies[4 * c : 4 * c + 4]:
            copy.wait()

        def make_u():
            return bf16_product(k_ref[:, cols], v_ref[:, cols])

        def make_dy():
            dy = bf16_product(ct_ref[:, cols], q_ref[:, cols])
            return flipped(reverse, dy).astype(jnp.bfloat16)

        @pl.when(odd)
        def _():
            near_ref = near_own_ref if c * block >= half else near_other_ref
            near_ref[:, sent] = make_dy()
            if c * block >= half:
                own_ref[:, sent] = make_u()

        @pl.when(jnp.logical_not(odd))
        def _():
            near_ref = near_own_ref if c * block < half else near_other_ref
            near_ref[:, sent] = make_u()
            if c * block < half:
                own_ref[:, sent] = make_dy()


def gates(starts, after, q, k, v, ct):
    taps, channels = q.shape

    def shape(*dims):
        return jax.ShapeDtypeStruct(dims, jnp.bfloat16)

    half = channels // 2
    return pl.pallas_call(
        gates_kernel,
        in_specs=[SMEM, pl.BlockSpec(memory_space=pl.ANY)]
        + [pl.BlockSpec(memory_space=pltpu.HBM)] * 4,
        out_specs=[VMEM] * 8,
        out_shape=[shape(taps, channels)] * 4 + [shape(taps, half)] * 3 + [shape(2, 16, LANES)],
        scratch_shapes=[pltpu.SemaphoreType.DMA((CHUNKS, 4))],
        name="gates",
        cost_estimate=pl.CostEstimate(
            flops=2 * taps * taps * channels, bytes_accessed=12 * taps * channels, transcendentals=0
        ),
        compiler_params=pltpu.CompilerParams(vmem_limit_bytes=GATES_VMEM),
    )(starts, after, q, k, v, ct)


def toeplitz_kernel(filters_ref, after_ref, out_ref, done_ref):
    del after_ref
    count, taps = filters_ref.shape
    lines = filters_ref[...].astype(jnp.float32)
    current = iota((taps, taps), 0) <= iota((taps, taps), 1)
    for f in range(count):
        tile = jnp.broadcast_to(lines[f : f + 1], (taps, taps))
        tile = pltpu.roll(tile, 0, 1, stride=1, stride_axis=0)
        out_ref[f, :taps] = jnp.where(current, 0.0, tile).astype(jnp.bfloat16)
        out_ref[f, taps:] = jnp.where(current, tile, 0.0).astype(jnp.bfloat16)
    done_ref[...] = jnp.zeros_like(done_ref)


def toeplitz(filters, after):
    count, taps = filters.shape
    return pl.pallas_call(
        toeplitz_kernel,
        in_specs=[VMEM, pl.BlockSpec(memory_space=pl.ANY)],
        out_specs=[VMEM] * 2,
        out_shape=[
            jax.ShapeDtypeStruct((count, 2 * taps, taps), jnp.bfloat16),
            jax.ShapeDtypeStruct((8, LANES), jnp.float32),
        ],
        name="toeplitz",
        cost_estimate=pl.CostEstimate(
            flops=count * taps * taps * 64, bytes_accessed=4 * count * taps * taps, transcendentals=0
        ),
        compiler_params=pltpu.CompilerParams(vmem_limit_bytes=8 * MIB),
    )(filters, after)


def filter_grad_kernel(
    width, near_ref, own_ref, keep_ref, near_in_ref, extra_ref, far_in_ref, out_ref, lines
):
    taps, half = far_in_ref.shape
    per_group = LANES // width
    odd = lax.axis_index("ctx") % 2
    keep_far = keep_ref[odd]
    keep_near = keep_ref[1 - odd]
    lane_filter = iota((ROW_BLOCK, LANES), 1) // width
    fold = iota((ROW_BLOCK, taps), 1) + iota((ROW_BLOCK, taps), 0) < ROW_BLOCK
    for group in range(half // LANES):
        at = group * LANES
        cols = pl.ds(at, LANES)
        near = near_ref[:, cols]
        pairs = (
            (own_ref[:, cols], masked(far_in_ref[:, cols], keep_far), near),
            (near_in_ref[:, cols], masked(near, keep_near), extra_ref[:, cols]),
        )
        left, right = [], []
        for moving, beyond, fixed in pairs:
            window = jnp.concatenate([beyond, fixed], axis=0)
            for start in range(0, taps, ROW_BLOCK):
                piece = moving[start : start + ROW_BLOCK]
                left.append(
                    jnp.concatenate(
                        [jnp.where(lane_filter == i, piece, 0) for i in range(per_group)], axis=0
                    )
                )
                right.append(window[taps - ROW_BLOCK - start : 2 * taps - start])
        product = lax.dot_general(
            jnp.concatenate(left, axis=1),
            jnp.concatenate(right, axis=1),
            (((1,), (1,)), ((), ())),
            preferred_element_type=jnp.float32,
        )
        rows = []
        for i in range(per_group):
            tile = product[i * ROW_BLOCK : (i + 1) * ROW_BLOCK]
            high = jnp.concatenate(
                [tile[:, taps:], jnp.zeros((ROW_BLOCK, taps - ROW_BLOCK), jnp.float32)], axis=1
            )
            tile = jnp.where(fold, high, tile[:, :taps])
            tile = pltpu.roll(tile, taps - ROW_BLOCK + 1, 1, stride=1, stride_axis=0)
            rows.append(jnp.sum(tile, axis=0, keepdims=True))
        lines[group * per_group : (group + 1) * per_group] = jnp.concatenate(rows, axis=0)
    flip = jnp.where((iota((taps, taps), 0) + iota((taps, taps), 1)) % taps == 0, 1.0, 0.0)
    out_ref[...] = jnp.dot(
        lines[...], flip, preferred_element_type=jnp.float32, precision=lax.Precision.HIGHEST
    )


def filter_gradient(near, own, keep, near_in, extra, far_in, width):
    taps, half = own.shape
    count = half // width
    return pl.pallas_call(
        functools.partial(filter_grad_kernel, width),
        in_specs=[VMEM] * 6,
        out_specs=VMEM,
        out_shape=jax.ShapeDtypeStruct((count, taps), jnp.float32),
        scratch_shapes=[pltpu.VMEM((count, taps), jnp.float32)],
        name="filter_gradient",
        cost_estimate=pl.CostEstimate(
            flops=4 * count * taps * taps * 256, bytes_accessed=16 * taps * half, transcendentals=0
        ),
        compiler_params=pltpu.CompilerParams(vmem_limit_bytes=8 * MIB),
    )(near, own, keep, near_in, extra, far_in)


def outputs_kernel(
    width, base, q_ref, k_ref, v_ref, ct_ref, tiles_ref, near_ref, far_ref, keep_ref,
    near_in_ref, far_in_ref, *rest,
):
    *results, sems = rest[-5:]
    *targets, done_ref = rest[-10:-5]
    out, grad_q, grad_k, grad_v = results
    taps, half = far_ref.shape
    channels = out.shape[1]
    per_group = LANES // width
    odd = lax.axis_index("ctx") % 2
    keep_far = keep_ref[odd]
    keep_near = keep_ref[1 - odd]
    second = odd if base < half else 1 - odd
    base = base % half
    first = pl.multiple_of(second * half, half)
    reverse = reversal(taps)
    copies = []

    def send(which, at, sem):
        own = pl.ds(at, CHUNK)
        cols = pl.ds(pl.multiple_of(first + base + at, CHUNK), CHUNK)
        copy = pltpu.make_async_copy(results[which].at[:, own], targets[which].at[:, cols], sem)
        copy.start()
        copies.append(copy)

    for chunk in range(0, channels, CHUNK):
        whole = pl.ds(pl.multiple_of(first + base + chunk, CHUNK), CHUNK)
        k_turned = flipped(reverse, k_ref[:, whole])
        v_turned = flipped(reverse, v_ref[:, whole])
        k_parts, v_parts = [], []
        for lane in range(0, CHUNK, LANES):
            own = pl.ds(chunk + lane, LANES)
            sent = pl.ds(base + chunk + lane, LANES)
            at = pl.multiple_of(first + base + chunk + lane, LANES)
            cols = pl.ds(at, LANES)
            near_lines = jnp.concatenate(
                [masked(far_in_ref[:, sent], keep_far).T, near_ref[:, sent].T], axis=1
            )
            far_lines = jnp.concatenate(
                [masked(near_in_ref[:, sent], keep_near).T, far_ref[:, sent].T], axis=1
            )
            near_parts, far_parts = [], []
            for i in range(per_group):
                rows = slice(i * width, (i + 1) * width)
                both = jnp.concatenate([near_lines[rows], far_lines[rows]], axis=0)
                part = jnp.dot(both, tiles_ref[at // width + i], preferred_element_type=jnp.float32)
                near_parts.append(part[:width])
                far_parts.append(part[width:])
            near_sum = jnp.concatenate(near_parts, axis=0)
            far_sum = jnp.concatenate(far_parts, axis=0)
            y = jnp.where(odd == 1, far_sum, near_sum).T
            mixed = jnp.where(odd == 1, near_sum, far_sum).T
            out[:, own] = (q_ref[:, cols].astype(jnp.float32) * y).astype(jnp.bfloat16)
            grad_q[:, own] = (ct_ref[:, cols].astype(jnp.float32) * y).astype(jnp.bfloat16)
            lanes = slice(lane, lane + LANES)
            k_parts.append((mixed * v_turned[:, lanes]).astype(jnp.bfloat16))
            v_parts.append((mixed * k_turned[:, lanes]).astype(jnp.bfloat16))
        own = pl.ds(chunk, CHUNK)
        turn = chunk // CHUNK
        send(0, chunk, sems.at[turn, 0])
        send(1, chunk, sems.at[turn, 1])
        grad_k[:, own] = flipped(reverse, jnp.concatenate(k_parts, axis=1)).astype(jnp.bfloat16)
        send(2, chunk, sems.at[turn, 2])
        grad_v[:, own] = flipped(reverse, jnp.concatenate(v_parts, axis=1)).astype(jnp.bfloat16)
        send(3, chunk, sems.at[turn, 3])
    for copy in copies:
        copy.wait()
    done_ref[...] = jnp.zeros_like(done_ref)


def outputs(piece, operands, results, after, width):
    taps, channels = operands[0].shape
    part = channels // PIECES
    anywhere = pl.BlockSpec(memory_space=pl.ANY)
    shape = jax.ShapeDtypeStruct((taps, channels), jnp.bfloat16)
    *results, done = pl.pallas_call(
        functools.partial(outputs_kernel, width, piece * part),
        in_specs=[VMEM] * len(operands) + [anywhere] * (1 + len(results)),
        out_specs=[anywhere] * 4 + [VMEM],
        out_shape=[shape] * 4 + [jax.ShapeDtypeStruct((8, LANES), jnp.float32)],
        input_output_aliases={len(operands) + 1 + i: i for i in range(len(results))},
        scratch_shapes=[pltpu.VMEM((taps, part), jnp.bfloat16)] * 4
        + [pltpu.SemaphoreType.DMA((part // CHUNK, 4))],
        name=f"outputs_{piece}",
        cost_estimate=pl.CostEstimate(
            flops=16 * (part // width) * taps * taps * 256,
            bytes_accessed=24 * taps * part,
            transcendentals=0,
        ),
        compiler_params=pltpu.CompilerParams(vmem_limit_bytes=8 * MIB),
    )(*operands, after, *results)
    return results, done


def per_device(gate_in, key_in, value_in, cotangent, doc_starts, filters):
    taps = filters.shape[1]
    width = gate_in.shape[2] // filters.shape[0]
    assert gate_in.shape[1] == taps
    q, k, v, ct = gate_in[0], key_in[0], value_in[0], cotangent[0]
    other = first_gate(q, k, v, ct)
    other_in = exchange(other, "ctx", 1)
    q, k, v, ct, near_own, near_other, own, keep = gates(doc_starts[0], other, q, k, v, ct)
    near_in_own = exchange(near_other, "ctx", 0)
    extra = exchange(other, "ctx", 0)
    own_in = exchange(own, "ctx", 1)
    near_in_other = exchange(near_own, "ctx", 0)
    mine = filter_gradient(near_own, own, keep, near_in_own, extra, other_in, width)
    halves = (
        (near_own, own, keep, near_in_own, other_in),
        (near_other, other, keep, near_in_other, own_in),
    )
    tiles = None
    results = []

    def beside(after, turn):
        nonlocal tiles, results
        if turn == 0:
            tiles, done = toeplitz(filters, after)
            return done
        if turn > PIECES:
            return after
        operands = (q, k, v, ct, tiles, *halves[turn - 1])
        results, done = outputs(turn - 1, operands, results, after, width)
        return done

    mine = sum_devices(mine, beside)
    filter_grad = join(mine, exchange(mine, "ctx", 0))
    return tuple(array[None] for array in results) + (filter_grad,)


def solution(mesh):
    split = P("dp", "ctx", None)
    return jax.shard_map(
        per_device,
        mesh=mesh,
        in_specs=(split, split, split, split, P("dp", None), P()),
        out_specs=(split, split, split, split, P()),
        check_vma=False,
    )
```

```python
import functools

import jax
import jax.numpy as jnp
from jax import lax
from jax.experimental import pallas as pl
from jax.experimental.pallas import tpu as pltpu
from jax.sharding import PartitionSpec as P

LANES = 128
ROW_BLOCK = 32
MIB = 1024 * 1024
CHUNKS = 4
PIECES = 2
FIRST_TURN = 2
CHUNK = 512
FIRST_VMEM = 213 * MIB // 4
GATES_VMEM = 101 * MIB // 2
VMEM = pl.BlockSpec(memory_space=pltpu.VMEM)
SMEM = pl.BlockSpec(memory_space=pltpu.SMEM)


def iota(shape, dim):
    return lax.broadcasted_iota(jnp.int32, shape, dim)


def exchange(array, axis, first):
    size = lax.axis_size(axis)
    pairs = []
    for low in range(first, size - 1, 2):
        pairs += [(low, low + 1), (low + 1, low)]
    return lax.ppermute(array, axis, pairs)


def swapped(array, axis, step):
    size = lax.axis_size(axis)
    return lax.ppermute(array, axis, [(i, i ^ step) for i in range(size)])


def swapped(array, axis, step):
    size = lax.axis_size(axis)
    return lax.ppermute(array, axis, [(i, i ^ step) for i in range(size)])


def along(array, axis):
    size = lax.axis_size(axis)
    pairs = [(i, i + 2 if i % 2 else i - 2) for i in range(size)]
    return lax.ppermute(array, axis, [(i, j) for i, j in pairs if 0 <= j < size])


def add_kernel(mine_ref, other_ref, after_ref, out_ref):
    del after_ref
    out_ref[...] = mine_ref[...] + other_ref[...]


def add(mine, other, after):
    return pl.pallas_call(
        add_kernel,
        in_specs=[VMEM] * 2 + [pl.BlockSpec(memory_space=pl.ANY)],
        out_specs=VMEM,
        out_shape=jax.ShapeDtypeStruct(mine.shape, mine.dtype),
        name="add",
        compiler_params=pltpu.CompilerParams(vmem_limit_bytes=MIB),
    )(mine, other, after)


def sum_devices(mine, beside):
    turn = 0
    for axis, step in (("dp", 1), ("ctx", 2)):
        while step < lax.axis_size(axis):
            mine = add(mine, swapped(mine, axis, step), beside(mine, turn))
            step, turn = 2 * step, turn + 1
    return mine


def join_kernel(mine_ref, other_ref, out_ref):
    count = mine_ref.shape[0]
    odd = lax.axis_index("ctx") % 2
    out_ref[pl.ds(pl.multiple_of(odd * count, count), count)] = mine_ref[...]
    out_ref[pl.ds(pl.multiple_of((1 - odd) * count, count), count)] = other_ref[...]


def join(mine, other):
    count, taps = mine.shape
    return pl.pallas_call(
        join_kernel,
        in_specs=[VMEM] * 2,
        out_specs=VMEM,
        out_shape=jax.ShapeDtypeStruct((2 * count, taps), mine.dtype),
        name="join",
        compiler_params=pltpu.CompilerParams(vmem_limit_bytes=MIB),
    )(mine, other)


def reversal(taps):
    flip = iota((taps, taps), 0) + iota((taps, taps), 1) == taps - 1
    return jnp.where(flip, 1.0, 0.0).astype(jnp.bfloat16)


def flipped(reverse, array):
    return jnp.dot(reverse, array, preferred_element_type=jnp.float32)


def masked(array, keep):
    return array * jnp.concatenate([keep] * (array.shape[0] // keep.shape[0]), axis=0)


def bf16_product(one, two):
    return (one.astype(jnp.float32) * two.astype(jnp.float32)).astype(jnp.bfloat16)


def first_kernel(q_hbm, k_hbm, v_hbm, ct_hbm, other_ref, held, sems):
    taps, half = other_ref.shape
    block = half // CHUNKS
    odd = lax.axis_index("ctx") % 2 == 1
    reverse = reversal(taps)

    def make(sources, start, finish):
        copies = []
        for c in range(CHUNKS):
            for a, source in enumerate(sources):
                copy = pltpu.make_async_copy(
                    source.at[:, pl.ds(start + c * block, block)],
                    held.at[a, :, pl.ds(c * block, block)],
                    sems.at[c, a],
                )
                copy.start()
                copies.append(copy)
        for c in range(CHUNKS):
            cols = pl.ds(c * block, block)
            for copy in copies[2 * c : 2 * c + 2]:
                copy.wait()
            other_ref[:, cols] = finish(bf16_product(held[0, :, cols], held[1, :, cols]))

    @pl.when(odd)
    def _():
        make((k_hbm, v_hbm), 0, lambda u: u)

    @pl.when(jnp.logical_not(odd))
    def _():
        make((ct_hbm, q_hbm), half, lambda dy: flipped(reverse, dy).astype(jnp.bfloat16))


def first_gate(q, k, v, ct):
    taps, channels = q.shape
    half = channels // 2
    return pl.pallas_call(
        first_kernel,
        in_specs=[pl.BlockSpec(memory_space=pltpu.HBM)] * 4,
        out_specs=VMEM,
        out_shape=jax.ShapeDtypeStruct((taps, half), jnp.bfloat16),
        scratch_shapes=[
            pltpu.VMEM((2, taps, half), jnp.bfloat16),
            pltpu.SemaphoreType.DMA((CHUNKS, 2)),
        ],
        name="first_gate",
        cost_estimate=pl.CostEstimate(
            flops=taps * taps * channels, bytes_accessed=3 * taps * channels, transcendentals=0
        ),
        compiler_params=pltpu.CompilerParams(vmem_limit_bytes=FIRST_VMEM),
    )(q, k, v, ct)


def gates_kernel(
    after_ref, q_hbm, k_hbm, v_hbm, ct_hbm,
    q_ref, k_ref, v_ref, ct_ref, near_own_ref, near_other_ref, own_ref, sems,
):
    del after_ref
    taps, channels = q_ref.shape
    half = channels // 2
    block = channels // CHUNKS
    pairs = ((k_hbm, k_ref), (v_hbm, v_ref), (q_hbm, q_ref), (ct_hbm, ct_ref))
    copies = []
    for c in range(CHUNKS):
        cols = pl.ds(c * block, block)
        for a, (source, target) in enumerate(pairs):
            copy = pltpu.make_async_copy(source.at[:, cols], target.at[:, cols], sems.at[c, a])
            copy.start()
            copies.append(copy)
    odd = lax.axis_index("ctx") % 2 == 1
    reverse = reversal(taps)
    for c in range(CHUNKS):
        cols = pl.ds(c * block, block)
        sent = pl.ds(c * block % half, block)
        for copy in copies[4 * c : 4 * c + 4]:
            copy.wait()

        def make_u():
            return bf16_product(k_ref[:, cols], v_ref[:, cols])

        def make_dy():
            dy = bf16_product(ct_ref[:, cols], q_ref[:, cols])
            return flipped(reverse, dy).astype(jnp.bfloat16)

        @pl.when(odd)
        def _():
            near_ref = near_own_ref if c * block >= half else near_other_ref
            near_ref[:, sent] = make_dy()
            if c * block >= half:
                own_ref[:, sent] = make_u()

        @pl.when(jnp.logical_not(odd))
        def _():
            near_ref = near_own_ref if c * block < half else near_other_ref
            near_ref[:, sent] = make_u()
            if c * block < half:
                own_ref[:, sent] = make_dy()


def gates(after, q, k, v, ct):
    taps, channels = q.shape

    def shape(*dims):
        return jax.ShapeDtypeStruct(dims, jnp.bfloat16)

    half = channels // 2
    return pl.pallas_call(
        gates_kernel,
        in_specs=[pl.BlockSpec(memory_space=pl.ANY)]
        + [pl.BlockSpec(memory_space=pltpu.HBM)] * 4,
        out_specs=[VMEM] * 7,
        out_shape=[shape(taps, channels)] * 4 + [shape(taps, half)] * 3,
        scratch_shapes=[pltpu.SemaphoreType.DMA((CHUNKS, 4))],
        name="gates",
        cost_estimate=pl.CostEstimate(
            flops=2 * taps * taps * channels, bytes_accessed=12 * taps * channels, transcendentals=0
        ),
        compiler_params=pltpu.CompilerParams(vmem_limit_bytes=GATES_VMEM),
    )(after, q, k, v, ct)


def masks_kernel(taps, starts_ref, after_ref, keep_ref):
    del after_ref
    here = lax.axis_index("ctx")
    for side in range(2):
        found = here < 0
        for d in range(starts_ref.shape[0]):
            found = jnp.logical_or(found, starts_ref[d] == (here + side) * taps)
        keep = jnp.where(found, 0.0, 1.0)
        keep_ref[side] = jnp.full(keep_ref.shape[1:], keep).astype(jnp.bfloat16)


def masks(starts, after):
    return pl.pallas_call(
        functools.partial(masks_kernel, after.shape[0]),
        in_specs=[SMEM, pl.BlockSpec(memory_space=pl.ANY)],
        out_specs=VMEM,
        out_shape=jax.ShapeDtypeStruct((2, 16, LANES), jnp.bfloat16),
        name="masks",
        compiler_params=pltpu.CompilerParams(vmem_limit_bytes=MIB),
    )(starts, after)


def toeplitz_kernel(filters_ref, after_ref, out_ref, done_ref):
    del after_ref
    count, taps = filters_ref.shape
    lines = filters_ref[...].astype(jnp.float32)
    current = iota((taps, taps), 0) <= iota((taps, taps), 1)
    for f in range(count):
        tile = jnp.broadcast_to(lines[f : f + 1], (taps, taps))
        tile = pltpu.roll(tile, 0, 1, stride=1, stride_axis=0)
        out_ref[f, :taps] = jnp.where(current, 0.0, tile).astype(jnp.bfloat16)
        out_ref[f, taps:] = jnp.where(current, tile, 0.0).astype(jnp.bfloat16)
    done_ref[...] = jnp.zeros_like(done_ref)


def toeplitz(filters, after):
    count, taps = filters.shape
    return pl.pallas_call(
        toeplitz_kernel,
        in_specs=[VMEM, pl.BlockSpec(memory_space=pl.ANY)],
        out_specs=[VMEM] * 2,
        out_shape=[
            jax.ShapeDtypeStruct((count, 2 * taps, taps), jnp.bfloat16),
            jax.ShapeDtypeStruct((8, LANES), jnp.float32),
        ],
        name="toeplitz",
        cost_estimate=pl.CostEstimate(
            flops=count * taps * taps * 64, bytes_accessed=4 * count * taps * taps, transcendentals=0
        ),
        compiler_params=pltpu.CompilerParams(vmem_limit_bytes=8 * MIB),
    )(filters, after)


def filter_grad_kernel(
    width, near_ref, own_ref, keep_ref, near_in_ref, extra_ref, far_in_ref, out_ref, lines
):
    taps, half = far_in_ref.shape
    per_group = LANES // width
    odd = lax.axis_index("ctx") % 2
    keep_far = keep_ref[odd]
    keep_near = keep_ref[1 - odd]
    lane_filter = iota((ROW_BLOCK, LANES), 1) // width
    fold = iota((ROW_BLOCK, taps), 1) + iota((ROW_BLOCK, taps), 0) < ROW_BLOCK
    for group in range(half // LANES):
        at = group * LANES
        cols = pl.ds(at, LANES)
        near = near_ref[:, cols]
        pairs = (
            (own_ref[:, cols], masked(far_in_ref[:, cols], keep_far), near),
            (near_in_ref[:, cols], masked(near, keep_near), extra_ref[:, cols]),
        )
        left, right = [], []
        for moving, beyond, fixed in pairs:
            window = jnp.concatenate([beyond, fixed], axis=0)
            for start in range(0, taps, ROW_BLOCK):
                piece = moving[start : start + ROW_BLOCK]
                left.append(
                    jnp.concatenate(
                        [jnp.where(lane_filter == i, piece, 0) for i in range(per_group)], axis=0
                    )
                )
                right.append(window[taps - ROW_BLOCK - start : 2 * taps - start])
        product = lax.dot_general(
            jnp.concatenate(left, axis=1),
            jnp.concatenate(right, axis=1),
            (((1,), (1,)), ((), ())),
            preferred_element_type=jnp.float32,
        )
        rows = []
        for i in range(per_group):
            tile = product[i * ROW_BLOCK : (i + 1) * ROW_BLOCK]
            high = jnp.concatenate(
                [tile[:, taps:], jnp.zeros((ROW_BLOCK, taps - ROW_BLOCK), jnp.float32)], axis=1
            )
            tile = jnp.where(fold, high, tile[:, :taps])
            tile = pltpu.roll(tile, taps - ROW_BLOCK + 1, 1, stride=1, stride_axis=0)
            rows.append(jnp.sum(tile, axis=0, keepdims=True))
        lines[group * per_group : (group + 1) * per_group] = jnp.concatenate(rows, axis=0)
    flip = jnp.where((iota((taps, taps), 0) + iota((taps, taps), 1)) % taps == 0, 1.0, 0.0)
    out_ref[...] = jnp.dot(
        lines[...], flip, preferred_element_type=jnp.float32, precision=lax.Precision.HIGHEST
    )


def filter_gradient(near, own, keep, near_in, extra, far_in, width):
    taps, half = own.shape
    count = half // width
    return pl.pallas_call(
        functools.partial(filter_grad_kernel, width),
        in_specs=[VMEM] * 6,
        out_specs=VMEM,
        out_shape=jax.ShapeDtypeStruct((count, taps), jnp.float32),
        scratch_shapes=[pltpu.VMEM((count, taps), jnp.float32)],
        name="filter_gradient",
        cost_estimate=pl.CostEstimate(
            flops=4 * count * taps * taps * 256, bytes_accessed=16 * taps * half, transcendentals=0
        ),
        compiler_params=pltpu.CompilerParams(vmem_limit_bytes=8 * MIB),
    )(near, own, keep, near_in, extra, far_in)


def outputs_kernel(
    width, base, q_ref, k_ref, v_ref, ct_ref, tiles_ref, near_ref, far_ref, keep_ref,
    near_in_ref, far_in_ref, *rest,
):
    *results, sems = rest[-5:]
    *targets, done_ref = rest[-10:-5]
    out, grad_q, grad_k, grad_v = results
    taps, half = far_ref.shape
    channels = out.shape[1]
    per_group = LANES // width
    odd = lax.axis_index("ctx") % 2
    keep_far = keep_ref[odd]
    keep_near = keep_ref[1 - odd]
    second = odd if base < half else 1 - odd
    base = base % half
    first = pl.multiple_of(second * half, half)
    reverse = reversal(taps)
    copies = []

    def send(which, at, sem):
        own = pl.ds(at, CHUNK)
        cols = pl.ds(pl.multiple_of(first + base + at, CHUNK), CHUNK)
        copy = pltpu.make_async_copy(results[which].at[:, own], targets[which].at[:, cols], sem)
        copy.start()
        copies.append(copy)

    for chunk in range(0, channels, CHUNK):
        whole = pl.ds(pl.multiple_of(first + base + chunk, CHUNK), CHUNK)
        k_turned = flipped(reverse, k_ref[:, whole])
        v_turned = flipped(reverse, v_ref[:, whole])
        k_parts, v_parts = [], []
        for lane in range(0, CHUNK, LANES):
            own = pl.ds(chunk + lane, LANES)
            sent = pl.ds(base + chunk + lane, LANES)
            at = pl.multiple_of(first + base + chunk + lane, LANES)
            cols = pl.ds(at, LANES)
            near_lines = jnp.concatenate(
                [masked(far_in_ref[:, sent], keep_far).T, near_ref[:, sent].T], axis=1
            )
            far_lines = jnp.concatenate(
                [masked(near_in_ref[:, sent], keep_near).T, far_ref[:, sent].T], axis=1
            )
            near_parts, far_parts = [], []
            for i in range(per_group):
                rows = slice(i * width, (i + 1) * width)
                both = jnp.concatenate([near_lines[rows], far_lines[rows]], axis=0)
                part = jnp.dot(both, tiles_ref[at // width + i], preferred_element_type=jnp.float32)
                near_parts.append(part[:width])
                far_parts.append(part[width:])
            near_sum = jnp.concatenate(near_parts, axis=0)
            far_sum = jnp.concatenate(far_parts, axis=0)
            y = jnp.where(odd == 1, far_sum, near_sum).T
            mixed = jnp.where(odd == 1, near_sum, far_sum).T
            out[:, own] = (q_ref[:, cols].astype(jnp.float32) * y).astype(jnp.bfloat16)
            grad_q[:, own] = (ct_ref[:, cols].astype(jnp.float32) * y).astype(jnp.bfloat16)
            lanes = slice(lane, lane + LANES)
            k_parts.append((mixed * v_turned[:, lanes]).astype(jnp.bfloat16))
            v_parts.append((mixed * k_turned[:, lanes]).astype(jnp.bfloat16))
        own = pl.ds(chunk, CHUNK)
        turn = chunk // CHUNK
        send(0, chunk, sems.at[turn, 0])
        send(1, chunk, sems.at[turn, 1])
        grad_k[:, own] = flipped(reverse, jnp.concatenate(k_parts, axis=1)).astype(jnp.bfloat16)
        send(2, chunk, sems.at[turn, 2])
        grad_v[:, own] = flipped(reverse, jnp.concatenate(v_parts, axis=1)).astype(jnp.bfloat16)
        send(3, chunk, sems.at[turn, 3])
    for copy in copies:
        copy.wait()
    done_ref[...] = jnp.zeros_like(done_ref)


def outputs(piece, operands, results, after, width):
    taps, channels = operands[0].shape
    part = channels // PIECES
    anywhere = pl.BlockSpec(memory_space=pl.ANY)
    shape = jax.ShapeDtypeStruct((taps, channels), jnp.bfloat16)
    *results, done = pl.pallas_call(
        functools.partial(outputs_kernel, width, piece * part),
        in_specs=[VMEM] * len(operands) + [anywhere] * (1 + len(results)),
        out_specs=[anywhere] * 4 + [VMEM],
        out_shape=[shape] * 4 + [jax.ShapeDtypeStruct((8, LANES), jnp.float32)],
        input_output_aliases={len(operands) + 1 + i: i for i in range(len(results))},
        scratch_shapes=[pltpu.VMEM((taps, part), jnp.bfloat16)] * 4
        + [pltpu.SemaphoreType.DMA((part // CHUNK, 4))],
        name=f"outputs_{piece}",
        cost_estimate=pl.CostEstimate(
            flops=16 * (part // width) * taps * taps * 256,
            bytes_accessed=24 * taps * part,
            transcendentals=0,
        ),
        compiler_params=pltpu.CompilerParams(vmem_limit_bytes=8 * MIB),
    )(*operands, after, *results)
    return results, done


def per_device(gate_in, key_in, value_in, cotangent, doc_starts, filters):
    taps = filters.shape[1]
    width = gate_in.shape[2] // filters.shape[0]
    assert gate_in.shape[1] == taps
    q, k, v, ct = gate_in[0], key_in[0], value_in[0], cotangent[0]
    other = first_gate(q, k, v, ct)
    other_in = exchange(other, "ctx", 1)
    q, k, v, ct, near_own, near_other, own = gates(other, q, k, v, ct)
    near_in_own = exchange(near_other, "ctx", 0)
    extra = exchange(other, "ctx", 0)
    own_in = exchange(own, "ctx", 1)
    near_in_other = exchange(near_own, "ctx", 0)
    keep = masks(doc_starts[0], near_other)
    mine = filter_gradient(near_own, own, keep, near_in_own, extra, other_in, width)
    halves = (
        (near_own, own, keep, near_in_own, other_in),
        (near_other, other, keep, near_in_other, own_in),
    )
    tiles = None
    results = []

    def beside(after, turn):
        nonlocal tiles, results
        piece = turn - FIRST_TURN
        if turn == 0:
            tiles, done = toeplitz(filters, after)
            return done
        if not 0 <= piece < PIECES:
            return after
        operands = (q, k, v, ct, tiles, *halves[piece])
        results, done = outputs(piece, operands, results, after, width)
        return done

    mine = sum_devices(mine, beside)
    filter_grad = join(mine, exchange(mine, "ctx", 0))
    return tuple(array[None] for array in results) + (filter_grad,)


def solution(mesh):
    split = P("dp", "ctx", None)
    return jax.shard_map(
        per_device,
        mesh=mesh,
        in_specs=(split, split, split, split, P("dp", None), P()),
        out_specs=(split, split, split, split, P()),
        check_vma=False,
    )
```

```python
import functools

import jax
import jax.numpy as jnp
from jax import lax
from jax.experimental import pallas as pl
from jax.experimental.pallas import tpu as pltpu
from jax.sharding import PartitionSpec as P

LANES = 128
ROW_BLOCK = 32
MIB = 1024 * 1024
CHUNKS = 4
PIECES = 2
FIRST_TURN = 2
CHUNK = 512
FIRST_VMEM = 213 * MIB // 4
GATES_VMEM = 101 * MIB // 2
VMEM = pl.BlockSpec(memory_space=pltpu.VMEM)
SMEM = pl.BlockSpec(memory_space=pltpu.SMEM)


def iota(shape, dim):
    return lax.broadcasted_iota(jnp.int32, shape, dim)


def exchange(array, axis, first):
    size = lax.axis_size(axis)
    pairs = []
    for low in range(first, size - 1, 2):
        pairs += [(low, low + 1), (low + 1, low)]
    return lax.ppermute(array, axis, pairs)


def swapped_odd(array, axis, step):
    seqs, blocks = lax.axis_size("dp"), lax.axis_size("ctx")
    pairs = []
    for seq in range(seqs):
        for block in range(1, blocks, 2):
            to_seq, to_block = (seq ^ step, block) if axis == "dp" else (seq, block ^ step)
            pairs.append((seq * blocks + block, to_seq * blocks + to_block))
    return lax.ppermute(array, ("dp", "ctx"), pairs)


def add_kernel(mine_ref, other_ref, after_ref, out_ref):
    del after_ref
    out_ref[...] = mine_ref[...] + other_ref[...]


def add(mine, other, after):
    return pl.pallas_call(
        add_kernel,
        in_specs=[VMEM] * 2 + [pl.BlockSpec(memory_space=pl.ANY)],
        out_specs=VMEM,
        out_shape=jax.ShapeDtypeStruct(mine.shape, mine.dtype),
        name="add",
        compiler_params=pltpu.CompilerParams(vmem_limit_bytes=MIB),
    )(mine, other, after)


def sum_devices(mine, beside):
    turn = 0
    for axis, step in (("dp", 1), ("ctx", 2)):
        while step < lax.axis_size(axis):
            mine = add(mine, swapped_odd(mine, axis, step), beside(mine, turn))
            step, turn = 2 * step, turn + 1
    return mine


def join_kernel(mine_ref, other_ref, out_ref):
    odd = lax.axis_index("ctx") % 2 == 1
    out_ref[...] = jnp.where(odd, mine_ref[...], other_ref[...])


def from_odd(mine):
    pairs = [(i, i - 1) for i in range(1, lax.axis_size("ctx"), 2)]
    return pl.pallas_call(
        join_kernel,
        in_specs=[VMEM] * 2,
        out_specs=VMEM,
        out_shape=jax.ShapeDtypeStruct(mine.shape, mine.dtype),
        name="join",
        compiler_params=pltpu.CompilerParams(vmem_limit_bytes=MIB),
    )(mine, lax.ppermute(mine, "ctx", pairs))


def reversal(taps):
    flip = iota((taps, taps), 0) + iota((taps, taps), 1) == taps - 1
    return jnp.where(flip, 1.0, 0.0).astype(jnp.bfloat16)


def flipped(reverse, array):
    return jnp.dot(reverse, array, preferred_element_type=jnp.float32)


def masked(array, keep):
    return array * jnp.concatenate([keep] * (array.shape[0] // keep.shape[0]), axis=0)


def bf16_product(one, two):
    return (one.astype(jnp.float32) * two.astype(jnp.float32)).astype(jnp.bfloat16)


def first_kernel(q_hbm, k_hbm, v_hbm, ct_hbm, other_ref, held, sems):
    taps, half = other_ref.shape
    block = half // CHUNKS
    odd = lax.axis_index("ctx") % 2 == 1
    reverse = reversal(taps)

    def make(sources, start, finish):
        copies = []
        for c in range(CHUNKS):
            for a, source in enumerate(sources):
                copy = pltpu.make_async_copy(
                    source.at[:, pl.ds(start + c * block, block)],
                    held.at[a, :, pl.ds(c * block, block)],
                    sems.at[c, a],
                )
                copy.start()
                copies.append(copy)
        for c in range(CHUNKS):
            cols = pl.ds(c * block, block)
            for copy in copies[2 * c : 2 * c + 2]:
                copy.wait()
            other_ref[:, cols] = finish(bf16_product(held[0, :, cols], held[1, :, cols]))

    @pl.when(odd)
    def _():
        make((k_hbm, v_hbm), 0, lambda u: u)

    @pl.when(jnp.logical_not(odd))
    def _():
        make((ct_hbm, q_hbm), half, lambda dy: flipped(reverse, dy).astype(jnp.bfloat16))


def first_gate(q, k, v, ct):
    taps, channels = q.shape
    half = channels // 2
    return pl.pallas_call(
        first_kernel,
        in_specs=[pl.BlockSpec(memory_space=pltpu.HBM)] * 4,
        out_specs=VMEM,
        out_shape=jax.ShapeDtypeStruct((taps, half), jnp.bfloat16),
        scratch_shapes=[
            pltpu.VMEM((2, taps, half), jnp.bfloat16),
            pltpu.SemaphoreType.DMA((CHUNKS, 2)),
        ],
        name="first_gate",
        cost_estimate=pl.CostEstimate(
            flops=taps * taps * channels, bytes_accessed=3 * taps * channels, transcendentals=0
        ),
        compiler_params=pltpu.CompilerParams(vmem_limit_bytes=FIRST_VMEM),
    )(q, k, v, ct)


def gates_kernel(
    after_ref, q_hbm, k_hbm, v_hbm, ct_hbm,
    q_ref, k_ref, v_ref, ct_ref, near_own_ref, near_other_ref, own_ref, sems,
):
    del after_ref
    taps, channels = q_ref.shape
    half = channels // 2
    block = channels // CHUNKS
    pairs = ((k_hbm, k_ref), (v_hbm, v_ref), (q_hbm, q_ref), (ct_hbm, ct_ref))
    copies = []
    for c in range(CHUNKS):
        cols = pl.ds(c * block, block)
        for a, (source, target) in enumerate(pairs):
            copy = pltpu.make_async_copy(source.at[:, cols], target.at[:, cols], sems.at[c, a])
            copy.start()
            copies.append(copy)
    odd = lax.axis_index("ctx") % 2 == 1
    reverse = reversal(taps)
    for c in range(CHUNKS):
        cols = pl.ds(c * block, block)
        sent = pl.ds(c * block % half, block)
        for copy in copies[4 * c : 4 * c + 4]:
            copy.wait()

        def make_u():
            return bf16_product(k_ref[:, cols], v_ref[:, cols])

        def make_dy():
            dy = bf16_product(ct_ref[:, cols], q_ref[:, cols])
            return flipped(reverse, dy).astype(jnp.bfloat16)

        @pl.when(odd)
        def _():
            near_ref = near_own_ref if c * block >= half else near_other_ref
            near_ref[:, sent] = make_dy()
            if c * block >= half:
                own_ref[:, sent] = make_u()

        @pl.when(jnp.logical_not(odd))
        def _():
            near_ref = near_own_ref if c * block < half else near_other_ref
            near_ref[:, sent] = make_u()
            if c * block < half:
                own_ref[:, sent] = make_dy()


def gates(after, q, k, v, ct):
    taps, channels = q.shape

    def shape(*dims):
        return jax.ShapeDtypeStruct(dims, jnp.bfloat16)

    half = channels // 2
    return pl.pallas_call(
        gates_kernel,
        in_specs=[pl.BlockSpec(memory_space=pl.ANY)]
        + [pl.BlockSpec(memory_space=pltpu.HBM)] * 4,
        out_specs=[VMEM] * 7,
        out_shape=[shape(taps, channels)] * 4 + [shape(taps, half)] * 3,
        scratch_shapes=[pltpu.SemaphoreType.DMA((CHUNKS, 4))],
        name="gates",
        cost_estimate=pl.CostEstimate(
            flops=2 * taps * taps * channels, bytes_accessed=12 * taps * channels, transcendentals=0
        ),
        compiler_params=pltpu.CompilerParams(vmem_limit_bytes=GATES_VMEM),
    )(after, q, k, v, ct)


def masks_kernel(taps, starts_ref, after_ref, keep_ref):
    del after_ref
    here = lax.axis_index("ctx")
    for side in range(2):
        found = here < 0
        for d in range(starts_ref.shape[0]):
            found = jnp.logical_or(found, starts_ref[d] == (here + side) * taps)
        keep = jnp.where(found, 0.0, 1.0)
        keep_ref[side] = jnp.full(keep_ref.shape[1:], keep).astype(jnp.bfloat16)


def masks(starts, after):
    return pl.pallas_call(
        functools.partial(masks_kernel, after.shape[0]),
        in_specs=[SMEM, pl.BlockSpec(memory_space=pl.ANY)],
        out_specs=VMEM,
        out_shape=jax.ShapeDtypeStruct((2, 16, LANES), jnp.bfloat16),
        name="masks",
        compiler_params=pltpu.CompilerParams(vmem_limit_bytes=MIB),
    )(starts, after)


def toeplitz_kernel(filters_ref, after_ref, out_ref, done_ref):
    del after_ref
    count, taps = filters_ref.shape
    lines = filters_ref[...].astype(jnp.float32)
    current = iota((taps, taps), 0) <= iota((taps, taps), 1)
    for f in range(count):
        tile = jnp.broadcast_to(lines[f : f + 1], (taps, taps))
        tile = pltpu.roll(tile, 0, 1, stride=1, stride_axis=0)
        out_ref[f, :taps] = jnp.where(current, 0.0, tile).astype(jnp.bfloat16)
        out_ref[f, taps:] = jnp.where(current, tile, 0.0).astype(jnp.bfloat16)
    done_ref[...] = jnp.zeros_like(done_ref)


def toeplitz(filters, after):
    count, taps = filters.shape
    return pl.pallas_call(
        toeplitz_kernel,
        in_specs=[VMEM, pl.BlockSpec(memory_space=pl.ANY)],
        out_specs=[VMEM] * 2,
        out_shape=[
            jax.ShapeDtypeStruct((count, 2 * taps, taps), jnp.bfloat16),
            jax.ShapeDtypeStruct((8, LANES), jnp.float32),
        ],
        name="toeplitz",
        cost_estimate=pl.CostEstimate(
            flops=count * taps * taps * 64, bytes_accessed=4 * count * taps * taps, transcendentals=0
        ),
        compiler_params=pltpu.CompilerParams(vmem_limit_bytes=8 * MIB),
    )(filters, after)


def filter_grad_kernel(
    width, near_ref, own_ref, keep_ref, near_in_ref, extra_ref, far_in_ref, out_ref, lines
):
    taps, half = far_in_ref.shape
    per_group = LANES // width
    odd = lax.axis_index("ctx") % 2
    keep_far = keep_ref[odd]
    keep_near = keep_ref[1 - odd]
    lane_filter = iota((ROW_BLOCK, LANES), 1) // width
    fold = iota((ROW_BLOCK, taps), 1) + iota((ROW_BLOCK, taps), 0) < ROW_BLOCK
    for group in range(half // LANES):
        at = group * LANES
        cols = pl.ds(at, LANES)
        near = near_ref[:, cols]
        pairs = (
            (own_ref[:, cols], masked(far_in_ref[:, cols], keep_far), near),
            (near_in_ref[:, cols], masked(near, keep_near), extra_ref[:, cols]),
        )
        left, right = [], []
        for moving, beyond, fixed in pairs:
            window = jnp.concatenate([beyond, fixed], axis=0)
            for start in range(0, taps, ROW_BLOCK):
                piece = moving[start : start + ROW_BLOCK]
                left.append(
                    jnp.concatenate(
                        [jnp.where(lane_filter == i, piece, 0) for i in range(per_group)], axis=0
                    )
                )
                right.append(window[taps - ROW_BLOCK - start : 2 * taps - start])
        product = lax.dot_general(
            jnp.concatenate(left, axis=1),
            jnp.concatenate(right, axis=1),
            (((1,), (1,)), ((), ())),
            preferred_element_type=jnp.float32,
        )
        rows = []
        for i in range(per_group):
            tile = product[i * ROW_BLOCK : (i + 1) * ROW_BLOCK]
            high = jnp.concatenate(
                [tile[:, taps:], jnp.zeros((ROW_BLOCK, taps - ROW_BLOCK), jnp.float32)], axis=1
            )
            tile = jnp.where(fold, high, tile[:, :taps])
            tile = pltpu.roll(tile, taps - ROW_BLOCK + 1, 1, stride=1, stride_axis=0)
            rows.append(jnp.sum(tile, axis=0, keepdims=True))
        lines[group * per_group : (group + 1) * per_group] = jnp.concatenate(rows, axis=0)
    flip = jnp.where((iota((taps, taps), 0) + iota((taps, taps), 1)) % taps == 0, 1.0, 0.0)
    grads = jnp.dot(
        lines[...], flip, preferred_element_type=jnp.float32, precision=lax.Precision.HIGHEST
    )
    count = grads.shape[0]
    out_ref[pl.ds(pl.multiple_of(odd * count, count), count)] = grads
    out_ref[pl.ds(pl.multiple_of((1 - odd) * count, count), count)] = jnp.zeros_like(grads)


def filter_gradient(near, own, keep, near_in, extra, far_in, width):
    taps, half = own.shape
    count = half // width
    return pl.pallas_call(
        functools.partial(filter_grad_kernel, width),
        in_specs=[VMEM] * 6,
        out_specs=VMEM,
        out_shape=jax.ShapeDtypeStruct((2 * count, taps), jnp.float32),
        scratch_shapes=[pltpu.VMEM((count, taps), jnp.float32)],
        name="filter_gradient",
        cost_estimate=pl.CostEstimate(
            flops=4 * count * taps * taps * 256, bytes_accessed=16 * taps * half, transcendentals=0
        ),
        compiler_params=pltpu.CompilerParams(vmem_limit_bytes=8 * MIB),
    )(near, own, keep, near_in, extra, far_in)


def outputs_kernel(
    width, base, q_ref, k_ref, v_ref, ct_ref, tiles_ref, near_ref, far_ref, keep_ref,
    near_in_ref, far_in_ref, *rest,
):
    *results, sems = rest[-5:]
    *targets, done_ref = rest[-10:-5]
    out, grad_q, grad_k, grad_v = results
    taps, half = far_ref.shape
    channels = out.shape[1]
    per_group = LANES // width
    odd = lax.axis_index("ctx") % 2
    keep_far = keep_ref[odd]
    keep_near = keep_ref[1 - odd]
    second = odd if base < half else 1 - odd
    base = base % half
    first = pl.multiple_of(second * half, half)
    reverse = reversal(taps)
    copies = []

    def send(which, at, sem):
        own = pl.ds(at, CHUNK)
        cols = pl.ds(pl.multiple_of(first + base + at, CHUNK), CHUNK)
        copy = pltpu.make_async_copy(results[which].at[:, own], targets[which].at[:, cols], sem)
        copy.start()
        copies.append(copy)

    for chunk in range(0, channels, CHUNK):
        whole = pl.ds(pl.multiple_of(first + base + chunk, CHUNK), CHUNK)
        k_turned = flipped(reverse, k_ref[:, whole])
        v_turned = flipped(reverse, v_ref[:, whole])
        k_parts, v_parts = [], []
        for lane in range(0, CHUNK, LANES):
            own = pl.ds(chunk + lane, LANES)
            sent = pl.ds(base + chunk + lane, LANES)
            at = pl.multiple_of(first + base + chunk + lane, LANES)
            cols = pl.ds(at, LANES)
            near_lines = jnp.concatenate(
                [masked(far_in_ref[:, sent], keep_far).T, near_ref[:, sent].T], axis=1
            )
            far_lines = jnp.concatenate(
                [masked(near_in_ref[:, sent], keep_near).T, far_ref[:, sent].T], axis=1
            )
            near_parts, far_parts = [], []
            for i in range(per_group):
                rows = slice(i * width, (i + 1) * width)
                both = jnp.concatenate([near_lines[rows], far_lines[rows]], axis=0)
                part = jnp.dot(both, tiles_ref[at // width + i], preferred_element_type=jnp.float32)
                near_parts.append(part[:width])
                far_parts.append(part[width:])
            near_sum = jnp.concatenate(near_parts, axis=0)
            far_sum = jnp.concatenate(far_parts, axis=0)
            y = jnp.where(odd == 1, far_sum, near_sum).T
            mixed = jnp.where(odd == 1, near_sum, far_sum).T
            out[:, own] = (q_ref[:, cols].astype(jnp.float32) * y).astype(jnp.bfloat16)
            grad_q[:, own] = (ct_ref[:, cols].astype(jnp.float32) * y).astype(jnp.bfloat16)
            lanes = slice(lane, lane + LANES)
            k_parts.append((mixed * v_turned[:, lanes]).astype(jnp.bfloat16))
            v_parts.append((mixed * k_turned[:, lanes]).astype(jnp.bfloat16))
        own = pl.ds(chunk, CHUNK)
        turn = chunk // CHUNK
        send(0, chunk, sems.at[turn, 0])
        send(1, chunk, sems.at[turn, 1])
        grad_k[:, own] = flipped(reverse, jnp.concatenate(k_parts, axis=1)).astype(jnp.bfloat16)
        send(2, chunk, sems.at[turn, 2])
        grad_v[:, own] = flipped(reverse, jnp.concatenate(v_parts, axis=1)).astype(jnp.bfloat16)
        send(3, chunk, sems.at[turn, 3])
    for copy in copies:
        copy.wait()
    done_ref[...] = jnp.zeros_like(done_ref)


def outputs(piece, operands, results, after, width):
    taps, channels = operands[0].shape
    part = channels // PIECES
    anywhere = pl.BlockSpec(memory_space=pl.ANY)
    shape = jax.ShapeDtypeStruct((taps, channels), jnp.bfloat16)
    *results, done = pl.pallas_call(
        functools.partial(outputs_kernel, width, piece * part),
        in_specs=[VMEM] * len(operands) + [anywhere] * (1 + len(results)),
        out_specs=[anywhere] * 4 + [VMEM],
        out_shape=[shape] * 4 + [jax.ShapeDtypeStruct((8, LANES), jnp.float32)],
        input_output_aliases={len(operands) + 1 + i: i for i in range(len(results))},
        scratch_shapes=[pltpu.VMEM((taps, part), jnp.bfloat16)] * 4
        + [pltpu.SemaphoreType.DMA((part // CHUNK, 4))],
        name=f"outputs_{piece}",
        cost_estimate=pl.CostEstimate(
            flops=16 * (part // width) * taps * taps * 256,
            bytes_accessed=24 * taps * part,
            transcendentals=0,
        ),
        compiler_params=pltpu.CompilerParams(vmem_limit_bytes=8 * MIB),
    )(*operands, after, *results)
    return results, done


def per_device(gate_in, key_in, value_in, cotangent, doc_starts, filters):
    taps = filters.shape[1]
    width = gate_in.shape[2] // filters.shape[0]
    assert gate_in.shape[1] == taps
    q, k, v, ct = gate_in[0], key_in[0], value_in[0], cotangent[0]
    other = first_gate(q, k, v, ct)
    other_in = exchange(other, "ctx", 1)
    q, k, v, ct, near_own, near_other, own = gates(other, q, k, v, ct)
    near_in_own = exchange(near_other, "ctx", 0)
    extra = exchange(other, "ctx", 0)
    own_in = exchange(own, "ctx", 1)
    near_in_other = exchange(near_own, "ctx", 0)
    keep = masks(doc_starts[0], near_other)
    mine = filter_gradient(near_own, own, keep, near_in_own, extra, other_in, width)
    halves = (
        (near_own, own, keep, near_in_own, other_in),
        (near_other, other, keep, near_in_other, own_in),
    )
    tiles, done = toeplitz(filters, mine)
    mine = add(mine, exchange(mine, "ctx", 0), done)
    results = []

    def beside(after, turn):
        nonlocal results
        piece = turn - FIRST_TURN
        if not 0 <= piece < PIECES:
            return after
        operands = (q, k, v, ct, tiles, *halves[piece])
        results, done = outputs(piece, operands, results, after, width)
        return done

    filter_grad = from_odd(sum_devices(mine, beside))
    return tuple(array[None] for array in results) + (filter_grad,)


def solution(mesh):
    split = P("dp", "ctx", None)
    return jax.shard_map(
        per_device,
        mesh=mesh,
        in_specs=(split, split, split, split, P("dp", None), P()),
        out_specs=(split, split, split, split, P()),
        check_vma=False,
    )
```

```python
import functools

import jax
import jax.numpy as jnp
from jax import lax
from jax.experimental import pallas as pl
from jax.experimental.pallas import tpu as pltpu
from jax.sharding import PartitionSpec as P

LANES = 128
ROW_BLOCK = 32
MIB = 1024 * 1024
CHUNKS = 4
PIECES = 2
FIRST_TURN = 2
CHUNK = 512
FIRST_VMEM = 213 * MIB // 4
GATES_VMEM = 101 * MIB // 2
VMEM = pl.BlockSpec(memory_space=pltpu.VMEM)
SMEM = pl.BlockSpec(memory_space=pltpu.SMEM)


def iota(shape, dim):
    return lax.broadcasted_iota(jnp.int32, shape, dim)


def exchange(array, first):
    seqs, blocks = lax.axis_size("dp"), lax.axis_size("ctx")
    pairs = []
    for seq in range(seqs):
        for block in range(blocks):
            to_seq, to_block = seq, (block - first ^ 1) + first
            if not 0 <= to_block < blocks:
                to_seq, to_block = seq ^ 1, block
            pairs.append((seq * blocks + block, to_seq * blocks + to_block))
    return lax.ppermute(array, ("dp", "ctx"), pairs)


def swapped(array, axis, step):
    size = lax.axis_size(axis)
    return lax.ppermute(array, axis, [(i, i ^ step) for i in range(size)])


def swapped(array, axis, step):
    size = lax.axis_size(axis)
    return lax.ppermute(array, axis, [(i, i ^ step) for i in range(size)])


def along(array, axis):
    size = lax.axis_size(axis)
    pairs = [(i, i + 2 if i % 2 else i - 2) for i in range(size)]
    return lax.ppermute(array, axis, [(i, j) for i, j in pairs if 0 <= j < size])


def add_kernel(mine_ref, other_ref, after_ref, out_ref):
    del after_ref
    out_ref[...] = mine_ref[...] + other_ref[...]


def add(mine, other, after):
    return pl.pallas_call(
        add_kernel,
        in_specs=[VMEM] * 2 + [pl.BlockSpec(memory_space=pl.ANY)],
        out_specs=VMEM,
        out_shape=jax.ShapeDtypeStruct(mine.shape, mine.dtype),
        name="add",
        compiler_params=pltpu.CompilerParams(vmem_limit_bytes=MIB),
    )(mine, other, after)


def sum_devices(mine, beside):
    turn = 0
    for axis, step in (("dp", 1), ("ctx", 2)):
        while step < lax.axis_size(axis):
            mine = add(mine, swapped(mine, axis, step), beside(mine, turn))
            step, turn = 2 * step, turn + 1
    return mine


def join_kernel(mine_ref, other_ref, out_ref):
    count = mine_ref.shape[0]
    odd = lax.axis_index("ctx") % 2
    out_ref[pl.ds(pl.multiple_of(odd * count, count), count)] = mine_ref[...]
    out_ref[pl.ds(pl.multiple_of((1 - odd) * count, count), count)] = other_ref[...]


def join(mine, other):
    count, taps = mine.shape
    return pl.pallas_call(
        join_kernel,
        in_specs=[VMEM] * 2,
        out_specs=VMEM,
        out_shape=jax.ShapeDtypeStruct((2 * count, taps), mine.dtype),
        name="join",
        compiler_params=pltpu.CompilerParams(vmem_limit_bytes=MIB),
    )(mine, other)


def reversal(taps):
    flip = iota((taps, taps), 0) + iota((taps, taps), 1) == taps - 1
    return jnp.where(flip, 1.0, 0.0).astype(jnp.bfloat16)


def flipped(reverse, array):
    return jnp.dot(reverse, array, preferred_element_type=jnp.float32)


def masked(array, keep):
    return array * jnp.concatenate([keep] * (array.shape[0] // keep.shape[0]), axis=0)


def bf16_product(one, two):
    return (one.astype(jnp.float32) * two.astype(jnp.float32)).astype(jnp.bfloat16)


def first_kernel(q_hbm, k_hbm, v_hbm, ct_hbm, other_ref, held, sems):
    taps, half = other_ref.shape
    block = half // CHUNKS
    odd = lax.axis_index("ctx") % 2 == 1
    reverse = reversal(taps)

    def make(sources, start, finish):
        copies = []
        for c in range(CHUNKS):
            for a, source in enumerate(sources):
                copy = pltpu.make_async_copy(
                    source.at[:, pl.ds(start + c * block, block)],
                    held.at[a, :, pl.ds(c * block, block)],
                    sems.at[c, a],
                )
                copy.start()
                copies.append(copy)
        for c in range(CHUNKS):
            cols = pl.ds(c * block, block)
            for copy in copies[2 * c : 2 * c + 2]:
                copy.wait()
            other_ref[:, cols] = finish(bf16_product(held[0, :, cols], held[1, :, cols]))

    @pl.when(odd)
    def _():
        make((k_hbm, v_hbm), 0, lambda u: u)

    @pl.when(jnp.logical_not(odd))
    def _():
        make((ct_hbm, q_hbm), half, lambda dy: flipped(reverse, dy).astype(jnp.bfloat16))


def first_gate(q, k, v, ct):
    taps, channels = q.shape
    half = channels // 2
    return pl.pallas_call(
        first_kernel,
        in_specs=[pl.BlockSpec(memory_space=pltpu.HBM)] * 4,
        out_specs=VMEM,
        out_shape=jax.ShapeDtypeStruct((taps, half), jnp.bfloat16),
        scratch_shapes=[
            pltpu.VMEM((2, taps, half), jnp.bfloat16),
            pltpu.SemaphoreType.DMA((CHUNKS, 2)),
        ],
        name="first_gate",
        cost_estimate=pl.CostEstimate(
            flops=taps * taps * channels, bytes_accessed=3 * taps * channels, transcendentals=0
        ),
        compiler_params=pltpu.CompilerParams(vmem_limit_bytes=FIRST_VMEM),
    )(q, k, v, ct)


def gates_kernel(
    after_ref, q_hbm, k_hbm, v_hbm, ct_hbm,
    q_ref, k_ref, v_ref, ct_ref, near_own_ref, near_other_ref, own_ref, sems,
):
    del after_ref
    taps, channels = q_ref.shape
    half = channels // 2
    block = channels // CHUNKS
    pairs = ((k_hbm, k_ref), (v_hbm, v_ref), (q_hbm, q_ref), (ct_hbm, ct_ref))
    copies = []
    for c in range(CHUNKS):
        cols = pl.ds(c * block, block)
        for a, (source, target) in enumerate(pairs):
            copy = pltpu.make_async_copy(source.at[:, cols], target.at[:, cols], sems.at[c, a])
            copy.start()
            copies.append(copy)
    odd = lax.axis_index("ctx") % 2 == 1
    reverse = reversal(taps)
    for c in range(CHUNKS):
        cols = pl.ds(c * block, block)
        sent = pl.ds(c * block % half, block)
        for copy in copies[4 * c : 4 * c + 4]:
            copy.wait()

        def make_u():
            return bf16_product(k_ref[:, cols], v_ref[:, cols])

        def make_dy():
            dy = bf16_product(ct_ref[:, cols], q_ref[:, cols])
            return flipped(reverse, dy).astype(jnp.bfloat16)

        @pl.when(odd)
        def _():
            near_ref = near_own_ref if c * block >= half else near_other_ref
            near_ref[:, sent] = make_dy()
            if c * block >= half:
                own_ref[:, sent] = make_u()

        @pl.when(jnp.logical_not(odd))
        def _():
            near_ref = near_own_ref if c * block < half else near_other_ref
            near_ref[:, sent] = make_u()
            if c * block < half:
                own_ref[:, sent] = make_dy()


def gates(after, q, k, v, ct):
    taps, channels = q.shape

    def shape(*dims):
        return jax.ShapeDtypeStruct(dims, jnp.bfloat16)

    half = channels // 2
    return pl.pallas_call(
        gates_kernel,
        in_specs=[pl.BlockSpec(memory_space=pl.ANY)]
        + [pl.BlockSpec(memory_space=pltpu.HBM)] * 4,
        out_specs=[VMEM] * 7,
        out_shape=[shape(taps, channels)] * 4 + [shape(taps, half)] * 3,
        scratch_shapes=[pltpu.SemaphoreType.DMA((CHUNKS, 4))],
        name="gates",
        cost_estimate=pl.CostEstimate(
            flops=2 * taps * taps * channels, bytes_accessed=12 * taps * channels, transcendentals=0
        ),
        compiler_params=pltpu.CompilerParams(vmem_limit_bytes=GATES_VMEM),
    )(after, q, k, v, ct)


def masks_kernel(taps, starts_ref, after_ref, keep_ref):
    del after_ref
    here = lax.axis_index("ctx")
    for side in range(2):
        found = (here + side) % lax.axis_size("ctx") == 0
        for d in range(starts_ref.shape[0]):
            found = jnp.logical_or(found, starts_ref[d] == (here + side) * taps)
        keep = jnp.where(found, 0.0, 1.0)
        keep_ref[side] = jnp.full(keep_ref.shape[1:], keep).astype(jnp.bfloat16)


def masks(starts, after):
    return pl.pallas_call(
        functools.partial(masks_kernel, after.shape[0]),
        in_specs=[SMEM, pl.BlockSpec(memory_space=pl.ANY)],
        out_specs=VMEM,
        out_shape=jax.ShapeDtypeStruct((2, 16, LANES), jnp.bfloat16),
        name="masks",
        compiler_params=pltpu.CompilerParams(vmem_limit_bytes=MIB),
    )(starts, after)


def toeplitz_kernel(filters_ref, after_ref, out_ref, done_ref):
    del after_ref
    count, taps = filters_ref.shape
    lines = filters_ref[...].astype(jnp.float32)
    current = iota((taps, taps), 0) <= iota((taps, taps), 1)
    for f in range(count):
        tile = jnp.broadcast_to(lines[f : f + 1], (taps, taps))
        tile = pltpu.roll(tile, 0, 1, stride=1, stride_axis=0)
        out_ref[f, :taps] = jnp.where(current, 0.0, tile).astype(jnp.bfloat16)
        out_ref[f, taps:] = jnp.where(current, tile, 0.0).astype(jnp.bfloat16)
    done_ref[...] = jnp.zeros_like(done_ref)


def toeplitz(filters, after):
    count, taps = filters.shape
    return pl.pallas_call(
        toeplitz_kernel,
        in_specs=[VMEM, pl.BlockSpec(memory_space=pl.ANY)],
        out_specs=[VMEM] * 2,
        out_shape=[
            jax.ShapeDtypeStruct((count, 2 * taps, taps), jnp.bfloat16),
            jax.ShapeDtypeStruct((8, LANES), jnp.float32),
        ],
        name="toeplitz",
        cost_estimate=pl.CostEstimate(
            flops=count * taps * taps * 64, bytes_accessed=4 * count * taps * taps, transcendentals=0
        ),
        compiler_params=pltpu.CompilerParams(vmem_limit_bytes=8 * MIB),
    )(filters, after)


def filter_grad_kernel(
    width, near_ref, own_ref, keep_ref, near_in_ref, extra_ref, far_in_ref, out_ref, lines
):
    taps, half = far_in_ref.shape
    per_group = LANES // width
    odd = lax.axis_index("ctx") % 2
    keep_far = keep_ref[odd]
    keep_near = keep_ref[1 - odd]
    lane_filter = iota((ROW_BLOCK, LANES), 1) // width
    fold = iota((ROW_BLOCK, taps), 1) + iota((ROW_BLOCK, taps), 0) < ROW_BLOCK
    for group in range(half // LANES):
        at = group * LANES
        cols = pl.ds(at, LANES)
        near = near_ref[:, cols]
        pairs = (
            (own_ref[:, cols], masked(far_in_ref[:, cols], keep_far), near),
            (near_in_ref[:, cols], masked(near, keep_near), extra_ref[:, cols]),
        )
        left, right = [], []
        for moving, beyond, fixed in pairs:
            window = jnp.concatenate([beyond, fixed], axis=0)
            for start in range(0, taps, ROW_BLOCK):
                piece = moving[start : start + ROW_BLOCK]
                left.append(
                    jnp.concatenate(
                        [jnp.where(lane_filter == i, piece, 0) for i in range(per_group)], axis=0
                    )
                )
                right.append(window[taps - ROW_BLOCK - start : 2 * taps - start])
        product = lax.dot_general(
            jnp.concatenate(left, axis=1),
            jnp.concatenate(right, axis=1),
            (((1,), (1,)), ((), ())),
            preferred_element_type=jnp.float32,
        )
        rows = []
        for i in range(per_group):
            tile = product[i * ROW_BLOCK : (i + 1) * ROW_BLOCK]
            high = jnp.concatenate(
                [tile[:, taps:], jnp.zeros((ROW_BLOCK, taps - ROW_BLOCK), jnp.float32)], axis=1
            )
            tile = jnp.where(fold, high, tile[:, :taps])
            tile = pltpu.roll(tile, taps - ROW_BLOCK + 1, 1, stride=1, stride_axis=0)
            rows.append(jnp.sum(tile, axis=0, keepdims=True))
        lines[group * per_group : (group + 1) * per_group] = jnp.concatenate(rows, axis=0)
    flip = jnp.where((iota((taps, taps), 0) + iota((taps, taps), 1)) % taps == 0, 1.0, 0.0)
    out_ref[...] = jnp.dot(
        lines[...], flip, preferred_element_type=jnp.float32, precision=lax.Precision.HIGHEST
    )


def filter_gradient(near, own, keep, near_in, extra, far_in, width):
    taps, half = own.shape
    count = half // width
    return pl.pallas_call(
        functools.partial(filter_grad_kernel, width),
        in_specs=[VMEM] * 6,
        out_specs=VMEM,
        out_shape=jax.ShapeDtypeStruct((count, taps), jnp.float32),
        scratch_shapes=[pltpu.VMEM((count, taps), jnp.float32)],
        name="filter_gradient",
        cost_estimate=pl.CostEstimate(
            flops=4 * count * taps * taps * 256, bytes_accessed=16 * taps * half, transcendentals=0
        ),
        compiler_params=pltpu.CompilerParams(vmem_limit_bytes=8 * MIB),
    )(near, own, keep, near_in, extra, far_in)


def outputs_kernel(
    width, base, q_ref, k_ref, v_ref, ct_ref, tiles_ref, near_ref, far_ref, keep_ref,
    near_in_ref, far_in_ref, *rest,
):
    *results, sems = rest[-5:]
    *targets, done_ref = rest[-10:-5]
    out, grad_q, grad_k, grad_v = results
    taps, half = far_ref.shape
    channels = out.shape[1]
    per_group = LANES // width
    odd = lax.axis_index("ctx") % 2
    keep_far = keep_ref[odd]
    keep_near = keep_ref[1 - odd]
    second = odd if base < half else 1 - odd
    base = base % half
    first = pl.multiple_of(second * half, half)
    reverse = reversal(taps)
    copies = []

    def send(which, at, sem):
        own = pl.ds(at, CHUNK)
        cols = pl.ds(pl.multiple_of(first + base + at, CHUNK), CHUNK)
        copy = pltpu.make_async_copy(results[which].at[:, own], targets[which].at[:, cols], sem)
        copy.start()
        copies.append(copy)

    for chunk in range(0, channels, CHUNK):
        whole = pl.ds(pl.multiple_of(first + base + chunk, CHUNK), CHUNK)
        k_turned = flipped(reverse, k_ref[:, whole])
        v_turned = flipped(reverse, v_ref[:, whole])
        k_parts, v_parts = [], []
        for lane in range(0, CHUNK, LANES):
            own = pl.ds(chunk + lane, LANES)
            sent = pl.ds(base + chunk + lane, LANES)
            at = pl.multiple_of(first + base + chunk + lane, LANES)
            cols = pl.ds(at, LANES)
            near_lines = jnp.concatenate(
                [masked(far_in_ref[:, sent], keep_far).T, near_ref[:, sent].T], axis=1
            )
            far_lines = jnp.concatenate(
                [masked(near_in_ref[:, sent], keep_near).T, far_ref[:, sent].T], axis=1
            )
            near_parts, far_parts = [], []
            for i in range(per_group):
                rows = slice(i * width, (i + 1) * width)
                both = jnp.concatenate([near_lines[rows], far_lines[rows]], axis=0)
                part = jnp.dot(both, tiles_ref[at // width + i], preferred_element_type=jnp.float32)
                near_parts.append(part[:width])
                far_parts.append(part[width:])
            near_sum = jnp.concatenate(near_parts, axis=0)
            far_sum = jnp.concatenate(far_parts, axis=0)
            y = jnp.where(odd == 1, far_sum, near_sum).T
            mixed = jnp.where(odd == 1, near_sum, far_sum).T
            out[:, own] = (q_ref[:, cols].astype(jnp.float32) * y).astype(jnp.bfloat16)
            grad_q[:, own] = (ct_ref[:, cols].astype(jnp.float32) * y).astype(jnp.bfloat16)
            lanes = slice(lane, lane + LANES)
            k_parts.append((mixed * v_turned[:, lanes]).astype(jnp.bfloat16))
            v_parts.append((mixed * k_turned[:, lanes]).astype(jnp.bfloat16))
        own = pl.ds(chunk, CHUNK)
        turn = chunk // CHUNK
        send(0, chunk, sems.at[turn, 0])
        send(1, chunk, sems.at[turn, 1])
        grad_k[:, own] = flipped(reverse, jnp.concatenate(k_parts, axis=1)).astype(jnp.bfloat16)
        send(2, chunk, sems.at[turn, 2])
        grad_v[:, own] = flipped(reverse, jnp.concatenate(v_parts, axis=1)).astype(jnp.bfloat16)
        send(3, chunk, sems.at[turn, 3])
    for copy in copies:
        copy.wait()
    done_ref[...] = jnp.zeros_like(done_ref)


def outputs(piece, operands, results, after, width):
    taps, channels = operands[0].shape
    part = channels // PIECES
    anywhere = pl.BlockSpec(memory_space=pl.ANY)
    shape = jax.ShapeDtypeStruct((taps, channels), jnp.bfloat16)
    *results, done = pl.pallas_call(
        functools.partial(outputs_kernel, width, piece * part),
        in_specs=[VMEM] * len(operands) + [anywhere] * (1 + len(results)),
        out_specs=[anywhere] * 4 + [VMEM],
        out_shape=[shape] * 4 + [jax.ShapeDtypeStruct((8, LANES), jnp.float32)],
        input_output_aliases={len(operands) + 1 + i: i for i in range(len(results))},
        scratch_shapes=[pltpu.VMEM((taps, part), jnp.bfloat16)] * 4
        + [pltpu.SemaphoreType.DMA((part // CHUNK, 4))],
        name=f"outputs_{piece}",
        cost_estimate=pl.CostEstimate(
            flops=16 * (part // width) * taps * taps * 256,
            bytes_accessed=24 * taps * part,
            transcendentals=0,
        ),
        compiler_params=pltpu.CompilerParams(vmem_limit_bytes=8 * MIB),
    )(*operands, after, *results)
    return results, done


def per_device(gate_in, key_in, value_in, cotangent, doc_starts, filters):
    taps = filters.shape[1]
    width = gate_in.shape[2] // filters.shape[0]
    assert gate_in.shape[1] == taps
    q, k, v, ct = gate_in[0], key_in[0], value_in[0], cotangent[0]
    other = first_gate(q, k, v, ct)
    other_in = exchange(other, 1)
    q, k, v, ct, near_own, near_other, own = gates(other, q, k, v, ct)
    near_in_own = exchange(near_other, 0)
    extra = exchange(other, 0)
    own_in = exchange(own, 1)
    near_in_other = exchange(near_own, 0)
    keep = masks(doc_starts[0], near_other)
    mine = filter_gradient(near_own, own, keep, near_in_own, extra, other_in, width)
    halves = (
        (near_own, own, keep, near_in_own, other_in),
        (near_other, other, keep, near_in_other, own_in),
    )
    tiles = None
    results = []

    def beside(after, turn):
        nonlocal tiles, results
        piece = turn - FIRST_TURN
        if turn == 0:
            tiles, done = toeplitz(filters, after)
            return done
        if not 0 <= piece < PIECES:
            return after
        operands = (q, k, v, ct, tiles, *halves[piece])
        results, done = outputs(piece, operands, results, after, width)
        return done

    mine = sum_devices(mine, beside)
    filter_grad = join(mine, exchange(mine, 0))
    return tuple(array[None] for array in results) + (filter_grad,)


def solution(mesh):
    split = P("dp", "ctx", None)
    return jax.shard_map(
        per_device,
        mesh=mesh,
        in_specs=(split, split, split, split, P("dp", None), P()),
        out_specs=(split, split, split, split, P()),
        check_vma=False,
    )
```

```python
import functools

import jax
import jax.numpy as jnp
from jax import lax
from jax.experimental import pallas as pl
from jax.experimental.pallas import tpu as pltpu
from jax.sharding import PartitionSpec as P

LANES = 128
ROW_BLOCK = 32
MIB = 1024 * 1024
CHUNKS = 4
PIECES = 2
FIRST_TURN = 1
CHUNK = 512
FIRST_VMEM = 213 * MIB // 4
GATES_VMEM = 101 * MIB // 2
VMEM = pl.BlockSpec(memory_space=pltpu.VMEM)
SMEM = pl.BlockSpec(memory_space=pltpu.SMEM)


def iota(shape, dim):
    return lax.broadcasted_iota(jnp.int32, shape, dim)


def exchange(array, first):
    seqs, blocks = lax.axis_size("dp"), lax.axis_size("ctx")
    pairs = []
    for seq in range(seqs):
        for block in range(blocks):
            to_seq, to_block = seq, (block - first ^ 1) + first
            if not 0 <= to_block < blocks:
                to_seq, to_block = seq ^ 1, block
            pairs.append((seq * blocks + block, to_seq * blocks + to_block))
    return lax.ppermute(array, ("dp", "ctx"), pairs)


def swapped(array, axis, step):
    size = lax.axis_size(axis)
    return lax.ppermute(array, axis, [(i, i ^ step) for i in range(size)])


def swapped(array, axis, step):
    size = lax.axis_size(axis)
    return lax.ppermute(array, axis, [(i, i ^ step) for i in range(size)])


def along(array, axis):
    size = lax.axis_size(axis)
    pairs = [(i, i + 2 if i % 2 else i - 2) for i in range(size)]
    return lax.ppermute(array, axis, [(i, j) for i, j in pairs if 0 <= j < size])


def add_kernel(*refs):
    *terms, _, out_ref = [ref for ref in refs]
    terms = [term[...] for term in terms]
    while len(terms) > 1:
        terms = [sum(terms[i + 1 : i + 2], terms[i]) for i in range(0, len(terms), 2)]
    out_ref[...] = terms[0]


def add(terms, after):
    return pl.pallas_call(
        add_kernel,
        in_specs=[VMEM] * len(terms) + [pl.BlockSpec(memory_space=pl.ANY)],
        out_specs=VMEM,
        out_shape=jax.ShapeDtypeStruct(terms[0].shape, terms[0].dtype),
        name="add",
        compiler_params=pltpu.CompilerParams(vmem_limit_bytes=MIB),
    )(*terms, after)


def sum_devices(mine, beside):
    turn = 0
    for axis, step, radix in (("dp", 1, 4), ("ctx", 2, 2)):
        size = lax.axis_size(axis)
        while step < size:
            count = radix if radix * step <= size else 2
            others = [swapped(mine, axis, step * i) for i in range(1, count)]
            mine = add([mine] + others, beside(mine, turn))
            step, turn = count * step, turn + 1
    return mine


def join_kernel(mine_ref, other_ref, out_ref):
    count = mine_ref.shape[0]
    odd = lax.axis_index("ctx") % 2
    out_ref[pl.ds(pl.multiple_of(odd * count, count), count)] = mine_ref[...]
    out_ref[pl.ds(pl.multiple_of((1 - odd) * count, count), count)] = other_ref[...]


def join(mine, other):
    count, taps = mine.shape
    return pl.pallas_call(
        join_kernel,
        in_specs=[VMEM] * 2,
        out_specs=VMEM,
        out_shape=jax.ShapeDtypeStruct((2 * count, taps), mine.dtype),
        name="join",
        compiler_params=pltpu.CompilerParams(vmem_limit_bytes=MIB),
    )(mine, other)


def reversal(taps):
    flip = iota((taps, taps), 0) + iota((taps, taps), 1) == taps - 1
    return jnp.where(flip, 1.0, 0.0).astype(jnp.bfloat16)


def flipped(reverse, array):
    return jnp.dot(reverse, array, preferred_element_type=jnp.float32)


def masked(array, keep):
    return array * jnp.concatenate([keep] * (array.shape[0] // keep.shape[0]), axis=0)


def bf16_product(one, two):
    return (one.astype(jnp.float32) * two.astype(jnp.float32)).astype(jnp.bfloat16)


def first_kernel(q_hbm, k_hbm, v_hbm, ct_hbm, other_ref, held, sems):
    taps, half = other_ref.shape
    block = half // CHUNKS
    odd = lax.axis_index("ctx") % 2 == 1
    reverse = reversal(taps)

    def make(sources, start, finish):
        copies = []
        for c in range(CHUNKS):
            for a, source in enumerate(sources):
                copy = pltpu.make_async_copy(
                    source.at[:, pl.ds(start + c * block, block)],
                    held.at[a, :, pl.ds(c * block, block)],
                    sems.at[c, a],
                )
                copy.start()
                copies.append(copy)
        for c in range(CHUNKS):
            cols = pl.ds(c * block, block)
            for copy in copies[2 * c : 2 * c + 2]:
                copy.wait()
            other_ref[:, cols] = finish(bf16_product(held[0, :, cols], held[1, :, cols]))

    @pl.when(odd)
    def _():
        make((k_hbm, v_hbm), 0, lambda u: u)

    @pl.when(jnp.logical_not(odd))
    def _():
        make((ct_hbm, q_hbm), half, lambda dy: flipped(reverse, dy).astype(jnp.bfloat16))


def first_gate(q, k, v, ct):
    taps, channels = q.shape
    half = channels // 2
    return pl.pallas_call(
        first_kernel,
        in_specs=[pl.BlockSpec(memory_space=pltpu.HBM)] * 4,
        out_specs=VMEM,
        out_shape=jax.ShapeDtypeStruct((taps, half), jnp.bfloat16),
        scratch_shapes=[
            pltpu.VMEM((2, taps, half), jnp.bfloat16),
            pltpu.SemaphoreType.DMA((CHUNKS, 2)),
        ],
        name="first_gate",
        cost_estimate=pl.CostEstimate(
            flops=taps * taps * channels, bytes_accessed=3 * taps * channels, transcendentals=0
        ),
        compiler_params=pltpu.CompilerParams(vmem_limit_bytes=FIRST_VMEM),
    )(q, k, v, ct)


def gates_kernel(
    after_ref, q_hbm, k_hbm, v_hbm, ct_hbm,
    q_ref, k_ref, v_ref, ct_ref, near_own_ref, near_other_ref, own_ref, sems,
):
    del after_ref
    taps, channels = q_ref.shape
    half = channels // 2
    block = channels // CHUNKS
    pairs = ((k_hbm, k_ref), (v_hbm, v_ref), (q_hbm, q_ref), (ct_hbm, ct_ref))
    copies = []
    for c in range(CHUNKS):
        cols = pl.ds(c * block, block)
        for a, (source, target) in enumerate(pairs):
            copy = pltpu.make_async_copy(source.at[:, cols], target.at[:, cols], sems.at[c, a])
            copy.start()
            copies.append(copy)
    odd = lax.axis_index("ctx") % 2 == 1
    reverse = reversal(taps)
    for c in range(CHUNKS):
        cols = pl.ds(c * block, block)
        sent = pl.ds(c * block % half, block)
        for copy in copies[4 * c : 4 * c + 4]:
            copy.wait()

        def make_u():
            return bf16_product(k_ref[:, cols], v_ref[:, cols])

        def make_dy():
            dy = bf16_product(ct_ref[:, cols], q_ref[:, cols])
            return flipped(reverse, dy).astype(jnp.bfloat16)

        @pl.when(odd)
        def _():
            near_ref = near_own_ref if c * block >= half else near_other_ref
            near_ref[:, sent] = make_dy()
            if c * block >= half:
                own_ref[:, sent] = make_u()

        @pl.when(jnp.logical_not(odd))
        def _():
            near_ref = near_own_ref if c * block < half else near_other_ref
            near_ref[:, sent] = make_u()
            if c * block < half:
                own_ref[:, sent] = make_dy()


def gates(after, q, k, v, ct):
    taps, channels = q.shape

    def shape(*dims):
        return jax.ShapeDtypeStruct(dims, jnp.bfloat16)

    half = channels // 2
    return pl.pallas_call(
        gates_kernel,
        in_specs=[pl.BlockSpec(memory_space=pl.ANY)]
        + [pl.BlockSpec(memory_space=pltpu.HBM)] * 4,
        out_specs=[VMEM] * 7,
        out_shape=[shape(taps, channels)] * 4 + [shape(taps, half)] * 3,
        scratch_shapes=[pltpu.SemaphoreType.DMA((CHUNKS, 4))],
        name="gates",
        cost_estimate=pl.CostEstimate(
            flops=2 * taps * taps * channels, bytes_accessed=12 * taps * channels, transcendentals=0
        ),
        compiler_params=pltpu.CompilerParams(vmem_limit_bytes=GATES_VMEM),
    )(after, q, k, v, ct)


def masks_kernel(taps, starts_ref, after_ref, keep_ref):
    del after_ref
    here = lax.axis_index("ctx")
    for side in range(2):
        found = (here + side) % lax.axis_size("ctx") == 0
        for d in range(starts_ref.shape[0]):
            found = jnp.logical_or(found, starts_ref[d] == (here + side) * taps)
        keep = jnp.where(found, 0.0, 1.0)
        keep_ref[side] = jnp.full(keep_ref.shape[1:], keep).astype(jnp.bfloat16)


def masks(starts, after):
    return pl.pallas_call(
        functools.partial(masks_kernel, after.shape[0]),
        in_specs=[SMEM, pl.BlockSpec(memory_space=pl.ANY)],
        out_specs=VMEM,
        out_shape=jax.ShapeDtypeStruct((2, 16, LANES), jnp.bfloat16),
        name="masks",
        compiler_params=pltpu.CompilerParams(vmem_limit_bytes=MIB),
    )(starts, after)


def toeplitz_kernel(filters_ref, after_ref, out_ref, done_ref):
    del after_ref
    count, taps = filters_ref.shape
    lines = filters_ref[...].astype(jnp.float32)
    current = iota((taps, taps), 0) <= iota((taps, taps), 1)
    for f in range(count):
        tile = jnp.broadcast_to(lines[f : f + 1], (taps, taps))
        tile = pltpu.roll(tile, 0, 1, stride=1, stride_axis=0)
        out_ref[f, :taps] = jnp.where(current, 0.0, tile).astype(jnp.bfloat16)
        out_ref[f, taps:] = jnp.where(current, tile, 0.0).astype(jnp.bfloat16)
    done_ref[...] = jnp.zeros_like(done_ref)


def toeplitz(filters, after):
    count, taps = filters.shape
    return pl.pallas_call(
        toeplitz_kernel,
        in_specs=[VMEM, pl.BlockSpec(memory_space=pl.ANY)],
        out_specs=[VMEM] * 2,
        out_shape=[
            jax.ShapeDtypeStruct((count, 2 * taps, taps), jnp.bfloat16),
            jax.ShapeDtypeStruct((8, LANES), jnp.float32),
        ],
        name="toeplitz",
        cost_estimate=pl.CostEstimate(
            flops=count * taps * taps * 64, bytes_accessed=4 * count * taps * taps, transcendentals=0
        ),
        compiler_params=pltpu.CompilerParams(vmem_limit_bytes=8 * MIB),
    )(filters, after)


def filter_grad_kernel(
    width, near_ref, own_ref, keep_ref, near_in_ref, extra_ref, far_in_ref, after_ref, out_ref, lines
):
    del after_ref
    taps, half = far_in_ref.shape
    per_group = LANES // width
    odd = lax.axis_index("ctx") % 2
    keep_far = keep_ref[odd]
    keep_near = keep_ref[1 - odd]
    lane_filter = iota((ROW_BLOCK, LANES), 1) // width
    fold = iota((ROW_BLOCK, taps), 1) + iota((ROW_BLOCK, taps), 0) < ROW_BLOCK
    for group in range(half // LANES):
        at = group * LANES
        cols = pl.ds(at, LANES)
        near = near_ref[:, cols]
        pairs = (
            (own_ref[:, cols], masked(far_in_ref[:, cols], keep_far), near),
            (near_in_ref[:, cols], masked(near, keep_near), extra_ref[:, cols]),
        )
        left, right = [], []
        for moving, beyond, fixed in pairs:
            window = jnp.concatenate([beyond, fixed], axis=0)
            for start in range(0, taps, ROW_BLOCK):
                piece = moving[start : start + ROW_BLOCK]
                left.append(
                    jnp.concatenate(
                        [jnp.where(lane_filter == i, piece, 0) for i in range(per_group)], axis=0
                    )
                )
                right.append(window[taps - ROW_BLOCK - start : 2 * taps - start])
        product = lax.dot_general(
            jnp.concatenate(left, axis=1),
            jnp.concatenate(right, axis=1),
            (((1,), (1,)), ((), ())),
            preferred_element_type=jnp.float32,
        )
        rows = []
        for i in range(per_group):
            tile = product[i * ROW_BLOCK : (i + 1) * ROW_BLOCK]
            high = jnp.concatenate(
                [tile[:, taps:], jnp.zeros((ROW_BLOCK, taps - ROW_BLOCK), jnp.float32)], axis=1
            )
            tile = jnp.where(fold, high, tile[:, :taps])
            tile = pltpu.roll(tile, taps - ROW_BLOCK + 1, 1, stride=1, stride_axis=0)
            rows.append(jnp.sum(tile, axis=0, keepdims=True))
        lines[group * per_group : (group + 1) * per_group] = jnp.concatenate(rows, axis=0)
    flip = jnp.where((iota((taps, taps), 0) + iota((taps, taps), 1)) % taps == 0, 1.0, 0.0)
    out_ref[...] = jnp.dot(
        lines[...], flip, preferred_element_type=jnp.float32, precision=lax.Precision.HIGHEST
    )


def filter_gradient(near, own, keep, near_in, extra, far_in, after, width):
    taps, half = own.shape
    count = half // width
    return pl.pallas_call(
        functools.partial(filter_grad_kernel, width),
        in_specs=[VMEM] * 6 + [pl.BlockSpec(memory_space=pl.ANY)],
        out_specs=VMEM,
        out_shape=jax.ShapeDtypeStruct((count, taps), jnp.float32),
        scratch_shapes=[pltpu.VMEM((count, taps), jnp.float32)],
        name="filter_gradient",
        cost_estimate=pl.CostEstimate(
            flops=4 * count * taps * taps * 256, bytes_accessed=16 * taps * half, transcendentals=0
        ),
        compiler_params=pltpu.CompilerParams(vmem_limit_bytes=8 * MIB),
    )(near, own, keep, near_in, extra, far_in, after)


def outputs_kernel(
    width, base, q_ref, k_ref, v_ref, ct_ref, tiles_ref, near_ref, far_ref, keep_ref,
    near_in_ref, far_in_ref, *rest,
):
    *results, sems = rest[-5:]
    *targets, done_ref = rest[-10:-5]
    out, grad_q, grad_k, grad_v = results
    taps, half = far_ref.shape
    channels = out.shape[1]
    per_group = LANES // width
    odd = lax.axis_index("ctx") % 2
    keep_far = keep_ref[odd]
    keep_near = keep_ref[1 - odd]
    second = odd if base < half else 1 - odd
    base = base % half
    first = pl.multiple_of(second * half, half)
    reverse = reversal(taps)
    copies = []

    def send(which, at, sem):
        own = pl.ds(at, CHUNK)
        cols = pl.ds(pl.multiple_of(first + base + at, CHUNK), CHUNK)
        copy = pltpu.make_async_copy(results[which].at[:, own], targets[which].at[:, cols], sem)
        copy.start()
        copies.append(copy)

    for chunk in range(0, channels, CHUNK):
        whole = pl.ds(pl.multiple_of(first + base + chunk, CHUNK), CHUNK)
        k_turned = flipped(reverse, k_ref[:, whole])
        v_turned = flipped(reverse, v_ref[:, whole])
        k_parts, v_parts = [], []
        for lane in range(0, CHUNK, LANES):
            own = pl.ds(chunk + lane, LANES)
            sent = pl.ds(base + chunk + lane, LANES)
            at = pl.multiple_of(first + base + chunk + lane, LANES)
            cols = pl.ds(at, LANES)
            near_lines = jnp.concatenate(
                [masked(far_in_ref[:, sent], keep_far).T, near_ref[:, sent].T], axis=1
            )
            far_lines = jnp.concatenate(
                [masked(near_in_ref[:, sent], keep_near).T, far_ref[:, sent].T], axis=1
            )
            near_parts, far_parts = [], []
            for i in range(per_group):
                rows = slice(i * width, (i + 1) * width)
                both = jnp.concatenate([near_lines[rows], far_lines[rows]], axis=0)
                part = jnp.dot(both, tiles_ref[at // width + i], preferred_element_type=jnp.float32)
                near_parts.append(part[:width])
                far_parts.append(part[width:])
            near_sum = jnp.concatenate(near_parts, axis=0)
            far_sum = jnp.concatenate(far_parts, axis=0)
            y = jnp.where(odd == 1, far_sum, near_sum).T
            mixed = jnp.where(odd == 1, near_sum, far_sum).T
            out[:, own] = (q_ref[:, cols].astype(jnp.float32) * y).astype(jnp.bfloat16)
            grad_q[:, own] = (ct_ref[:, cols].astype(jnp.float32) * y).astype(jnp.bfloat16)
            lanes = slice(lane, lane + LANES)
            k_parts.append((mixed * v_turned[:, lanes]).astype(jnp.bfloat16))
            v_parts.append((mixed * k_turned[:, lanes]).astype(jnp.bfloat16))
        own = pl.ds(chunk, CHUNK)
        turn = chunk // CHUNK
        send(0, chunk, sems.at[turn, 0])
        send(1, chunk, sems.at[turn, 1])
        grad_k[:, own] = flipped(reverse, jnp.concatenate(k_parts, axis=1)).astype(jnp.bfloat16)
        send(2, chunk, sems.at[turn, 2])
        grad_v[:, own] = flipped(reverse, jnp.concatenate(v_parts, axis=1)).astype(jnp.bfloat16)
        send(3, chunk, sems.at[turn, 3])
    for copy in copies:
        copy.wait()
    done_ref[...] = jnp.zeros_like(done_ref)


def outputs(piece, operands, results, after, width):
    taps, channels = operands[0].shape
    part = channels // PIECES
    anywhere = pl.BlockSpec(memory_space=pl.ANY)
    shape = jax.ShapeDtypeStruct((taps, channels), jnp.bfloat16)
    *results, done = pl.pallas_call(
        functools.partial(outputs_kernel, width, piece * part),
        in_specs=[VMEM] * len(operands) + [anywhere] * (1 + len(results)),
        out_specs=[anywhere] * 4 + [VMEM],
        out_shape=[shape] * 4 + [jax.ShapeDtypeStruct((8, LANES), jnp.float32)],
        input_output_aliases={len(operands) + 1 + i: i for i in range(len(results))},
        scratch_shapes=[pltpu.VMEM((taps, part), jnp.bfloat16)] * 4
        + [pltpu.SemaphoreType.DMA((part // CHUNK, 4))],
        name=f"outputs_{piece}",
        cost_estimate=pl.CostEstimate(
            flops=16 * (part // width) * taps * taps * 256,
            bytes_accessed=24 * taps * part,
            transcendentals=0,
        ),
        compiler_params=pltpu.CompilerParams(vmem_limit_bytes=8 * MIB),
    )(*operands, after, *results)
    return results, done


def per_device(gate_in, key_in, value_in, cotangent, doc_starts, filters):
    taps = filters.shape[1]
    width = gate_in.shape[2] // filters.shape[0]
    assert gate_in.shape[1] == taps
    q, k, v, ct = gate_in[0], key_in[0], value_in[0], cotangent[0]
    other = first_gate(q, k, v, ct)
    other_in = exchange(other, 1)
    q, k, v, ct, near_own, near_other, own = gates(other, q, k, v, ct)
    near_in_own = exchange(near_other, 0)
    extra = exchange(other, 0)
    own_in = exchange(own, 1)
    near_in_other = exchange(near_own, 0)
    keep = masks(doc_starts[0], near_other)
    mine = filter_gradient(near_own, own, keep, near_in_own, extra, other_in, near_in_other, width)
    halves = (
        (near_own, own, keep, near_in_own, other_in),
        (near_other, other, keep, near_in_other, own_in),
    )
    tiles = None
    results = []

    def beside(after, turn):
        nonlocal tiles, results
        piece = turn - FIRST_TURN
        if turn == 0:
            tiles, done = toeplitz(filters, after)
            return done
        if not 0 <= piece < PIECES:
            return after
        operands = (q, k, v, ct, tiles, *halves[piece])
        results, done = outputs(piece, operands, results, after, width)
        return done

    mine = sum_devices(mine, beside)
    filter_grad = join(mine, exchange(mine, 0))
    return tuple(array[None] for array in results) + (filter_grad,)


def solution(mesh):
    split = P("dp", "ctx", None)
    return jax.shard_map(
        per_device,
        mesh=mesh,
        in_specs=(split, split, split, split, P("dp", None), P()),
        out_specs=(split, split, split, split, P()),
        check_vma=False,
    )
```

```python
import functools

import jax
import jax.numpy as jnp
from jax import lax
from jax.experimental import pallas as pl
from jax.experimental.pallas import tpu as pltpu
from jax.sharding import PartitionSpec as P

LANES = 128
ROW_BLOCK = 32
MIB = 1024 * 1024
CHUNKS = 4
PIECES = 2
CHUNK = 512
FIRST_VMEM = 213 * MIB // 4
GATES_VMEM = 101 * MIB // 2
VMEM = pl.BlockSpec(memory_space=pltpu.VMEM)
SMEM = pl.BlockSpec(memory_space=pltpu.SMEM)


def iota(shape, dim):
    return lax.broadcasted_iota(jnp.int32, shape, dim)


def exchange(array, first):
    seqs, blocks = lax.axis_size("dp"), lax.axis_size("ctx")
    pairs = []
    for seq in range(seqs):
        for block in range(blocks):
            to_seq, to_block = seq, (block - first ^ 1) + first
            if not 0 <= to_block < blocks:
                to_seq, to_block = seq ^ 1, block
            pairs.append((seq * blocks + block, to_seq * blocks + to_block))
    return lax.ppermute(array, ("dp", "ctx"), pairs)


def swapped(array, axis, step):
    size = lax.axis_size(axis)
    return lax.ppermute(array, axis, [(i, i ^ step) for i in range(size)])


def swapped(array, axis, step):
    size = lax.axis_size(axis)
    return lax.ppermute(array, axis, [(i, i ^ step) for i in range(size)])


def along(array, axis):
    size = lax.axis_size(axis)
    pairs = [(i, i + 2 if i % 2 else i - 2) for i in range(size)]
    return lax.ppermute(array, axis, [(i, j) for i, j in pairs if 0 <= j < size])


def add_kernel(*refs):
    *terms, _, out_ref = [ref for ref in refs]
    terms = [term[...] for term in terms]
    while len(terms) > 1:
        terms = [sum(terms[i + 1 : i + 2], terms[i]) for i in range(0, len(terms), 2)]
    out_ref[...] = terms[0]


def add(terms, after):
    return pl.pallas_call(
        add_kernel,
        in_specs=[VMEM] * len(terms) + [pl.BlockSpec(memory_space=pl.ANY)],
        out_specs=VMEM,
        out_shape=jax.ShapeDtypeStruct(terms[0].shape, terms[0].dtype),
        name="add",
        compiler_params=pltpu.CompilerParams(vmem_limit_bytes=MIB),
    )(*terms, after)


def sum_devices(mine, beside):
    turn = 0
    for axis, step in (("dp", 1), ("ctx", 2)):
        size = lax.axis_size(axis)
        while step < size:
            count = 4 if 4 * step <= size else 2
            others = [swapped(mine, axis, step * i) for i in range(1, count)]
            mine = add([mine] + others, beside(mine, turn))
            step, turn = count * step, turn + 1
    return mine


def join_kernel(mine_ref, other_ref, out_ref):
    count = mine_ref.shape[0]
    odd = lax.axis_index("ctx") % 2
    out_ref[pl.ds(pl.multiple_of(odd * count, count), count)] = mine_ref[...]
    out_ref[pl.ds(pl.multiple_of((1 - odd) * count, count), count)] = other_ref[...]


def join(mine, other):
    count, taps = mine.shape
    return pl.pallas_call(
        join_kernel,
        in_specs=[VMEM] * 2,
        out_specs=VMEM,
        out_shape=jax.ShapeDtypeStruct((2 * count, taps), mine.dtype),
        name="join",
        compiler_params=pltpu.CompilerParams(vmem_limit_bytes=MIB),
    )(mine, other)


def reversal(taps):
    flip = iota((taps, taps), 0) + iota((taps, taps), 1) == taps - 1
    return jnp.where(flip, 1.0, 0.0).astype(jnp.bfloat16)


def flipped(reverse, array):
    return jnp.dot(reverse, array, preferred_element_type=jnp.float32)


def masked(array, keep):
    return array * jnp.concatenate([keep] * (array.shape[0] // keep.shape[0]), axis=0)


def bf16_product(one, two):
    return (one.astype(jnp.float32) * two.astype(jnp.float32)).astype(jnp.bfloat16)


def first_kernel(q_hbm, k_hbm, v_hbm, ct_hbm, other_ref, held, sems):
    taps, half = other_ref.shape
    block = half // CHUNKS
    odd = lax.axis_index("ctx") % 2 == 1
    reverse = reversal(taps)

    def make(sources, start, finish):
        copies = []
        for c in range(CHUNKS):
            for a, source in enumerate(sources):
                copy = pltpu.make_async_copy(
                    source.at[:, pl.ds(start + c * block, block)],
                    held.at[a, :, pl.ds(c * block, block)],
                    sems.at[c, a],
                )
                copy.start()
                copies.append(copy)
        for copy in copies:
            copy.wait()
        other_ref[...] = finish(bf16_product(held[0], held[1]))

    @pl.when(odd)
    def _():
        make((k_hbm, v_hbm), 0, lambda u: u)

    @pl.when(jnp.logical_not(odd))
    def _():
        make((ct_hbm, q_hbm), half, lambda dy: flipped(reverse, dy).astype(jnp.bfloat16))


def first_gate(q, k, v, ct):
    taps, channels = q.shape
    half = channels // 2
    return pl.pallas_call(
        first_kernel,
        in_specs=[pl.BlockSpec(memory_space=pltpu.HBM)] * 4,
        out_specs=VMEM,
        out_shape=jax.ShapeDtypeStruct((taps, half), jnp.bfloat16),
        scratch_shapes=[
            pltpu.VMEM((2, taps, half), jnp.bfloat16),
            pltpu.SemaphoreType.DMA((CHUNKS, 2)),
        ],
        name="first_gate",
        cost_estimate=pl.CostEstimate(
            flops=taps * taps * channels, bytes_accessed=3 * taps * channels, transcendentals=0
        ),
        compiler_params=pltpu.CompilerParams(vmem_limit_bytes=FIRST_VMEM),
    )(q, k, v, ct)


def gates_kernel(
    after_ref, q_hbm, k_hbm, v_hbm, ct_hbm,
    q_ref, k_ref, v_ref, ct_ref, near_own_ref, near_other_ref, own_ref, sems,
):
    del after_ref
    taps, channels = q_ref.shape
    half = channels // 2
    block = channels // CHUNKS
    pairs = ((k_hbm, k_ref), (v_hbm, v_ref), (q_hbm, q_ref), (ct_hbm, ct_ref))
    copies = []
    for c in range(CHUNKS):
        cols = pl.ds(c * block, block)
        for a, (source, target) in enumerate(pairs):
            copy = pltpu.make_async_copy(source.at[:, cols], target.at[:, cols], sems.at[c, a])
            copy.start()
            copies.append(copy)
    odd = lax.axis_index("ctx") % 2 == 1
    reverse = reversal(taps)
    for c in range(CHUNKS):
        cols = pl.ds(c * block, block)
        sent = pl.ds(c * block % half, block)
        for copy in copies[4 * c : 4 * c + 4]:
            copy.wait()

        def make_u():
            return bf16_product(k_ref[:, cols], v_ref[:, cols])

        def make_dy():
            dy = bf16_product(ct_ref[:, cols], q_ref[:, cols])
            return flipped(reverse, dy).astype(jnp.bfloat16)

        @pl.when(odd)
        def _():
            near_ref = near_own_ref if c * block >= half else near_other_ref
            near_ref[:, sent] = make_dy()
            if c * block >= half:
                own_ref[:, sent] = make_u()

        @pl.when(jnp.logical_not(odd))
        def _():
            near_ref = near_own_ref if c * block < half else near_other_ref
            near_ref[:, sent] = make_u()
            if c * block < half:
                own_ref[:, sent] = make_dy()


def gates(after, q, k, v, ct):
    taps, channels = q.shape

    def shape(*dims):
        return jax.ShapeDtypeStruct(dims, jnp.bfloat16)

    half = channels // 2
    return pl.pallas_call(
        gates_kernel,
        in_specs=[pl.BlockSpec(memory_space=pl.ANY)]
        + [pl.BlockSpec(memory_space=pltpu.HBM)] * 4,
        out_specs=[VMEM] * 7,
        out_shape=[shape(taps, channels)] * 4 + [shape(taps, half)] * 3,
        scratch_shapes=[pltpu.SemaphoreType.DMA((CHUNKS, 4))],
        name="gates",
        cost_estimate=pl.CostEstimate(
            flops=2 * taps * taps * channels, bytes_accessed=12 * taps * channels, transcendentals=0
        ),
        compiler_params=pltpu.CompilerParams(vmem_limit_bytes=GATES_VMEM),
    )(after, q, k, v, ct)


def masks_kernel(taps, starts_ref, after_ref, keep_ref):
    del after_ref
    here = lax.axis_index("ctx")
    for side in range(2):
        found = (here + side) % lax.axis_size("ctx") == 0
        for d in range(starts_ref.shape[0]):
            found = jnp.logical_or(found, starts_ref[d] == (here + side) * taps)
        keep = jnp.where(found, 0.0, 1.0)
        keep_ref[side] = jnp.full(keep_ref.shape[1:], keep).astype(jnp.bfloat16)


def masks(starts, after):
    return pl.pallas_call(
        functools.partial(masks_kernel, after.shape[0]),
        in_specs=[SMEM, pl.BlockSpec(memory_space=pl.ANY)],
        out_specs=VMEM,
        out_shape=jax.ShapeDtypeStruct((2, 16, LANES), jnp.bfloat16),
        name="masks",
        compiler_params=pltpu.CompilerParams(vmem_limit_bytes=MIB),
    )(starts, after)


def toeplitz_kernel(filters_ref, after_ref, out_ref, done_ref):
    del after_ref
    count, taps = filters_ref.shape
    lines = filters_ref[...].astype(jnp.float32)
    current = iota((taps, taps), 0) <= iota((taps, taps), 1)
    for f in range(count):
        tile = jnp.broadcast_to(lines[f : f + 1], (taps, taps))
        tile = pltpu.roll(tile, 0, 1, stride=1, stride_axis=0)
        out_ref[f, :taps] = jnp.where(current, 0.0, tile).astype(jnp.bfloat16)
        out_ref[f, taps:] = jnp.where(current, tile, 0.0).astype(jnp.bfloat16)
    done_ref[...] = jnp.zeros_like(done_ref)


def toeplitz(filters, after):
    count, taps = filters.shape
    return pl.pallas_call(
        toeplitz_kernel,
        in_specs=[VMEM, pl.BlockSpec(memory_space=pl.ANY)],
        out_specs=[VMEM] * 2,
        out_shape=[
            jax.ShapeDtypeStruct((count, 2 * taps, taps), jnp.bfloat16),
            jax.ShapeDtypeStruct((8, LANES), jnp.float32),
        ],
        name="toeplitz",
        cost_estimate=pl.CostEstimate(
            flops=count * taps * taps * 64, bytes_accessed=4 * count * taps * taps, transcendentals=0
        ),
        compiler_params=pltpu.CompilerParams(vmem_limit_bytes=8 * MIB),
    )(filters, after)


def filter_grad_kernel(
    width, near_ref, own_ref, keep_ref, near_in_ref, extra_ref, far_in_ref, after_ref, out_ref, lines
):
    del after_ref
    taps, half = far_in_ref.shape
    per_group = LANES // width
    odd = lax.axis_index("ctx") % 2
    keep_far = keep_ref[odd]
    keep_near = keep_ref[1 - odd]
    lane_filter = iota((ROW_BLOCK, LANES), 1) // width
    fold = iota((ROW_BLOCK, taps), 1) + iota((ROW_BLOCK, taps), 0) < ROW_BLOCK
    for group in range(half // LANES):
        at = group * LANES
        cols = pl.ds(at, LANES)
        near = near_ref[:, cols]
        pairs = (
            (own_ref[:, cols], masked(far_in_ref[:, cols], keep_far), near),
            (near_in_ref[:, cols], masked(near, keep_near), extra_ref[:, cols]),
        )
        left, right = [], []
        for moving, beyond, fixed in pairs:
            window = jnp.concatenate([beyond, fixed], axis=0)
            for start in range(0, taps, ROW_BLOCK):
                piece = moving[start : start + ROW_BLOCK]
                left.append(
                    jnp.concatenate(
                        [jnp.where(lane_filter == i, piece, 0) for i in range(per_group)], axis=0
                    )
                )
                right.append(window[taps - ROW_BLOCK - start : 2 * taps - start])
        product = lax.dot_general(
            jnp.concatenate(left, axis=1),
            jnp.concatenate(right, axis=1),
            (((1,), (1,)), ((), ())),
            preferred_element_type=jnp.float32,
        )
        rows = []
        for i in range(per_group):
            tile = product[i * ROW_BLOCK : (i + 1) * ROW_BLOCK]
            high = jnp.concatenate(
                [tile[:, taps:], jnp.zeros((ROW_BLOCK, taps - ROW_BLOCK), jnp.float32)], axis=1
            )
            tile = jnp.where(fold, high, tile[:, :taps])
            tile = pltpu.roll(tile, taps - ROW_BLOCK + 1, 1, stride=1, stride_axis=0)
            rows.append(jnp.sum(tile, axis=0, keepdims=True))
        lines[group * per_group : (group + 1) * per_group] = jnp.concatenate(rows, axis=0)
    flip = jnp.where((iota((taps, taps), 0) + iota((taps, taps), 1)) % taps == 0, 1.0, 0.0)
    out_ref[...] = jnp.dot(
        lines[...], flip, preferred_element_type=jnp.float32, precision=lax.Precision.HIGHEST
    )


def filter_gradient(near, own, keep, near_in, extra, far_in, after, width):
    taps, half = own.shape
    count = half // width
    return pl.pallas_call(
        functools.partial(filter_grad_kernel, width),
        in_specs=[VMEM] * 6 + [pl.BlockSpec(memory_space=pl.ANY)],
        out_specs=VMEM,
        out_shape=jax.ShapeDtypeStruct((count, taps), jnp.float32),
        scratch_shapes=[pltpu.VMEM((count, taps), jnp.float32)],
        name="filter_gradient",
        cost_estimate=pl.CostEstimate(
            flops=4 * count * taps * taps * 256, bytes_accessed=16 * taps * half, transcendentals=0
        ),
        compiler_params=pltpu.CompilerParams(vmem_limit_bytes=8 * MIB),
    )(near, own, keep, near_in, extra, far_in, after)


def outputs_kernel(
    width, base, q_ref, k_ref, v_ref, ct_ref, tiles_ref, near_ref, far_ref, keep_ref,
    near_in_ref, far_in_ref, *rest,
):
    *results, sems = rest[-5:]
    *targets, done_ref = rest[-10:-5]
    out, grad_q, grad_k, grad_v = results
    taps, half = far_ref.shape
    channels = out.shape[1]
    per_group = LANES // width
    odd = lax.axis_index("ctx") % 2
    keep_far = keep_ref[odd]
    keep_near = keep_ref[1 - odd]
    second = odd if base < half else 1 - odd
    base = base % half
    first = pl.multiple_of(second * half, half)
    reverse = reversal(taps)
    copies = []

    def send(which, at, sem):
        own = pl.ds(at, CHUNK)
        cols = pl.ds(pl.multiple_of(first + base + at, CHUNK), CHUNK)
        copy = pltpu.make_async_copy(results[which].at[:, own], targets[which].at[:, cols], sem)
        copy.start()
        copies.append(copy)

    for chunk in range(0, channels, CHUNK):
        lines = []
        for lane in range(chunk, chunk + CHUNK, LANES):
            sent = pl.ds(base + lane, LANES)
            near_lines = jnp.concatenate(
                [masked(far_in_ref[:, sent], keep_far).T, near_ref[:, sent].T], axis=1
            )
            far_lines = jnp.concatenate(
                [masked(near_in_ref[:, sent], keep_near).T, far_ref[:, sent].T], axis=1
            )
            lines.append((lane, near_lines, far_lines))
        sums = []
        for lane, near_lines, far_lines in lines:
            at = (first + base + lane) // width
            near_parts, far_parts = [], []
            for i in range(per_group):
                rows = slice(i * width, (i + 1) * width)
                both = jnp.concatenate([near_lines[rows], far_lines[rows]], axis=0)
                part = jnp.dot(both, tiles_ref[at + i], preferred_element_type=jnp.float32)
                near_parts.append(part[:width])
                far_parts.append(part[width:])
            near_sum = jnp.concatenate(near_parts, axis=0)
            far_sum = jnp.concatenate(far_parts, axis=0)
            y = jnp.where(odd == 1, far_sum, near_sum).T
            mixed = jnp.where(odd == 1, near_sum, far_sum).T
            sums.append((lane, y, mixed))
        whole = pl.ds(pl.multiple_of(first + base + chunk, CHUNK), CHUNK)
        k_turned = flipped(reverse, k_ref[:, whole])
        v_turned = flipped(reverse, v_ref[:, whole])
        k_parts, v_parts = [], []
        for lane, y, mixed in sums:
            own = pl.ds(lane, LANES)
            cols = pl.ds(pl.multiple_of(first + base + lane, LANES), LANES)
            out[:, own] = (q_ref[:, cols].astype(jnp.float32) * y).astype(jnp.bfloat16)
            grad_q[:, own] = (ct_ref[:, cols].astype(jnp.float32) * y).astype(jnp.bfloat16)
            lanes = slice(lane - chunk, lane - chunk + LANES)
            k_parts.append((mixed * v_turned[:, lanes]).astype(jnp.bfloat16))
            v_parts.append((mixed * k_turned[:, lanes]).astype(jnp.bfloat16))
        own = pl.ds(chunk, CHUNK)
        turn = chunk // CHUNK
        send(0, chunk, sems.at[turn, 0])
        send(1, chunk, sems.at[turn, 1])
        grad_k[:, own] = flipped(reverse, jnp.concatenate(k_parts, axis=1)).astype(jnp.bfloat16)
        send(2, chunk, sems.at[turn, 2])
        grad_v[:, own] = flipped(reverse, jnp.concatenate(v_parts, axis=1)).astype(jnp.bfloat16)
        send(3, chunk, sems.at[turn, 3])
    for copy in copies:
        copy.wait()
    done_ref[...] = jnp.zeros_like(done_ref)


def outputs(piece, operands, results, after, width):
    taps, channels = operands[0].shape
    part = channels // PIECES
    anywhere = pl.BlockSpec(memory_space=pl.ANY)
    shape = jax.ShapeDtypeStruct((taps, channels), jnp.bfloat16)
    *results, done = pl.pallas_call(
        functools.partial(outputs_kernel, width, piece * part),
        in_specs=[VMEM] * len(operands) + [anywhere] * (1 + len(results)),
        out_specs=[anywhere] * 4 + [VMEM],
        out_shape=[shape] * 4 + [jax.ShapeDtypeStruct((8, LANES), jnp.float32)],
        input_output_aliases={len(operands) + 1 + i: i for i in range(len(results))},
        scratch_shapes=[pltpu.VMEM((taps, part), jnp.bfloat16)] * 4
        + [pltpu.SemaphoreType.DMA((part // CHUNK, 4))],
        name=f"outputs_{piece}",
        cost_estimate=pl.CostEstimate(
            flops=16 * (part // width) * taps * taps * 256,
            bytes_accessed=24 * taps * part,
            transcendentals=0,
        ),
        compiler_params=pltpu.CompilerParams(vmem_limit_bytes=8 * MIB),
    )(*operands, after, *results)
    return results, done


def per_device(gate_in, key_in, value_in, cotangent, doc_starts, filters):
    taps = filters.shape[1]
    width = gate_in.shape[2] // filters.shape[0]
    assert gate_in.shape[1] == taps
    q, k, v, ct = gate_in[0], key_in[0], value_in[0], cotangent[0]
    other = first_gate(q, k, v, ct)
    other_in = exchange(other, 1)
    q, k, v, ct, near_own, near_other, own = gates(other, q, k, v, ct)
    near_in_own = exchange(near_other, 0)
    extra = exchange(other, 0)
    own_in = exchange(own, 1)
    near_in_other = exchange(near_own, 0)
    keep = masks(doc_starts[0], near_other)
    mine = filter_gradient(near_own, own, keep, near_in_own, extra, other_in, near_in_other, width)
    halves = (
        (near_own, own, keep, near_in_own, other_in),
        (near_other, other, keep, near_in_other, own_in),
    )
    tiles = None
    results = []

    def beside(after, turn):
        nonlocal tiles, results
        if turn == 0:
            tiles, after = toeplitz(filters, after)
        elif turn == 1:
            for piece in range(PIECES):
                operands = (q, k, v, ct, tiles, *halves[piece])
                results, after = outputs(piece, operands, results, after, width)
        return after

    mine = sum_devices(mine, beside)
    filter_grad = join(mine, exchange(mine, 0))
    return tuple(array[None] for array in results) + (filter_grad,)


def solution(mesh):
    split = P("dp", "ctx", None)
    return jax.shard_map(
        per_device,
        mesh=mesh,
        in_specs=(split, split, split, split, P("dp", None), P()),
        out_specs=(split, split, split, split, P()),
        check_vma=False,
    )
```

```python
import functools

import jax
import jax.numpy as jnp
from jax import lax
from jax.experimental import pallas as pl
from jax.experimental.pallas import tpu as pltpu
from jax.sharding import PartitionSpec as P

LANES = 128
ROW_BLOCK = 32
MIB = 1024 * 1024
CHUNKS = 4
PIECES = 2
CHUNK = 512
FIRST_VMEM = 213 * MIB // 4
GATES_VMEM = 101 * MIB // 2
VMEM = pl.BlockSpec(memory_space=pltpu.VMEM)
SMEM = pl.BlockSpec(memory_space=pltpu.SMEM)


def iota(shape, dim):
    return lax.broadcasted_iota(jnp.int32, shape, dim)


def exchange(array, first):
    seqs, blocks = lax.axis_size("dp"), lax.axis_size("ctx")
    pairs = []
    for seq in range(seqs):
        for block in range(blocks):
            to_seq, to_block = seq, (block - first ^ 1) + first
            if not 0 <= to_block < blocks:
                to_seq, to_block = seq ^ 1, block
            pairs.append((seq * blocks + block, to_seq * blocks + to_block))
    return lax.ppermute(array, ("dp", "ctx"), pairs)


def swapped(array, axis, step):
    size = lax.axis_size(axis)
    return lax.ppermute(array, axis, [(i, i ^ step) for i in range(size)])


def swapped(array, axis, step):
    size = lax.axis_size(axis)
    return lax.ppermute(array, axis, [(i, i ^ step) for i in range(size)])


def along(array, axis):
    size = lax.axis_size(axis)
    pairs = [(i, i + 2 if i % 2 else i - 2) for i in range(size)]
    return lax.ppermute(array, axis, [(i, j) for i, j in pairs if 0 <= j < size])


def add_kernel(*refs):
    *terms, _, out_ref = [ref for ref in refs]
    terms = [term[...] for term in terms]
    while len(terms) > 1:
        terms = [sum(terms[i + 1 : i + 2], terms[i]) for i in range(0, len(terms), 2)]
    out_ref[...] = terms[0]


def add(terms, after):
    return pl.pallas_call(
        add_kernel,
        in_specs=[VMEM] * len(terms) + [pl.BlockSpec(memory_space=pl.ANY)],
        out_specs=VMEM,
        out_shape=jax.ShapeDtypeStruct(terms[0].shape, terms[0].dtype),
        name="add",
        compiler_params=pltpu.CompilerParams(vmem_limit_bytes=MIB),
    )(*terms, after)


def sum_devices(mine, beside):
    turn = 0
    for axis, step in (("dp", 1), ("ctx", 2)):
        size = lax.axis_size(axis)
        while step < size:
            count = 4 if axis == "dp" and 4 * step <= size else 2
            others = [swapped(mine, axis, step * i) for i in range(1, count)]
            mine = add([mine] + others, beside(mine, turn))
            step, turn = count * step, turn + 1
    return mine


def join_kernel(mine_ref, other_ref, out_ref):
    count = mine_ref.shape[0]
    odd = lax.axis_index("ctx") % 2
    out_ref[pl.ds(pl.multiple_of(odd * count, count), count)] = mine_ref[...]
    out_ref[pl.ds(pl.multiple_of((1 - odd) * count, count), count)] = other_ref[...]


def join(mine, other):
    count, taps = mine.shape
    return pl.pallas_call(
        join_kernel,
        in_specs=[VMEM] * 2,
        out_specs=VMEM,
        out_shape=jax.ShapeDtypeStruct((2 * count, taps), mine.dtype),
        name="join",
        compiler_params=pltpu.CompilerParams(vmem_limit_bytes=MIB),
    )(mine, other)


def reversal(taps):
    flip = iota((taps, taps), 0) + iota((taps, taps), 1) == taps - 1
    return jnp.where(flip, 1.0, 0.0).astype(jnp.bfloat16)


def flipped(reverse, array):
    return jnp.dot(reverse, array, preferred_element_type=jnp.float32)


def masked(array, keep):
    return array * jnp.concatenate([keep] * (array.shape[0] // keep.shape[0]), axis=0)


def bf16_product(one, two):
    return (one.astype(jnp.float32) * two.astype(jnp.float32)).astype(jnp.bfloat16)


def first_kernel(q_hbm, k_hbm, v_hbm, ct_hbm, other_ref, held, sems):
    taps, half = other_ref.shape
    block = half // CHUNKS
    odd = lax.axis_index("ctx") % 2 == 1
    reverse = reversal(taps)

    def make(sources, start, finish):
        copies = []
        for c in range(CHUNKS):
            for a, source in enumerate(sources):
                copy = pltpu.make_async_copy(
                    source.at[:, pl.ds(start + c * block, block)],
                    held.at[a, :, pl.ds(c * block, block)],
                    sems.at[c, a],
                )
                copy.start()
                copies.append(copy)
        for copy in copies:
            copy.wait()
        other_ref[...] = finish(bf16_product(held[0], held[1]))

    @pl.when(odd)
    def _():
        make((k_hbm, v_hbm), 0, lambda u: u)

    @pl.when(jnp.logical_not(odd))
    def _():
        make((ct_hbm, q_hbm), half, lambda dy: flipped(reverse, dy).astype(jnp.bfloat16))


def first_gate(q, k, v, ct):
    taps, channels = q.shape
    half = channels // 2
    return pl.pallas_call(
        first_kernel,
        in_specs=[pl.BlockSpec(memory_space=pltpu.HBM)] * 4,
        out_specs=VMEM,
        out_shape=jax.ShapeDtypeStruct((taps, half), jnp.bfloat16),
        scratch_shapes=[
            pltpu.VMEM((2, taps, half), jnp.bfloat16),
            pltpu.SemaphoreType.DMA((CHUNKS, 2)),
        ],
        name="first_gate",
        cost_estimate=pl.CostEstimate(
            flops=taps * taps * channels, bytes_accessed=3 * taps * channels, transcendentals=0
        ),
        compiler_params=pltpu.CompilerParams(vmem_limit_bytes=FIRST_VMEM),
    )(q, k, v, ct)


def gates_kernel(
    after_ref, q_hbm, k_hbm, v_hbm, ct_hbm,
    q_ref, k_ref, v_ref, ct_ref, near_own_ref, near_other_ref, own_ref, sems,
):
    del after_ref
    taps, channels = q_ref.shape
    half = channels // 2
    block = channels // CHUNKS
    pairs = ((k_hbm, k_ref), (v_hbm, v_ref), (q_hbm, q_ref), (ct_hbm, ct_ref))
    copies = []
    for c in range(CHUNKS):
        cols = pl.ds(c * block, block)
        for a, (source, target) in enumerate(pairs):
            copy = pltpu.make_async_copy(source.at[:, cols], target.at[:, cols], sems.at[c, a])
            copy.start()
            copies.append(copy)
    odd = lax.axis_index("ctx") % 2 == 1
    reverse = reversal(taps)
    for c in range(CHUNKS):
        cols = pl.ds(c * block, block)
        sent = pl.ds(c * block % half, block)
        for copy in copies[4 * c : 4 * c + 4]:
            copy.wait()

        def make_u():
            return bf16_product(k_ref[:, cols], v_ref[:, cols])

        def make_dy():
            dy = bf16_product(ct_ref[:, cols], q_ref[:, cols])
            return flipped(reverse, dy).astype(jnp.bfloat16)

        @pl.when(odd)
        def _():
            near_ref = near_own_ref if c * block >= half else near_other_ref
            near_ref[:, sent] = make_dy()
            if c * block >= half:
                own_ref[:, sent] = make_u()

        @pl.when(jnp.logical_not(odd))
        def _():
            near_ref = near_own_ref if c * block < half else near_other_ref
            near_ref[:, sent] = make_u()
            if c * block < half:
                own_ref[:, sent] = make_dy()


def gates(after, q, k, v, ct):
    taps, channels = q.shape

    def shape(*dims):
        return jax.ShapeDtypeStruct(dims, jnp.bfloat16)

    half = channels // 2
    return pl.pallas_call(
        gates_kernel,
        in_specs=[pl.BlockSpec(memory_space=pl.ANY)]
        + [pl.BlockSpec(memory_space=pltpu.HBM)] * 4,
        out_specs=[VMEM] * 7,
        out_shape=[shape(taps, channels)] * 4 + [shape(taps, half)] * 3,
        scratch_shapes=[pltpu.SemaphoreType.DMA((CHUNKS, 4))],
        name="gates",
        cost_estimate=pl.CostEstimate(
            flops=2 * taps * taps * channels, bytes_accessed=12 * taps * channels, transcendentals=0
        ),
        compiler_params=pltpu.CompilerParams(vmem_limit_bytes=GATES_VMEM),
    )(after, q, k, v, ct)


def masks_kernel(taps, starts_ref, after_ref, keep_ref):
    del after_ref
    here = lax.axis_index("ctx")
    for side in range(2):
        found = (here + side) % lax.axis_size("ctx") == 0
        for d in range(starts_ref.shape[0]):
            found = jnp.logical_or(found, starts_ref[d] == (here + side) * taps)
        keep = jnp.where(found, 0.0, 1.0)
        keep_ref[side] = jnp.full(keep_ref.shape[1:], keep).astype(jnp.bfloat16)


def masks(starts, after):
    return pl.pallas_call(
        functools.partial(masks_kernel, after.shape[0]),
        in_specs=[SMEM, pl.BlockSpec(memory_space=pl.ANY)],
        out_specs=VMEM,
        out_shape=jax.ShapeDtypeStruct((2, 16, LANES), jnp.bfloat16),
        name="masks",
        compiler_params=pltpu.CompilerParams(vmem_limit_bytes=MIB),
    )(starts, after)


def toeplitz_kernel(filters_ref, after_ref, out_ref, done_ref):
    del after_ref
    count, taps = filters_ref.shape
    lines = filters_ref[...].astype(jnp.float32)
    current = iota((taps, taps), 0) <= iota((taps, taps), 1)
    for f in range(count):
        tile = jnp.broadcast_to(lines[f : f + 1], (taps, taps))
        tile = pltpu.roll(tile, 0, 1, stride=1, stride_axis=0)
        out_ref[f, :taps] = jnp.where(current, 0.0, tile).astype(jnp.bfloat16)
        out_ref[f, taps:] = jnp.where(current, tile, 0.0).astype(jnp.bfloat16)
    done_ref[...] = jnp.zeros_like(done_ref)


def toeplitz(filters, after):
    count, taps = filters.shape
    return pl.pallas_call(
        toeplitz_kernel,
        in_specs=[VMEM, pl.BlockSpec(memory_space=pl.ANY)],
        out_specs=[VMEM] * 2,
        out_shape=[
            jax.ShapeDtypeStruct((count, 2 * taps, taps), jnp.bfloat16),
            jax.ShapeDtypeStruct((8, LANES), jnp.float32),
        ],
        name="toeplitz",
        cost_estimate=pl.CostEstimate(
            flops=count * taps * taps * 64, bytes_accessed=4 * count * taps * taps, transcendentals=0
        ),
        compiler_params=pltpu.CompilerParams(vmem_limit_bytes=8 * MIB),
    )(filters, after)


def filter_grad_kernel(
    width, near_ref, own_ref, keep_ref, near_in_ref, extra_ref, far_in_ref, after_ref, out_ref, lines
):
    del after_ref
    taps, half = far_in_ref.shape
    per_group = LANES // width
    odd = lax.axis_index("ctx") % 2
    keep_far = keep_ref[odd]
    keep_near = keep_ref[1 - odd]
    lane_filter = iota((ROW_BLOCK, LANES), 1) // width
    fold = iota((ROW_BLOCK, taps), 1) + iota((ROW_BLOCK, taps), 0) < ROW_BLOCK
    for group in range(half // LANES):
        at = group * LANES
        cols = pl.ds(at, LANES)
        near = near_ref[:, cols]
        pairs = (
            (own_ref[:, cols], masked(far_in_ref[:, cols], keep_far), near),
            (near_in_ref[:, cols], masked(near, keep_near), extra_ref[:, cols]),
        )
        left, right = [], []
        for moving, beyond, fixed in pairs:
            window = jnp.concatenate([beyond, fixed], axis=0)
            for start in range(0, taps, ROW_BLOCK):
                piece = moving[start : start + ROW_BLOCK]
                left.append(
                    jnp.concatenate(
                        [jnp.where(lane_filter == i, piece, 0) for i in range(per_group)], axis=0
                    )
                )
                right.append(window[taps - ROW_BLOCK - start : 2 * taps - start])
        product = lax.dot_general(
            jnp.concatenate(left, axis=1),
            jnp.concatenate(right, axis=1),
            (((1,), (1,)), ((), ())),
            preferred_element_type=jnp.float32,
        )
        rows = []
        for i in range(per_group):
            tile = product[i * ROW_BLOCK : (i + 1) * ROW_BLOCK]
            high = jnp.concatenate(
                [tile[:, taps:], jnp.zeros((ROW_BLOCK, taps - ROW_BLOCK), jnp.float32)], axis=1
            )
            tile = jnp.where(fold, high, tile[:, :taps])
            tile = pltpu.roll(tile, taps - ROW_BLOCK + 1, 1, stride=1, stride_axis=0)
            rows.append(jnp.sum(tile, axis=0, keepdims=True))
        lines[group * per_group : (group + 1) * per_group] = jnp.concatenate(rows, axis=0)
    flip = jnp.where((iota((taps, taps), 0) + iota((taps, taps), 1)) % taps == 0, 1.0, 0.0)
    out_ref[...] = jnp.dot(
        lines[...], flip, preferred_element_type=jnp.float32, precision=lax.Precision.HIGHEST
    )


def filter_gradient(near, own, keep, near_in, extra, far_in, after, width):
    taps, half = own.shape
    count = half // width
    return pl.pallas_call(
        functools.partial(filter_grad_kernel, width),
        in_specs=[VMEM] * 6 + [pl.BlockSpec(memory_space=pl.ANY)],
        out_specs=VMEM,
        out_shape=jax.ShapeDtypeStruct((count, taps), jnp.float32),
        scratch_shapes=[pltpu.VMEM((count, taps), jnp.float32)],
        name="filter_gradient",
        cost_estimate=pl.CostEstimate(
            flops=4 * count * taps * taps * 256, bytes_accessed=16 * taps * half, transcendentals=0
        ),
        compiler_params=pltpu.CompilerParams(vmem_limit_bytes=8 * MIB),
    )(near, own, keep, near_in, extra, far_in, after)


def outputs_kernel(
    width, base, q_ref, k_ref, v_ref, ct_ref, tiles_ref, near_ref, far_ref, keep_ref,
    near_in_ref, far_in_ref, *rest,
):
    *results, sems = rest[-5:]
    *targets, done_ref = rest[-10:-5]
    out, grad_q, grad_k, grad_v = results
    taps, half = far_ref.shape
    channels = out.shape[1]
    per_group = LANES // width
    odd = lax.axis_index("ctx") % 2
    keep_far = keep_ref[odd]
    keep_near = keep_ref[1 - odd]
    second = odd if base < half else 1 - odd
    base = base % half
    first = pl.multiple_of(second * half, half)
    reverse = reversal(taps)
    copies = []

    def send(which, at, sem):
        own = pl.ds(at, CHUNK)
        cols = pl.ds(pl.multiple_of(first + base + at, CHUNK), CHUNK)
        copy = pltpu.make_async_copy(results[which].at[:, own], targets[which].at[:, cols], sem)
        copy.start()
        copies.append(copy)

    for chunk in range(0, channels, CHUNK):
        lines = []
        for lane in range(chunk, chunk + CHUNK, LANES):
            sent = pl.ds(base + lane, LANES)
            near_lines = jnp.concatenate(
                [masked(far_in_ref[:, sent], keep_far).T, near_ref[:, sent].T], axis=1
            )
            far_lines = jnp.concatenate(
                [masked(near_in_ref[:, sent], keep_near).T, far_ref[:, sent].T], axis=1
            )
            lines.append((lane, near_lines, far_lines))
        sums = []
        for lane, near_lines, far_lines in lines:
            at = (first + base + lane) // width
            near_parts, far_parts = [], []
            for i in range(per_group):
                rows = slice(i * width, (i + 1) * width)
                both = jnp.concatenate([near_lines[rows], far_lines[rows]], axis=0)
                part = jnp.dot(both, tiles_ref[at + i], preferred_element_type=jnp.float32)
                near_parts.append(part[:width])
                far_parts.append(part[width:])
            near_sum = jnp.concatenate(near_parts, axis=0)
            far_sum = jnp.concatenate(far_parts, axis=0)
            y = jnp.where(odd == 1, far_sum, near_sum).T
            mixed = jnp.where(odd == 1, near_sum, far_sum).T
            sums.append((lane, y, mixed))
        whole = pl.ds(pl.multiple_of(first + base + chunk, CHUNK), CHUNK)
        k_turned = flipped(reverse, k_ref[:, whole])
        v_turned = flipped(reverse, v_ref[:, whole])
        k_parts, v_parts = [], []
        for lane, y, mixed in sums:
            own = pl.ds(lane, LANES)
            cols = pl.ds(pl.multiple_of(first + base + lane, LANES), LANES)
            out[:, own] = (q_ref[:, cols].astype(jnp.float32) * y).astype(jnp.bfloat16)
            grad_q[:, own] = (ct_ref[:, cols].astype(jnp.float32) * y).astype(jnp.bfloat16)
            lanes = slice(lane - chunk, lane - chunk + LANES)
            k_parts.append((mixed * v_turned[:, lanes]).astype(jnp.bfloat16))
            v_parts.append((mixed * k_turned[:, lanes]).astype(jnp.bfloat16))
        own = pl.ds(chunk, CHUNK)
        turn = chunk // CHUNK
        send(0, chunk, sems.at[turn, 0])
        send(1, chunk, sems.at[turn, 1])
        grad_k[:, own] = flipped(reverse, jnp.concatenate(k_parts, axis=1)).astype(jnp.bfloat16)
        send(2, chunk, sems.at[turn, 2])
        grad_v[:, own] = flipped(reverse, jnp.concatenate(v_parts, axis=1)).astype(jnp.bfloat16)
        send(3, chunk, sems.at[turn, 3])
    for copy in copies:
        copy.wait()
    done_ref[...] = jnp.zeros_like(done_ref)


def outputs(piece, operands, results, after, width):
    taps, channels = operands[0].shape
    part = channels // PIECES
    anywhere = pl.BlockSpec(memory_space=pl.ANY)
    shape = jax.ShapeDtypeStruct((taps, channels), jnp.bfloat16)
    *results, done = pl.pallas_call(
        functools.partial(outputs_kernel, width, piece * part),
        in_specs=[VMEM] * len(operands) + [anywhere] * (1 + len(results)),
        out_specs=[anywhere] * 4 + [VMEM],
        out_shape=[shape] * 4 + [jax.ShapeDtypeStruct((8, LANES), jnp.float32)],
        input_output_aliases={len(operands) + 1 + i: i for i in range(len(results))},
        scratch_shapes=[pltpu.VMEM((taps, part), jnp.bfloat16)] * 4
        + [pltpu.SemaphoreType.DMA((part // CHUNK, 4))],
        name=f"outputs_{piece}",
        cost_estimate=pl.CostEstimate(
            flops=16 * (part // width) * taps * taps * 256,
            bytes_accessed=24 * taps * part,
            transcendentals=0,
        ),
        compiler_params=pltpu.CompilerParams(vmem_limit_bytes=8 * MIB),
    )(*operands, after, *results)
    return results, done


def per_device(gate_in, key_in, value_in, cotangent, doc_starts, filters):
    taps = filters.shape[1]
    width = gate_in.shape[2] // filters.shape[0]
    assert gate_in.shape[1] == taps
    q, k, v, ct = gate_in[0], key_in[0], value_in[0], cotangent[0]
    other = first_gate(q, k, v, ct)
    other_in = exchange(other, 1)
    q, k, v, ct, near_own, near_other, own = gates(other, q, k, v, ct)
    near_in_own = exchange(near_other, 0)
    extra = exchange(other, 0)
    own_in = exchange(own, 1)
    near_in_other = exchange(near_own, 0)
    keep = masks(doc_starts[0], near_other)
    mine = filter_gradient(near_own, own, keep, near_in_own, extra, other_in, near_in_other, width)
    halves = (
        (near_own, own, keep, near_in_own, other_in),
        (near_other, other, keep, near_in_other, own_in),
    )
    tiles = None
    results = []

    def beside(after, turn):
        nonlocal tiles, results
        if turn == 0:
            tiles, after = toeplitz(filters, after)
        elif turn <= PIECES:
            operands = (q, k, v, ct, tiles, *halves[turn - 1])
            results, after = outputs(turn - 1, operands, results, after, width)
        return after

    mine = sum_devices(mine, beside)
    filter_grad = join(mine, exchange(mine, 0))
    return tuple(array[None] for array in results) + (filter_grad,)


def solution(mesh):
    split = P("dp", "ctx", None)
    return jax.shard_map(
        per_device,
        mesh=mesh,
        in_specs=(split, split, split, split, P("dp", None), P()),
        out_specs=(split, split, split, split, P()),
        check_vma=False,
    )
```

```python
import functools

import jax
import jax.numpy as jnp
from jax import lax
from jax.experimental import pallas as pl
from jax.experimental.pallas import tpu as pltpu
from jax.sharding import PartitionSpec as P

LANES = 128
ROW_BLOCK = 32
MIB = 1024 * 1024
CHUNKS = 4
FIRST_CHUNKS = 2
PIECES = 2
CHUNK = 512
FIRST_VMEM = 213 * MIB // 4
GATES_VMEM = 101 * MIB // 2
VMEM = pl.BlockSpec(memory_space=pltpu.VMEM)
SMEM = pl.BlockSpec(memory_space=pltpu.SMEM)


def iota(shape, dim):
    return lax.broadcasted_iota(jnp.int32, shape, dim)


def exchange(array, first):
    seqs, blocks = lax.axis_size("dp"), lax.axis_size("ctx")
    pairs = []
    for seq in range(seqs):
        for block in range(blocks):
            to_seq, to_block = seq, (block - first ^ 1) + first
            if not 0 <= to_block < blocks:
                to_seq, to_block = seq ^ 1, block
            pairs.append((seq * blocks + block, to_seq * blocks + to_block))
    return lax.ppermute(array, ("dp", "ctx"), pairs)


def swapped(array, seq_bits, block_bits):
    seqs, blocks = lax.axis_size("dp"), lax.axis_size("ctx")
    pairs = [
        (seq * blocks + block, (seq ^ seq_bits) * blocks + (block ^ block_bits))
        for seq in range(seqs)
        for block in range(blocks)
    ]
    return lax.ppermute(array, ("dp", "ctx"), pairs)


def add_kernel(*refs):
    *terms, _, out_ref = [ref for ref in refs]
    terms = [term[...] for term in terms]
    while len(terms) > 1:
        terms = [sum(terms[i + 1 : i + 2], terms[i]) for i in range(0, len(terms), 2)]
    out_ref[...] = terms[0]


def add(terms, after):
    return pl.pallas_call(
        add_kernel,
        in_specs=[VMEM] * len(terms) + [pl.BlockSpec(memory_space=pl.ANY)],
        out_specs=VMEM,
        out_shape=jax.ShapeDtypeStruct(terms[0].shape, terms[0].dtype),
        name="add",
        compiler_params=pltpu.CompilerParams(vmem_limit_bytes=MIB),
    )(*terms, after)


def sum_devices(mine, beside):
    def bits(axis, first):
        return [1 << i for i in range(first, lax.axis_size(axis).bit_length() - 1)]

    seq_bits = [(bit, 0) for bit in bits("dp", 0)]
    block_bits = [(0, bit) for bit in bits("ctx", 1)]
    together = min(len(seq_bits), len(block_bits))
    stages = list(zip(seq_bits, block_bits))
    rest = seq_bits[together:] + block_bits[together:]
    stages += [rest[i : i + 2] for i in range(0, len(rest), 2)]
    for turn, stage in enumerate(stages):
        moves = list(stage)
        if len(moves) == 2:
            moves.append((moves[0][0] | moves[1][0], moves[0][1] | moves[1][1]))
        others = [swapped(mine, *move) for move in moves]
        mine = add([mine] + others, beside(mine, turn))
    return mine


def join_kernel(mine_ref, other_ref, out_ref):
    count = mine_ref.shape[0]
    odd = lax.axis_index("ctx") % 2
    out_ref[pl.ds(pl.multiple_of(odd * count, count), count)] = mine_ref[...]
    out_ref[pl.ds(pl.multiple_of((1 - odd) * count, count), count)] = other_ref[...]


def join(mine, other):
    count, taps = mine.shape
    return pl.pallas_call(
        join_kernel,
        in_specs=[VMEM] * 2,
        out_specs=VMEM,
        out_shape=jax.ShapeDtypeStruct((2 * count, taps), mine.dtype),
        name="join",
        compiler_params=pltpu.CompilerParams(vmem_limit_bytes=MIB),
    )(mine, other)


def reversal(taps):
    flip = iota((taps, taps), 0) + iota((taps, taps), 1) == taps - 1
    return jnp.where(flip, 1.0, 0.0).astype(jnp.bfloat16)


def flipped(reverse, array):
    return jnp.dot(reverse, array, preferred_element_type=jnp.float32)


def masked(array, keep):
    return array * jnp.concatenate([keep] * (array.shape[0] // keep.shape[0]), axis=0)


def bf16_product(one, two):
    return (one.astype(jnp.float32) * two.astype(jnp.float32)).astype(jnp.bfloat16)


def first_kernel(q_hbm, k_hbm, v_hbm, ct_hbm, other_ref, held, sems):
    taps, half = other_ref.shape
    block = half // FIRST_CHUNKS
    odd = lax.axis_index("ctx") % 2 == 1
    reverse = reversal(taps)

    def make(sources, start, finish):
        copies = []
        for c in range(FIRST_CHUNKS):
            for a, source in enumerate(sources):
                copy = pltpu.make_async_copy(
                    source.at[:, pl.ds(start + c * block, block)],
                    held.at[a, :, pl.ds(c * block, block)],
                    sems.at[c, a],
                )
                copy.start()
                copies.append(copy)
        for copy in copies:
            copy.wait()
        other_ref[...] = finish(bf16_product(held[0], held[1]))

    @pl.when(odd)
    def _():
        make((k_hbm, v_hbm), 0, lambda u: u)

    @pl.when(jnp.logical_not(odd))
    def _():
        make((ct_hbm, q_hbm), half, lambda dy: flipped(reverse, dy).astype(jnp.bfloat16))


def first_gate(q, k, v, ct):
    taps, channels = q.shape
    half = channels // 2
    return pl.pallas_call(
        first_kernel,
        in_specs=[pl.BlockSpec(memory_space=pltpu.HBM)] * 4,
        out_specs=VMEM,
        out_shape=jax.ShapeDtypeStruct((taps, half), jnp.bfloat16),
        scratch_shapes=[
            pltpu.VMEM((2, taps, half), jnp.bfloat16),
            pltpu.SemaphoreType.DMA((FIRST_CHUNKS, 2)),
        ],
        name="first_gate",
        cost_estimate=pl.CostEstimate(
            flops=taps * taps * channels, bytes_accessed=3 * taps * channels, transcendentals=0
        ),
        compiler_params=pltpu.CompilerParams(vmem_limit_bytes=FIRST_VMEM),
    )(q, k, v, ct)


def gates_kernel(
    after_ref, q_hbm, k_hbm, v_hbm, ct_hbm,
    q_ref, k_ref, v_ref, ct_ref, near_own_ref, near_other_ref, own_ref, sems,
):
    del after_ref
    taps, channels = q_ref.shape
    half = channels // 2
    block = channels // CHUNKS
    pairs = ((k_hbm, k_ref), (v_hbm, v_ref), (q_hbm, q_ref), (ct_hbm, ct_ref))
    copies = []
    for c in range(CHUNKS):
        cols = pl.ds(c * block, block)
        for a, (source, target) in enumerate(pairs):
            copy = pltpu.make_async_copy(source.at[:, cols], target.at[:, cols], sems.at[c, a])
            copy.start()
            copies.append(copy)
    odd = lax.axis_index("ctx") % 2 == 1
    reverse = reversal(taps)
    for c in range(CHUNKS):
        cols = pl.ds(c * block, block)
        sent = pl.ds(c * block % half, block)
        for copy in copies[4 * c : 4 * c + 4]:
            copy.wait()

        def make_u():
            return bf16_product(k_ref[:, cols], v_ref[:, cols])

        def make_dy():
            dy = bf16_product(ct_ref[:, cols], q_ref[:, cols])
            return flipped(reverse, dy).astype(jnp.bfloat16)

        @pl.when(odd)
        def _():
            near_ref = near_own_ref if c * block >= half else near_other_ref
            near_ref[:, sent] = make_dy()
            if c * block >= half:
                own_ref[:, sent] = make_u()

        @pl.when(jnp.logical_not(odd))
        def _():
            near_ref = near_own_ref if c * block < half else near_other_ref
            near_ref[:, sent] = make_u()
            if c * block < half:
                own_ref[:, sent] = make_dy()


def gates(after, q, k, v, ct):
    taps, channels = q.shape

    def shape(*dims):
        return jax.ShapeDtypeStruct(dims, jnp.bfloat16)

    half = channels // 2
    return pl.pallas_call(
        gates_kernel,
        in_specs=[pl.BlockSpec(memory_space=pl.ANY)]
        + [pl.BlockSpec(memory_space=pltpu.HBM)] * 4,
        out_specs=[VMEM] * 7,
        out_shape=[shape(taps, channels)] * 4 + [shape(taps, half)] * 3,
        scratch_shapes=[pltpu.SemaphoreType.DMA((CHUNKS, 4))],
        name="gates",
        cost_estimate=pl.CostEstimate(
            flops=2 * taps * taps * channels, bytes_accessed=12 * taps * channels, transcendentals=0
        ),
        compiler_params=pltpu.CompilerParams(vmem_limit_bytes=GATES_VMEM),
    )(after, q, k, v, ct)


def masks_kernel(taps, starts_ref, after_ref, keep_ref):
    del after_ref
    here = lax.axis_index("ctx")
    for side in range(2):
        found = (here + side) % lax.axis_size("ctx") == 0
        for d in range(starts_ref.shape[0]):
            found = jnp.logical_or(found, starts_ref[d] == (here + side) * taps)
        keep = jnp.where(found, 0.0, 1.0)
        keep_ref[side] = jnp.full(keep_ref.shape[1:], keep).astype(jnp.bfloat16)


def masks(starts, after):
    return pl.pallas_call(
        functools.partial(masks_kernel, after.shape[0]),
        in_specs=[SMEM, pl.BlockSpec(memory_space=pl.ANY)],
        out_specs=VMEM,
        out_shape=jax.ShapeDtypeStruct((2, 16, LANES), jnp.bfloat16),
        name="masks",
        compiler_params=pltpu.CompilerParams(vmem_limit_bytes=MIB),
    )(starts, after)


def toeplitz_kernel(filters_ref, after_ref, through_in_ref, out_ref, done_ref, through_ref):
    del after_ref, through_in_ref, through_ref
    count, taps = filters_ref.shape
    lines = filters_ref[...].astype(jnp.float32)
    current = iota((taps, taps), 0) <= iota((taps, taps), 1)
    for f in range(count):
        tile = jnp.broadcast_to(lines[f : f + 1], (taps, taps))
        tile = pltpu.roll(tile, 0, 1, stride=1, stride_axis=0)
        out_ref[f, :taps] = jnp.where(current, 0.0, tile).astype(jnp.bfloat16)
        out_ref[f, taps:] = jnp.where(current, tile, 0.0).astype(jnp.bfloat16)
    done_ref[...] = jnp.zeros_like(done_ref)


def toeplitz(filters, after, through):
    count, taps = filters.shape
    anywhere = pl.BlockSpec(memory_space=pl.ANY)
    return pl.pallas_call(
        toeplitz_kernel,
        in_specs=[VMEM, anywhere, anywhere],
        out_specs=[VMEM, VMEM, anywhere],
        out_shape=[
            jax.ShapeDtypeStruct((count, 2 * taps, taps), jnp.bfloat16),
            jax.ShapeDtypeStruct((8, LANES), jnp.float32),
            jax.ShapeDtypeStruct(through.shape, through.dtype),
        ],
        input_output_aliases={2: 2},
        name="toeplitz",
        cost_estimate=pl.CostEstimate(
            flops=count * taps * taps * 64, bytes_accessed=4 * count * taps * taps, transcendentals=0
        ),
        compiler_params=pltpu.CompilerParams(vmem_limit_bytes=8 * MIB),
    )(filters, after, through)


def filter_grad_kernel(
    width, near_ref, own_ref, keep_ref, near_in_ref, extra_ref, far_in_ref, after_ref, out_ref, lines
):
    del after_ref
    taps, half = far_in_ref.shape
    per_group = LANES // width
    odd = lax.axis_index("ctx") % 2
    keep_far = keep_ref[odd]
    keep_near = keep_ref[1 - odd]
    lane_filter = iota((ROW_BLOCK, LANES), 1) // width
    fold = iota((ROW_BLOCK, taps), 1) + iota((ROW_BLOCK, taps), 0) < ROW_BLOCK
    for group in range(half // LANES):
        at = group * LANES
        cols = pl.ds(at, LANES)
        near = near_ref[:, cols]
        pairs = (
            (own_ref[:, cols], masked(far_in_ref[:, cols], keep_far), near),
            (near_in_ref[:, cols], masked(near, keep_near), extra_ref[:, cols]),
        )
        left, right = [], []
        for moving, beyond, fixed in pairs:
            window = jnp.concatenate([beyond, fixed], axis=0)
            for start in range(0, taps, ROW_BLOCK):
                piece = moving[start : start + ROW_BLOCK]
                left.append(
                    jnp.concatenate(
                        [jnp.where(lane_filter == i, piece, 0) for i in range(per_group)], axis=0
                    )
                )
                right.append(window[taps - ROW_BLOCK - start : 2 * taps - start])
        product = lax.dot_general(
            jnp.concatenate(left, axis=1),
            jnp.concatenate(right, axis=1),
            (((1,), (1,)), ((), ())),
            preferred_element_type=jnp.float32,
        )
        rows = []
        for i in range(per_group):
            tile = product[i * ROW_BLOCK : (i + 1) * ROW_BLOCK]
            high = jnp.concatenate(
                [tile[:, taps:], jnp.zeros((ROW_BLOCK, taps - ROW_BLOCK), jnp.float32)], axis=1
            )
            tile = jnp.where(fold, high, tile[:, :taps])
            tile = pltpu.roll(tile, taps - ROW_BLOCK + 1, 1, stride=1, stride_axis=0)
            rows.append(jnp.sum(tile, axis=0, keepdims=True))
        lines[group * per_group : (group + 1) * per_group] = jnp.concatenate(rows, axis=0)
    flip = jnp.where((iota((taps, taps), 0) + iota((taps, taps), 1)) % taps == 0, 1.0, 0.0)
    out_ref[...] = jnp.dot(
        lines[...], flip, preferred_element_type=jnp.float32, precision=lax.Precision.HIGHEST
    )


def filter_gradient(near, own, keep, near_in, extra, far_in, after, width):
    taps, half = own.shape
    count = half // width
    return pl.pallas_call(
        functools.partial(filter_grad_kernel, width),
        in_specs=[VMEM] * 6 + [pl.BlockSpec(memory_space=pl.ANY)],
        out_specs=VMEM,
        out_shape=jax.ShapeDtypeStruct((count, taps), jnp.float32),
        scratch_shapes=[pltpu.VMEM((count, taps), jnp.float32)],
        name="filter_gradient",
        cost_estimate=pl.CostEstimate(
            flops=4 * count * taps * taps * 256, bytes_accessed=16 * taps * half, transcendentals=0
        ),
        compiler_params=pltpu.CompilerParams(vmem_limit_bytes=8 * MIB),
    )(near, own, keep, near_in, extra, far_in, after)


def outputs_kernel(
    width, base, q_ref, k_ref, v_ref, ct_ref, tiles_ref, near_ref, far_ref, keep_ref,
    near_in_ref, far_in_ref, *rest,
):
    *results, sems = rest[-5:]
    *targets, done_ref = rest[-10:-5]
    out, grad_q, grad_k, grad_v = results
    taps, half = far_ref.shape
    channels = out.shape[1]
    per_group = LANES // width
    odd = lax.axis_index("ctx") % 2
    keep_far = keep_ref[odd]
    keep_near = keep_ref[1 - odd]
    second = odd if base < half else 1 - odd
    base = base % half
    first = pl.multiple_of(second * half, half)
    reverse = reversal(taps)
    copies = []

    def send(which, at, sem):
        own = pl.ds(at, CHUNK)
        cols = pl.ds(pl.multiple_of(first + base + at, CHUNK), CHUNK)
        copy = pltpu.make_async_copy(results[which].at[:, own], targets[which].at[:, cols], sem)
        copy.start()
        copies.append(copy)

    for chunk in range(0, channels, CHUNK):
        lines = []
        for lane in range(chunk, chunk + CHUNK, LANES):
            sent = pl.ds(base + lane, LANES)
            near_lines = jnp.concatenate(
                [masked(far_in_ref[:, sent], keep_far).T, near_ref[:, sent].T], axis=1
            )
            far_lines = jnp.concatenate(
                [masked(near_in_ref[:, sent], keep_near).T, far_ref[:, sent].T], axis=1
            )
            lines.append((lane, near_lines, far_lines))
        sums = []
        for lane, near_lines, far_lines in lines:
            at = (first + base + lane) // width
            near_parts, far_parts = [], []
            for i in range(per_group):
                rows = slice(i * width, (i + 1) * width)
                both = jnp.concatenate([near_lines[rows], far_lines[rows]], axis=0)
                part = jnp.dot(both, tiles_ref[at + i], preferred_element_type=jnp.float32)
                near_parts.append(part[:width])
                far_parts.append(part[width:])
            near_sum = jnp.concatenate(near_parts, axis=0)
            far_sum = jnp.concatenate(far_parts, axis=0)
            y = jnp.where(odd == 1, far_sum, near_sum).T
            mixed = jnp.where(odd == 1, near_sum, far_sum).T
            sums.append((lane, y, mixed))
        whole = pl.ds(pl.multiple_of(first + base + chunk, CHUNK), CHUNK)
        k_turned = flipped(reverse, k_ref[:, whole])
        v_turned = flipped(reverse, v_ref[:, whole])
        k_parts, v_parts = [], []
        for lane, y, mixed in sums:
            own = pl.ds(lane, LANES)
            cols = pl.ds(pl.multiple_of(first + base + lane, LANES), LANES)
            out[:, own] = (q_ref[:, cols].astype(jnp.float32) * y).astype(jnp.bfloat16)
            grad_q[:, own] = (ct_ref[:, cols].astype(jnp.float32) * y).astype(jnp.bfloat16)
            lanes = slice(lane - chunk, lane - chunk + LANES)
            k_parts.append((mixed * v_turned[:, lanes]).astype(jnp.bfloat16))
            v_parts.append((mixed * k_turned[:, lanes]).astype(jnp.bfloat16))
        own = pl.ds(chunk, CHUNK)
        turn = chunk // CHUNK
        send(0, chunk, sems.at[turn, 0])
        send(1, chunk, sems.at[turn, 1])
        grad_k[:, own] = flipped(reverse, jnp.concatenate(k_parts, axis=1)).astype(jnp.bfloat16)
        send(2, chunk, sems.at[turn, 2])
        grad_v[:, own] = flipped(reverse, jnp.concatenate(v_parts, axis=1)).astype(jnp.bfloat16)
        send(3, chunk, sems.at[turn, 3])
    for copy in copies:
        copy.wait()
    done_ref[...] = jnp.zeros_like(done_ref)


def outputs(piece, operands, results, after, width):
    taps, channels = operands[0].shape
    part = channels // PIECES
    anywhere = pl.BlockSpec(memory_space=pl.ANY)
    shape = jax.ShapeDtypeStruct((taps, channels), jnp.bfloat16)
    *results, done = pl.pallas_call(
        functools.partial(outputs_kernel, width, piece * part),
        in_specs=[VMEM] * len(operands) + [anywhere] * (1 + len(results)),
        out_specs=[anywhere] * 4 + [VMEM],
        out_shape=[shape] * 4 + [jax.ShapeDtypeStruct((8, LANES), jnp.float32)],
        input_output_aliases={len(operands) + 1 + i: i for i in range(len(results))},
        scratch_shapes=[pltpu.VMEM((taps, part), jnp.bfloat16)] * 4
        + [pltpu.SemaphoreType.DMA((part // CHUNK, 4))],
        name=f"outputs_{piece}",
        cost_estimate=pl.CostEstimate(
            flops=16 * (part // width) * taps * taps * 256,
            bytes_accessed=24 * taps * part,
            transcendentals=0,
        ),
        compiler_params=pltpu.CompilerParams(vmem_limit_bytes=8 * MIB),
    )(*operands, after, *results)
    return results, done


def per_device(gate_in, key_in, value_in, cotangent, doc_starts, filters):
    taps = filters.shape[1]
    width = gate_in.shape[2] // filters.shape[0]
    assert gate_in.shape[1] == taps
    q, k, v, ct = gate_in[0], key_in[0], value_in[0], cotangent[0]
    other = first_gate(q, k, v, ct)
    other_in = exchange(other, 1)
    q, k, v, ct, near_own, near_other, own = gates(other, q, k, v, ct)
    near_in_own = exchange(near_other, 0)
    extra = exchange(other, 0)
    near_in_other = exchange(near_own, 0)
    keep = masks(doc_starts[0], near_other)
    mine = filter_gradient(near_own, own, keep, near_in_own, extra, other_in, near_in_other, width)
    tiles, halves, results = None, None, []

    def beside(after, turn):
        nonlocal tiles, halves, results
        if turn == 0:
            tiles, after, sent = toeplitz(filters, after, own)
            own_in = exchange(sent, 1)
            halves = (
                (near_own, sent, keep, near_in_own, other_in),
                (near_other, other, keep, near_in_other, own_in),
            )
        if turn < PIECES:
            operands = (q, k, v, ct, tiles, *halves[turn])
            results, after = outputs(turn, operands, results, after, width)
        return after

    mine = sum_devices(mine, beside)
    filter_grad = join(mine, exchange(mine, 0))
    return tuple(array[None] for array in results) + (filter_grad,)


def solution(mesh):
    split = P("dp", "ctx", None)
    return jax.shard_map(
        per_device,
        mesh=mesh,
        in_specs=(split, split, split, split, P("dp", None), P()),
        out_specs=(split, split, split, split, P()),
        check_vma=False,
    )
```

```python
import functools

import jax
import jax.numpy as jnp
from jax import lax
from jax.experimental import pallas as pl
from jax.experimental.pallas import tpu as pltpu
from jax.sharding import PartitionSpec as P

LANES = 128
ROW_BLOCK = 32
MIB = 1024 * 1024
CHUNKS = 4
PIECES = 2
CHUNK = 512
FIRST_VMEM = 213 * MIB // 4
GATES_VMEM = 101 * MIB // 2
VMEM = pl.BlockSpec(memory_space=pltpu.VMEM)
SMEM = pl.BlockSpec(memory_space=pltpu.SMEM)


def iota(shape, dim):
    return lax.broadcasted_iota(jnp.int32, shape, dim)


def exchange(array, first):
    seqs, blocks = lax.axis_size("dp"), lax.axis_size("ctx")
    pairs = []
    for seq in range(seqs):
        for block in range(blocks):
            to_seq, to_block = seq, (block - first ^ 1) + first
            if not 0 <= to_block < blocks:
                to_seq, to_block = seq ^ 1, block
            pairs.append((seq * blocks + block, to_seq * blocks + to_block))
    return lax.ppermute(array, ("dp", "ctx"), pairs)


def swapped(array, axis, step):
    size = lax.axis_size(axis)
    return lax.ppermute(array, axis, [(i, i ^ step) for i in range(size)])


def swapped(array, axis, step):
    size = lax.axis_size(axis)
    return lax.ppermute(array, axis, [(i, i ^ step) for i in range(size)])


def along(array, axis):
    size = lax.axis_size(axis)
    pairs = [(i, i + 2 if i % 2 else i - 2) for i in range(size)]
    return lax.ppermute(array, axis, [(i, j) for i, j in pairs if 0 <= j < size])


def add_kernel(*refs):
    *terms, _, out_ref = [ref for ref in refs]
    terms = [term[...] for term in terms]
    while len(terms) > 1:
        terms = [sum(terms[i + 1 : i + 2], terms[i]) for i in range(0, len(terms), 2)]
    out_ref[...] = terms[0]


def add(terms, after):
    return pl.pallas_call(
        add_kernel,
        in_specs=[VMEM] * len(terms) + [pl.BlockSpec(memory_space=pl.ANY)],
        out_specs=VMEM,
        out_shape=jax.ShapeDtypeStruct(terms[0].shape, terms[0].dtype),
        name="add",
        compiler_params=pltpu.CompilerParams(vmem_limit_bytes=MIB),
    )(*terms, after)


def sum_devices(mine, beside):
    turn = 0
    for axis, step in (("ctx", 2), ("dp", 1)):
        size = lax.axis_size(axis)
        while step < size:
            count = 4 if axis == "dp" and 4 * step <= size else 2
            others = [swapped(mine, axis, step * i) for i in range(1, count)]
            mine = add([mine] + others, beside(mine, turn))
            step, turn = count * step, turn + 1
    return mine


def join_kernel(mine_ref, other_ref, out_ref):
    count = mine_ref.shape[0]
    odd = lax.axis_index("ctx") % 2
    out_ref[pl.ds(pl.multiple_of(odd * count, count), count)] = mine_ref[...]
    out_ref[pl.ds(pl.multiple_of((1 - odd) * count, count), count)] = other_ref[...]


def join(mine, other):
    count, taps = mine.shape
    return pl.pallas_call(
        join_kernel,
        in_specs=[VMEM] * 2,
        out_specs=VMEM,
        out_shape=jax.ShapeDtypeStruct((2 * count, taps), mine.dtype),
        name="join",
        compiler_params=pltpu.CompilerParams(vmem_limit_bytes=MIB),
    )(mine, other)


def reversal(taps):
    flip = iota((taps, taps), 0) + iota((taps, taps), 1) == taps - 1
    return jnp.where(flip, 1.0, 0.0).astype(jnp.bfloat16)


def flipped(reverse, array):
    return jnp.dot(reverse, array, preferred_element_type=jnp.float32)


def masked(array, keep):
    return array * jnp.concatenate([keep] * (array.shape[0] // keep.shape[0]), axis=0)


def bf16_product(one, two):
    return (one.astype(jnp.float32) * two.astype(jnp.float32)).astype(jnp.bfloat16)


def first_kernel(q_hbm, k_hbm, v_hbm, ct_hbm, other_ref, held, sems):
    taps, half = other_ref.shape
    block = half // CHUNKS
    odd = lax.axis_index("ctx") % 2 == 1
    reverse = reversal(taps)

    def make(sources, start, finish):
        copies = []
        for c in range(CHUNKS):
            for a, source in enumerate(sources):
                copy = pltpu.make_async_copy(
                    source.at[:, pl.ds(start + c * block, block)],
                    held.at[a, :, pl.ds(c * block, block)],
                    sems.at[c, a],
                )
                copy.start()
                copies.append(copy)
        for copy in copies:
            copy.wait()
        other_ref[...] = finish(bf16_product(held[0], held[1]))

    @pl.when(odd)
    def _():
        make((k_hbm, v_hbm), 0, lambda u: u)

    @pl.when(jnp.logical_not(odd))
    def _():
        make((ct_hbm, q_hbm), half, lambda dy: flipped(reverse, dy).astype(jnp.bfloat16))


def first_gate(q, k, v, ct):
    taps, channels = q.shape
    half = channels // 2
    return pl.pallas_call(
        first_kernel,
        in_specs=[pl.BlockSpec(memory_space=pltpu.HBM)] * 4,
        out_specs=VMEM,
        out_shape=jax.ShapeDtypeStruct((taps, half), jnp.bfloat16),
        scratch_shapes=[
            pltpu.VMEM((2, taps, half), jnp.bfloat16),
            pltpu.SemaphoreType.DMA((CHUNKS, 2)),
        ],
        name="first_gate",
        cost_estimate=pl.CostEstimate(
            flops=taps * taps * channels, bytes_accessed=3 * taps * channels, transcendentals=0
        ),
        compiler_params=pltpu.CompilerParams(vmem_limit_bytes=FIRST_VMEM),
    )(q, k, v, ct)


def gates_kernel(
    after_ref, q_hbm, k_hbm, v_hbm, ct_hbm,
    q_ref, k_ref, v_ref, ct_ref, near_own_ref, near_other_ref, own_ref, sems,
):
    del after_ref
    taps, channels = q_ref.shape
    half = channels // 2
    block = channels // CHUNKS
    pairs = ((k_hbm, k_ref), (v_hbm, v_ref), (q_hbm, q_ref), (ct_hbm, ct_ref))
    copies = []
    for c in range(CHUNKS):
        cols = pl.ds(c * block, block)
        for a, (source, target) in enumerate(pairs):
            copy = pltpu.make_async_copy(source.at[:, cols], target.at[:, cols], sems.at[c, a])
            copy.start()
            copies.append(copy)
    odd = lax.axis_index("ctx") % 2 == 1
    reverse = reversal(taps)
    for c in range(CHUNKS):
        cols = pl.ds(c * block, block)
        sent = pl.ds(c * block % half, block)
        for copy in copies[4 * c : 4 * c + 4]:
            copy.wait()

        def make_u():
            return bf16_product(k_ref[:, cols], v_ref[:, cols])

        def make_dy():
            dy = bf16_product(ct_ref[:, cols], q_ref[:, cols])
            return flipped(reverse, dy).astype(jnp.bfloat16)

        @pl.when(odd)
        def _():
            near_ref = near_own_ref if c * block >= half else near_other_ref
            near_ref[:, sent] = make_dy()
            if c * block >= half:
                own_ref[:, sent] = make_u()

        @pl.when(jnp.logical_not(odd))
        def _():
            near_ref = near_own_ref if c * block < half else near_other_ref
            near_ref[:, sent] = make_u()
            if c * block < half:
                own_ref[:, sent] = make_dy()


def gates(after, q, k, v, ct):
    taps, channels = q.shape

    def shape(*dims):
        return jax.ShapeDtypeStruct(dims, jnp.bfloat16)

    half = channels // 2
    return pl.pallas_call(
        gates_kernel,
        in_specs=[pl.BlockSpec(memory_space=pl.ANY)]
        + [pl.BlockSpec(memory_space=pltpu.HBM)] * 4,
        out_specs=[VMEM] * 7,
        out_shape=[shape(taps, channels)] * 4 + [shape(taps, half)] * 3,
        scratch_shapes=[pltpu.SemaphoreType.DMA((CHUNKS, 4))],
        name="gates",
        cost_estimate=pl.CostEstimate(
            flops=2 * taps * taps * channels, bytes_accessed=12 * taps * channels, transcendentals=0
        ),
        compiler_params=pltpu.CompilerParams(vmem_limit_bytes=GATES_VMEM),
    )(after, q, k, v, ct)


def masks_kernel(taps, starts_ref, after_ref, keep_ref):
    del after_ref
    here = lax.axis_index("ctx")
    for side in range(2):
        found = (here + side) % lax.axis_size("ctx") == 0
        for d in range(starts_ref.shape[0]):
            found = jnp.logical_or(found, starts_ref[d] == (here + side) * taps)
        keep = jnp.where(found, 0.0, 1.0)
        keep_ref[side] = jnp.full(keep_ref.shape[1:], keep).astype(jnp.bfloat16)


def masks(starts, after):
    return pl.pallas_call(
        functools.partial(masks_kernel, after.shape[0]),
        in_specs=[SMEM, pl.BlockSpec(memory_space=pl.ANY)],
        out_specs=VMEM,
        out_shape=jax.ShapeDtypeStruct((2, 16, LANES), jnp.bfloat16),
        name="masks",
        compiler_params=pltpu.CompilerParams(vmem_limit_bytes=MIB),
    )(starts, after)


def toeplitz_kernel(filters_ref, after_ref, out_ref, done_ref):
    del after_ref
    count, taps = filters_ref.shape
    lines = filters_ref[...].astype(jnp.float32)
    current = iota((taps, taps), 0) <= iota((taps, taps), 1)
    for f in range(count):
        tile = jnp.broadcast_to(lines[f : f + 1], (taps, taps))
        tile = pltpu.roll(tile, 0, 1, stride=1, stride_axis=0)
        out_ref[f, :taps] = jnp.where(current, 0.0, tile).astype(jnp.bfloat16)
        out_ref[f, taps:] = jnp.where(current, tile, 0.0).astype(jnp.bfloat16)
    done_ref[...] = jnp.zeros_like(done_ref)


def toeplitz(filters, after):
    count, taps = filters.shape
    return pl.pallas_call(
        toeplitz_kernel,
        in_specs=[VMEM, pl.BlockSpec(memory_space=pl.ANY)],
        out_specs=[VMEM] * 2,
        out_shape=[
            jax.ShapeDtypeStruct((count, 2 * taps, taps), jnp.bfloat16),
            jax.ShapeDtypeStruct((8, LANES), jnp.float32),
        ],
        name="toeplitz",
        cost_estimate=pl.CostEstimate(
            flops=count * taps * taps * 64, bytes_accessed=4 * count * taps * taps, transcendentals=0
        ),
        compiler_params=pltpu.CompilerParams(vmem_limit_bytes=8 * MIB),
    )(filters, after)


def filter_grad_kernel(
    width, near_ref, own_ref, keep_ref, near_in_ref, extra_ref, far_in_ref, after_ref, out_ref, lines
):
    del after_ref
    taps, half = far_in_ref.shape
    per_group = LANES // width
    odd = lax.axis_index("ctx") % 2
    keep_far = keep_ref[odd]
    keep_near = keep_ref[1 - odd]
    lane_filter = iota((ROW_BLOCK, LANES), 1) // width
    fold = iota((ROW_BLOCK, taps), 1) + iota((ROW_BLOCK, taps), 0) < ROW_BLOCK
    for group in range(half // LANES):
        at = group * LANES
        cols = pl.ds(at, LANES)
        near = near_ref[:, cols]
        pairs = (
            (own_ref[:, cols], masked(far_in_ref[:, cols], keep_far), near),
            (near_in_ref[:, cols], masked(near, keep_near), extra_ref[:, cols]),
        )
        left, right = [], []
        for moving, beyond, fixed in pairs:
            window = jnp.concatenate([beyond, fixed], axis=0)
            for start in range(0, taps, ROW_BLOCK):
                piece = moving[start : start + ROW_BLOCK]
                left.append(
                    jnp.concatenate(
                        [jnp.where(lane_filter == i, piece, 0) for i in range(per_group)], axis=0
                    )
                )
                right.append(window[taps - ROW_BLOCK - start : 2 * taps - start])
        product = lax.dot_general(
            jnp.concatenate(left, axis=1),
            jnp.concatenate(right, axis=1),
            (((1,), (1,)), ((), ())),
            preferred_element_type=jnp.float32,
        )
        rows = []
        for i in range(per_group):
            tile = product[i * ROW_BLOCK : (i + 1) * ROW_BLOCK]
            high = jnp.concatenate(
                [tile[:, taps:], jnp.zeros((ROW_BLOCK, taps - ROW_BLOCK), jnp.float32)], axis=1
            )
            tile = jnp.where(fold, high, tile[:, :taps])
            tile = pltpu.roll(tile, taps - ROW_BLOCK + 1, 1, stride=1, stride_axis=0)
            rows.append(jnp.sum(tile, axis=0, keepdims=True))
        lines[group * per_group : (group + 1) * per_group] = jnp.concatenate(rows, axis=0)
    flip = jnp.where((iota((taps, taps), 0) + iota((taps, taps), 1)) % taps == 0, 1.0, 0.0)
    out_ref[...] = jnp.dot(
        lines[...], flip, preferred_element_type=jnp.float32, precision=lax.Precision.HIGHEST
    )


def filter_gradient(near, own, keep, near_in, extra, far_in, after, width):
    taps, half = own.shape
    count = half // width
    return pl.pallas_call(
        functools.partial(filter_grad_kernel, width),
        in_specs=[VMEM] * 6 + [pl.BlockSpec(memory_space=pl.ANY)],
        out_specs=VMEM,
        out_shape=jax.ShapeDtypeStruct((count, taps), jnp.float32),
        scratch_shapes=[pltpu.VMEM((count, taps), jnp.float32)],
        name="filter_gradient",
        cost_estimate=pl.CostEstimate(
            flops=4 * count * taps * taps * 256, bytes_accessed=16 * taps * half, transcendentals=0
        ),
        compiler_params=pltpu.CompilerParams(vmem_limit_bytes=8 * MIB),
    )(near, own, keep, near_in, extra, far_in, after)


def outputs_kernel(
    width, base, q_ref, k_ref, v_ref, ct_ref, tiles_ref, near_ref, far_ref, keep_ref,
    near_in_ref, far_in_ref, *rest,
):
    *results, sems = rest[-5:]
    *targets, done_ref = rest[-10:-5]
    out, grad_q, grad_k, grad_v = results
    taps, half = far_ref.shape
    channels = out.shape[1]
    per_group = LANES // width
    odd = lax.axis_index("ctx") % 2
    keep_far = keep_ref[odd]
    keep_near = keep_ref[1 - odd]
    second = odd if base < half else 1 - odd
    base = base % half
    first = pl.multiple_of(second * half, half)
    reverse = reversal(taps)
    copies = []

    def send(which, at, sem):
        own = pl.ds(at, CHUNK)
        cols = pl.ds(pl.multiple_of(first + base + at, CHUNK), CHUNK)
        copy = pltpu.make_async_copy(results[which].at[:, own], targets[which].at[:, cols], sem)
        copy.start()
        copies.append(copy)

    for chunk in range(0, channels, CHUNK):
        lines = []
        for lane in range(chunk, chunk + CHUNK, LANES):
            sent = pl.ds(base + lane, LANES)
            near_lines = jnp.concatenate(
                [masked(far_in_ref[:, sent], keep_far).T, near_ref[:, sent].T], axis=1
            )
            far_lines = jnp.concatenate(
                [masked(near_in_ref[:, sent], keep_near).T, far_ref[:, sent].T], axis=1
            )
            lines.append((lane, near_lines, far_lines))
        sums = []
        for lane, near_lines, far_lines in lines:
            at = (first + base + lane) // width
            near_parts, far_parts = [], []
            for i in range(per_group):
                rows = slice(i * width, (i + 1) * width)
                both = jnp.concatenate([near_lines[rows], far_lines[rows]], axis=0)
                part = jnp.dot(both, tiles_ref[at + i], preferred_element_type=jnp.float32)
                near_parts.append(part[:width])
                far_parts.append(part[width:])
            near_sum = jnp.concatenate(near_parts, axis=0)
            far_sum = jnp.concatenate(far_parts, axis=0)
            y = jnp.where(odd == 1, far_sum, near_sum).T
            mixed = jnp.where(odd == 1, near_sum, far_sum).T
            sums.append((lane, y, mixed))
        whole = pl.ds(pl.multiple_of(first + base + chunk, CHUNK), CHUNK)
        k_turned = flipped(reverse, k_ref[:, whole])
        v_turned = flipped(reverse, v_ref[:, whole])
        k_parts, v_parts = [], []
        for lane, y, mixed in sums:
            own = pl.ds(lane, LANES)
            cols = pl.ds(pl.multiple_of(first + base + lane, LANES), LANES)
            out[:, own] = (q_ref[:, cols].astype(jnp.float32) * y).astype(jnp.bfloat16)
            grad_q[:, own] = (ct_ref[:, cols].astype(jnp.float32) * y).astype(jnp.bfloat16)
            lanes = slice(lane - chunk, lane - chunk + LANES)
            k_parts.append((mixed * v_turned[:, lanes]).astype(jnp.bfloat16))
            v_parts.append((mixed * k_turned[:, lanes]).astype(jnp.bfloat16))
        own = pl.ds(chunk, CHUNK)
        turn = chunk // CHUNK
        send(0, chunk, sems.at[turn, 0])
        send(1, chunk, sems.at[turn, 1])
        grad_k[:, own] = flipped(reverse, jnp.concatenate(k_parts, axis=1)).astype(jnp.bfloat16)
        send(2, chunk, sems.at[turn, 2])
        grad_v[:, own] = flipped(reverse, jnp.concatenate(v_parts, axis=1)).astype(jnp.bfloat16)
        send(3, chunk, sems.at[turn, 3])
    for copy in copies:
        copy.wait()
    done_ref[...] = jnp.zeros_like(done_ref)


def outputs(piece, operands, results, after, width):
    taps, channels = operands[0].shape
    part = channels // PIECES
    anywhere = pl.BlockSpec(memory_space=pl.ANY)
    shape = jax.ShapeDtypeStruct((taps, channels), jnp.bfloat16)
    *results, done = pl.pallas_call(
        functools.partial(outputs_kernel, width, piece * part),
        in_specs=[VMEM] * len(operands) + [anywhere] * (1 + len(results)),
        out_specs=[anywhere] * 4 + [VMEM],
        out_shape=[shape] * 4 + [jax.ShapeDtypeStruct((8, LANES), jnp.float32)],
        input_output_aliases={len(operands) + 1 + i: i for i in range(len(results))},
        scratch_shapes=[pltpu.VMEM((taps, part), jnp.bfloat16)] * 4
        + [pltpu.SemaphoreType.DMA((part // CHUNK, 4))],
        name=f"outputs_{piece}",
        cost_estimate=pl.CostEstimate(
            flops=16 * (part // width) * taps * taps * 256,
            bytes_accessed=24 * taps * part,
            transcendentals=0,
        ),
        compiler_params=pltpu.CompilerParams(vmem_limit_bytes=8 * MIB),
    )(*operands, after, *results)
    return results, done


def per_device(gate_in, key_in, value_in, cotangent, doc_starts, filters):
    taps = filters.shape[1]
    width = gate_in.shape[2] // filters.shape[0]
    assert gate_in.shape[1] == taps
    q, k, v, ct = gate_in[0], key_in[0], value_in[0], cotangent[0]
    other = first_gate(q, k, v, ct)
    other_in = exchange(other, 1)
    q, k, v, ct, near_own, near_other, own = gates(other, q, k, v, ct)
    near_in_own = exchange(near_other, 0)
    extra = exchange(other, 0)
    own_in = exchange(own, 1)
    near_in_other = exchange(near_own, 0)
    keep = masks(doc_starts[0], near_other)
    mine = filter_gradient(near_own, own, keep, near_in_own, extra, other_in, near_in_other, width)
    halves = (
        (near_own, own, keep, near_in_own, other_in),
        (near_other, other, keep, near_in_other, own_in),
    )
    tiles = None
    results = []

    def beside(after, turn):
        nonlocal tiles, results
        if turn == 0:
            tiles, after = toeplitz(filters, after)
        if turn < PIECES:
            operands = (q, k, v, ct, tiles, *halves[turn])
            results, after = outputs(turn, operands, results, after, width)
        return after

    mine = sum_devices(mine, beside)
    filter_grad = join(mine, exchange(mine, 0))
    return tuple(array[None] for array in results) + (filter_grad,)


def solution(mesh):
    split = P("dp", "ctx", None)
    return jax.shard_map(
        per_device,
        mesh=mesh,
        in_specs=(split, split, split, split, P("dp", None), P()),
        out_specs=(split, split, split, split, P()),
        check_vma=False,
    )
```

```python
import functools

import jax
import jax.numpy as jnp
from jax import lax
from jax.experimental import pallas as pl
from jax.experimental.pallas import tpu as pltpu
from jax.sharding import PartitionSpec as P

LANES = 128
ROW_BLOCK = 32
MIB = 1024 * 1024
CHUNKS = 4
PIECES = 2
CHUNK = 256
FIRST_VMEM = 213 * MIB // 4
GATES_VMEM = 101 * MIB // 2
VMEM = pl.BlockSpec(memory_space=pltpu.VMEM)
SMEM = pl.BlockSpec(memory_space=pltpu.SMEM)


def iota(shape, dim):
    return lax.broadcasted_iota(jnp.int32, shape, dim)


def exchange(array, first):
    seqs, blocks = lax.axis_size("dp"), lax.axis_size("ctx")
    pairs = []
    for seq in range(seqs):
        for block in range(blocks):
            to_seq, to_block = seq, (block - first ^ 1) + first
            if not 0 <= to_block < blocks:
                to_seq, to_block = seq ^ 1, block
            pairs.append((seq * blocks + block, to_seq * blocks + to_block))
    return lax.ppermute(array, ("dp", "ctx"), pairs)


def swapped(array, axis, step):
    size = lax.axis_size(axis)
    return lax.ppermute(array, axis, [(i, i ^ step) for i in range(size)])


def swapped(array, axis, step):
    size = lax.axis_size(axis)
    return lax.ppermute(array, axis, [(i, i ^ step) for i in range(size)])


def along(array, axis):
    size = lax.axis_size(axis)
    pairs = [(i, i + 2 if i % 2 else i - 2) for i in range(size)]
    return lax.ppermute(array, axis, [(i, j) for i, j in pairs if 0 <= j < size])


def add_kernel(*refs):
    *terms, _, out_ref = [ref for ref in refs]
    terms = [term[...] for term in terms]
    while len(terms) > 1:
        terms = [sum(terms[i + 1 : i + 2], terms[i]) for i in range(0, len(terms), 2)]
    out_ref[...] = terms[0]


def add(terms, after):
    return pl.pallas_call(
        add_kernel,
        in_specs=[VMEM] * len(terms) + [pl.BlockSpec(memory_space=pl.ANY)],
        out_specs=VMEM,
        out_shape=jax.ShapeDtypeStruct(terms[0].shape, terms[0].dtype),
        name="add",
        compiler_params=pltpu.CompilerParams(vmem_limit_bytes=MIB),
    )(*terms, after)


def sum_devices(mine, beside):
    turn = 0
    for axis, step in (("dp", 1), ("ctx", 2)):
        size = lax.axis_size(axis)
        while step < size:
            count = 4 if axis == "dp" and 4 * step <= size else 2
            others = [swapped(mine, axis, step * i) for i in range(1, count)]
            mine = add([mine] + others, beside(mine, turn))
            step, turn = count * step, turn + 1
    return mine


def join_kernel(mine_ref, other_ref, out_ref):
    count = mine_ref.shape[0]
    odd = lax.axis_index("ctx") % 2
    out_ref[pl.ds(pl.multiple_of(odd * count, count), count)] = mine_ref[...]
    out_ref[pl.ds(pl.multiple_of((1 - odd) * count, count), count)] = other_ref[...]


def join(mine, other):
    count, taps = mine.shape
    return pl.pallas_call(
        join_kernel,
        in_specs=[VMEM] * 2,
        out_specs=VMEM,
        out_shape=jax.ShapeDtypeStruct((2 * count, taps), mine.dtype),
        name="join",
        compiler_params=pltpu.CompilerParams(vmem_limit_bytes=MIB),
    )(mine, other)


def reversal(taps):
    flip = iota((taps, taps), 0) + iota((taps, taps), 1) == taps - 1
    return jnp.where(flip, 1.0, 0.0).astype(jnp.bfloat16)


def flipped(reverse, array):
    return jnp.dot(reverse, array, preferred_element_type=jnp.float32)


def masked(array, keep):
    return array * jnp.concatenate([keep] * (array.shape[0] // keep.shape[0]), axis=0)


def bf16_product(one, two):
    return (one.astype(jnp.float32) * two.astype(jnp.float32)).astype(jnp.bfloat16)


def first_kernel(q_hbm, k_hbm, v_hbm, ct_hbm, other_ref, held, sems):
    taps, half = other_ref.shape
    block = half // CHUNKS
    odd = lax.axis_index("ctx") % 2 == 1
    reverse = reversal(taps)

    def make(sources, start, finish):
        copies = []
        for c in range(CHUNKS):
            for a, source in enumerate(sources):
                copy = pltpu.make_async_copy(
                    source.at[:, pl.ds(start + c * block, block)],
                    held.at[a, :, pl.ds(c * block, block)],
                    sems.at[c, a],
                )
                copy.start()
                copies.append(copy)
        for copy in copies:
            copy.wait()
        other_ref[...] = finish(bf16_product(held[0], held[1]))

    @pl.when(odd)
    def _():
        make((k_hbm, v_hbm), 0, lambda u: u)

    @pl.when(jnp.logical_not(odd))
    def _():
        make((ct_hbm, q_hbm), half, lambda dy: flipped(reverse, dy).astype(jnp.bfloat16))


def first_gate(q, k, v, ct):
    taps, channels = q.shape
    half = channels // 2
    return pl.pallas_call(
        first_kernel,
        in_specs=[pl.BlockSpec(memory_space=pltpu.HBM)] * 4,
        out_specs=VMEM,
        out_shape=jax.ShapeDtypeStruct((taps, half), jnp.bfloat16),
        scratch_shapes=[
            pltpu.VMEM((2, taps, half), jnp.bfloat16),
            pltpu.SemaphoreType.DMA((CHUNKS, 2)),
        ],
        name="first_gate",
        cost_estimate=pl.CostEstimate(
            flops=taps * taps * channels, bytes_accessed=3 * taps * channels, transcendentals=0
        ),
        compiler_params=pltpu.CompilerParams(vmem_limit_bytes=FIRST_VMEM),
    )(q, k, v, ct)


def gates_kernel(
    after_ref, q_hbm, k_hbm, v_hbm, ct_hbm,
    q_ref, k_ref, v_ref, ct_ref, near_own_ref, near_other_ref, own_ref, sems,
):
    del after_ref
    taps, channels = q_ref.shape
    half = channels // 2
    block = channels // CHUNKS
    pairs = ((k_hbm, k_ref), (v_hbm, v_ref), (q_hbm, q_ref), (ct_hbm, ct_ref))
    copies = []
    for c in range(CHUNKS):
        cols = pl.ds(c * block, block)
        for a, (source, target) in enumerate(pairs):
            copy = pltpu.make_async_copy(source.at[:, cols], target.at[:, cols], sems.at[c, a])
            copy.start()
            copies.append(copy)
    odd = lax.axis_index("ctx") % 2 == 1
    reverse = reversal(taps)
    for c in range(CHUNKS):
        cols = pl.ds(c * block, block)
        sent = pl.ds(c * block % half, block)
        for copy in copies[4 * c : 4 * c + 4]:
            copy.wait()

        def make_u():
            return bf16_product(k_ref[:, cols], v_ref[:, cols])

        def make_dy():
            dy = bf16_product(ct_ref[:, cols], q_ref[:, cols])
            return flipped(reverse, dy).astype(jnp.bfloat16)

        @pl.when(odd)
        def _():
            near_ref = near_own_ref if c * block >= half else near_other_ref
            near_ref[:, sent] = make_dy()
            if c * block >= half:
                own_ref[:, sent] = make_u()

        @pl.when(jnp.logical_not(odd))
        def _():
            near_ref = near_own_ref if c * block < half else near_other_ref
            near_ref[:, sent] = make_u()
            if c * block < half:
                own_ref[:, sent] = make_dy()


def gates(after, q, k, v, ct):
    taps, channels = q.shape

    def shape(*dims):
        return jax.ShapeDtypeStruct(dims, jnp.bfloat16)

    half = channels // 2
    return pl.pallas_call(
        gates_kernel,
        in_specs=[pl.BlockSpec(memory_space=pl.ANY)]
        + [pl.BlockSpec(memory_space=pltpu.HBM)] * 4,
        out_specs=[VMEM] * 7,
        out_shape=[shape(taps, channels)] * 4 + [shape(taps, half)] * 3,
        scratch_shapes=[pltpu.SemaphoreType.DMA((CHUNKS, 4))],
        name="gates",
        cost_estimate=pl.CostEstimate(
            flops=2 * taps * taps * channels, bytes_accessed=12 * taps * channels, transcendentals=0
        ),
        compiler_params=pltpu.CompilerParams(vmem_limit_bytes=GATES_VMEM),
    )(after, q, k, v, ct)


def masks_kernel(taps, starts_ref, after_ref, keep_ref):
    del after_ref
    here = lax.axis_index("ctx")
    for side in range(2):
        found = (here + side) % lax.axis_size("ctx") == 0
        for d in range(starts_ref.shape[0]):
            found = jnp.logical_or(found, starts_ref[d] == (here + side) * taps)
        keep = jnp.where(found, 0.0, 1.0)
        keep_ref[side] = jnp.full(keep_ref.shape[1:], keep).astype(jnp.bfloat16)


def masks(starts, after):
    return pl.pallas_call(
        functools.partial(masks_kernel, after.shape[0]),
        in_specs=[SMEM, pl.BlockSpec(memory_space=pl.ANY)],
        out_specs=VMEM,
        out_shape=jax.ShapeDtypeStruct((2, 16, LANES), jnp.bfloat16),
        name="masks",
        compiler_params=pltpu.CompilerParams(vmem_limit_bytes=MIB),
    )(starts, after)


def toeplitz_kernel(filters_ref, after_ref, out_ref, done_ref):
    del after_ref
    count, taps = filters_ref.shape
    lines = filters_ref[...].astype(jnp.float32)
    current = iota((taps, taps), 0) <= iota((taps, taps), 1)
    for f in range(count):
        tile = jnp.broadcast_to(lines[f : f + 1], (taps, taps))
        tile = pltpu.roll(tile, 0, 1, stride=1, stride_axis=0)
        out_ref[f, :taps] = jnp.where(current, 0.0, tile).astype(jnp.bfloat16)
        out_ref[f, taps:] = jnp.where(current, tile, 0.0).astype(jnp.bfloat16)
    done_ref[...] = jnp.zeros_like(done_ref)


def toeplitz(filters, after):
    count, taps = filters.shape
    return pl.pallas_call(
        toeplitz_kernel,
        in_specs=[VMEM, pl.BlockSpec(memory_space=pl.ANY)],
        out_specs=[VMEM] * 2,
        out_shape=[
            jax.ShapeDtypeStruct((count, 2 * taps, taps), jnp.bfloat16),
            jax.ShapeDtypeStruct((8, LANES), jnp.float32),
        ],
        name="toeplitz",
        cost_estimate=pl.CostEstimate(
            flops=count * taps * taps * 64, bytes_accessed=4 * count * taps * taps, transcendentals=0
        ),
        compiler_params=pltpu.CompilerParams(vmem_limit_bytes=8 * MIB),
    )(filters, after)


def filter_grad_kernel(
    width, near_ref, own_ref, keep_ref, near_in_ref, extra_ref, far_in_ref, after_ref, out_ref, lines
):
    del after_ref
    taps, half = far_in_ref.shape
    per_group = LANES // width
    odd = lax.axis_index("ctx") % 2
    keep_far = keep_ref[odd]
    keep_near = keep_ref[1 - odd]
    lane_filter = iota((ROW_BLOCK, LANES), 1) // width
    fold = iota((ROW_BLOCK, taps), 1) + iota((ROW_BLOCK, taps), 0) < ROW_BLOCK
    for group in range(half // LANES):
        at = group * LANES
        cols = pl.ds(at, LANES)
        near = near_ref[:, cols]
        pairs = (
            (own_ref[:, cols], masked(far_in_ref[:, cols], keep_far), near),
            (near_in_ref[:, cols], masked(near, keep_near), extra_ref[:, cols]),
        )
        left, right = [], []
        for moving, beyond, fixed in pairs:
            window = jnp.concatenate([beyond, fixed], axis=0)
            for start in range(0, taps, ROW_BLOCK):
                piece = moving[start : start + ROW_BLOCK]
                left.append(
                    jnp.concatenate(
                        [jnp.where(lane_filter == i, piece, 0) for i in range(per_group)], axis=0
                    )
                )
                right.append(window[taps - ROW_BLOCK - start : 2 * taps - start])
        product = lax.dot_general(
            jnp.concatenate(left, axis=1),
            jnp.concatenate(right, axis=1),
            (((1,), (1,)), ((), ())),
            preferred_element_type=jnp.float32,
        )
        rows = []
        for i in range(per_group):
            tile = product[i * ROW_BLOCK : (i + 1) * ROW_BLOCK]
            high = jnp.concatenate(
                [tile[:, taps:], jnp.zeros((ROW_BLOCK, taps - ROW_BLOCK), jnp.float32)], axis=1
            )
            tile = jnp.where(fold, high, tile[:, :taps])
            tile = pltpu.roll(tile, taps - ROW_BLOCK + 1, 1, stride=1, stride_axis=0)
            rows.append(jnp.sum(tile, axis=0, keepdims=True))
        lines[group * per_group : (group + 1) * per_group] = jnp.concatenate(rows, axis=0)
    flip = jnp.where((iota((taps, taps), 0) + iota((taps, taps), 1)) % taps == 0, 1.0, 0.0)
    out_ref[...] = jnp.dot(
        lines[...], flip, preferred_element_type=jnp.float32, precision=lax.Precision.HIGHEST
    )


def filter_gradient(near, own, keep, near_in, extra, far_in, after, width):
    taps, half = own.shape
    count = half // width
    return pl.pallas_call(
        functools.partial(filter_grad_kernel, width),
        in_specs=[VMEM] * 6 + [pl.BlockSpec(memory_space=pl.ANY)],
        out_specs=VMEM,
        out_shape=jax.ShapeDtypeStruct((count, taps), jnp.float32),
        scratch_shapes=[pltpu.VMEM((count, taps), jnp.float32)],
        name="filter_gradient",
        cost_estimate=pl.CostEstimate(
            flops=4 * count * taps * taps * 256, bytes_accessed=16 * taps * half, transcendentals=0
        ),
        compiler_params=pltpu.CompilerParams(vmem_limit_bytes=8 * MIB),
    )(near, own, keep, near_in, extra, far_in, after)


def outputs_kernel(
    width, base, q_ref, k_ref, v_ref, ct_ref, tiles_ref, near_ref, far_ref, keep_ref,
    near_in_ref, far_in_ref, *rest,
):
    *results, sems = rest[-5:]
    *targets, done_ref = rest[-10:-5]
    out, grad_q, grad_k, grad_v = results
    taps, half = far_ref.shape
    channels = out.shape[1]
    per_group = LANES // width
    odd = lax.axis_index("ctx") % 2
    keep_far = keep_ref[odd]
    keep_near = keep_ref[1 - odd]
    second = odd if base < half else 1 - odd
    base = base % half
    first = pl.multiple_of(second * half, half)
    reverse = reversal(taps)
    copies = []

    def send(which, at, sem):
        own = pl.ds(at, CHUNK)
        cols = pl.ds(pl.multiple_of(first + base + at, CHUNK), CHUNK)
        copy = pltpu.make_async_copy(results[which].at[:, own], targets[which].at[:, cols], sem)
        copy.start()
        copies.append(copy)

    for chunk in range(0, channels, CHUNK):
        lines = []
        for lane in range(chunk, chunk + CHUNK, LANES):
            sent = pl.ds(base + lane, LANES)
            near_lines = jnp.concatenate(
                [masked(far_in_ref[:, sent], keep_far).T, near_ref[:, sent].T], axis=1
            )
            far_lines = jnp.concatenate(
                [masked(near_in_ref[:, sent], keep_near).T, far_ref[:, sent].T], axis=1
            )
            lines.append((lane, near_lines, far_lines))
        sums = []
        for lane, near_lines, far_lines in lines:
            at = (first + base + lane) // width
            near_parts, far_parts = [], []
            for i in range(per_group):
                rows = slice(i * width, (i + 1) * width)
                both = jnp.concatenate([near_lines[rows], far_lines[rows]], axis=0)
                part = jnp.dot(both, tiles_ref[at + i], preferred_element_type=jnp.float32)
                near_parts.append(part[:width])
                far_parts.append(part[width:])
            near_sum = jnp.concatenate(near_parts, axis=0)
            far_sum = jnp.concatenate(far_parts, axis=0)
            y = jnp.where(odd == 1, far_sum, near_sum).T
            mixed = jnp.where(odd == 1, near_sum, far_sum).T
            sums.append((lane, y, mixed))
        whole = pl.ds(pl.multiple_of(first + base + chunk, CHUNK), CHUNK)
        k_turned = flipped(reverse, k_ref[:, whole])
        v_turned = flipped(reverse, v_ref[:, whole])
        k_parts, v_parts = [], []
        for lane, y, mixed in sums:
            own = pl.ds(lane, LANES)
            cols = pl.ds(pl.multiple_of(first + base + lane, LANES), LANES)
            out[:, own] = (q_ref[:, cols].astype(jnp.float32) * y).astype(jnp.bfloat16)
            grad_q[:, own] = (ct_ref[:, cols].astype(jnp.float32) * y).astype(jnp.bfloat16)
            lanes = slice(lane - chunk, lane - chunk + LANES)
            k_parts.append((mixed * v_turned[:, lanes]).astype(jnp.bfloat16))
            v_parts.append((mixed * k_turned[:, lanes]).astype(jnp.bfloat16))
        own = pl.ds(chunk, CHUNK)
        turn = chunk // CHUNK
        send(0, chunk, sems.at[turn, 0])
        send(1, chunk, sems.at[turn, 1])
        grad_k[:, own] = flipped(reverse, jnp.concatenate(k_parts, axis=1)).astype(jnp.bfloat16)
        send(2, chunk, sems.at[turn, 2])
        grad_v[:, own] = flipped(reverse, jnp.concatenate(v_parts, axis=1)).astype(jnp.bfloat16)
        send(3, chunk, sems.at[turn, 3])
    for copy in copies:
        copy.wait()
    done_ref[...] = jnp.zeros_like(done_ref)


def outputs(piece, operands, results, after, width):
    taps, channels = operands[0].shape
    part = channels // PIECES
    anywhere = pl.BlockSpec(memory_space=pl.ANY)
    shape = jax.ShapeDtypeStruct((taps, channels), jnp.bfloat16)
    *results, done = pl.pallas_call(
        functools.partial(outputs_kernel, width, piece * part),
        in_specs=[VMEM] * len(operands) + [anywhere] * (1 + len(results)),
        out_specs=[anywhere] * 4 + [VMEM],
        out_shape=[shape] * 4 + [jax.ShapeDtypeStruct((8, LANES), jnp.float32)],
        input_output_aliases={len(operands) + 1 + i: i for i in range(len(results))},
        scratch_shapes=[pltpu.VMEM((taps, part), jnp.bfloat16)] * 4
        + [pltpu.SemaphoreType.DMA((part // CHUNK, 4))],
        name=f"outputs_{piece}",
        cost_estimate=pl.CostEstimate(
            flops=16 * (part // width) * taps * taps * 256,
            bytes_accessed=24 * taps * part,
            transcendentals=0,
        ),
        compiler_params=pltpu.CompilerParams(vmem_limit_bytes=8 * MIB),
    )(*operands, after, *results)
    return results, done


def per_device(gate_in, key_in, value_in, cotangent, doc_starts, filters):
    taps = filters.shape[1]
    width = gate_in.shape[2] // filters.shape[0]
    assert gate_in.shape[1] == taps
    q, k, v, ct = gate_in[0], key_in[0], value_in[0], cotangent[0]
    other = first_gate(q, k, v, ct)
    other_in = exchange(other, 1)
    q, k, v, ct, near_own, near_other, own = gates(other, q, k, v, ct)
    near_in_own = exchange(near_other, 0)
    extra = exchange(other, 0)
    own_in = exchange(own, 1)
    near_in_other = exchange(near_own, 0)
    keep = masks(doc_starts[0], near_other)
    mine = filter_gradient(near_own, own, keep, near_in_own, extra, other_in, near_in_other, width)
    halves = (
        (near_own, own, keep, near_in_own, other_in),
        (near_other, other, keep, near_in_other, own_in),
    )
    tiles = None
    results = []

    def beside(after, turn):
        nonlocal tiles, results
        if turn == 0:
            tiles, after = toeplitz(filters, after)
        elif turn <= PIECES:
            operands = (q, k, v, ct, tiles, *halves[turn - 1])
            results, after = outputs(turn - 1, operands, results, after, width)
        return after

    mine = sum_devices(mine, beside)
    filter_grad = join(mine, exchange(mine, 0))
    return tuple(array[None] for array in results) + (filter_grad,)


def solution(mesh):
    split = P("dp", "ctx", None)
    return jax.shard_map(
        per_device,
        mesh=mesh,
        in_specs=(split, split, split, split, P("dp", None), P()),
        out_specs=(split, split, split, split, P()),
        check_vma=False,
    )
```

```python
import functools

import jax
import jax.numpy as jnp
from jax import lax
from jax.experimental import pallas as pl
from jax.experimental.pallas import tpu as pltpu
from jax.sharding import PartitionSpec as P

LANES = 128
ROW_BLOCK = 32
MIB = 1024 * 1024
CHUNKS = 4
PIECES = 2
CHUNK = 512
FIRST_VMEM = 213 * MIB // 4
GATES_VMEM = 101 * MIB // 2
VMEM = pl.BlockSpec(memory_space=pltpu.VMEM)
SMEM = pl.BlockSpec(memory_space=pltpu.SMEM)


def iota(shape, dim):
    return lax.broadcasted_iota(jnp.int32, shape, dim)


def exchange(array, first):
    seqs, blocks = lax.axis_size("dp"), lax.axis_size("ctx")
    pairs = []
    for seq in range(seqs):
        for block in range(blocks):
            to_seq, to_block = seq, (block - first ^ 1) + first
            if not 0 <= to_block < blocks:
                to_seq, to_block = seq ^ 1, block
            pairs.append((seq * blocks + block, to_seq * blocks + to_block))
    return lax.ppermute(array, ("dp", "ctx"), pairs)


def swapped(array, axis, step):
    size = lax.axis_size(axis)
    return lax.ppermute(array, axis, [(i, i ^ step) for i in range(size)])


def swapped(array, axis, step):
    size = lax.axis_size(axis)
    return lax.ppermute(array, axis, [(i, i ^ step) for i in range(size)])


def along(array, axis):
    size = lax.axis_size(axis)
    pairs = [(i, i + 2 if i % 2 else i - 2) for i in range(size)]
    return lax.ppermute(array, axis, [(i, j) for i, j in pairs if 0 <= j < size])


def add_kernel(*refs):
    *terms, _, out_ref = [ref for ref in refs]
    terms = [term[...] for term in terms]
    while len(terms) > 1:
        terms = [sum(terms[i + 1 : i + 2], terms[i]) for i in range(0, len(terms), 2)]
    out_ref[...] = terms[0]


def add(terms, after):
    return pl.pallas_call(
        add_kernel,
        in_specs=[VMEM] * len(terms) + [pl.BlockSpec(memory_space=pl.ANY)],
        out_specs=VMEM,
        out_shape=jax.ShapeDtypeStruct(terms[0].shape, terms[0].dtype),
        name="add",
        compiler_params=pltpu.CompilerParams(vmem_limit_bytes=MIB),
    )(*terms, after)


def sum_devices(mine, beside):
    turn = 0
    for axis, step in (("dp", 1), ("ctx", 2)):
        size = lax.axis_size(axis)
        while step < size:
            count = 4 if axis == "dp" and 4 * step <= size else 2
            others = [swapped(mine, axis, step * i) for i in range(1, count)]
            mine = add([mine] + others, beside(mine, turn))
            step, turn = count * step, turn + 1
    return mine


def join_kernel(mine_ref, other_ref, out_ref):
    count = mine_ref.shape[0]
    odd = lax.axis_index("ctx") % 2
    out_ref[pl.ds(pl.multiple_of(odd * count, count), count)] = mine_ref[...]
    out_ref[pl.ds(pl.multiple_of((1 - odd) * count, count), count)] = other_ref[...]


def join(mine, other):
    count, taps = mine.shape
    return pl.pallas_call(
        join_kernel,
        in_specs=[VMEM] * 2,
        out_specs=VMEM,
        out_shape=jax.ShapeDtypeStruct((2 * count, taps), mine.dtype),
        name="join",
        compiler_params=pltpu.CompilerParams(vmem_limit_bytes=MIB),
    )(mine, other)


def reversal(taps):
    flip = iota((taps, taps), 0) + iota((taps, taps), 1) == taps - 1
    return jnp.where(flip, 1.0, 0.0).astype(jnp.bfloat16)


def flipped(reverse, array):
    return jnp.dot(reverse, array, preferred_element_type=jnp.float32)


def masked(array, keep):
    return array * jnp.concatenate([keep] * (array.shape[0] // keep.shape[0]), axis=0)


def bf16_product(one, two):
    return (one.astype(jnp.float32) * two.astype(jnp.float32)).astype(jnp.bfloat16)


def first_kernel(q_hbm, k_hbm, v_hbm, ct_hbm, other_ref, held, sems):
    taps, half = other_ref.shape
    block = half // CHUNKS
    odd = lax.axis_index("ctx") % 2 == 1
    reverse = reversal(taps)

    def make(sources, start, finish):
        copies = []
        for c in range(CHUNKS):
            for a, source in enumerate(sources):
                copy = pltpu.make_async_copy(
                    source.at[:, pl.ds(start + c * block, block)],
                    held.at[a, :, pl.ds(c * block, block)],
                    sems.at[c, a],
                )
                copy.start()
                copies.append(copy)
        for copy in copies:
            copy.wait()
        other_ref[...] = finish(bf16_product(held[0], held[1]))

    @pl.when(odd)
    def _():
        make((k_hbm, v_hbm), 0, lambda u: u)

    @pl.when(jnp.logical_not(odd))
    def _():
        make((ct_hbm, q_hbm), half, lambda dy: flipped(reverse, dy).astype(jnp.bfloat16))


def first_gate(q, k, v, ct):
    taps, channels = q.shape
    half = channels // 2
    return pl.pallas_call(
        first_kernel,
        in_specs=[pl.BlockSpec(memory_space=pltpu.HBM)] * 4,
        out_specs=VMEM,
        out_shape=jax.ShapeDtypeStruct((taps, half), jnp.bfloat16),
        scratch_shapes=[
            pltpu.VMEM((2, taps, half), jnp.bfloat16),
            pltpu.SemaphoreType.DMA((CHUNKS, 2)),
        ],
        name="first_gate",
        cost_estimate=pl.CostEstimate(
            flops=taps * taps * channels, bytes_accessed=3 * taps * channels, transcendentals=0
        ),
        compiler_params=pltpu.CompilerParams(vmem_limit_bytes=FIRST_VMEM),
    )(q, k, v, ct)


def gates_kernel(
    after_ref, q_hbm, k_hbm, v_hbm, ct_hbm,
    q_ref, k_ref, v_ref, ct_ref, near_own_ref, near_other_ref, own_ref, sems,
):
    del after_ref
    taps, channels = q_ref.shape
    half = channels // 2
    block = channels // CHUNKS
    pairs = ((k_hbm, k_ref), (v_hbm, v_ref), (q_hbm, q_ref), (ct_hbm, ct_ref))
    copies = []
    for c in range(CHUNKS):
        cols = pl.ds(c * block, block)
        for a, (source, target) in enumerate(pairs):
            copy = pltpu.make_async_copy(source.at[:, cols], target.at[:, cols], sems.at[c, a])
            copy.start()
            copies.append(copy)
    odd = lax.axis_index("ctx") % 2 == 1
    reverse = reversal(taps)
    for c in range(CHUNKS):
        cols = pl.ds(c * block, block)
        sent = pl.ds(c * block % half, block)
        for copy in copies[4 * c : 4 * c + 4]:
            copy.wait()

        def make_u():
            return bf16_product(k_ref[:, cols], v_ref[:, cols])

        def make_dy():
            dy = bf16_product(ct_ref[:, cols], q_ref[:, cols])
            return flipped(reverse, dy).astype(jnp.bfloat16)

        @pl.when(odd)
        def _():
            near_ref = near_own_ref if c * block >= half else near_other_ref
            near_ref[:, sent] = make_dy()
            if c * block >= half:
                own_ref[:, sent] = make_u()

        @pl.when(jnp.logical_not(odd))
        def _():
            near_ref = near_own_ref if c * block < half else near_other_ref
            near_ref[:, sent] = make_u()
            if c * block < half:
                own_ref[:, sent] = make_dy()


def gates(after, q, k, v, ct):
    taps, channels = q.shape

    def shape(*dims):
        return jax.ShapeDtypeStruct(dims, jnp.bfloat16)

    half = channels // 2
    return pl.pallas_call(
        gates_kernel,
        in_specs=[pl.BlockSpec(memory_space=pl.ANY)]
        + [pl.BlockSpec(memory_space=pltpu.HBM)] * 4,
        out_specs=[VMEM] * 7,
        out_shape=[shape(taps, channels)] * 4 + [shape(taps, half)] * 3,
        scratch_shapes=[pltpu.SemaphoreType.DMA((CHUNKS, 4))],
        name="gates",
        cost_estimate=pl.CostEstimate(
            flops=2 * taps * taps * channels, bytes_accessed=12 * taps * channels, transcendentals=0
        ),
        compiler_params=pltpu.CompilerParams(vmem_limit_bytes=GATES_VMEM),
    )(after, q, k, v, ct)


def masks_kernel(taps, starts_ref, after_ref, keep_ref):
    del after_ref
    here = lax.axis_index("ctx")
    for side in range(2):
        found = (here + side) % lax.axis_size("ctx") == 0
        for d in range(starts_ref.shape[0]):
            found = jnp.logical_or(found, starts_ref[d] == (here + side) * taps)
        keep = jnp.where(found, 0.0, 1.0)
        keep_ref[side] = jnp.full(keep_ref.shape[1:], keep).astype(jnp.bfloat16)


def masks(starts, after):
    return pl.pallas_call(
        functools.partial(masks_kernel, after.shape[0]),
        in_specs=[SMEM, pl.BlockSpec(memory_space=pl.ANY)],
        out_specs=VMEM,
        out_shape=jax.ShapeDtypeStruct((2, 16, LANES), jnp.bfloat16),
        name="masks",
        compiler_params=pltpu.CompilerParams(vmem_limit_bytes=MIB),
    )(starts, after)


def toeplitz_kernel(filters_ref, after_ref, out_ref, done_ref):
    del after_ref
    count, taps = filters_ref.shape
    lines = filters_ref[...].astype(jnp.float32)
    current = iota((taps, taps), 0) <= iota((taps, taps), 1)
    for f in range(count):
        tile = jnp.broadcast_to(lines[f : f + 1], (taps, taps))
        tile = pltpu.roll(tile, 0, 1, stride=1, stride_axis=0)
        out_ref[f, :taps] = jnp.where(current, 0.0, tile).astype(jnp.bfloat16)
        out_ref[f, taps:] = jnp.where(current, tile, 0.0).astype(jnp.bfloat16)
    done_ref[...] = jnp.zeros_like(done_ref)


def toeplitz(filters, after):
    count, taps = filters.shape
    return pl.pallas_call(
        toeplitz_kernel,
        in_specs=[VMEM, pl.BlockSpec(memory_space=pl.ANY)],
        out_specs=[VMEM] * 2,
        out_shape=[
            jax.ShapeDtypeStruct((count, 2 * taps, taps), jnp.bfloat16),
            jax.ShapeDtypeStruct((8, LANES), jnp.float32),
        ],
        name="toeplitz",
        cost_estimate=pl.CostEstimate(
            flops=count * taps * taps * 64, bytes_accessed=4 * count * taps * taps, transcendentals=0
        ),
        compiler_params=pltpu.CompilerParams(vmem_limit_bytes=8 * MIB),
    )(filters, after)


def filter_grad_kernel(
    width, near_ref, own_ref, keep_ref, near_in_ref, extra_ref, far_in_ref, after_ref, out_ref, lines
):
    del after_ref
    taps, half = far_in_ref.shape
    per_group = LANES // width
    odd = lax.axis_index("ctx") % 2
    keep_far = keep_ref[odd]
    keep_near = keep_ref[1 - odd]
    lane_filter = iota((ROW_BLOCK, LANES), 1) // width
    fold = iota((ROW_BLOCK, taps), 1) + iota((ROW_BLOCK, taps), 0) < ROW_BLOCK
    for group in range(half // LANES):
        at = group * LANES
        cols = pl.ds(at, LANES)
        near = near_ref[:, cols]
        pairs = (
            (own_ref[:, cols], masked(far_in_ref[:, cols], keep_far), near),
            (near_in_ref[:, cols], masked(near, keep_near), extra_ref[:, cols]),
        )
        left, right = [], []
        for moving, beyond, fixed in pairs:
            window = jnp.concatenate([beyond, fixed], axis=0)
            for start in range(0, taps, ROW_BLOCK):
                piece = moving[start : start + ROW_BLOCK]
                left.append(
                    jnp.concatenate(
                        [jnp.where(lane_filter == i, piece, 0) for i in range(per_group)], axis=0
                    )
                )
                right.append(window[taps - ROW_BLOCK - start : 2 * taps - start])
        product = lax.dot_general(
            jnp.concatenate(left, axis=1),
            jnp.concatenate(right, axis=1),
            (((1,), (1,)), ((), ())),
            preferred_element_type=jnp.float32,
        )
        rows = []
        for i in range(per_group):
            tile = product[i * ROW_BLOCK : (i + 1) * ROW_BLOCK]
            high = jnp.concatenate(
                [tile[:, taps:], jnp.zeros((ROW_BLOCK, taps - ROW_BLOCK), jnp.float32)], axis=1
            )
            tile = jnp.where(fold, high, tile[:, :taps])
            tile = pltpu.roll(tile, taps - ROW_BLOCK + 1, 1, stride=1, stride_axis=0)
            rows.append(jnp.sum(tile, axis=0, keepdims=True))
        lines[group * per_group : (group + 1) * per_group] = jnp.concatenate(rows, axis=0)
    flip = jnp.where((iota((taps, taps), 0) + iota((taps, taps), 1)) % taps == 0, 1.0, 0.0)
    out_ref[...] = jnp.dot(
        lines[...], flip, preferred_element_type=jnp.float32, precision=lax.Precision.HIGHEST
    )


def filter_gradient(near, own, keep, near_in, extra, far_in, after, width):
    taps, half = own.shape
    count = half // width
    return pl.pallas_call(
        functools.partial(filter_grad_kernel, width),
        in_specs=[VMEM] * 6 + [pl.BlockSpec(memory_space=pl.ANY)],
        out_specs=VMEM,
        out_shape=jax.ShapeDtypeStruct((count, taps), jnp.float32),
        scratch_shapes=[pltpu.VMEM((count, taps), jnp.float32)],
        name="filter_gradient",
        cost_estimate=pl.CostEstimate(
            flops=4 * count * taps * taps * 256, bytes_accessed=16 * taps * half, transcendentals=0
        ),
        compiler_params=pltpu.CompilerParams(vmem_limit_bytes=8 * MIB),
    )(near, own, keep, near_in, extra, far_in, after)


def outputs_kernel(
    width, base, q_ref, k_ref, v_ref, ct_ref, tiles_ref, near_ref, far_ref, keep_ref,
    near_in_ref, far_in_ref, *rest,
):
    *results, sems = rest[-5:]
    *targets, done_ref = rest[-10:-5]
    out, grad_q, grad_k, grad_v = results
    taps, half = far_ref.shape
    channels = out.shape[1]
    per_group = LANES // width
    odd = lax.axis_index("ctx") % 2
    keep_far = keep_ref[odd]
    keep_near = keep_ref[1 - odd]
    second = odd if base < half else 1 - odd
    base = base % half
    first = pl.multiple_of(second * half, half)
    reverse = reversal(taps)
    copies = []

    def send(which, at, sem):
        own = pl.ds(at, CHUNK)
        cols = pl.ds(pl.multiple_of(first + base + at, CHUNK), CHUNK)
        copy = pltpu.make_async_copy(results[which].at[:, own], targets[which].at[:, cols], sem)
        copy.start()
        copies.append(copy)

    lines = []
    for lane in range(0, channels, LANES):
        sent = pl.ds(base + lane, LANES)
        near_lines = jnp.concatenate(
            [masked(far_in_ref[:, sent], keep_far).T, near_ref[:, sent].T], axis=1
        )
        far_lines = jnp.concatenate(
            [masked(near_in_ref[:, sent], keep_near).T, far_ref[:, sent].T], axis=1
        )
        lines.append((lane, near_lines, far_lines))
    sums = []
    for lane, near_lines, far_lines in lines:
        at = (first + base + lane) // width
        near_parts, far_parts = [], []
        for i in range(per_group):
            rows = slice(i * width, (i + 1) * width)
            both = jnp.concatenate([near_lines[rows], far_lines[rows]], axis=0)
            part = jnp.dot(both, tiles_ref[at + i], preferred_element_type=jnp.float32)
            near_parts.append(part[:width])
            far_parts.append(part[width:])
        near_sum = jnp.concatenate(near_parts, axis=0)
        far_sum = jnp.concatenate(far_parts, axis=0)
        y = jnp.where(odd == 1, far_sum, near_sum).T
        mixed = jnp.where(odd == 1, near_sum, far_sum).T
        sums.append((lane, y, mixed))
    for chunk in range(0, channels, CHUNK):
        whole = pl.ds(pl.multiple_of(first + base + chunk, CHUNK), CHUNK)
        k_turned = flipped(reverse, k_ref[:, whole])
        v_turned = flipped(reverse, v_ref[:, whole])
        k_parts, v_parts = [], []
        for lane, y, mixed in sums[chunk // LANES : (chunk + CHUNK) // LANES]:
            own = pl.ds(lane, LANES)
            cols = pl.ds(pl.multiple_of(first + base + lane, LANES), LANES)
            out[:, own] = (q_ref[:, cols].astype(jnp.float32) * y).astype(jnp.bfloat16)
            grad_q[:, own] = (ct_ref[:, cols].astype(jnp.float32) * y).astype(jnp.bfloat16)
            lanes = slice(lane - chunk, lane - chunk + LANES)
            k_parts.append((mixed * v_turned[:, lanes]).astype(jnp.bfloat16))
            v_parts.append((mixed * k_turned[:, lanes]).astype(jnp.bfloat16))
        own = pl.ds(chunk, CHUNK)
        turn = chunk // CHUNK
        send(0, chunk, sems.at[turn, 0])
        send(1, chunk, sems.at[turn, 1])
        grad_k[:, own] = flipped(reverse, jnp.concatenate(k_parts, axis=1)).astype(jnp.bfloat16)
        send(2, chunk, sems.at[turn, 2])
        grad_v[:, own] = flipped(reverse, jnp.concatenate(v_parts, axis=1)).astype(jnp.bfloat16)
        send(3, chunk, sems.at[turn, 3])
    for copy in copies:
        copy.wait()
    done_ref[...] = jnp.zeros_like(done_ref)


def outputs(piece, operands, results, after, width):
    taps, channels = operands[0].shape
    part = channels // PIECES
    anywhere = pl.BlockSpec(memory_space=pl.ANY)
    shape = jax.ShapeDtypeStruct((taps, channels), jnp.bfloat16)
    *results, done = pl.pallas_call(
        functools.partial(outputs_kernel, width, piece * part),
        in_specs=[VMEM] * len(operands) + [anywhere] * (1 + len(results)),
        out_specs=[anywhere] * 4 + [VMEM],
        out_shape=[shape] * 4 + [jax.ShapeDtypeStruct((8, LANES), jnp.float32)],
        input_output_aliases={len(operands) + 1 + i: i for i in range(len(results))},
        scratch_shapes=[pltpu.VMEM((taps, part), jnp.bfloat16)] * 4
        + [pltpu.SemaphoreType.DMA((part // CHUNK, 4))],
        name=f"outputs_{piece}",
        cost_estimate=pl.CostEstimate(
            flops=16 * (part // width) * taps * taps * 256,
            bytes_accessed=24 * taps * part,
            transcendentals=0,
        ),
        compiler_params=pltpu.CompilerParams(vmem_limit_bytes=8 * MIB),
    )(*operands, after, *results)
    return results, done


def per_device(gate_in, key_in, value_in, cotangent, doc_starts, filters):
    taps = filters.shape[1]
    width = gate_in.shape[2] // filters.shape[0]
    assert gate_in.shape[1] == taps
    q, k, v, ct = gate_in[0], key_in[0], value_in[0], cotangent[0]
    other = first_gate(q, k, v, ct)
    other_in = exchange(other, 1)
    q, k, v, ct, near_own, near_other, own = gates(other, q, k, v, ct)
    near_in_own = exchange(near_other, 0)
    extra = exchange(other, 0)
    own_in = exchange(own, 1)
    near_in_other = exchange(near_own, 0)
    keep = masks(doc_starts[0], near_other)
    mine = filter_gradient(near_own, own, keep, near_in_own, extra, other_in, near_in_other, width)
    halves = (
        (near_own, own, keep, near_in_own, other_in),
        (near_other, other, keep, near_in_other, own_in),
    )
    tiles = None
    results = []

    def beside(after, turn):
        nonlocal tiles, results
        if turn == 0:
            tiles, after = toeplitz(filters, after)
        elif turn <= PIECES:
            operands = (q, k, v, ct, tiles, *halves[turn - 1])
            results, after = outputs(turn - 1, operands, results, after, width)
        return after

    mine = sum_devices(mine, beside)
    filter_grad = join(mine, exchange(mine, 0))
    return tuple(array[None] for array in results) + (filter_grad,)


def solution(mesh):
    split = P("dp", "ctx", None)
    return jax.shard_map(
        per_device,
        mesh=mesh,
        in_specs=(split, split, split, split, P("dp", None), P()),
        out_specs=(split, split, split, split, P()),
        check_vma=False,
    )
```

```python
import functools

import jax
import jax.numpy as jnp
from jax import lax
from jax.experimental import pallas as pl
from jax.experimental.pallas import tpu as pltpu
from jax.sharding import PartitionSpec as P

LANES = 128
ROW_BLOCK = 32
MIB = 1024 * 1024
CHUNKS = 4
CHUNK = 512
FIRST_VMEM = 213 * MIB // 4
GATES_VMEM = 101 * MIB // 2
VMEM = pl.BlockSpec(memory_space=pltpu.VMEM)
SMEM = pl.BlockSpec(memory_space=pltpu.SMEM)


def iota(shape, dim):
    return lax.broadcasted_iota(jnp.int32, shape, dim)


def exchange(array, first):
    seqs, blocks = lax.axis_size("dp"), lax.axis_size("ctx")
    pairs = []
    for seq in range(seqs):
        for block in range(blocks):
            to_seq, to_block = seq, (block - first ^ 1) + first
            if not 0 <= to_block < blocks:
                to_seq, to_block = seq ^ 1, block
            pairs.append((seq * blocks + block, to_seq * blocks + to_block))
    return lax.ppermute(array, ("dp", "ctx"), pairs)


def swapped(array, axis, step):
    size = lax.axis_size(axis)
    return lax.ppermute(array, axis, [(i, i ^ step) for i in range(size)])


def swapped(array, axis, step):
    size = lax.axis_size(axis)
    return lax.ppermute(array, axis, [(i, i ^ step) for i in range(size)])


def along(array, axis):
    size = lax.axis_size(axis)
    pairs = [(i, i + 2 if i % 2 else i - 2) for i in range(size)]
    return lax.ppermute(array, axis, [(i, j) for i, j in pairs if 0 <= j < size])


def add_kernel(*refs):
    *terms, _, out_ref = [ref for ref in refs]
    terms = [term[...] for term in terms]
    while len(terms) > 1:
        terms = [sum(terms[i + 1 : i + 2], terms[i]) for i in range(0, len(terms), 2)]
    out_ref[...] = terms[0]


def add(terms, after):
    return pl.pallas_call(
        add_kernel,
        in_specs=[VMEM] * len(terms) + [pl.BlockSpec(memory_space=pl.ANY)],
        out_specs=VMEM,
        out_shape=jax.ShapeDtypeStruct(terms[0].shape, terms[0].dtype),
        name="add",
        compiler_params=pltpu.CompilerParams(vmem_limit_bytes=MIB),
    )(*terms, after)


def sum_devices(mine, beside):
    turn = 0
    for axis, step in (("dp", 1), ("ctx", 2)):
        size = lax.axis_size(axis)
        while step < size:
            count = 4 if axis == "dp" and 4 * step <= size else 2
            others = [swapped(mine, axis, step * i) for i in range(1, count)]
            mine = add([mine] + others, beside(mine, turn))
            step, turn = count * step, turn + 1
    return mine


def join_kernel(mine_ref, other_ref, after_ref, out_ref):
    del after_ref
    count = mine_ref.shape[0]
    odd = lax.axis_index("ctx") % 2
    out_ref[pl.ds(pl.multiple_of(odd * count, count), count)] = mine_ref[...]
    out_ref[pl.ds(pl.multiple_of((1 - odd) * count, count), count)] = other_ref[...]


def join(mine, other, after):
    count, taps = mine.shape
    return pl.pallas_call(
        join_kernel,
        in_specs=[VMEM] * 2 + [pl.BlockSpec(memory_space=pl.ANY)],
        out_specs=VMEM,
        out_shape=jax.ShapeDtypeStruct((2 * count, taps), mine.dtype),
        name="join",
        compiler_params=pltpu.CompilerParams(vmem_limit_bytes=MIB),
    )(mine, other, after)


def reversal(taps):
    flip = iota((taps, taps), 0) + iota((taps, taps), 1) == taps - 1
    return jnp.where(flip, 1.0, 0.0).astype(jnp.bfloat16)


def flipped(reverse, array):
    return jnp.dot(reverse, array, preferred_element_type=jnp.float32)


def masked(array, keep):
    return array * jnp.concatenate([keep] * (array.shape[0] // keep.shape[0]), axis=0)


def bf16_product(one, two):
    return (one.astype(jnp.float32) * two.astype(jnp.float32)).astype(jnp.bfloat16)


def first_kernel(q_hbm, k_hbm, v_hbm, ct_hbm, other_ref, held, sems):
    taps, half = other_ref.shape
    block = half // CHUNKS
    odd = lax.axis_index("ctx") % 2 == 1
    reverse = reversal(taps)

    def make(sources, start, finish):
        copies = []
        for c in range(CHUNKS):
            for a, source in enumerate(sources):
                copy = pltpu.make_async_copy(
                    source.at[:, pl.ds(start + c * block, block)],
                    held.at[a, :, pl.ds(c * block, block)],
                    sems.at[c, a],
                )
                copy.start()
                copies.append(copy)
        for copy in copies:
            copy.wait()
        other_ref[...] = finish(bf16_product(held[0], held[1]))

    @pl.when(odd)
    def _():
        make((k_hbm, v_hbm), 0, lambda u: u)

    @pl.when(jnp.logical_not(odd))
    def _():
        make((ct_hbm, q_hbm), half, lambda dy: flipped(reverse, dy).astype(jnp.bfloat16))


def first_gate(q, k, v, ct):
    taps, channels = q.shape
    half = channels // 2
    return pl.pallas_call(
        first_kernel,
        in_specs=[pl.BlockSpec(memory_space=pltpu.HBM)] * 4,
        out_specs=VMEM,
        out_shape=jax.ShapeDtypeStruct((taps, half), jnp.bfloat16),
        scratch_shapes=[
            pltpu.VMEM((2, taps, half), jnp.bfloat16),
            pltpu.SemaphoreType.DMA((CHUNKS, 2)),
        ],
        name="first_gate",
        cost_estimate=pl.CostEstimate(
            flops=taps * taps * channels, bytes_accessed=3 * taps * channels, transcendentals=0
        ),
        compiler_params=pltpu.CompilerParams(vmem_limit_bytes=FIRST_VMEM),
    )(q, k, v, ct)


def gates_kernel(
    after_ref, q_hbm, k_hbm, v_hbm, ct_hbm,
    q_ref, k_ref, v_ref, ct_ref, near_own_ref, near_other_ref, own_ref, sems,
):
    del after_ref
    taps, channels = q_ref.shape
    half = channels // 2
    block = channels // CHUNKS
    pairs = ((k_hbm, k_ref), (v_hbm, v_ref), (q_hbm, q_ref), (ct_hbm, ct_ref))
    copies = []
    for c in range(CHUNKS):
        cols = pl.ds(c * block, block)
        for a, (source, target) in enumerate(pairs):
            copy = pltpu.make_async_copy(source.at[:, cols], target.at[:, cols], sems.at[c, a])
            copy.start()
            copies.append(copy)
    odd = lax.axis_index("ctx") % 2 == 1
    reverse = reversal(taps)
    for c in range(CHUNKS):
        cols = pl.ds(c * block, block)
        sent = pl.ds(c * block % half, block)
        for copy in copies[4 * c : 4 * c + 4]:
            copy.wait()

        def make_u():
            return bf16_product(k_ref[:, cols], v_ref[:, cols])

        def make_dy():
            dy = bf16_product(ct_ref[:, cols], q_ref[:, cols])
            return flipped(reverse, dy).astype(jnp.bfloat16)

        @pl.when(odd)
        def _():
            near_ref = near_own_ref if c * block >= half else near_other_ref
            near_ref[:, sent] = make_dy()
            if c * block >= half:
                own_ref[:, sent] = make_u()

        @pl.when(jnp.logical_not(odd))
        def _():
            near_ref = near_own_ref if c * block < half else near_other_ref
            near_ref[:, sent] = make_u()
            if c * block < half:
                own_ref[:, sent] = make_dy()


def gates(after, q, k, v, ct):
    taps, channels = q.shape

    def shape(*dims):
        return jax.ShapeDtypeStruct(dims, jnp.bfloat16)

    half = channels // 2
    return pl.pallas_call(
        gates_kernel,
        in_specs=[pl.BlockSpec(memory_space=pl.ANY)]
        + [pl.BlockSpec(memory_space=pltpu.HBM)] * 4,
        out_specs=[VMEM] * 7,
        out_shape=[shape(taps, channels)] * 4 + [shape(taps, half)] * 3,
        scratch_shapes=[pltpu.SemaphoreType.DMA((CHUNKS, 4))],
        name="gates",
        cost_estimate=pl.CostEstimate(
            flops=2 * taps * taps * channels, bytes_accessed=12 * taps * channels, transcendentals=0
        ),
        compiler_params=pltpu.CompilerParams(vmem_limit_bytes=GATES_VMEM),
    )(after, q, k, v, ct)


def masks_kernel(taps, starts_ref, after_ref, keep_ref):
    del after_ref
    here = lax.axis_index("ctx")
    for side in range(2):
        found = (here + side) % lax.axis_size("ctx") == 0
        for d in range(starts_ref.shape[0]):
            found = jnp.logical_or(found, starts_ref[d] == (here + side) * taps)
        keep = jnp.where(found, 0.0, 1.0)
        keep_ref[side] = jnp.full(keep_ref.shape[1:], keep).astype(jnp.bfloat16)


def masks(starts, after):
    return pl.pallas_call(
        functools.partial(masks_kernel, after.shape[0]),
        in_specs=[SMEM, pl.BlockSpec(memory_space=pl.ANY)],
        out_specs=VMEM,
        out_shape=jax.ShapeDtypeStruct((2, 16, LANES), jnp.bfloat16),
        name="masks",
        compiler_params=pltpu.CompilerParams(vmem_limit_bytes=MIB),
    )(starts, after)


def toeplitz_kernel(filters_ref, after_ref, out_ref, done_ref):
    del after_ref
    count, taps = filters_ref.shape
    lines = filters_ref[...].astype(jnp.float32)
    current = iota((taps, taps), 0) <= iota((taps, taps), 1)
    for f in range(count):
        tile = jnp.broadcast_to(lines[f : f + 1], (taps, taps))
        tile = pltpu.roll(tile, 0, 1, stride=1, stride_axis=0)
        out_ref[f, :taps] = jnp.where(current, 0.0, tile).astype(jnp.bfloat16)
        out_ref[f, taps:] = jnp.where(current, tile, 0.0).astype(jnp.bfloat16)
    done_ref[...] = jnp.zeros_like(done_ref)


def toeplitz(filters, after):
    count, taps = filters.shape
    return pl.pallas_call(
        toeplitz_kernel,
        in_specs=[VMEM, pl.BlockSpec(memory_space=pl.ANY)],
        out_specs=[VMEM] * 2,
        out_shape=[
            jax.ShapeDtypeStruct((count, 2 * taps, taps), jnp.bfloat16),
            jax.ShapeDtypeStruct((8, LANES), jnp.float32),
        ],
        name="toeplitz",
        cost_estimate=pl.CostEstimate(
            flops=count * taps * taps * 64, bytes_accessed=4 * count * taps * taps, transcendentals=0
        ),
        compiler_params=pltpu.CompilerParams(vmem_limit_bytes=8 * MIB),
    )(filters, after)


def filter_grad_kernel(
    width, near_ref, own_ref, keep_ref, near_in_ref, extra_ref, far_in_ref, after_ref, out_ref, lines
):
    del after_ref
    taps, half = far_in_ref.shape
    per_group = LANES // width
    odd = lax.axis_index("ctx") % 2
    keep_far = keep_ref[odd]
    keep_near = keep_ref[1 - odd]
    lane_filter = iota((ROW_BLOCK, LANES), 1) // width
    fold = iota((ROW_BLOCK, taps), 1) + iota((ROW_BLOCK, taps), 0) < ROW_BLOCK
    for group in range(half // LANES):
        at = group * LANES
        cols = pl.ds(at, LANES)
        near = near_ref[:, cols]
        pairs = (
            (own_ref[:, cols], masked(far_in_ref[:, cols], keep_far), near),
            (near_in_ref[:, cols], masked(near, keep_near), extra_ref[:, cols]),
        )
        left, right = [], []
        for moving, beyond, fixed in pairs:
            window = jnp.concatenate([beyond, fixed], axis=0)
            for start in range(0, taps, ROW_BLOCK):
                piece = moving[start : start + ROW_BLOCK]
                left.append(
                    jnp.concatenate(
                        [jnp.where(lane_filter == i, piece, 0) for i in range(per_group)], axis=0
                    )
                )
                right.append(window[taps - ROW_BLOCK - start : 2 * taps - start])
        product = lax.dot_general(
            jnp.concatenate(left, axis=1),
            jnp.concatenate(right, axis=1),
            (((1,), (1,)), ((), ())),
            preferred_element_type=jnp.float32,
        )
        rows = []
        for i in range(per_group):
            tile = product[i * ROW_BLOCK : (i + 1) * ROW_BLOCK]
            high = jnp.concatenate(
                [tile[:, taps:], jnp.zeros((ROW_BLOCK, taps - ROW_BLOCK), jnp.float32)], axis=1
            )
            tile = jnp.where(fold, high, tile[:, :taps])
            tile = pltpu.roll(tile, taps - ROW_BLOCK + 1, 1, stride=1, stride_axis=0)
            rows.append(jnp.sum(tile, axis=0, keepdims=True))
        lines[group * per_group : (group + 1) * per_group] = jnp.concatenate(rows, axis=0)
    flip = jnp.where((iota((taps, taps), 0) + iota((taps, taps), 1)) % taps == 0, 1.0, 0.0)
    out_ref[...] = jnp.dot(
        lines[...], flip, preferred_element_type=jnp.float32, precision=lax.Precision.HIGHEST
    )


def filter_gradient(near, own, keep, near_in, extra, far_in, after, width):
    taps, half = own.shape
    count = half // width
    return pl.pallas_call(
        functools.partial(filter_grad_kernel, width),
        in_specs=[VMEM] * 6 + [pl.BlockSpec(memory_space=pl.ANY)],
        out_specs=VMEM,
        out_shape=jax.ShapeDtypeStruct((count, taps), jnp.float32),
        scratch_shapes=[pltpu.VMEM((count, taps), jnp.float32)],
        name="filter_gradient",
        cost_estimate=pl.CostEstimate(
            flops=4 * count * taps * taps * 256, bytes_accessed=16 * taps * half, transcendentals=0
        ),
        compiler_params=pltpu.CompilerParams(vmem_limit_bytes=8 * MIB),
    )(near, own, keep, near_in, extra, far_in, after)


def outputs_kernel(
    width, base, q_ref, k_ref, v_ref, ct_ref, tiles_ref, near_ref, far_ref, keep_ref,
    near_in_ref, far_in_ref, *rest,
):
    *results, sems = rest[-5:]
    *targets, done_ref = rest[-10:-5]
    out, grad_q, grad_k, grad_v = results
    taps, half = far_ref.shape
    channels = out.shape[1]
    per_group = LANES // width
    odd = lax.axis_index("ctx") % 2
    keep_far = keep_ref[odd]
    keep_near = keep_ref[1 - odd]
    second = odd if base < half else 1 - odd
    base = base % half
    first = pl.multiple_of(second * half, half)
    reverse = reversal(taps)
    copies = []

    def send(which, at, sem):
        own = pl.ds(at, CHUNK)
        cols = pl.ds(pl.multiple_of(first + base + at, CHUNK), CHUNK)
        copy = pltpu.make_async_copy(results[which].at[:, own], targets[which].at[:, cols], sem)
        copy.start()
        copies.append(copy)

    lines = []
    for lane in range(0, channels, LANES):
        sent = pl.ds(base + lane, LANES)
        near_lines = jnp.concatenate(
            [masked(far_in_ref[:, sent], keep_far).T, near_ref[:, sent].T], axis=1
        )
        far_lines = jnp.concatenate(
            [masked(near_in_ref[:, sent], keep_near).T, far_ref[:, sent].T], axis=1
        )
        lines.append((lane, near_lines, far_lines))
    sums = []
    for lane, near_lines, far_lines in lines:
        at = (first + base + lane) // width
        near_parts, far_parts = [], []
        for i in range(per_group):
            rows = slice(i * width, (i + 1) * width)
            both = jnp.concatenate([near_lines[rows], far_lines[rows]], axis=0)
            part = jnp.dot(both, tiles_ref[at + i], preferred_element_type=jnp.float32)
            near_parts.append(part[:width])
            far_parts.append(part[width:])
        near_sum = jnp.concatenate(near_parts, axis=0)
        far_sum = jnp.concatenate(far_parts, axis=0)
        y = jnp.where(odd == 1, far_sum, near_sum).T
        mixed = jnp.where(odd == 1, near_sum, far_sum).T
        sums.append((lane, y, mixed))
    for chunk in range(0, channels, CHUNK):
        whole = pl.ds(pl.multiple_of(first + base + chunk, CHUNK), CHUNK)
        k_turned = flipped(reverse, k_ref[:, whole])
        v_turned = flipped(reverse, v_ref[:, whole])
        k_parts, v_parts = [], []
        for lane, y, mixed in sums[chunk // LANES : (chunk + CHUNK) // LANES]:
            own = pl.ds(lane, LANES)
            cols = pl.ds(pl.multiple_of(first + base + lane, LANES), LANES)
            out[:, own] = (q_ref[:, cols].astype(jnp.float32) * y).astype(jnp.bfloat16)
            grad_q[:, own] = (ct_ref[:, cols].astype(jnp.float32) * y).astype(jnp.bfloat16)
            lanes = slice(lane - chunk, lane - chunk + LANES)
            k_parts.append((mixed * v_turned[:, lanes]).astype(jnp.bfloat16))
            v_parts.append((mixed * k_turned[:, lanes]).astype(jnp.bfloat16))
        own = pl.ds(chunk, CHUNK)
        turn = chunk // CHUNK
        send(0, chunk, sems.at[turn, 0])
        send(1, chunk, sems.at[turn, 1])
        grad_k[:, own] = flipped(reverse, jnp.concatenate(k_parts, axis=1)).astype(jnp.bfloat16)
        send(2, chunk, sems.at[turn, 2])
        grad_v[:, own] = flipped(reverse, jnp.concatenate(v_parts, axis=1)).astype(jnp.bfloat16)
        send(3, chunk, sems.at[turn, 3])
    for copy in copies:
        copy.wait()
    done_ref[...] = jnp.zeros_like(done_ref)


def outputs(base, part, operands, results, after, width):
    taps, channels = operands[0].shape
    anywhere = pl.BlockSpec(memory_space=pl.ANY)
    shape = jax.ShapeDtypeStruct((taps, channels), jnp.bfloat16)
    *results, done = pl.pallas_call(
        functools.partial(outputs_kernel, width, base),
        in_specs=[VMEM] * len(operands) + [anywhere] * (1 + len(results)),
        out_specs=[anywhere] * 4 + [VMEM],
        out_shape=[shape] * 4 + [jax.ShapeDtypeStruct((8, LANES), jnp.float32)],
        input_output_aliases={len(operands) + 1 + i: i for i in range(len(results))},
        scratch_shapes=[pltpu.VMEM((taps, part), jnp.bfloat16)] * 4
        + [pltpu.SemaphoreType.DMA((part // CHUNK, 4))],
        name=f"outputs_{base}",
        cost_estimate=pl.CostEstimate(
            flops=16 * (part // width) * taps * taps * 256,
            bytes_accessed=24 * taps * part,
            transcendentals=0,
        ),
        compiler_params=pltpu.CompilerParams(vmem_limit_bytes=8 * MIB),
    )(*operands, after, *results)
    return results, done


def per_device(gate_in, key_in, value_in, cotangent, doc_starts, filters):
    taps = filters.shape[1]
    width = gate_in.shape[2] // filters.shape[0]
    assert gate_in.shape[1] == taps
    q, k, v, ct = gate_in[0], key_in[0], value_in[0], cotangent[0]
    other = first_gate(q, k, v, ct)
    other_in = exchange(other, 1)
    q, k, v, ct, near_own, near_other, own = gates(other, q, k, v, ct)
    near_in_own = exchange(near_other, 0)
    extra = exchange(other, 0)
    own_in = exchange(own, 1)
    near_in_other = exchange(near_own, 0)
    keep = masks(doc_starts[0], near_other)
    mine = filter_gradient(near_own, own, keep, near_in_own, extra, other_in, near_in_other, width)
    halves = (
        (near_own, own, keep, near_in_own, other_in),
        (near_other, other, keep, near_in_other, own_in),
    )
    half = near_own.shape[1]
    pieces = [(0, half), (half, half // 2), (half + half // 2, half // 2)]
    tiles = None
    results = []

    def next_piece(after):
        nonlocal results
        base, part = pieces.pop(0)
        operands = (q, k, v, ct, tiles, *halves[base // half])
        results, after = outputs(base, part, operands, results, after, width)
        return after

    def beside(after, turn):
        nonlocal tiles
        if turn == 0:
            tiles, after = toeplitz(filters, after)
        elif len(pieces) > 1:
            after = next_piece(after)
        return after

    mine = sum_devices(mine, beside)
    after = mine
    while pieces:
        after = next_piece(after)
    filter_grad = join(mine, exchange(mine, 0), after)
    return tuple(array[None] for array in results) + (filter_grad,)


def solution(mesh):
    split = P("dp", "ctx", None)
    return jax.shard_map(
        per_device,
        mesh=mesh,
        in_specs=(split, split, split, split, P("dp", None), P()),
        out_specs=(split, split, split, split, P()),
        check_vma=False,
    )
```

```python
import functools

import jax
import jax.numpy as jnp
from jax import lax
from jax.experimental import pallas as pl
from jax.experimental.pallas import tpu as pltpu
from jax.sharding import PartitionSpec as P

LANES = 128
ROW_BLOCK = 64
MIB = 1024 * 1024
CHUNKS = 4
PIECES = 2
CHUNK = 512
FIRST_VMEM = 213 * MIB // 4
GATES_VMEM = 101 * MIB // 2
VMEM = pl.BlockSpec(memory_space=pltpu.VMEM)
SMEM = pl.BlockSpec(memory_space=pltpu.SMEM)


def iota(shape, dim):
    return lax.broadcasted_iota(jnp.int32, shape, dim)


def exchange(array, first):
    seqs, blocks = lax.axis_size("dp"), lax.axis_size("ctx")
    pairs = []
    for seq in range(seqs):
        for block in range(blocks):
            to_seq, to_block = seq, (block - first ^ 1) + first
            if not 0 <= to_block < blocks:
                to_seq, to_block = seq ^ 1, block
            pairs.append((seq * blocks + block, to_seq * blocks + to_block))
    return lax.ppermute(array, ("dp", "ctx"), pairs)


def swapped(array, axis, step):
    size = lax.axis_size(axis)
    return lax.ppermute(array, axis, [(i, i ^ step) for i in range(size)])


def swapped(array, axis, step):
    size = lax.axis_size(axis)
    return lax.ppermute(array, axis, [(i, i ^ step) for i in range(size)])


def along(array, axis):
    size = lax.axis_size(axis)
    pairs = [(i, i + 2 if i % 2 else i - 2) for i in range(size)]
    return lax.ppermute(array, axis, [(i, j) for i, j in pairs if 0 <= j < size])


def add_kernel(*refs):
    *terms, _, out_ref = [ref for ref in refs]
    terms = [term[...] for term in terms]
    while len(terms) > 1:
        terms = [sum(terms[i + 1 : i + 2], terms[i]) for i in range(0, len(terms), 2)]
    out_ref[...] = terms[0]


def add(terms, after):
    return pl.pallas_call(
        add_kernel,
        in_specs=[VMEM] * len(terms) + [pl.BlockSpec(memory_space=pl.ANY)],
        out_specs=VMEM,
        out_shape=jax.ShapeDtypeStruct(terms[0].shape, terms[0].dtype),
        name="add",
        compiler_params=pltpu.CompilerParams(vmem_limit_bytes=MIB),
    )(*terms, after)


def sum_devices(mine, beside):
    turn = 0
    for axis, step in (("dp", 1), ("ctx", 2)):
        size = lax.axis_size(axis)
        while step < size:
            count = 4 if axis == "dp" and 4 * step <= size else 2
            others = [swapped(mine, axis, step * i) for i in range(1, count)]
            mine = add([mine] + others, beside(mine, turn))
            step, turn = count * step, turn + 1
    return mine


def join_kernel(mine_ref, other_ref, out_ref):
    count = mine_ref.shape[0]
    odd = lax.axis_index("ctx") % 2
    out_ref[pl.ds(pl.multiple_of(odd * count, count), count)] = mine_ref[...]
    out_ref[pl.ds(pl.multiple_of((1 - odd) * count, count), count)] = other_ref[...]


def join(mine, other):
    count, taps = mine.shape
    return pl.pallas_call(
        join_kernel,
        in_specs=[VMEM] * 2,
        out_specs=VMEM,
        out_shape=jax.ShapeDtypeStruct((2 * count, taps), mine.dtype),
        name="join",
        compiler_params=pltpu.CompilerParams(vmem_limit_bytes=MIB),
    )(mine, other)


def reversal(taps):
    flip = iota((taps, taps), 0) + iota((taps, taps), 1) == taps - 1
    return jnp.where(flip, 1.0, 0.0).astype(jnp.bfloat16)


def flipped(reverse, array):
    return jnp.dot(reverse, array, preferred_element_type=jnp.float32)


def masked(array, keep):
    return array * jnp.concatenate([keep] * (array.shape[0] // keep.shape[0]), axis=0)


def bf16_product(one, two):
    return (one.astype(jnp.float32) * two.astype(jnp.float32)).astype(jnp.bfloat16)


def first_kernel(q_hbm, k_hbm, v_hbm, ct_hbm, other_ref, held, sems):
    taps, half = other_ref.shape
    block = half // CHUNKS
    odd = lax.axis_index("ctx") % 2 == 1
    reverse = reversal(taps)

    def make(sources, start, finish):
        copies = []
        for c in range(CHUNKS):
            for a, source in enumerate(sources):
                copy = pltpu.make_async_copy(
                    source.at[:, pl.ds(start + c * block, block)],
                    held.at[a, :, pl.ds(c * block, block)],
                    sems.at[c, a],
                )
                copy.start()
                copies.append(copy)
        for copy in copies:
            copy.wait()
        other_ref[...] = finish(bf16_product(held[0], held[1]))

    @pl.when(odd)
    def _():
        make((k_hbm, v_hbm), 0, lambda u: u)

    @pl.when(jnp.logical_not(odd))
    def _():
        make((ct_hbm, q_hbm), half, lambda dy: flipped(reverse, dy).astype(jnp.bfloat16))


def first_gate(q, k, v, ct):
    taps, channels = q.shape
    half = channels // 2
    return pl.pallas_call(
        first_kernel,
        in_specs=[pl.BlockSpec(memory_space=pltpu.HBM)] * 4,
        out_specs=VMEM,
        out_shape=jax.ShapeDtypeStruct((taps, half), jnp.bfloat16),
        scratch_shapes=[
            pltpu.VMEM((2, taps, half), jnp.bfloat16),
            pltpu.SemaphoreType.DMA((CHUNKS, 2)),
        ],
        name="first_gate",
        cost_estimate=pl.CostEstimate(
            flops=taps * taps * channels, bytes_accessed=3 * taps * channels, transcendentals=0
        ),
        compiler_params=pltpu.CompilerParams(vmem_limit_bytes=FIRST_VMEM),
    )(q, k, v, ct)


def gates_kernel(
    after_ref, q_hbm, k_hbm, v_hbm, ct_hbm,
    q_ref, k_ref, v_ref, ct_ref, near_own_ref, near_other_ref, own_ref, sems,
):
    del after_ref
    taps, channels = q_ref.shape
    half = channels // 2
    block = channels // CHUNKS
    pairs = ((k_hbm, k_ref), (v_hbm, v_ref), (q_hbm, q_ref), (ct_hbm, ct_ref))
    copies = []
    for c in range(CHUNKS):
        cols = pl.ds(c * block, block)
        for a, (source, target) in enumerate(pairs):
            copy = pltpu.make_async_copy(source.at[:, cols], target.at[:, cols], sems.at[c, a])
            copy.start()
            copies.append(copy)
    odd = lax.axis_index("ctx") % 2 == 1
    reverse = reversal(taps)
    for c in range(CHUNKS):
        cols = pl.ds(c * block, block)
        sent = pl.ds(c * block % half, block)
        for copy in copies[4 * c : 4 * c + 4]:
            copy.wait()

        def make_u():
            return bf16_product(k_ref[:, cols], v_ref[:, cols])

        def make_dy():
            dy = bf16_product(ct_ref[:, cols], q_ref[:, cols])
            return flipped(reverse, dy).astype(jnp.bfloat16)

        @pl.when(odd)
        def _():
            near_ref = near_own_ref if c * block >= half else near_other_ref
            near_ref[:, sent] = make_dy()
            if c * block >= half:
                own_ref[:, sent] = make_u()

        @pl.when(jnp.logical_not(odd))
        def _():
            near_ref = near_own_ref if c * block < half else near_other_ref
            near_ref[:, sent] = make_u()
            if c * block < half:
                own_ref[:, sent] = make_dy()


def gates(after, q, k, v, ct):
    taps, channels = q.shape

    def shape(*dims):
        return jax.ShapeDtypeStruct(dims, jnp.bfloat16)

    half = channels // 2
    return pl.pallas_call(
        gates_kernel,
        in_specs=[pl.BlockSpec(memory_space=pl.ANY)]
        + [pl.BlockSpec(memory_space=pltpu.HBM)] * 4,
        out_specs=[VMEM] * 7,
        out_shape=[shape(taps, channels)] * 4 + [shape(taps, half)] * 3,
        scratch_shapes=[pltpu.SemaphoreType.DMA((CHUNKS, 4))],
        name="gates",
        cost_estimate=pl.CostEstimate(
            flops=2 * taps * taps * channels, bytes_accessed=12 * taps * channels, transcendentals=0
        ),
        compiler_params=pltpu.CompilerParams(vmem_limit_bytes=GATES_VMEM),
    )(after, q, k, v, ct)


def masks_kernel(taps, starts_ref, after_ref, keep_ref):
    del after_ref
    here = lax.axis_index("ctx")
    for side in range(2):
        found = (here + side) % lax.axis_size("ctx") == 0
        for d in range(starts_ref.shape[0]):
            found = jnp.logical_or(found, starts_ref[d] == (here + side) * taps)
        keep = jnp.where(found, 0.0, 1.0)
        keep_ref[side] = jnp.full(keep_ref.shape[1:], keep).astype(jnp.bfloat16)


def masks(starts, after):
    return pl.pallas_call(
        functools.partial(masks_kernel, after.shape[0]),
        in_specs=[SMEM, pl.BlockSpec(memory_space=pl.ANY)],
        out_specs=VMEM,
        out_shape=jax.ShapeDtypeStruct((2, 16, LANES), jnp.bfloat16),
        name="masks",
        compiler_params=pltpu.CompilerParams(vmem_limit_bytes=MIB),
    )(starts, after)


def toeplitz_kernel(filters_ref, after_ref, out_ref, done_ref):
    del after_ref
    count, taps = filters_ref.shape
    lines = filters_ref[...].astype(jnp.float32)
    current = iota((taps, taps), 0) <= iota((taps, taps), 1)
    for f in range(count):
        tile = jnp.broadcast_to(lines[f : f + 1], (taps, taps))
        tile = pltpu.roll(tile, 0, 1, stride=1, stride_axis=0)
        out_ref[f, :taps] = jnp.where(current, 0.0, tile).astype(jnp.bfloat16)
        out_ref[f, taps:] = jnp.where(current, tile, 0.0).astype(jnp.bfloat16)
    done_ref[...] = jnp.zeros_like(done_ref)


def toeplitz(filters, after):
    count, taps = filters.shape
    return pl.pallas_call(
        toeplitz_kernel,
        in_specs=[VMEM, pl.BlockSpec(memory_space=pl.ANY)],
        out_specs=[VMEM] * 2,
        out_shape=[
            jax.ShapeDtypeStruct((count, 2 * taps, taps), jnp.bfloat16),
            jax.ShapeDtypeStruct((8, LANES), jnp.float32),
        ],
        name="toeplitz",
        cost_estimate=pl.CostEstimate(
            flops=count * taps * taps * 64, bytes_accessed=4 * count * taps * taps, transcendentals=0
        ),
        compiler_params=pltpu.CompilerParams(vmem_limit_bytes=8 * MIB),
    )(filters, after)


def filter_grad_kernel(
    width, near_ref, own_ref, keep_ref, near_in_ref, extra_ref, far_in_ref, after_ref, out_ref, lines
):
    del after_ref
    taps, half = far_in_ref.shape
    per_group = LANES // width
    odd = lax.axis_index("ctx") % 2
    keep_far = keep_ref[odd]
    keep_near = keep_ref[1 - odd]
    lane_filter = iota((ROW_BLOCK, LANES), 1) // width
    fold = iota((ROW_BLOCK, taps), 1) + iota((ROW_BLOCK, taps), 0) < ROW_BLOCK
    for group in range(half // LANES):
        at = group * LANES
        cols = pl.ds(at, LANES)
        near = near_ref[:, cols]
        pairs = (
            (own_ref[:, cols], masked(far_in_ref[:, cols], keep_far), near),
            (near_in_ref[:, cols], masked(near, keep_near), extra_ref[:, cols]),
        )
        left, right = [], []
        for moving, beyond, fixed in pairs:
            window = jnp.concatenate([beyond, fixed], axis=0)
            for start in range(0, taps, ROW_BLOCK):
                piece = moving[start : start + ROW_BLOCK]
                left.append(
                    jnp.concatenate(
                        [jnp.where(lane_filter == i, piece, 0) for i in range(per_group)], axis=0
                    )
                )
                right.append(window[taps - ROW_BLOCK - start : 2 * taps - start])
        product = lax.dot_general(
            jnp.concatenate(left, axis=1),
            jnp.concatenate(right, axis=1),
            (((1,), (1,)), ((), ())),
            preferred_element_type=jnp.float32,
        )
        rows = []
        for i in range(per_group):
            tile = product[i * ROW_BLOCK : (i + 1) * ROW_BLOCK]
            high = jnp.concatenate(
                [tile[:, taps:], jnp.zeros((ROW_BLOCK, taps - ROW_BLOCK), jnp.float32)], axis=1
            )
            tile = jnp.where(fold, high, tile[:, :taps])
            tile = pltpu.roll(tile, taps - ROW_BLOCK + 1, 1, stride=1, stride_axis=0)
            rows.append(jnp.sum(tile, axis=0, keepdims=True))
        lines[group * per_group : (group + 1) * per_group] = jnp.concatenate(rows, axis=0)
    flip = jnp.where((iota((taps, taps), 0) + iota((taps, taps), 1)) % taps == 0, 1.0, 0.0)
    out_ref[...] = jnp.dot(
        lines[...], flip, preferred_element_type=jnp.float32, precision=lax.Precision.HIGHEST
    )


def filter_gradient(near, own, keep, near_in, extra, far_in, after, width):
    taps, half = own.shape
    count = half // width
    return pl.pallas_call(
        functools.partial(filter_grad_kernel, width),
        in_specs=[VMEM] * 6 + [pl.BlockSpec(memory_space=pl.ANY)],
        out_specs=VMEM,
        out_shape=jax.ShapeDtypeStruct((count, taps), jnp.float32),
        scratch_shapes=[pltpu.VMEM((count, taps), jnp.float32)],
        name="filter_gradient",
        cost_estimate=pl.CostEstimate(
            flops=4 * count * taps * taps * 256, bytes_accessed=16 * taps * half, transcendentals=0
        ),
        compiler_params=pltpu.CompilerParams(vmem_limit_bytes=8 * MIB),
    )(near, own, keep, near_in, extra, far_in, after)


def outputs_kernel(
    width, base, q_ref, k_ref, v_ref, ct_ref, tiles_ref, near_ref, far_ref, keep_ref,
    near_in_ref, far_in_ref, *rest,
):
    *results, sems = rest[-5:]
    *targets, done_ref = rest[-10:-5]
    out, grad_q, grad_k, grad_v = results
    taps, half = far_ref.shape
    channels = out.shape[1]
    per_group = LANES // width
    odd = lax.axis_index("ctx") % 2
    keep_far = keep_ref[odd]
    keep_near = keep_ref[1 - odd]
    second = odd if base < half else 1 - odd
    base = base % half
    first = pl.multiple_of(second * half, half)
    reverse = reversal(taps)
    copies = []

    def send(which, at, sem):
        own = pl.ds(at, CHUNK)
        cols = pl.ds(pl.multiple_of(first + base + at, CHUNK), CHUNK)
        copy = pltpu.make_async_copy(results[which].at[:, own], targets[which].at[:, cols], sem)
        copy.start()
        copies.append(copy)

    lines = []
    for lane in range(0, channels, LANES):
        sent = pl.ds(base + lane, LANES)
        near_lines = jnp.concatenate(
            [masked(far_in_ref[:, sent], keep_far).T, near_ref[:, sent].T], axis=1
        )
        far_lines = jnp.concatenate(
            [masked(near_in_ref[:, sent], keep_near).T, far_ref[:, sent].T], axis=1
        )
        lines.append((lane, near_lines, far_lines))
    sums = []
    for lane, near_lines, far_lines in lines:
        at = (first + base + lane) // width
        near_parts, far_parts = [], []
        for i in range(per_group):
            rows = slice(i * width, (i + 1) * width)
            both = jnp.concatenate([near_lines[rows], far_lines[rows]], axis=0)
            part = jnp.dot(both, tiles_ref[at + i], preferred_element_type=jnp.float32)
            near_parts.append(part[:width])
            far_parts.append(part[width:])
        near_sum = jnp.concatenate(near_parts, axis=0)
        far_sum = jnp.concatenate(far_parts, axis=0)
        y = jnp.where(odd == 1, far_sum, near_sum).T
        mixed = jnp.where(odd == 1, near_sum, far_sum).T
        sums.append((lane, y, mixed))
    for chunk in range(0, channels, CHUNK):
        whole = pl.ds(pl.multiple_of(first + base + chunk, CHUNK), CHUNK)
        k_turned = flipped(reverse, k_ref[:, whole])
        v_turned = flipped(reverse, v_ref[:, whole])
        k_parts, v_parts = [], []
        for lane, y, mixed in sums[chunk // LANES : (chunk + CHUNK) // LANES]:
            own = pl.ds(lane, LANES)
            cols = pl.ds(pl.multiple_of(first + base + lane, LANES), LANES)
            out[:, own] = (q_ref[:, cols].astype(jnp.float32) * y).astype(jnp.bfloat16)
            grad_q[:, own] = (ct_ref[:, cols].astype(jnp.float32) * y).astype(jnp.bfloat16)
            lanes = slice(lane - chunk, lane - chunk + LANES)
            k_parts.append((mixed * v_turned[:, lanes]).astype(jnp.bfloat16))
            v_parts.append((mixed * k_turned[:, lanes]).astype(jnp.bfloat16))
        own = pl.ds(chunk, CHUNK)
        turn = chunk // CHUNK
        send(0, chunk, sems.at[turn, 0])
        send(1, chunk, sems.at[turn, 1])
        grad_k[:, own] = flipped(reverse, jnp.concatenate(k_parts, axis=1)).astype(jnp.bfloat16)
        send(2, chunk, sems.at[turn, 2])
        grad_v[:, own] = flipped(reverse, jnp.concatenate(v_parts, axis=1)).astype(jnp.bfloat16)
        send(3, chunk, sems.at[turn, 3])
    for copy in copies:
        copy.wait()
    done_ref[...] = jnp.zeros_like(done_ref)


def outputs(piece, operands, results, after, width):
    taps, channels = operands[0].shape
    part = channels // PIECES
    anywhere = pl.BlockSpec(memory_space=pl.ANY)
    shape = jax.ShapeDtypeStruct((taps, channels), jnp.bfloat16)
    *results, done = pl.pallas_call(
        functools.partial(outputs_kernel, width, piece * part),
        in_specs=[VMEM] * len(operands) + [anywhere] * (1 + len(results)),
        out_specs=[anywhere] * 4 + [VMEM],
        out_shape=[shape] * 4 + [jax.ShapeDtypeStruct((8, LANES), jnp.float32)],
        input_output_aliases={len(operands) + 1 + i: i for i in range(len(results))},
        scratch_shapes=[pltpu.VMEM((taps, part), jnp.bfloat16)] * 4
        + [pltpu.SemaphoreType.DMA((part // CHUNK, 4))],
        name=f"outputs_{piece}",
        cost_estimate=pl.CostEstimate(
            flops=16 * (part // width) * taps * taps * 256,
            bytes_accessed=24 * taps * part,
            transcendentals=0,
        ),
        compiler_params=pltpu.CompilerParams(vmem_limit_bytes=8 * MIB),
    )(*operands, after, *results)
    return results, done


def per_device(gate_in, key_in, value_in, cotangent, doc_starts, filters):
    taps = filters.shape[1]
    width = gate_in.shape[2] // filters.shape[0]
    assert gate_in.shape[1] == taps
    q, k, v, ct = gate_in[0], key_in[0], value_in[0], cotangent[0]
    other = first_gate(q, k, v, ct)
    other_in = exchange(other, 1)
    q, k, v, ct, near_own, near_other, own = gates(other, q, k, v, ct)
    near_in_own = exchange(near_other, 0)
    extra = exchange(other, 0)
    own_in = exchange(own, 1)
    near_in_other = exchange(near_own, 0)
    keep = masks(doc_starts[0], near_other)
    mine = filter_gradient(near_own, own, keep, near_in_own, extra, other_in, near_in_other, width)
    halves = (
        (near_own, own, keep, near_in_own, other_in),
        (near_other, other, keep, near_in_other, own_in),
    )
    tiles = None
    results = []

    def beside(after, turn):
        nonlocal tiles, results
        if turn == 0:
            tiles, after = toeplitz(filters, after)
        elif turn <= PIECES:
            operands = (q, k, v, ct, tiles, *halves[turn - 1])
            results, after = outputs(turn - 1, operands, results, after, width)
        return after

    mine = sum_devices(mine, beside)
    filter_grad = join(mine, exchange(mine, 0))
    return tuple(array[None] for array in results) + (filter_grad,)


def solution(mesh):
    split = P("dp", "ctx", None)
    return jax.shard_map(
        per_device,
        mesh=mesh,
        in_specs=(split, split, split, split, P("dp", None), P()),
        out_specs=(split, split, split, split, P()),
        check_vma=False,
    )
```

```python
import functools

import jax
import jax.numpy as jnp
from jax import lax
from jax.experimental import pallas as pl
from jax.experimental.pallas import tpu as pltpu
from jax.sharding import PartitionSpec as P

LANES = 128
ROW_BLOCK = 64
MIB = 1024 * 1024
CHUNKS = 4
PIECES = 2
CHUNK = 1024
FIRST_VMEM = 213 * MIB // 4
GATES_VMEM = 101 * MIB // 2
VMEM = pl.BlockSpec(memory_space=pltpu.VMEM)
SMEM = pl.BlockSpec(memory_space=pltpu.SMEM)


def iota(shape, dim):
    return lax.broadcasted_iota(jnp.int32, shape, dim)


def exchange(array, first):
    seqs, blocks = lax.axis_size("dp"), lax.axis_size("ctx")
    pairs = []
    for seq in range(seqs):
        for block in range(blocks):
            to_seq, to_block = seq, (block - first ^ 1) + first
            if not 0 <= to_block < blocks:
                to_seq, to_block = seq ^ 1, block
            pairs.append((seq * blocks + block, to_seq * blocks + to_block))
    return lax.ppermute(array, ("dp", "ctx"), pairs)


def swapped(array, axis, step):
    size = lax.axis_size(axis)
    return lax.ppermute(array, axis, [(i, i ^ step) for i in range(size)])


def swapped(array, axis, step):
    size = lax.axis_size(axis)
    return lax.ppermute(array, axis, [(i, i ^ step) for i in range(size)])


def along(array, axis):
    size = lax.axis_size(axis)
    pairs = [(i, i + 2 if i % 2 else i - 2) for i in range(size)]
    return lax.ppermute(array, axis, [(i, j) for i, j in pairs if 0 <= j < size])


def add_kernel(*refs):
    *terms, _, out_ref = [ref for ref in refs]
    terms = [term[...] for term in terms]
    while len(terms) > 1:
        terms = [sum(terms[i + 1 : i + 2], terms[i]) for i in range(0, len(terms), 2)]
    out_ref[...] = terms[0]


def add(terms, after):
    return pl.pallas_call(
        add_kernel,
        in_specs=[VMEM] * len(terms) + [pl.BlockSpec(memory_space=pl.ANY)],
        out_specs=VMEM,
        out_shape=jax.ShapeDtypeStruct(terms[0].shape, terms[0].dtype),
        name="add",
        compiler_params=pltpu.CompilerParams(vmem_limit_bytes=MIB),
    )(*terms, after)


def sum_devices(mine, beside):
    turn = 0
    for axis, step in (("dp", 1), ("ctx", 2)):
        size = lax.axis_size(axis)
        while step < size:
            count = 4 if axis == "dp" and 4 * step <= size else 2
            others = [swapped(mine, axis, step * i) for i in range(1, count)]
            mine = add([mine] + others, beside(mine, turn))
            step, turn = count * step, turn + 1
    return mine


def join_kernel(mine_ref, other_ref, out_ref):
    count = mine_ref.shape[0]
    odd = lax.axis_index("ctx") % 2
    out_ref[pl.ds(pl.multiple_of(odd * count, count), count)] = mine_ref[...]
    out_ref[pl.ds(pl.multiple_of((1 - odd) * count, count), count)] = other_ref[...]


def join(mine, other):
    count, taps = mine.shape
    return pl.pallas_call(
        join_kernel,
        in_specs=[VMEM] * 2,
        out_specs=VMEM,
        out_shape=jax.ShapeDtypeStruct((2 * count, taps), mine.dtype),
        name="join",
        compiler_params=pltpu.CompilerParams(vmem_limit_bytes=MIB),
    )(mine, other)


def reversal(taps):
    flip = iota((taps, taps), 0) + iota((taps, taps), 1) == taps - 1
    return jnp.where(flip, 1.0, 0.0).astype(jnp.bfloat16)


def flipped(reverse, array):
    return jnp.dot(reverse, array, preferred_element_type=jnp.float32)


def masked(array, keep):
    return array * jnp.concatenate([keep] * (array.shape[0] // keep.shape[0]), axis=0)


def bf16_product(one, two):
    return (one.astype(jnp.float32) * two.astype(jnp.float32)).astype(jnp.bfloat16)


def first_kernel(q_hbm, k_hbm, v_hbm, ct_hbm, other_ref, held, sems):
    taps, half = other_ref.shape
    block = half // CHUNKS
    odd = lax.axis_index("ctx") % 2 == 1
    reverse = reversal(taps)

    def make(sources, start, finish):
        copies = []
        for c in range(CHUNKS):
            for a, source in enumerate(sources):
                copy = pltpu.make_async_copy(
                    source.at[:, pl.ds(start + c * block, block)],
                    held.at[a, :, pl.ds(c * block, block)],
                    sems.at[c, a],
                )
                copy.start()
                copies.append(copy)
        for copy in copies:
            copy.wait()
        other_ref[...] = finish(bf16_product(held[0], held[1]))

    @pl.when(odd)
    def _():
        make((k_hbm, v_hbm), 0, lambda u: u)

    @pl.when(jnp.logical_not(odd))
    def _():
        make((ct_hbm, q_hbm), half, lambda dy: flipped(reverse, dy).astype(jnp.bfloat16))


def first_gate(q, k, v, ct):
    taps, channels = q.shape
    half = channels // 2
    return pl.pallas_call(
        first_kernel,
        in_specs=[pl.BlockSpec(memory_space=pltpu.HBM)] * 4,
        out_specs=VMEM,
        out_shape=jax.ShapeDtypeStruct((taps, half), jnp.bfloat16),
        scratch_shapes=[
            pltpu.VMEM((2, taps, half), jnp.bfloat16),
            pltpu.SemaphoreType.DMA((CHUNKS, 2)),
        ],
        name="first_gate",
        cost_estimate=pl.CostEstimate(
            flops=taps * taps * channels, bytes_accessed=3 * taps * channels, transcendentals=0
        ),
        compiler_params=pltpu.CompilerParams(vmem_limit_bytes=FIRST_VMEM),
    )(q, k, v, ct)


def gates_kernel(
    after_ref, q_hbm, k_hbm, v_hbm, ct_hbm,
    q_ref, k_ref, v_ref, ct_ref, near_own_ref, near_other_ref, own_ref, sems,
):
    del after_ref
    taps, channels = q_ref.shape
    half = channels // 2
    block = channels // CHUNKS
    pairs = ((k_hbm, k_ref), (v_hbm, v_ref), (q_hbm, q_ref), (ct_hbm, ct_ref))
    copies = []
    for c in range(CHUNKS):
        cols = pl.ds(c * block, block)
        for a, (source, target) in enumerate(pairs):
            copy = pltpu.make_async_copy(source.at[:, cols], target.at[:, cols], sems.at[c, a])
            copy.start()
            copies.append(copy)
    odd = lax.axis_index("ctx") % 2 == 1
    reverse = reversal(taps)
    for c in range(CHUNKS):
        cols = pl.ds(c * block, block)
        sent = pl.ds(c * block % half, block)
        for copy in copies[4 * c : 4 * c + 4]:
            copy.wait()

        def make_u():
            return bf16_product(k_ref[:, cols], v_ref[:, cols])

        def make_dy():
            dy = bf16_product(ct_ref[:, cols], q_ref[:, cols])
            return flipped(reverse, dy).astype(jnp.bfloat16)

        @pl.when(odd)
        def _():
            near_ref = near_own_ref if c * block >= half else near_other_ref
            near_ref[:, sent] = make_dy()
            if c * block >= half:
                own_ref[:, sent] = make_u()

        @pl.when(jnp.logical_not(odd))
        def _():
            near_ref = near_own_ref if c * block < half else near_other_ref
            near_ref[:, sent] = make_u()
            if c * block < half:
                own_ref[:, sent] = make_dy()


def gates(after, q, k, v, ct):
    taps, channels = q.shape

    def shape(*dims):
        return jax.ShapeDtypeStruct(dims, jnp.bfloat16)

    half = channels // 2
    return pl.pallas_call(
        gates_kernel,
        in_specs=[pl.BlockSpec(memory_space=pl.ANY)]
        + [pl.BlockSpec(memory_space=pltpu.HBM)] * 4,
        out_specs=[VMEM] * 7,
        out_shape=[shape(taps, channels)] * 4 + [shape(taps, half)] * 3,
        scratch_shapes=[pltpu.SemaphoreType.DMA((CHUNKS, 4))],
        name="gates",
        cost_estimate=pl.CostEstimate(
            flops=2 * taps * taps * channels, bytes_accessed=12 * taps * channels, transcendentals=0
        ),
        compiler_params=pltpu.CompilerParams(vmem_limit_bytes=GATES_VMEM),
    )(after, q, k, v, ct)


def masks_kernel(taps, starts_ref, after_ref, keep_ref):
    del after_ref
    here = lax.axis_index("ctx")
    for side in range(2):
        found = (here + side) % lax.axis_size("ctx") == 0
        for d in range(starts_ref.shape[0]):
            found = jnp.logical_or(found, starts_ref[d] == (here + side) * taps)
        keep = jnp.where(found, 0.0, 1.0)
        keep_ref[side] = jnp.full(keep_ref.shape[1:], keep).astype(jnp.bfloat16)


def masks(starts, after):
    return pl.pallas_call(
        functools.partial(masks_kernel, after.shape[0]),
        in_specs=[SMEM, pl.BlockSpec(memory_space=pl.ANY)],
        out_specs=VMEM,
        out_shape=jax.ShapeDtypeStruct((2, 16, LANES), jnp.bfloat16),
        name="masks",
        compiler_params=pltpu.CompilerParams(vmem_limit_bytes=MIB),
    )(starts, after)


def toeplitz_kernel(filters_ref, after_ref, out_ref, done_ref):
    del after_ref
    count, taps = filters_ref.shape
    lines = filters_ref[...].astype(jnp.float32)
    current = iota((taps, taps), 0) <= iota((taps, taps), 1)
    for f in range(count):
        tile = jnp.broadcast_to(lines[f : f + 1], (taps, taps))
        tile = pltpu.roll(tile, 0, 1, stride=1, stride_axis=0)
        out_ref[f, :taps] = jnp.where(current, 0.0, tile).astype(jnp.bfloat16)
        out_ref[f, taps:] = jnp.where(current, tile, 0.0).astype(jnp.bfloat16)
    done_ref[...] = jnp.zeros_like(done_ref)


def toeplitz(filters, after):
    count, taps = filters.shape
    return pl.pallas_call(
        toeplitz_kernel,
        in_specs=[VMEM, pl.BlockSpec(memory_space=pl.ANY)],
        out_specs=[VMEM] * 2,
        out_shape=[
            jax.ShapeDtypeStruct((count, 2 * taps, taps), jnp.bfloat16),
            jax.ShapeDtypeStruct((8, LANES), jnp.float32),
        ],
        name="toeplitz",
        cost_estimate=pl.CostEstimate(
            flops=count * taps * taps * 64, bytes_accessed=4 * count * taps * taps, transcendentals=0
        ),
        compiler_params=pltpu.CompilerParams(vmem_limit_bytes=8 * MIB),
    )(filters, after)


def filter_grad_kernel(
    width, near_ref, own_ref, keep_ref, near_in_ref, extra_ref, far_in_ref, after_ref, out_ref, lines
):
    del after_ref
    taps, half = far_in_ref.shape
    per_group = LANES // width
    odd = lax.axis_index("ctx") % 2
    keep_far = keep_ref[odd]
    keep_near = keep_ref[1 - odd]
    lane_filter = iota((ROW_BLOCK, LANES), 1) // width
    fold = iota((ROW_BLOCK, taps), 1) + iota((ROW_BLOCK, taps), 0) < ROW_BLOCK
    for group in range(half // LANES):
        at = group * LANES
        cols = pl.ds(at, LANES)
        near = near_ref[:, cols]
        pairs = (
            (own_ref[:, cols], masked(far_in_ref[:, cols], keep_far), near),
            (near_in_ref[:, cols], masked(near, keep_near), extra_ref[:, cols]),
        )
        left, right = [], []
        for moving, beyond, fixed in pairs:
            window = jnp.concatenate([beyond, fixed], axis=0)
            for start in range(0, taps, ROW_BLOCK):
                piece = moving[start : start + ROW_BLOCK]
                left.append(
                    jnp.concatenate(
                        [jnp.where(lane_filter == i, piece, 0) for i in range(per_group)], axis=0
                    )
                )
                right.append(window[taps - ROW_BLOCK - start : 2 * taps - start])
        product = lax.dot_general(
            jnp.concatenate(left, axis=1),
            jnp.concatenate(right, axis=1),
            (((1,), (1,)), ((), ())),
            preferred_element_type=jnp.float32,
        )
        rows = []
        for i in range(per_group):
            tile = product[i * ROW_BLOCK : (i + 1) * ROW_BLOCK]
            high = jnp.concatenate(
                [tile[:, taps:], jnp.zeros((ROW_BLOCK, taps - ROW_BLOCK), jnp.float32)], axis=1
            )
            tile = jnp.where(fold, high, tile[:, :taps])
            tile = pltpu.roll(tile, taps - ROW_BLOCK + 1, 1, stride=1, stride_axis=0)
            rows.append(jnp.sum(tile, axis=0, keepdims=True))
        lines[group * per_group : (group + 1) * per_group] = jnp.concatenate(rows, axis=0)
    flip = jnp.where((iota((taps, taps), 0) + iota((taps, taps), 1)) % taps == 0, 1.0, 0.0)
    out_ref[...] = jnp.dot(
        lines[...], flip, preferred_element_type=jnp.float32, precision=lax.Precision.HIGHEST
    )


def filter_gradient(near, own, keep, near_in, extra, far_in, after, width):
    taps, half = own.shape
    count = half // width
    return pl.pallas_call(
        functools.partial(filter_grad_kernel, width),
        in_specs=[VMEM] * 6 + [pl.BlockSpec(memory_space=pl.ANY)],
        out_specs=VMEM,
        out_shape=jax.ShapeDtypeStruct((count, taps), jnp.float32),
        scratch_shapes=[pltpu.VMEM((count, taps), jnp.float32)],
        name="filter_gradient",
        cost_estimate=pl.CostEstimate(
            flops=4 * count * taps * taps * 256, bytes_accessed=16 * taps * half, transcendentals=0
        ),
        compiler_params=pltpu.CompilerParams(vmem_limit_bytes=8 * MIB),
    )(near, own, keep, near_in, extra, far_in, after)


def outputs_kernel(
    width, base, q_ref, k_ref, v_ref, ct_ref, tiles_ref, near_ref, far_ref, keep_ref,
    near_in_ref, far_in_ref, *rest,
):
    *results, sems = rest[-5:]
    *targets, done_ref = rest[-10:-5]
    out, grad_q, grad_k, grad_v = results
    taps, half = far_ref.shape
    channels = out.shape[1]
    per_group = LANES // width
    odd = lax.axis_index("ctx") % 2
    keep_far = keep_ref[odd]
    keep_near = keep_ref[1 - odd]
    second = odd if base < half else 1 - odd
    base = base % half
    first = pl.multiple_of(second * half, half)
    reverse = reversal(taps)
    copies = []

    def send(which, at, sem):
        own = pl.ds(at, CHUNK)
        cols = pl.ds(pl.multiple_of(first + base + at, CHUNK), CHUNK)
        copy = pltpu.make_async_copy(results[which].at[:, own], targets[which].at[:, cols], sem)
        copy.start()
        copies.append(copy)

    lines = []
    for lane in range(0, channels, LANES):
        sent = pl.ds(base + lane, LANES)
        near_lines = jnp.concatenate(
            [masked(far_in_ref[:, sent], keep_far).T, near_ref[:, sent].T], axis=1
        )
        far_lines = jnp.concatenate(
            [masked(near_in_ref[:, sent], keep_near).T, far_ref[:, sent].T], axis=1
        )
        lines.append((lane, near_lines, far_lines))
    sums = []
    for lane, near_lines, far_lines in lines:
        at = (first + base + lane) // width
        near_parts, far_parts = [], []
        for i in range(per_group):
            rows = slice(i * width, (i + 1) * width)
            both = jnp.concatenate([near_lines[rows], far_lines[rows]], axis=0)
            part = jnp.dot(both, tiles_ref[at + i], preferred_element_type=jnp.float32)
            near_parts.append(part[:width])
            far_parts.append(part[width:])
        near_sum = jnp.concatenate(near_parts, axis=0)
        far_sum = jnp.concatenate(far_parts, axis=0)
        y = jnp.where(odd == 1, far_sum, near_sum).T
        mixed = jnp.where(odd == 1, near_sum, far_sum).T
        sums.append((lane, y, mixed))
    for chunk in range(0, channels, CHUNK):
        whole = pl.ds(pl.multiple_of(first + base + chunk, CHUNK), CHUNK)
        k_turned = flipped(reverse, k_ref[:, whole])
        v_turned = flipped(reverse, v_ref[:, whole])
        k_parts, v_parts = [], []
        for lane, y, mixed in sums[chunk // LANES : (chunk + CHUNK) // LANES]:
            own = pl.ds(lane, LANES)
            cols = pl.ds(pl.multiple_of(first + base + lane, LANES), LANES)
            out[:, own] = (q_ref[:, cols].astype(jnp.float32) * y).astype(jnp.bfloat16)
            grad_q[:, own] = (ct_ref[:, cols].astype(jnp.float32) * y).astype(jnp.bfloat16)
            lanes = slice(lane - chunk, lane - chunk + LANES)
            k_parts.append((mixed * v_turned[:, lanes]).astype(jnp.bfloat16))
            v_parts.append((mixed * k_turned[:, lanes]).astype(jnp.bfloat16))
        own = pl.ds(chunk, CHUNK)
        turn = chunk // CHUNK
        send(0, chunk, sems.at[turn, 0])
        send(1, chunk, sems.at[turn, 1])
        grad_k[:, own] = flipped(reverse, jnp.concatenate(k_parts, axis=1)).astype(jnp.bfloat16)
        send(2, chunk, sems.at[turn, 2])
        grad_v[:, own] = flipped(reverse, jnp.concatenate(v_parts, axis=1)).astype(jnp.bfloat16)
        send(3, chunk, sems.at[turn, 3])
    for copy in copies:
        copy.wait()
    done_ref[...] = jnp.zeros_like(done_ref)


def outputs(piece, operands, results, after, width):
    taps, channels = operands[0].shape
    part = channels // PIECES
    anywhere = pl.BlockSpec(memory_space=pl.ANY)
    shape = jax.ShapeDtypeStruct((taps, channels), jnp.bfloat16)
    *results, done = pl.pallas_call(
        functools.partial(outputs_kernel, width, piece * part),
        in_specs=[VMEM] * len(operands) + [anywhere] * (1 + len(results)),
        out_specs=[anywhere] * 4 + [VMEM],
        out_shape=[shape] * 4 + [jax.ShapeDtypeStruct((8, LANES), jnp.float32)],
        input_output_aliases={len(operands) + 1 + i: i for i in range(len(results))},
        scratch_shapes=[pltpu.VMEM((taps, part), jnp.bfloat16)] * 4
        + [pltpu.SemaphoreType.DMA((part // CHUNK, 4))],
        name=f"outputs_{piece}",
        cost_estimate=pl.CostEstimate(
            flops=16 * (part // width) * taps * taps * 256,
            bytes_accessed=24 * taps * part,
            transcendentals=0,
        ),
        compiler_params=pltpu.CompilerParams(vmem_limit_bytes=8 * MIB),
    )(*operands, after, *results)
    return results, done


def per_device(gate_in, key_in, value_in, cotangent, doc_starts, filters):
    taps = filters.shape[1]
    width = gate_in.shape[2] // filters.shape[0]
    assert gate_in.shape[1] == taps
    q, k, v, ct = gate_in[0], key_in[0], value_in[0], cotangent[0]
    other = first_gate(q, k, v, ct)
    other_in = exchange(other, 1)
    q, k, v, ct, near_own, near_other, own = gates(other, q, k, v, ct)
    near_in_own = exchange(near_other, 0)
    extra = exchange(other, 0)
    own_in = exchange(own, 1)
    near_in_other = exchange(near_own, 0)
    keep = masks(doc_starts[0], near_other)
    mine = filter_gradient(near_own, own, keep, near_in_own, extra, other_in, near_in_other, width)
    halves = (
        (near_own, own, keep, near_in_own, other_in),
        (near_other, other, keep, near_in_other, own_in),
    )
    tiles = None
    results = []

    def beside(after, turn):
        nonlocal tiles, results
        if turn == 0:
            tiles, after = toeplitz(filters, after)
        elif turn <= PIECES:
            operands = (q, k, v, ct, tiles, *halves[turn - 1])
            results, after = outputs(turn - 1, operands, results, after, width)
        return after

    mine = sum_devices(mine, beside)
    filter_grad = join(mine, exchange(mine, 0))
    return tuple(array[None] for array in results) + (filter_grad,)


def solution(mesh):
    split = P("dp", "ctx", None)
    return jax.shard_map(
        per_device,
        mesh=mesh,
        in_specs=(split, split, split, split, P("dp", None), P()),
        out_specs=(split, split, split, split, P()),
        check_vma=False,
    )
```

```python
import functools

import jax
import jax.numpy as jnp
from jax import lax
from jax.experimental import pallas as pl
from jax.experimental.pallas import tpu as pltpu
from jax.sharding import PartitionSpec as P

LANES = 128
ROW_BLOCK = 64
MIB = 1024 * 1024
CHUNKS = 2
PIECES = 2
CHUNK = 1024
FIRST_VMEM = 213 * MIB // 4
GATES_VMEM = 101 * MIB // 2
VMEM = pl.BlockSpec(memory_space=pltpu.VMEM)
SMEM = pl.BlockSpec(memory_space=pltpu.SMEM)


def iota(shape, dim):
    return lax.broadcasted_iota(jnp.int32, shape, dim)


def exchange(array, first):
    seqs, blocks = lax.axis_size("dp"), lax.axis_size("ctx")
    pairs = []
    for seq in range(seqs):
        for block in range(blocks):
            to_seq, to_block = seq, (block - first ^ 1) + first
            if not 0 <= to_block < blocks:
                to_seq, to_block = seq ^ 1, block
            pairs.append((seq * blocks + block, to_seq * blocks + to_block))
    return lax.ppermute(array, ("dp", "ctx"), pairs)


def swapped(array, axis, step):
    size = lax.axis_size(axis)
    return lax.ppermute(array, axis, [(i, i ^ step) for i in range(size)])


def swapped(array, axis, step):
    size = lax.axis_size(axis)
    return lax.ppermute(array, axis, [(i, i ^ step) for i in range(size)])


def along(array, axis):
    size = lax.axis_size(axis)
    pairs = [(i, i + 2 if i % 2 else i - 2) for i in range(size)]
    return lax.ppermute(array, axis, [(i, j) for i, j in pairs if 0 <= j < size])


def add_kernel(*refs):
    *terms, _, out_ref = [ref for ref in refs]
    terms = [term[...] for term in terms]
    while len(terms) > 1:
        terms = [sum(terms[i + 1 : i + 2], terms[i]) for i in range(0, len(terms), 2)]
    out_ref[...] = terms[0]


def add(terms, after):
    return pl.pallas_call(
        add_kernel,
        in_specs=[VMEM] * len(terms) + [pl.BlockSpec(memory_space=pl.ANY)],
        out_specs=VMEM,
        out_shape=jax.ShapeDtypeStruct(terms[0].shape, terms[0].dtype),
        name="add",
        compiler_params=pltpu.CompilerParams(vmem_limit_bytes=MIB),
    )(*terms, after)


def sum_devices(mine, beside):
    turn = 0
    for axis, step in (("dp", 1), ("ctx", 2)):
        size = lax.axis_size(axis)
        while step < size:
            count = 4 if axis == "dp" and 4 * step <= size else 2
            others = [swapped(mine, axis, step * i) for i in range(1, count)]
            mine = add([mine] + others, beside(mine, turn))
            step, turn = count * step, turn + 1
    return mine


def join_kernel(mine_ref, other_ref, out_ref):
    count = mine_ref.shape[0]
    odd = lax.axis_index("ctx") % 2
    out_ref[pl.ds(pl.multiple_of(odd * count, count), count)] = mine_ref[...]
    out_ref[pl.ds(pl.multiple_of((1 - odd) * count, count), count)] = other_ref[...]


def join(mine, other):
    count, taps = mine.shape
    return pl.pallas_call(
        join_kernel,
        in_specs=[VMEM] * 2,
        out_specs=VMEM,
        out_shape=jax.ShapeDtypeStruct((2 * count, taps), mine.dtype),
        name="join",
        compiler_params=pltpu.CompilerParams(vmem_limit_bytes=MIB),
    )(mine, other)


def reversal(taps):
    flip = iota((taps, taps), 0) + iota((taps, taps), 1) == taps - 1
    return jnp.where(flip, 1.0, 0.0).astype(jnp.bfloat16)


def flipped(reverse, array):
    return jnp.dot(reverse, array, preferred_element_type=jnp.float32)


def masked(array, keep):
    return array * jnp.concatenate([keep] * (array.shape[0] // keep.shape[0]), axis=0)


def bf16_product(one, two):
    return (one.astype(jnp.float32) * two.astype(jnp.float32)).astype(jnp.bfloat16)


def first_kernel(q_hbm, k_hbm, v_hbm, ct_hbm, other_ref, held, sems):
    taps, half = other_ref.shape
    block = half // CHUNKS
    odd = lax.axis_index("ctx") % 2 == 1
    reverse = reversal(taps)

    def make(sources, start, finish):
        copies = []
        for c in range(CHUNKS):
            for a, source in enumerate(sources):
                copy = pltpu.make_async_copy(
                    source.at[:, pl.ds(start + c * block, block)],
                    held.at[a, :, pl.ds(c * block, block)],
                    sems.at[c, a],
                )
                copy.start()
                copies.append(copy)
        for copy in copies:
            copy.wait()
        other_ref[...] = finish(bf16_product(held[0], held[1]))

    @pl.when(odd)
    def _():
        make((k_hbm, v_hbm), 0, lambda u: u)

    @pl.when(jnp.logical_not(odd))
    def _():
        make((ct_hbm, q_hbm), half, lambda dy: flipped(reverse, dy).astype(jnp.bfloat16))


def first_gate(q, k, v, ct):
    taps, channels = q.shape
    half = channels // 2
    return pl.pallas_call(
        first_kernel,
        in_specs=[pl.BlockSpec(memory_space=pltpu.HBM)] * 4,
        out_specs=VMEM,
        out_shape=jax.ShapeDtypeStruct((taps, half), jnp.bfloat16),
        scratch_shapes=[
            pltpu.VMEM((2, taps, half), jnp.bfloat16),
            pltpu.SemaphoreType.DMA((CHUNKS, 2)),
        ],
        name="first_gate",
        cost_estimate=pl.CostEstimate(
            flops=taps * taps * channels, bytes_accessed=3 * taps * channels, transcendentals=0
        ),
        compiler_params=pltpu.CompilerParams(vmem_limit_bytes=FIRST_VMEM),
    )(q, k, v, ct)


def gates_kernel(
    after_ref, q_hbm, k_hbm, v_hbm, ct_hbm,
    q_ref, k_ref, v_ref, ct_ref, near_own_ref, near_other_ref, own_ref, sems,
):
    del after_ref
    taps, channels = q_ref.shape
    half = channels // 2
    block = channels // CHUNKS
    pairs = ((k_hbm, k_ref), (v_hbm, v_ref), (q_hbm, q_ref), (ct_hbm, ct_ref))
    copies = []
    for c in range(CHUNKS):
        cols = pl.ds(c * block, block)
        for a, (source, target) in enumerate(pairs):
            copy = pltpu.make_async_copy(source.at[:, cols], target.at[:, cols], sems.at[c, a])
            copy.start()
            copies.append(copy)
    odd = lax.axis_index("ctx") % 2 == 1
    reverse = reversal(taps)
    for c in range(CHUNKS):
        cols = pl.ds(c * block, block)
        sent = pl.ds(c * block % half, block)
        for copy in copies[4 * c : 4 * c + 4]:
            copy.wait()

        def make_u():
            return bf16_product(k_ref[:, cols], v_ref[:, cols])

        def make_dy():
            dy = bf16_product(ct_ref[:, cols], q_ref[:, cols])
            return flipped(reverse, dy).astype(jnp.bfloat16)

        @pl.when(odd)
        def _():
            near_ref = near_own_ref if c * block >= half else near_other_ref
            near_ref[:, sent] = make_dy()
            if c * block >= half:
                own_ref[:, sent] = make_u()

        @pl.when(jnp.logical_not(odd))
        def _():
            near_ref = near_own_ref if c * block < half else near_other_ref
            near_ref[:, sent] = make_u()
            if c * block < half:
                own_ref[:, sent] = make_dy()


def gates(after, q, k, v, ct):
    taps, channels = q.shape

    def shape(*dims):
        return jax.ShapeDtypeStruct(dims, jnp.bfloat16)

    half = channels // 2
    return pl.pallas_call(
        gates_kernel,
        in_specs=[pl.BlockSpec(memory_space=pl.ANY)]
        + [pl.BlockSpec(memory_space=pltpu.HBM)] * 4,
        out_specs=[VMEM] * 7,
        out_shape=[shape(taps, channels)] * 4 + [shape(taps, half)] * 3,
        scratch_shapes=[pltpu.SemaphoreType.DMA((CHUNKS, 4))],
        name="gates",
        cost_estimate=pl.CostEstimate(
            flops=2 * taps * taps * channels, bytes_accessed=12 * taps * channels, transcendentals=0
        ),
        compiler_params=pltpu.CompilerParams(vmem_limit_bytes=GATES_VMEM),
    )(after, q, k, v, ct)


def masks_kernel(taps, starts_ref, after_ref, keep_ref):
    del after_ref
    here = lax.axis_index("ctx")
    for side in range(2):
        found = (here + side) % lax.axis_size("ctx") == 0
        for d in range(starts_ref.shape[0]):
            found = jnp.logical_or(found, starts_ref[d] == (here + side) * taps)
        keep = jnp.where(found, 0.0, 1.0)
        keep_ref[side] = jnp.full(keep_ref.shape[1:], keep).astype(jnp.bfloat16)


def masks(starts, after):
    return pl.pallas_call(
        functools.partial(masks_kernel, after.shape[0]),
        in_specs=[SMEM, pl.BlockSpec(memory_space=pl.ANY)],
        out_specs=VMEM,
        out_shape=jax.ShapeDtypeStruct((2, 16, LANES), jnp.bfloat16),
        name="masks",
        compiler_params=pltpu.CompilerParams(vmem_limit_bytes=MIB),
    )(starts, after)


def toeplitz_kernel(filters_ref, after_ref, out_ref, done_ref):
    del after_ref
    count, taps = filters_ref.shape
    lines = filters_ref[...].astype(jnp.float32)
    current = iota((taps, taps), 0) <= iota((taps, taps), 1)
    for f in range(count):
        tile = jnp.broadcast_to(lines[f : f + 1], (taps, taps))
        tile = pltpu.roll(tile, 0, 1, stride=1, stride_axis=0)
        out_ref[f, :taps] = jnp.where(current, 0.0, tile).astype(jnp.bfloat16)
        out_ref[f, taps:] = jnp.where(current, tile, 0.0).astype(jnp.bfloat16)
    done_ref[...] = jnp.zeros_like(done_ref)


def toeplitz(filters, after):
    count, taps = filters.shape
    return pl.pallas_call(
        toeplitz_kernel,
        in_specs=[VMEM, pl.BlockSpec(memory_space=pl.ANY)],
        out_specs=[VMEM] * 2,
        out_shape=[
            jax.ShapeDtypeStruct((count, 2 * taps, taps), jnp.bfloat16),
            jax.ShapeDtypeStruct((8, LANES), jnp.float32),
        ],
        name="toeplitz",
        cost_estimate=pl.CostEstimate(
            flops=count * taps * taps * 64, bytes_accessed=4 * count * taps * taps, transcendentals=0
        ),
        compiler_params=pltpu.CompilerParams(vmem_limit_bytes=8 * MIB),
    )(filters, after)


def filter_grad_kernel(
    width, near_ref, own_ref, keep_ref, near_in_ref, extra_ref, far_in_ref, after_ref, out_ref, lines
):
    del after_ref
    taps, half = far_in_ref.shape
    per_group = LANES // width
    odd = lax.axis_index("ctx") % 2
    keep_far = keep_ref[odd]
    keep_near = keep_ref[1 - odd]
    lane_filter = iota((ROW_BLOCK, LANES), 1) // width
    fold = iota((ROW_BLOCK, taps), 1) + iota((ROW_BLOCK, taps), 0) < ROW_BLOCK
    for group in range(half // LANES):
        at = group * LANES
        cols = pl.ds(at, LANES)
        near = near_ref[:, cols]
        pairs = (
            (own_ref[:, cols], masked(far_in_ref[:, cols], keep_far), near),
            (near_in_ref[:, cols], masked(near, keep_near), extra_ref[:, cols]),
        )
        left, right = [], []
        for moving, beyond, fixed in pairs:
            window = jnp.concatenate([beyond, fixed], axis=0)
            for start in range(0, taps, ROW_BLOCK):
                piece = moving[start : start + ROW_BLOCK]
                left.append(
                    jnp.concatenate(
                        [jnp.where(lane_filter == i, piece, 0) for i in range(per_group)], axis=0
                    )
                )
                right.append(window[taps - ROW_BLOCK - start : 2 * taps - start])
        product = lax.dot_general(
            jnp.concatenate(left, axis=1),
            jnp.concatenate(right, axis=1),
            (((1,), (1,)), ((), ())),
            preferred_element_type=jnp.float32,
        )
        rows = []
        for i in range(per_group):
            tile = product[i * ROW_BLOCK : (i + 1) * ROW_BLOCK]
            high = jnp.concatenate(
                [tile[:, taps:], jnp.zeros((ROW_BLOCK, taps - ROW_BLOCK), jnp.float32)], axis=1
            )
            tile = jnp.where(fold, high, tile[:, :taps])
            tile = pltpu.roll(tile, taps - ROW_BLOCK + 1, 1, stride=1, stride_axis=0)
            rows.append(jnp.sum(tile, axis=0, keepdims=True))
        lines[group * per_group : (group + 1) * per_group] = jnp.concatenate(rows, axis=0)
    flip = jnp.where((iota((taps, taps), 0) + iota((taps, taps), 1)) % taps == 0, 1.0, 0.0)
    out_ref[...] = jnp.dot(
        lines[...], flip, preferred_element_type=jnp.float32, precision=lax.Precision.HIGHEST
    )


def filter_gradient(near, own, keep, near_in, extra, far_in, after, width):
    taps, half = own.shape
    count = half // width
    return pl.pallas_call(
        functools.partial(filter_grad_kernel, width),
        in_specs=[VMEM] * 6 + [pl.BlockSpec(memory_space=pl.ANY)],
        out_specs=VMEM,
        out_shape=jax.ShapeDtypeStruct((count, taps), jnp.float32),
        scratch_shapes=[pltpu.VMEM((count, taps), jnp.float32)],
        name="filter_gradient",
        cost_estimate=pl.CostEstimate(
            flops=4 * count * taps * taps * 256, bytes_accessed=16 * taps * half, transcendentals=0
        ),
        compiler_params=pltpu.CompilerParams(vmem_limit_bytes=8 * MIB),
    )(near, own, keep, near_in, extra, far_in, after)


def outputs_kernel(
    width, base, q_ref, k_ref, v_ref, ct_ref, tiles_ref, near_ref, far_ref, keep_ref,
    near_in_ref, far_in_ref, *rest,
):
    *results, sems = rest[-5:]
    *targets, done_ref = rest[-10:-5]
    out, grad_q, grad_k, grad_v = results
    taps, half = far_ref.shape
    channels = out.shape[1]
    per_group = LANES // width
    odd = lax.axis_index("ctx") % 2
    keep_far = keep_ref[odd]
    keep_near = keep_ref[1 - odd]
    second = odd if base < half else 1 - odd
    base = base % half
    first = pl.multiple_of(second * half, half)
    reverse = reversal(taps)
    copies = []

    def send(which, at, sem):
        own = pl.ds(at, CHUNK)
        cols = pl.ds(pl.multiple_of(first + base + at, CHUNK), CHUNK)
        copy = pltpu.make_async_copy(results[which].at[:, own], targets[which].at[:, cols], sem)
        copy.start()
        copies.append(copy)

    lines = []
    for lane in range(0, channels, LANES):
        sent = pl.ds(base + lane, LANES)
        near_lines = jnp.concatenate(
            [masked(far_in_ref[:, sent], keep_far).T, near_ref[:, sent].T], axis=1
        )
        far_lines = jnp.concatenate(
            [masked(near_in_ref[:, sent], keep_near).T, far_ref[:, sent].T], axis=1
        )
        lines.append((lane, near_lines, far_lines))
    sums = []
    for lane, near_lines, far_lines in lines:
        at = (first + base + lane) // width
        near_parts, far_parts = [], []
        for i in range(per_group):
            rows = slice(i * width, (i + 1) * width)
            both = jnp.concatenate([near_lines[rows], far_lines[rows]], axis=0)
            part = jnp.dot(both, tiles_ref[at + i], preferred_element_type=jnp.float32)
            near_parts.append(part[:width])
            far_parts.append(part[width:])
        near_sum = jnp.concatenate(near_parts, axis=0)
        far_sum = jnp.concatenate(far_parts, axis=0)
        y = jnp.where(odd == 1, far_sum, near_sum).T
        mixed = jnp.where(odd == 1, near_sum, far_sum).T
        sums.append((lane, y, mixed))
    for chunk in range(0, channels, CHUNK):
        whole = pl.ds(pl.multiple_of(first + base + chunk, CHUNK), CHUNK)
        k_turned = flipped(reverse, k_ref[:, whole])
        v_turned = flipped(reverse, v_ref[:, whole])
        k_parts, v_parts = [], []
        for lane, y, mixed in sums[chunk // LANES : (chunk + CHUNK) // LANES]:
            own = pl.ds(lane, LANES)
            cols = pl.ds(pl.multiple_of(first + base + lane, LANES), LANES)
            out[:, own] = (q_ref[:, cols].astype(jnp.float32) * y).astype(jnp.bfloat16)
            grad_q[:, own] = (ct_ref[:, cols].astype(jnp.float32) * y).astype(jnp.bfloat16)
            lanes = slice(lane - chunk, lane - chunk + LANES)
            k_parts.append((mixed * v_turned[:, lanes]).astype(jnp.bfloat16))
            v_parts.append((mixed * k_turned[:, lanes]).astype(jnp.bfloat16))
        own = pl.ds(chunk, CHUNK)
        turn = chunk // CHUNK
        send(0, chunk, sems.at[turn, 0])
        send(1, chunk, sems.at[turn, 1])
        grad_k[:, own] = flipped(reverse, jnp.concatenate(k_parts, axis=1)).astype(jnp.bfloat16)
        send(2, chunk, sems.at[turn, 2])
        grad_v[:, own] = flipped(reverse, jnp.concatenate(v_parts, axis=1)).astype(jnp.bfloat16)
        send(3, chunk, sems.at[turn, 3])
    for copy in copies:
        copy.wait()
    done_ref[...] = jnp.zeros_like(done_ref)


def outputs(piece, operands, results, after, width):
    taps, channels = operands[0].shape
    part = channels // PIECES
    anywhere = pl.BlockSpec(memory_space=pl.ANY)
    shape = jax.ShapeDtypeStruct((taps, channels), jnp.bfloat16)
    *results, done = pl.pallas_call(
        functools.partial(outputs_kernel, width, piece * part),
        in_specs=[VMEM] * len(operands) + [anywhere] * (1 + len(results)),
        out_specs=[anywhere] * 4 + [VMEM],
        out_shape=[shape] * 4 + [jax.ShapeDtypeStruct((8, LANES), jnp.float32)],
        input_output_aliases={len(operands) + 1 + i: i for i in range(len(results))},
        scratch_shapes=[pltpu.VMEM((taps, part), jnp.bfloat16)] * 4
        + [pltpu.SemaphoreType.DMA((part // CHUNK, 4))],
        name=f"outputs_{piece}",
        cost_estimate=pl.CostEstimate(
            flops=16 * (part // width) * taps * taps * 256,
            bytes_accessed=24 * taps * part,
            transcendentals=0,
        ),
        compiler_params=pltpu.CompilerParams(vmem_limit_bytes=8 * MIB),
    )(*operands, after, *results)
    return results, done


def per_device(gate_in, key_in, value_in, cotangent, doc_starts, filters):
    taps = filters.shape[1]
    width = gate_in.shape[2] // filters.shape[0]
    assert gate_in.shape[1] == taps
    q, k, v, ct = gate_in[0], key_in[0], value_in[0], cotangent[0]
    other = first_gate(q, k, v, ct)
    other_in = exchange(other, 1)
    q, k, v, ct, near_own, near_other, own = gates(other, q, k, v, ct)
    near_in_own = exchange(near_other, 0)
    extra = exchange(other, 0)
    own_in = exchange(own, 1)
    near_in_other = exchange(near_own, 0)
    keep = masks(doc_starts[0], near_other)
    mine = filter_gradient(near_own, own, keep, near_in_own, extra, other_in, near_in_other, width)
    halves = (
        (near_own, own, keep, near_in_own, other_in),
        (near_other, other, keep, near_in_other, own_in),
    )
    tiles = None
    results = []

    def beside(after, turn):
        nonlocal tiles, results
        if turn == 0:
            tiles, after = toeplitz(filters, after)
        elif turn <= PIECES:
            operands = (q, k, v, ct, tiles, *halves[turn - 1])
            results, after = outputs(turn - 1, operands, results, after, width)
        return after

    mine = sum_devices(mine, beside)
    filter_grad = join(mine, exchange(mine, 0))
    return tuple(array[None] for array in results) + (filter_grad,)


def solution(mesh):
    split = P("dp", "ctx", None)
    return jax.shard_map(
        per_device,
        mesh=mesh,
        in_specs=(split, split, split, split, P("dp", None), P()),
        out_specs=(split, split, split, split, P()),
        check_vma=False,
    )
```
